32 devices in a mesh: section: 2 (over core), dp: 4 (over z), mp: 4 (over y, x).
Axes of the slice: x: 2, y: 2, z: 4, core: 2. Of those that a mesh axis runs over, the one named last changes fastest.
Arguments:
- inputs: bfloat16 [8192, 768], P(('dp', 'mp')), may hold values from -6 to 6
- cotangent: bfloat16 [8192, 768], P(('dp', 'mp')), may hold values from -6 to 6
- doc_ids: int32 [8192], P('dp'), may hold values from -1 to 3, as said below
- norm_gain: float32 [2, 768], P('section'), may hold values from 0.25 to 1.75
- norm_bias: float32 [2, 768], P('section'), may hold values from -1.5 to 1.5
- w_query: bfloat16 [2, 768, 768], P('section', 'dp', 'mp'), may hold values from -0.21875 to 0.21875
- w_key: bfloat16 [2, 768, 768], P('section', 'dp', 'mp'), may hold values from -0.21875 to 0.21875
- w_value: bfloat16 [2, 768, 768], P('section', 'dp', 'mp'), may hold values from -0.21875 to 0.21875
- inner_gain: float32 [2, 768], P('section', 'mp'), may hold values from 0.25 to 1.75
- inner_bias: float32 [2, 768], P('section', 'mp'), may hold values from -1.5 to 1.5
- w_output: bfloat16 [2, 768, 768], P('section', 'mp', 'dp'), may hold values from -0.21875 to 0.21875
- feed_gain: float32 [2, 768], P('section'), may hold values from 0.25 to 1.75
- feed_bias: float32 [2, 768], P('section'), may hold values from -1.5 to 1.5
- w_up: bfloat16 [2, 768, 3072], P('section', 'dp', 'mp'), may hold values from -0.21875 to 0.21875
- middle_gain: float32 [2, 3072], P('section', 'mp'), may hold values from 0.25 to 1.75
- middle_bias: float32 [2, 3072], P('section', 'mp'), may hold values from -1.5 to 1.5
- w_down: bfloat16 [2, 3072, 768], P('section', 'mp', 'dp'), may hold values from -0.109375 to 0.109375
Outputs:
- layer_outputs: bfloat16 [2, 8192, 768], P('section', ('dp', 'mp'))
- input_grads: bfloat16 [2, 8192, 768], P('section', ('dp', 'mp'))
- grad_norm_gain: float32 [2, 768], P('section', ('dp', 'mp'))
- grad_norm_bias: float32 [2, 768], P('section', ('dp', 'mp'))
- grad_query: float32 [2, 768, 768], P('section', 'dp', 'mp')
- grad_key: float32 [2, 768, 768], P('section', 'dp', 'mp')
- grad_value: float32 [2, 768, 768], P('section', 'dp', 'mp')
- grad_inner_gain: float32 [2, 768], P('section', ('mp', 'dp'))
- grad_inner_bias: float32 [2, 768], P('section', ('mp', 'dp'))
- grad_output: float32 [2, 768, 768], P('section', 'mp', 'dp')
- grad_feed_gain: float32 [2, 768], P('section', ('dp', 'mp'))
- grad_feed_bias: float32 [2, 768], P('section', ('dp', 'mp'))
- grad_up: float32 [2, 768, 3072], P('section', 'dp', 'mp')
- grad_middle_gain: float32 [2, 3072], P('section', ('mp', 'dp'))
- grad_middle_bias: float32 [2, 3072], P('section', ('mp', 'dp'))
- grad_down: float32 [2, 3072, 768], P('section', 'mp', 'dp')
The draws below stay inside these ranges and needn't reach their ends.
Inputs may be any that keep to these rules, and one draw needn't show every extreme that they name: `doc_ids`: along the 1024 rows of each micro-batch document numbers never fall; padding rows (-1) come last; each micro-batch holds documents 0 to 3 and some padding, and document 2 starts within the first 256 rows and ends within the last 256 rows.
All inputs are finite; a program needn't handle non-finite values.
Results may differ from the reference program's by a relative error of at most 0.028.
Values may be sent and summed in bfloat16 or wider, within the bound.
No kernel may reach another device: no remote copies, remote signals or barrier semaphores. Data moves between devices by JAX's collectives and lax.ppermute only.
A program may use at most 192 MiB of HBM per device.

```python
import jax
import jax.numpy as jnp
from jax import lax

D = 768
HEADS = 12
HEAD_DIM = 64
FF = 3072
LAYERS = 2
MICRO = 2
SLICE = 256
ROWS = 1024
TOKENS = 8192
N_DP = 4
N_MP = 4


def draw_doc_ids(key, part):
    key = jax.random.fold_in(key, 7)
    batch_count = TOKENS // ROWS
    quarter = max(SLICE // 4, 2)
    key_list = jax.random.split(key, 4)
    head_one = jax.random.randint(key_list[0], (batch_count, 1), 1, quarter + 1)
    head_two = jax.random.randint(key_list[1], (batch_count, 1), 1, quarter + 1)
    tail_len = jax.random.randint(key_list[2], (batch_count, 1), 1, quarter + 1)
    pad_len = jax.random.randint(key_list[3], (batch_count, 1), 1, quarter + 1)
    position = jnp.arange(ROWS, dtype=jnp.int32)[None, :]
    long_end = ROWS - pad_len - tail_len
    labels = (position >= head_one).astype(jnp.int32) + (position >= head_one + head_two).astype(jnp.int32) + (position >= long_end).astype(jnp.int32)
    labels = jnp.where(position >= ROWS - pad_len, -1, labels).astype(jnp.int32)
    lane_count = ROWS // SLICE
    group_count = batch_count // MICRO
    return labels.reshape(group_count, MICRO, lane_count, SLICE).transpose(0, 2, 1, 3).reshape(TOKENS)


def shard_levels(own_key, shape, cuts, smallest, top_value):
    def one(axis_at, blocks):
        draws = jax.random.uniform(jax.random.fold_in(jax.random.fold_in(own_key, 6), axis_at), (blocks,), jnp.float32, smallest / len(cuts), top_value / len(cuts))
        return jnp.repeat(jnp.exp(draws), shape[axis_at] // blocks).reshape((-1,) + (1,) * (len(shape) - axis_at - 1))

    loudness = one(*cuts[0])
    for cut in cuts[1:]:
        loudness = loudness * one(*cut)
    return loudness


def scatter_about(key, shape, deviation, reach, pieces=(), kind=jnp.bfloat16):
    drawn = jax.random.normal(key, shape, jnp.float32) * deviation
    if len(pieces) > 0:
        drawn = shard_levels(key, shape, pieces, -0.22, 0.18) * drawn
    return jnp.clip(drawn, min=-reach, max=reach).astype(kind)


def setup_inputs(seed: int = 0) -> dict:
    keys = jax.random.split(jax.random.key(seed), 18)
    inputs = scatter_about(keys[0], (TOKENS, D), 1.0, 6.0, ((0, 16),))
    cotangent = scatter_about(keys[1], (TOKENS, D), 1.0, 6.0, ((0, 16),))
    doc_ids = draw_doc_ids(jax.random.fold_in(keys[17], 71), 0)
    norm_gain = jnp.clip(1.0 + 0.15 * jax.random.normal(keys[3], (LAYERS, D), jnp.float32), 0.25, 1.75)
    norm_bias = scatter_about(keys[4], (LAYERS, D), 0.3, 1.5, ((0, 2),), jnp.float32)
    w_query = scatter_about(keys[5], (LAYERS, D, D), D ** -0.5, 0.21875, ((0, 2), (1, 4), (2, 4)))
    w_key = scatter_about(keys[6], (LAYERS, D, D), D ** -0.5, 0.21875, ((0, 2), (1, 4), (2, 4)))
    w_value = scatter_about(keys[7], (LAYERS, D, D), D ** -0.5, 0.21875, ((0, 2), (1, 4), (2, 4)))
    inner_gain = jnp.clip(1.0 + 0.15 * jax.random.normal(keys[8], (LAYERS, D), jnp.float32), 0.25, 1.75)
    inner_bias = scatter_about(keys[9], (LAYERS, D), 0.3, 1.5, ((0, 2), (1, 4)), jnp.float32)
    w_output = scatter_about(keys[10], (LAYERS, D, D), D ** -0.5, 0.21875, ((0, 2), (1, 4), (2, 4)))
    feed_gain = jnp.clip(1.0 + 0.15 * jax.random.normal(keys[11], (LAYERS, D), jnp.float32), 0.25, 1.75)
    feed_bias = scatter_about(keys[12], (LAYERS, D), 0.3, 1.5, ((0, 2),), jnp.float32)
    w_up = scatter_about(keys[13], (LAYERS, D, FF), D ** -0.5, 0.21875, ((0, 2), (1, 4), (2, 4)))
    middle_gain = jnp.clip(1.0 + 0.15 * jax.random.normal(keys[14], (LAYERS, FF), jnp.float32), 0.25, 1.75)
    middle_bias = scatter_about(keys[15], (LAYERS, FF), 0.3, 1.5, ((0, 2), (1, 4)), jnp.float32)
    w_down = scatter_about(keys[16], (LAYERS, FF, D), FF ** -0.5, 0.109375, ((0, 2), (1, 4), (2, 4)))
    return dict(inputs=inputs, cotangent=cotangent, doc_ids=doc_ids, norm_gain=norm_gain, norm_bias=norm_bias, w_query=w_query, w_key=w_key, w_value=w_value, inner_gain=inner_gain, inner_bias=inner_bias, w_output=w_output, feed_gain=feed_gain, feed_bias=feed_bias, w_up=w_up, middle_gain=middle_gain, middle_bias=middle_bias, w_down=w_down)


EPS = 1e-05

@jax.custom_vjp
def low(v):
    return lax.optimization_barrier(v.astype(jnp.bfloat16)).astype(jnp.float32)

@jax.custom_vjp
def low_back(v):
    return v

def low_keep(v):
    return (low(v), None)

def low_pass(kept, grad):
    return (grad,)

def back_keep(v):
    return (v, None)

def back_low(kept, grad):
    return (low(grad),)
low.defvjp(low_keep, low_pass)
low_back.defvjp(back_keep, back_low)

def norm_rows(values, gain_vec, bias_vec):
    row_mean = lax.optimization_barrier(jnp.mean(values, axis=-1, keepdims=True))
    spread = lax.optimization_barrier(jnp.mean(values * values, axis=-1, keepdims=True)) - row_mean * row_mean
    return (values - row_mean) * lax.rsqrt(spread + EPS) * gain_vec + bias_vec

def exact(first_mat, second_mat):
    return jnp.dot(first_mat, second_mat, precision=lax.Precision.HIGHEST, preferred_element_type=jnp.float32)

def layer(layer_in, labels, params):
    norm_gain, norm_bias, w_query, w_key, w_value, inner_gain, inner_bias, w_output, feed_gain, feed_bias, w_up, middle_gain, middle_bias, w_down = params
    row_count = layer_in.shape[0]
    score_scale = HEAD_DIM ** (-0.5)
    head_rows = low(norm_rows(layer_in, norm_gain, norm_bias))
    query = low_back(low(exact(head_rows, w_query))).reshape(row_count, HEADS, HEAD_DIM)
    key_rows = low_back(low(exact(head_rows, w_key))).reshape(row_count, HEADS, HEAD_DIM)
    value_rows = low_back(low(exact(head_rows, w_value))).reshape(row_count, HEADS, HEAD_DIM)
    block_len = min(512, row_count)

    def attend(row_start):
        query_block = lax.dynamic_slice_in_dim(query, row_start, block_len, 0)
        label_block = lax.dynamic_slice_in_dim(labels, row_start, block_len, 0)
        scores = low_back(score_scale * jnp.einsum('qhd,khd->hqk', query_block, key_rows, precision=lax.Precision.HIGHEST))
        allowed = (label_block[:, None] == labels[None, :])[None]
        prob_block = low(jax.nn.softmax(jnp.where(allowed, scores, -1e+30), axis=-1))
        return jnp.einsum('hqk,khd->qhd', prob_block, value_rows, precision=lax.Precision.HIGHEST)
    row_starts = jnp.arange(row_count // block_len, dtype=jnp.int32) * block_len
    mixed = low_back(lax.map(jax.checkpoint(attend), row_starts).reshape(row_count, D))
    inner_rows = low(norm_rows(mixed, inner_gain, inner_bias))
    mid_input = layer_in + low_back(exact(inner_rows, w_output))
    feed_rows = low(norm_rows(mid_input, feed_gain, feed_bias))
    pre_act = low_back(exact(feed_rows, w_up))
    middle_rows = low(norm_rows(jax.nn.gelu(pre_act, approximate=False), middle_gain, middle_bias))
    result = mid_input + low_back(exact(middle_rows, w_down))
    row_mask = (labels >= 0).astype(jnp.float32)[:, None]
    return row_mask * result

def to_batches(array):
    return array.reshape(N_DP, N_MP, MICRO, SLICE, D).transpose(0, 2, 1, 3, 4).reshape(N_DP * MICRO, ROWS, D)

def from_batches(stacked):
    return stacked.reshape(N_DP, MICRO, N_MP, SLICE, D).transpose(0, 2, 1, 3, 4).reshape(TOKENS, D)

def reference(inputs, cotangent, doc_ids, norm_gain, norm_bias, w_query, w_key, w_value, inner_gain, inner_bias, w_output, feed_gain, feed_bias, w_up, middle_gain, middle_bias, w_down):
    weights = tuple((item.astype(jnp.float32) for item in (norm_gain, norm_bias, w_query, w_key, w_value, inner_gain, inner_bias, w_output, feed_gain, feed_bias, w_up, middle_gain, middle_bias, w_down)))
    lower_params = tuple((item[0] for item in weights))
    upper_params = tuple((item[1] for item in weights))
    zero_grads = tuple((jnp.zeros_like(item) for item in lower_params))
    input_batches = to_batches(inputs.astype(jnp.float32))
    cot_batches = to_batches(cotangent.astype(jnp.float32))
    label_batches = doc_ids.reshape(N_DP, N_MP, MICRO, SLICE).transpose(0, 2, 1, 3).reshape(N_DP * MICRO, ROWS)

    def one_batch(carry, item):
        batch_in, batch_cot, labels = item

        def run_layer(params, layer_in):
            return low(layer(layer_in, labels, params))
        mid_out, lower_back = jax.vjp(run_layer, lower_params, batch_in)
        top_out, upper_back = jax.vjp(run_layer, upper_params, mid_out)
        upper_grads, mid_grad = upper_back(batch_cot)
        mid_grad = low(mid_grad)
        lower_grads, in_grad = lower_back(mid_grad)
        in_grad = low(in_grad)
        carry = (jax.tree.map(jnp.add, carry[0], lower_grads), jax.tree.map(jnp.add, carry[1], upper_grads))
        return (carry, (mid_out, top_out, in_grad, mid_grad))
    (lower_sum, upper_sum), (mid_all, top_all, in_all, grad_all) = lax.scan(one_batch, (zero_grads, zero_grads), (input_batches, cot_batches, label_batches))
    layer_outputs = jnp.stack([from_batches(mid_all), from_batches(top_all)]).astype(jnp.bfloat16)
    input_grads = jnp.stack([from_batches(in_all), from_batches(grad_all)]).astype(jnp.bfloat16)
    grads = tuple((jnp.stack([lower_item, upper_item]) for lower_item, upper_item in zip(lower_sum, upper_sum)))
    return (layer_outputs, input_grads, grads[0], grads[1], grads[2], grads[3], grads[4], grads[5], grads[6], grads[7], grads[8], grads[9], grads[10], grads[11], grads[12], grads[13])
```

```python
from functools import partial

import jax
import jax.numpy as jnp
from jax import lax
from jax.sharding import PartitionSpec as P

D = 768
HEAD_DIM = 64
FF = 3072
MICRO = 2
LANES = 4

EPS = 1e-05
SCALE = HEAD_DIM ** (-0.5)
BOTH = ("section", "mp")
Y_PAIRS = [[0, 2], [1, 3]]


def core_swap(x):
    return lax.ppermute(x, "section", [(0, 1), (1, 0)])


def x_swap(x):
    return lax.ppermute(x, "mp", [(i, i ^ 1) for i in range(LANES)])


def layer_norm(values, gain_vec, bias_vec):
    row_mean = jnp.mean(values, axis=-1, keepdims=True)
    spread = jnp.mean(values * values, axis=-1, keepdims=True) - row_mean * row_mean
    return (values - row_mean) * lax.rsqrt(spread + EPS) * gain_vec + bias_vec


def dot_plain(first_mat, second_mat):
    return jnp.dot(first_mat, second_mat, preferred_element_type=jnp.float32)


def dot_second_turned(first_mat, second_mat):
    return lax.dot_general(
        first_mat, second_mat, (((1,), (1,)), ((), ())), preferred_element_type=jnp.float32
    )


def dot_first_turned(first_mat, second_mat):
    return lax.dot_general(
        first_mat, second_mat, (((0,), (0,)), ((), ())), preferred_element_type=jnp.float32
    )


def spread_rows(own):
    far = x_swap(own)
    return jnp.concatenate([own, core_swap(own), far, core_swap(far)], axis=0)


def settle_rows(partial_rows):
    parts = partial_rows.astype(jnp.bfloat16).reshape(4, -1, partial_rows.shape[-1])
    far = (parts[2].astype(jnp.float32) + core_swap(parts[3]).astype(jnp.float32)).astype(
        jnp.bfloat16
    )
    far = x_swap(far)
    near = parts[0].astype(jnp.float32) + core_swap(parts[1]).astype(jnp.float32)
    return near + far.astype(jnp.float32)


def turned(parts):
    return parts


def row_totals(*totals):
    stacked = jnp.stack(totals).reshape(len(totals), 2, 2, -1)
    stacked = stacked + core_swap(stacked)[:, :, ::-1]
    stacked = stacked + x_swap(stacked)[:, ::-1]
    return tuple(stacked.reshape(len(totals), -1))


def split_norm(values, gain_vec, bias_vec, feature_count):
    total_one, total_two = row_totals(jnp.sum(values, axis=-1), jnp.sum(values * values, axis=-1))
    row_mean = total_one[:, None] / feature_count
    spread = total_two[:, None] / feature_count - row_mean * row_mean
    scaled = lax.rsqrt(spread + EPS)
    normal = (values - row_mean) * scaled
    return (normal * gain_vec + bias_vec, normal, scaled)


def split_norm_back(upstream, normal, scaled, gain_vec, feature_count):
    inner_grad = upstream * gain_vec
    total_one, total_two = row_totals(
        jnp.sum(inner_grad, axis=-1), jnp.sum(inner_grad * normal, axis=-1)
    )
    back_grad = scaled * (
        inner_grad
        - total_one[:, None] / feature_count
        - normal * total_two[:, None] / feature_count
    )
    return (back_grad, jnp.sum(upstream * normal, axis=0), jnp.sum(upstream, axis=0))


def masked_scores(query, key_rows, labels):
    scores = (
        jnp.einsum("qhd,khd->hqk", query, key_rows, preferred_element_type=jnp.float32) * SCALE
    )
    return jnp.where((labels[:, None] == labels[None, :])[None], scores, -1e30)


def attend(query, key_rows, value_rows, labels):
    row_count, head_count, head_size = query.shape
    scores = masked_scores(query, key_rows, labels)
    row_peak = jnp.max(scores, axis=-1, keepdims=True)
    exp_terms = jnp.exp(scores - row_peak)
    row_total = jnp.sum(exp_terms, axis=-1, keepdims=True)
    prob = (exp_terms / row_total).astype(jnp.bfloat16)
    out = jnp.einsum("hqk,khd->qhd", prob, value_rows, preferred_element_type=jnp.float32)
    return out.reshape(row_count, -1), row_peak + jnp.log(row_total)


def attend_back(query, key_rows, value_rows, labels, logsum, grad_out):
    row_count = query.shape[0]
    scores = masked_scores(query, key_rows, labels)
    prob = jnp.exp(scores - logsum)
    prob_grad = jnp.einsum(
        "qhd,khd->hqk", grad_out, value_rows, preferred_element_type=jnp.float32
    )
    row_delta = jnp.sum(prob * prob_grad, axis=-1, keepdims=True)
    score_grad = (prob * (prob_grad - row_delta)).astype(jnp.bfloat16)
    ein = partial(jnp.einsum, preferred_element_type=jnp.float32)
    query_grad = ein("hqk,khd->qhd", score_grad, key_rows) * SCALE
    key_grad = ein("hqk,qhd->khd", score_grad, query) * SCALE
    value_grad = ein("hqk,qhd->khd", prob.astype(jnp.bfloat16), grad_out)
    return tuple(
        item.astype(jnp.bfloat16).reshape(row_count, -1)
        for item in (query_grad, key_grad, value_grad)
    )


def layer_forward(layer_input, labels, row_mask, matrices, small_params):
    qkv_mat, output_mat, up_mat, down_mat = matrices
    (
        first_gain,
        first_bias,
        inner_gain,
        inner_bias,
        second_gain,
        second_bias,
        middle_gain,
        middle_bias,
    ) = small_params
    head_rows = spread_rows(layer_norm(layer_input, first_gain, first_bias).astype(jnp.bfloat16))
    row_count = head_rows.shape[0]
    qkv = dot_plain(head_rows, qkv_mat).astype(jnp.bfloat16)
    query, key_rows, value_rows = (
        item.reshape(row_count, -1, HEAD_DIM) for item in jnp.split(qkv, 3, axis=1)
    )
    mixed, logsum = attend(query, key_rows, value_rows, labels)
    inner_out, mixed_normal, mixed_scaled = split_norm(mixed, inner_gain, inner_bias, D)
    inner_rows = inner_out.astype(jnp.bfloat16)
    mid_input = layer_input + settle_rows(dot_plain(inner_rows, output_mat))
    feed_rows = spread_rows(layer_norm(mid_input, second_gain, second_bias).astype(jnp.bfloat16))
    pre_act = dot_plain(feed_rows, up_mat)
    middle_out, middle_normal, middle_scaled = split_norm(
        jax.nn.gelu(pre_act, approximate=False), middle_gain, middle_bias, FF
    )
    middle_rows = middle_out.astype(jnp.bfloat16)
    result = mid_input + settle_rows(dot_plain(middle_rows, down_mat))
    layer_output = (row_mask * result).astype(jnp.bfloat16)
    kept_state = (
        layer_input,
        head_rows,
        query,
        key_rows,
        value_rows,
        logsum,
        mixed_normal,
        mixed_scaled,
        inner_rows,
        mid_input,
        feed_rows,
        pre_act,
        middle_normal,
        middle_scaled,
        middle_rows,
    )
    return (layer_output, kept_state)


def layer_backward(upstream, kept_state, labels, row_mask, matrices, small_params):
    qkv_mat, output_mat, up_mat, down_mat = matrices
    (
        first_gain,
        first_bias,
        inner_gain,
        inner_bias,
        second_gain,
        second_bias,
        middle_gain,
        middle_bias,
    ) = small_params
    (
        layer_input,
        head_rows,
        query,
        key_rows,
        value_rows,
        logsum,
        mixed_normal,
        mixed_scaled,
        inner_rows,
        mid_input,
        feed_rows,
        pre_act,
        middle_normal,
        middle_scaled,
        middle_rows,
    ) = kept_state
    result_grad = row_mask * upstream
    feed_grad_rows = spread_rows(result_grad.astype(jnp.bfloat16))
    middle_grad = dot_second_turned(feed_grad_rows, down_mat)
    grad_down = dot_first_turned(middle_rows, feed_grad_rows)
    act_grad, grad_middle_gain, grad_middle_bias = split_norm_back(
        middle_grad, middle_normal, middle_scaled, middle_gain, FF
    )
    gelu_out, gelu_back = jax.vjp(partial(jax.nn.gelu, approximate=False), pre_act)
    pre_grad = gelu_back(act_grad)[0].astype(jnp.bfloat16)
    grad_up = dot_first_turned(feed_rows, pre_grad)
    second_in_grad = settle_rows(dot_second_turned(pre_grad, up_mat))
    norm_out, second_back = jax.vjp(layer_norm, mid_input, second_gain, second_bias)
    mid_back, grad_second_gain, grad_second_bias = second_back(second_in_grad)
    mid_grad = result_grad + mid_back
    branch_grad_rows = spread_rows(mid_grad.astype(jnp.bfloat16))
    inner_grad = dot_second_turned(branch_grad_rows, output_mat)
    grad_output = dot_first_turned(inner_rows, branch_grad_rows)
    mixed_grad, grad_inner_gain, grad_inner_bias = split_norm_back(
        inner_grad, mixed_normal, mixed_scaled, inner_gain, D
    )
    mixed_grad = mixed_grad.astype(jnp.bfloat16).reshape(query.shape)
    qkv_grad = jnp.concatenate(
        attend_back(query, key_rows, value_rows, labels, logsum, mixed_grad), axis=1
    )
    grad_qkv = dot_first_turned(head_rows, qkv_grad)
    head_grad = settle_rows(dot_second_turned(qkv_grad, qkv_mat))
    first_out, first_back = jax.vjp(layer_norm, layer_input, first_gain, first_bias)
    input_back, grad_first_gain, grad_first_bias = first_back(head_grad)
    outer = jnp.stack([grad_first_gain, grad_first_bias, grad_second_gain, grad_second_bias])
    grads = (
        grad_qkv,
        grad_output,
        grad_up,
        grad_down,
        grad_inner_gain,
        grad_inner_bias,
        grad_middle_gain,
        grad_middle_bias,
        outer,
    )
    return ((mid_grad + input_back).astype(jnp.bfloat16), grads)


def on_device(
    inputs,
    cotangent,
    doc_ids,
    norm_gain,
    norm_bias,
    w_query,
    w_key,
    w_value,
    inner_gain,
    inner_bias,
    w_output,
    feed_gain,
    feed_bias,
    w_up,
    middle_gain,
    middle_bias,
    w_down,
):
    core = lax.axis_index("section")
    lane = lax.axis_index("mp")
    lane_x = lane % 2
    lane_y = lane // 2
    slice_len = inputs.shape[0] // MICRO
    rank = 2 * core + lane_x

    def rows_of(array, micro_index):
        return lax.dynamic_slice_in_dim(array, micro_index * slice_len, slice_len, 0)

    def own_slice(array):
        sent = lax.ppermute(
            rows_of(array, 1 - lane_y),
            BOTH,
            [(s * 4 + r, s * 4 + (r ^ 2)) for s in range(2) for r in range(4) if s == r // 2],
        )
        return jnp.where(core == lane_y, rows_of(array, lane_y), sent)

    def placed(array, layer):
        got = [
            lax.ppermute(
                array,
                BOTH,
                [(s * 4 + 2 * m + x, layer * 4 + 2 * s + x) for s in range(2) for x in range(2)],
            )
            for m in range(MICRO)
        ]
        return jnp.concatenate(got, axis=0)

    label_grid = lax.dynamic_index_in_dim(
        doc_ids.reshape(LANES, MICRO, slice_len), lane_y, 1, keepdims=False
    )
    order = jnp.stack([rank, 2 * (1 - core) + lane_x, rank ^ 1, 2 * (1 - core) + (1 - lane_x)])
    labels = jnp.take(label_grid, order, axis=0).reshape(-1)
    row_mask = (labels[:slice_len] >= 0).astype(jnp.float32)[:, None]

    def by_layer(own, other):
        return (jnp.where(core == 0, own, other), jnp.where(core == 0, other, own))

    def fetch(block, axis):
        whole = lax.all_gather(block, "dp", axis=axis, tiled=True)
        both = lax.all_gather(whole, "mp", axis=0, axis_index_groups=Y_PAIRS)
        own = lax.dynamic_index_in_dim(both, core, 0, keepdims=False)
        other = core_swap(lax.dynamic_index_in_dim(both, 1 - core, 0, keepdims=False))
        return by_layer(own, other)

    def fetch_vector(block, split):
        if not split:
            return by_layer(block, core_swap(block))
        both = lax.all_gather(block, "mp", axis=0, axis_index_groups=Y_PAIRS)
        own = lax.dynamic_index_in_dim(both, core, 0, keepdims=False)
        other = core_swap(lax.dynamic_index_in_dim(both, 1 - core, 0, keepdims=False))
        return by_layer(own, other)

    w_qkv = jnp.concatenate([w_query[0], w_key[0], w_value[0]], axis=1)
    matrices = list(
        zip(fetch(w_qkv, 0), fetch(w_output[0], 1), fetch(w_up[0], 0), fetch(w_down[0], 1))
    )
    small_params = list(
        zip(
            fetch_vector(norm_gain[0], False),
            fetch_vector(norm_bias[0], False),
            fetch_vector(inner_gain[0], True),
            fetch_vector(inner_bias[0], True),
            fetch_vector(feed_gain[0], False),
            fetch_vector(feed_bias[0], False),
            fetch_vector(middle_gain[0], True),
            fetch_vector(middle_bias[0], True),
        )
    )

    lower_in = own_slice(inputs)
    upstream = own_slice(cotangent)
    lower_out, lower_state = layer_forward(
        lower_in.astype(jnp.float32), labels, row_mask, matrices[0], small_params[0]
    )
    upper_out, upper_state = layer_forward(
        lower_out.astype(jnp.float32), labels, row_mask, matrices[1], small_params[1]
    )
    upper_grad, upper_grads = layer_backward(
        upstream.astype(jnp.float32), upper_state, labels, row_mask, matrices[1], small_params[1]
    )
    lower_grad, lower_grads = layer_backward(
        upper_grad.astype(jnp.float32), lower_state, labels, row_mask, matrices[0], small_params[0]
    )

    def spread_pair(lower_array, upper_array):
        lower_part, upper_part = placed(lower_array, 0), placed(upper_array, 1)
        return jnp.where(core == 0, lower_part, upper_part)[None]

    def collect(lower, upper, axis):
        lower, upper = lower.astype(jnp.bfloat16), upper.astype(jnp.bfloat16)
        own = jnp.where(core == 0, lower, upper)
        other = core_swap(jnp.where(core == 0, upper, lower))
        first, second = by_layer(own, other)
        both = jnp.stack([first, second])
        whole = lax.psum_scatter(
            both, "mp", scatter_dimension=0, axis_index_groups=Y_PAIRS, tiled=False
        )
        return lax.psum_scatter(whole, "dp", scatter_dimension=axis, tiled=True).astype(
            jnp.float32
        )[None]

    grads = [
        collect(lower, upper, axis)
        for lower, upper, axis in zip(lower_grads[:8], upper_grads[:8], (0, 1, 0, 1, 0, 0, 0, 0))
    ]
    outer = jnp.where(core == 0, lower_grads[8], upper_grads[8]) + core_swap(
        jnp.where(core == 0, upper_grads[8], lower_grads[8])
    )
    outer = lax.psum_scatter(outer, ("dp", "mp"), scatter_dimension=1, tiled=True)
    grad_query, grad_key, grad_value = jnp.split(grads[0], 3, axis=2)
    return (
        spread_pair(lower_out, upper_out),
        spread_pair(lower_grad, upper_grad),
        outer[0][None],
        outer[1][None],
        grad_query,
        grad_key,
        grad_value,
        grads[4],
        grads[5],
        grads[1],
        outer[2][None],
        outer[3][None],
        grads[2],
        grads[6],
        grads[7],
        grads[3],
    )


def solution(mesh):
    placed = (
        P(("dp", "mp"), None),
        P(("dp", "mp"), None),
        P("dp"),
        P("section", None),
        P("section", None),
        P("section", "dp", "mp"),
        P("section", "dp", "mp"),
        P("section", "dp", "mp"),
        P("section", "mp"),
        P("section", "mp"),
        P("section", "mp", "dp"),
        P("section", None),
        P("section", None),
        P("section", "dp", "mp"),
        P("section", "mp"),
        P("section", "mp"),
        P("section", "mp", "dp"),
    )
    return jax.shard_map(
        on_device,
        mesh=mesh,
        in_specs=placed,
        out_specs=(
            P("section", ("dp", "mp"), None),
            P("section", ("dp", "mp"), None),
            P("section", ("dp", "mp")),
            P("section", ("dp", "mp")),
            P("section", "dp", "mp"),
            P("section", "dp", "mp"),
            P("section", "dp", "mp"),
            P("section", ("mp", "dp")),
            P("section", ("mp", "dp")),
            P("section", "mp", "dp"),
            P("section", ("dp", "mp")),
            P("section", ("dp", "mp")),
            P("section", "dp", "mp"),
            P("section", ("mp", "dp")),
            P("section", ("mp", "dp")),
            P("section", "mp", "dp"),
        ),
        check_vma=False,
    )
```

```python
from functools import partial

import jax
import jax.numpy as jnp
from jax import lax
from jax.experimental import pallas as pl
from jax.experimental.pallas import tpu as pltpu
from jax.sharding import PartitionSpec as P

D = 768
HEAD_DIM = 64
FF = 3072
MICRO = 2
LANES = 4
EPS = 1e-05
SCALE = HEAD_DIM ** (-0.5)
LOG2E = 1.4426950408889634
SQRT_HALF = 0.7071067811865476
INV_SQRT_2PI = 0.3989422804014327
BOTH = ("section", "mp")
Y_PAIRS = [[0, 2], [1, 3]]
QKV = 3 * D // LANES
UNITS = FF // LANES
TAIL = 16
F32 = jnp.float32
BF16 = jnp.bfloat16

VMEM = pl.BlockSpec(memory_space=pltpu.VMEM)
ANY = pl.BlockSpec(memory_space=pl.ANY)
PARAMS = pltpu.CompilerParams(vmem_limit_bytes=48 * 1024 * 1024)


def call(name, body, outs, ins, scratch=(), after=(), cost=None):
    count = len(ins)

    def kernel(*refs):
        body(*refs[:count], *refs[count + len(after) :])

    return pl.pallas_call(
        kernel,
        out_shape=tuple(jax.ShapeDtypeStruct(shape, kind) for shape, kind in outs),
        in_specs=[VMEM] * count + [ANY] * len(after),
        out_specs=(VMEM,) * len(outs),
        scratch_shapes=list(scratch),
        compiler_params=PARAMS,
        name=name,
        cost_estimate=cost,
    )(*ins, *after)


def work(flops, size):
    return pl.CostEstimate(flops=int(flops), bytes_accessed=int(size), transcendentals=0)


def nn(a, b):
    return jnp.dot(a, b, preferred_element_type=F32)


def nt(a, b):
    return lax.dot_general(a, b, (((1,), (1,)), ((), ())), preferred_element_type=F32)


def tn(a, b):
    return lax.dot_general(a, b, (((0,), (0,)), ((), ())), preferred_element_type=F32)


def to_rows(*columns):
    count = columns[0].shape[0]
    lane = lax.broadcasted_iota(jnp.int32, (count, 128), 1)
    tile = jnp.zeros((count, 128), F32)
    for place, column in enumerate(columns):
        tile = jnp.where(lane == place, column, tile)
    return tile.T[:8]


def to_columns(rows):
    return jnp.concatenate([rows, jnp.zeros((120, rows.shape[1]), F32)], axis=0).T


def split_three(values):
    high = values.astype(BF16)
    rest = values - high.astype(F32)
    middle = rest.astype(BF16)
    return high, middle, (rest - middle.astype(F32)).astype(BF16)


def encode(rows):
    return jnp.concatenate(split_three(rows), axis=1)


def decode(tail):
    tail = tail.astype(F32)
    count = tail.shape[1] // 3
    return tail[:, :count] + tail[:, count : 2 * count] + tail[:, 2 * count :]


def decode_vectors(tail):
    tail = tail.astype(F32)
    return jnp.concatenate(
        [jnp.sum(tail[0:3], axis=0, keepdims=True), jnp.sum(tail[3:6], axis=0, keepdims=True)],
        axis=0,
    )


def encode_vectors(first, second):
    return jnp.concatenate(
        [*split_three(first), *split_three(second), jnp.zeros((2, first.shape[1]), BF16)], axis=0
    )


def split_norm(values):
    mean = jnp.mean(values, axis=-1, keepdims=True)
    spread = jnp.mean(values * values, axis=-1, keepdims=True) - mean * mean
    scaled = lax.rsqrt(spread + EPS)
    return (values - mean) * scaled, scaled


def norm_back(values, gain, upstream):
    normal, scaled = split_norm(values)
    inner = upstream * gain
    one = jnp.mean(inner, axis=-1, keepdims=True)
    two = jnp.mean(inner * normal, axis=-1, keepdims=True)
    back = scaled * (inner - one - normal * two)
    return (
        back,
        jnp.sum(upstream * normal, axis=0, keepdims=True),
        jnp.sum(upstream, axis=0, keepdims=True),
    )


def vector_rows(first, second):
    return jnp.concatenate([first, second, jnp.zeros((6, first.shape[1]), F32)], axis=0)


def folded_vectors(mat, gain, bias):
    rows = jnp.concatenate(
        [*split_three(gain), *split_three(bias), jnp.zeros((10, gain.shape[1]), BF16)], axis=0
    )
    folded = nt(rows, mat)
    return encode_vectors(
        jnp.sum(folded[0:3], axis=0, keepdims=True), jnp.sum(folded[3:6], axis=0, keepdims=True)
    )


def core_swap(x):
    return lax.ppermute(x, "section", [(0, 1), (1, 0)])


def x_swap(x):
    return lax.ppermute(x, "mp", [(i, i ^ 1) for i in range(LANES)])


def y_swap(x):
    return lax.ppermute(x, "mp", [(i, i ^ 2) for i in range(LANES)])


def gather_rows(own):
    far = x_swap(own)
    return own, core_swap(own), far, core_swap(far)


def pair_sum_body(first, second, out):
    rows = out.shape[0] - TAIL
    out[:rows] = (first[:rows].astype(F32) + second[:rows].astype(F32)).astype(BF16)
    half = rows + TAIL // 2
    out[rows:half] = encode(decode(first[rows:half]) + decode(second[rows:half]))
    folded = decode_vectors(first[half:]) + decode_vectors(second[half:])
    out[half:] = encode_vectors(folded[0:1], folded[1:2])


def settle(own, mate, far, far_mate):
    got = core_swap(far_mate)
    if own.shape[0] % 256:
        sent = call("pair_sum", pair_sum_body, [(far.shape, BF16)], [far, got])[0]
    else:
        sent = (far.astype(F32) + got.astype(F32)).astype(BF16)
    return own, core_swap(mate), x_swap(sent)


def project_body(first, second, mat, out):
    size = first.shape[0]
    for place, piece in enumerate((first, second)):
        out[place * size : (place + 1) * size, :] = nn(piece[...], mat[:, :QKV]).astype(BF16)


def project(first, second, mat):
    count = 2 * first.shape[0]
    return call(
        "project",
        project_body,
        [((count, QKV), BF16)],
        [first, second, mat],
        cost=work(2 * count * D * QKV, 2 * count * (D + QKV) + 2 * D * D),
    )[0]


def split_heads(source, target, first, start, head_count):
    size = source.shape[0]
    for head in range(head_count):
        lanes = slice(first + head * HEAD_DIM, first + (head + 1) * HEAD_DIM)
        target[head, start : start + size, :] = source[:, lanes]


def attend_body(
    q_start, q_ref, near, far, labels, mat, gain, bias, o_ref, p_one, p_two, sum_ref, ks, vs
):
    head_count = QKV // (3 * HEAD_DIM)
    width = head_count * HEAD_DIM
    half = near.shape[0]
    for start, ref in ((0, near), (half, far)):
        split_heads(ref, ks, width, start, head_count)
        split_heads(ref, vs, 2 * width, start, head_count)
    out_mat = mat[:, QKV:]
    folded = folded_vectors(out_mat, gain[...], bias[...])
    size = half // 2
    key_labels = labels[0:1, :]
    for place, p_ref in enumerate((p_one, p_two)):
        rows = slice(place * size, (place + 1) * size)
        first = q_start + place * size
        allowed = to_columns(labels[:, first : first + size])[:, 0:1] == key_labels
        outs = []
        sums = []
        for head in range(head_count):
            query = q_ref[rows, head * HEAD_DIM : (head + 1) * HEAD_DIM]
            scores = jnp.where(allowed, nt(query, ks[head]), -1e30)
            peak = jnp.max(scores, axis=-1, keepdims=True)
            terms = jnp.exp2((scores - peak) * (SCALE * LOG2E))
            total = jnp.sum(terms, axis=-1, keepdims=True)
            outs.append(nn(terms.astype(BF16), vs[head]) / total)
            sums.append(peak * (SCALE * LOG2E) + jnp.log(total) * LOG2E)
        out = jnp.concatenate(outs, axis=1)
        o_ref[rows, :] = out
        lane = lax.broadcasted_iota(jnp.int32, (size, 128), 1)
        tile = jnp.zeros((size, 128), F32)
        for spot, column in enumerate(sums):
            tile = jnp.where(lane == spot, column, tile)
        sum_ref[rows, :] = tile
        p_ref[:size] = nt((out * gain[...]).astype(BF16), out_mat).astype(BF16)
        stats = to_rows(
            jnp.sum(out, axis=-1, keepdims=True), jnp.sum(out * out, axis=-1, keepdims=True)
        )
        p_ref[size : size + TAIL // 2] = encode(stats)
        p_ref[size + TAIL // 2 :] = folded


def attend(q_start, queries, near, far, labels, mat, gain, bias, after=()):
    count, keys = queries.shape[0], 2 * near.shape[0]
    heads = QKV // (3 * HEAD_DIM)
    width = heads * HEAD_DIM
    by_head = pltpu.VMEM((heads, keys, HEAD_DIM), BF16)
    payload = ((count // 2 + TAIL, D), BF16)
    return call(
        "attend",
        partial(attend_body, q_start),
        [((count, width), F32), payload, payload, ((count, 128), F32)],
        [queries, near, far, labels, mat, gain, bias],
        [by_head, by_head],
        after,
        work(2 * count * (2 * keys * width * 4 + width * D), 4 * count * D),
    )


def attend_back_body(
    near, far, do_near, do_far, sum_near, sum_far, labels, near_out, far_out,
    qs, ks, vs, grads, dqs, dks, dvs, sums,
):
    head_count = QKV // (3 * HEAD_DIM)
    width = head_count * HEAD_DIM
    half = near.shape[0]
    for start, ref, grad in ((0, near, do_near), (half, far, do_far)):
        split_heads(ref, qs, 0, start, head_count)
        split_heads(ref, ks, width, start, head_count)
        split_heads(ref, vs, 2 * width, start, head_count)
        split_heads(grad, grads, 0, start, head_count)
    sums[:half] = sum_near[...]
    sums[half:] = sum_far[...]
    dks[...] = jnp.zeros_like(dks)
    dvs[...] = jnp.zeros_like(dvs)
    key_labels = labels[0:1, :]
    size = half // 2

    def block(index, carry):
        rows = pl.ds(pl.multiple_of(index * size, size), size)
        allowed = to_columns(labels[:, rows])[:, 0:1] == key_labels
        for head in range(head_count):
            query, grad = qs[head, rows, :], grads[head, rows, :]
            scores = jnp.where(allowed, nt(query, ks[head]), -1e30)
            prob = jnp.exp2(scores * (SCALE * LOG2E) - sums[rows, head : head + 1])
            prob_grad = nt(grad, vs[head])
            delta = jnp.sum(prob * prob_grad, axis=-1, keepdims=True)
            score_grad = (prob * (prob_grad - delta)).astype(BF16)
            dqs[head, rows, :] = nn(score_grad, ks[head]) * SCALE
            dks[head] += tn(query, score_grad)
            dvs[head] += tn(grad, prob.astype(BF16))
        return carry

    lax.fori_loop(0, 4, block, 0)
    for start, out in ((0, near_out), (half, far_out)):
        rows = slice(start, start + half)
        heads = range(head_count)
        out[...] = jnp.concatenate(
            [dqs[head, rows, :].astype(BF16) for head in heads]
            + [(dks[head, :, rows].T * SCALE).astype(BF16) for head in heads]
            + [dvs[head, :, rows].T.astype(BF16) for head in heads],
            axis=1,
        )


def attend_back(near, far, do_near, do_far, sum_near, sum_far, labels, after=()):
    half, width = do_near.shape
    keys = 2 * half
    heads = width // HEAD_DIM
    by_head = pltpu.VMEM((heads, keys, HEAD_DIM), BF16)
    turned = pltpu.VMEM((heads, HEAD_DIM, keys), F32)
    return call(
        "attend_back",
        attend_back_body,
        [(near.shape, BF16)] * 2,
        [near, far, do_near, do_far, sum_near, sum_far, labels],
        [by_head] * 4
        + [pltpu.VMEM((heads, keys, HEAD_DIM), F32), turned, turned, pltpu.VMEM((keys, 128), F32)],
        after,
        work(2 * keys * keys * width * 5 * 3, 8 * keys * D),
    )


def gelu_parts(x):
    spread = 0.5 + 0.5 * lax.erf(x * SQRT_HALF)
    return x * spread, spread


def feed_body(with_back, *refs):
    if with_back:
        one, two, back_one, back_two, up, down, gain, bias, f_ref, p_one, p_two, s_one, s_two = refs
    else:
        one, two, up, down, gain, bias, f_ref, p_one, p_two = refs
        back_one = back_two = s_one = s_two = None
    size = one.shape[0]
    folded = folded_vectors(down[...], gain[...], bias[...])
    for place, (piece, p_ref, back, s_ref) in enumerate(
        ((one, p_one, back_one, s_one), (two, p_two, back_two, s_two))
    ):
        rows = slice(place * size, (place + 1) * size)
        pre = nn(piece[...], up[...])
        f_ref[rows, :] = pre
        act, _ = gelu_parts(pre)
        p_ref[:size] = nt((act * gain[...]).astype(BF16), down[...]).astype(BF16)
        columns = [
            jnp.sum(act, axis=-1, keepdims=True),
            jnp.sum(act * act, axis=-1, keepdims=True),
        ]
        p_ref[size : size + TAIL // 2] = encode(to_rows(*columns))
        p_ref[size + TAIL // 2 :] = folded
        if with_back:
            inner = nn(back[...], down[...]) * gain[...]
            columns.append(jnp.sum(inner, axis=-1, keepdims=True))
            columns.append(jnp.sum(inner * act, axis=-1, keepdims=True))
            s_ref[...] = to_rows(*columns)


def feed(pieces, backs, up, down, gain, bias, after=()):
    size = pieces[0].shape[0]
    outs = [((2 * size, UNITS), F32)] + [((size + TAIL, D), BF16)] * 2
    if backs:
        outs += [((8, size), F32)] * 2
    return call(
        "feed",
        partial(feed_body, bool(backs)),
        outs,
        [*pieces, *backs, up, down, gain, bias],
        after=after,
        cost=work(2 * 2 * size * D * UNITS * 4, 8 * size * D * 4),
    )


def feed_back_body(with_stats, *refs):
    if with_stats:
        one, two, s_one, s_two, *refs = refs
    else:
        one, two, *refs = refs
        s_one = s_two = None
    f_ref, gain, bias, up, down, df_ref, n_ref, p_one, p_two, vec_ref = refs
    size = p_one.shape[0]
    gain_grad = jnp.zeros((1, UNITS), F32)
    bias_grad = jnp.zeros((1, UNITS), F32)
    for place, (piece, s_ref, p_ref) in enumerate(((one, s_one, p_one), (two, s_two, p_two))):
        rows = slice(place * size, (place + 1) * size)
        upstream = nn(piece[:size], down[...])
        pre = f_ref[rows, :]
        stats = s_ref[...] if with_stats else decode(piece[size : size + TAIL // 2])
        columns = to_columns(stats)
        mean, scaled, first, second = (columns[:, i : i + 1] for i in range(4))
        act, spread = gelu_parts(pre)
        normal = (act - mean) * scaled
        act_grad = scaled * (upstream * gain[...] - first - normal * second)
        slope = spread + pre * (jnp.exp(-0.5 * pre * pre) * INV_SQRT_2PI)
        pre_grad = (act_grad * slope).astype(BF16)
        df_ref[rows, :] = pre_grad
        n_ref[rows, :] = (normal * gain[...] + bias[...]).astype(BF16)
        p_ref[...] = nt(pre_grad, up[...]).astype(BF16)
        gain_grad += jnp.sum(upstream * normal, axis=0, keepdims=True)
        bias_grad += jnp.sum(upstream, axis=0, keepdims=True)
    vec_ref[...] = vector_rows(gain_grad, bias_grad)


def feed_back(pieces, stats, pre, gain, bias, up, down, after=()):
    count = pre.shape[0]
    size = count // 2
    return call(
        "feed_back",
        partial(feed_back_body, bool(stats)),
        [((count, UNITS), BF16)] * 2 + [((size, D), BF16)] * 2 + [((8, UNITS), F32)],
        [*pieces, *stats, pre, gain, bias, up, down],
        after=after,
        cost=work(2 * count * D * UNITS * 4, 8 * count * D),
    )


def grads_body(pieces, halves, size, *refs):
    out = refs[-1]
    place = 0
    column = 0
    for left_count, right_count in zip(pieces, halves):
        left = refs[place : place + left_count]
        right = refs[place + left_count : place + left_count + right_count]
        place += left_count + right_count
        width = right[0].shape[1]
        per = left_count // right_count
        total = None
        for index, piece in enumerate(left):
            start = (index % per) * size
            term = tn(piece[:size], right[index // per][start : start + size, :])
            total = term if total is None else total + term
        out[:, column : column + width] = total.astype(BF16)
        column += width


def grads_of(*pairs, after=()):
    pieces = tuple(len(left) for left, _ in pairs)
    halves = tuple(len(right) for _, right in pairs)
    size = pairs[0][1][0].shape[0] // 2
    args = [item for left, right in pairs for item in (*left, *right)]
    width = sum(right[0].shape[1] for _, right in pairs)
    return call(
        "grads",
        partial(grads_body, pieces, halves, size),
        [((D, width), BF16)],
        args,
        after=after,
        cost=work(2 * 4 * size * D * width, 8 * size * (D + width)),
    )[0]


def inner_back_body(one, two, o_ref, gain, bias, mat, do_ref, u_ref, vec_ref):
    size = o_ref.shape[0] // 2
    gain_grad = jnp.zeros((1, o_ref.shape[1]), F32)
    bias_grad = jnp.zeros((1, o_ref.shape[1]), F32)
    out_mat = mat[:, QKV:]
    for place, piece in enumerate((one, two)):
        rows = slice(place * size, (place + 1) * size)
        upstream = nn(piece[:size], out_mat)
        columns = to_columns(decode(piece[size : size + TAIL // 2]))
        mean, scaled, first, second = (columns[:, i : i + 1] for i in range(4))
        normal = (o_ref[rows, :] - mean) * scaled
        back = scaled * (upstream * gain[...] - first - normal * second)
        do_ref[rows, :] = back.astype(BF16)
        u_ref[rows, :] = (normal * gain[...] + bias[...]).astype(BF16)
        gain_grad += jnp.sum(upstream * normal, axis=0, keepdims=True)
        bias_grad += jnp.sum(upstream, axis=0, keepdims=True)
    vec_ref[...] = vector_rows(gain_grad, bias_grad)


def inner_back(pieces, out, gain, bias, mat, after=()):
    count, width = out.shape
    return call(
        "inner_back",
        inner_back_body,
        [((count, width), BF16)] * 2 + [((8, width), F32)],
        [*pieces, out, gain, bias, mat],
        after=after,
        cost=work(2 * count * D * width, 4 * count * D),
    )


def unproject_body(rows, mat, p_one, p_two):
    size = p_one.shape[0]
    for place, p_ref in enumerate((p_one, p_two)):
        p_ref[...] = nt(rows[place * size : (place + 1) * size], mat[:, :QKV]).astype(BF16)


def unproject(rows, mat, after=()):
    count = rows.shape[0]
    return call(
        "unproject",
        unproject_body,
        [((count // 2, D), BF16)] * 2,
        [rows, mat],
        after=after,
        cost=work(2 * count * D * QKV, 4 * count * D),
    )


def branch_of(own, mate, far, feature_count):
    rows = own.shape[0] - TAIL
    half = rows + TAIL // 2
    pieces = (own, mate, far)
    product = sum(piece[:rows].astype(F32) for piece in pieces)
    stats = sum(decode(piece[rows:half]) for piece in pieces) / feature_count
    folded = sum(decode_vectors(piece[half:]) for piece in pieces)
    mean = stats[0:1]
    scaled = lax.rsqrt(stats[1:2] - mean * mean + EPS)
    kept = jnp.concatenate([mean, scaled, jnp.zeros((6, rows), F32)], axis=0)
    columns = to_columns(kept)
    branch = columns[:, 1:2] * (product - columns[:, 0:1] * folded[0:1])
    return branch, folded[1:2], folded[0:1], kept


def enter_body(x_ref, gain, bias, h_ref):
    normal, _ = split_norm(x_ref[...].astype(F32))
    h_ref[...] = (normal * gain[...] + bias[...]).astype(BF16)


def enter(rows, gain, bias):
    return call("enter", enter_body, [(rows.shape, BF16)], [rows, gain, bias])[0]


def after_attend_body(x_ref, own, mate, far, gain, bias, x2_ref, z_ref, h_ref, fold_ref, kept_ref):
    branch, shift, folded, kept = branch_of(own, mate, far, D)
    mid = x_ref[...].astype(F32) + branch + shift
    x2_ref[...] = mid
    z_ref[...] = branch
    normal, _ = split_norm(mid)
    h_ref[...] = (normal * gain[...] + bias[...]).astype(BF16)
    fold_ref[...] = jnp.broadcast_to(folded, fold_ref.shape)
    kept_ref[...] = kept


def after_attend(x, pieces, gain, bias):
    rows = x.shape[0]
    return call(
        "after_attend",
        after_attend_body,
        [((rows, D), F32), ((rows, D), F32), ((rows, D), BF16), ((8, D), F32), ((8, rows), F32)],
        [x, *pieces, gain, bias],
    )


def mask_column(labels, rows):
    return (to_columns(labels[:, :rows])[:, 0:1] >= 0).astype(F32)


def after_feed_body(x2, own, mate, far, labels, gain, bias, y_ref, z_ref, h_ref, fold_ref, kept_ref):
    branch, shift, folded, kept = branch_of(own, mate, far, FF)
    out = (mask_column(labels, x2.shape[0]) * (x2[...] + branch + shift)).astype(BF16)
    y_ref[...] = out
    z_ref[...] = branch
    normal, _ = split_norm(out.astype(F32))
    h_ref[...] = (normal * gain[...] + bias[...]).astype(BF16)
    fold_ref[...] = jnp.broadcast_to(folded, fold_ref.shape)
    kept_ref[...] = kept


def after_feed(x2, pieces, labels, gain, bias):
    rows = x2.shape[0]
    return call(
        "after_feed",
        after_feed_body,
        [((rows, D), BF16), ((rows, D), F32), ((rows, D), BF16), ((8, D), F32), ((8, rows), F32)],
        [x2, *pieces, labels, gain, bias],
    )


def finish_feed_body(x2, own, mate, far, labels, y_ref):
    branch, shift, _, _ = branch_of(own, mate, far, FF)
    y_ref[...] = (mask_column(labels, x2.shape[0]) * (x2[...] + branch + shift)).astype(BF16)


def finish_feed(x2, pieces, labels):
    return call("finish_feed", finish_feed_body, [(x2.shape, BF16)], [x2, *pieces, labels])[0]


def payload_of(grad, branch, folded, kept, feature_count):
    sent = grad.astype(BF16)
    wide = sent.astype(F32)
    means = to_rows(
        jnp.sum(wide * folded, axis=-1, keepdims=True),
        jnp.sum(wide * branch, axis=-1, keepdims=True),
    )
    stats = jnp.concatenate([kept[0:2], means[0:2] / feature_count, kept[4:8]], axis=0)
    tail = jnp.concatenate([encode(stats), jnp.zeros((TAIL // 2, D), BF16)], axis=0)
    return jnp.concatenate([sent, tail], axis=0)


def feed_norm_back_body(
    own, mate, far, g_ref, labels, x2, gain, branch, folded, kept, dx_ref, out_ref, vec_ref
):
    upstream = own[...].astype(F32) + mate[...].astype(F32) + far[...].astype(F32)
    back, gain_grad, bias_grad = norm_back(x2[...], gain[...], upstream)
    total = mask_column(labels, x2.shape[0]) * g_ref[...].astype(F32) + back
    dx_ref[...] = total
    out_ref[...] = payload_of(total, branch[...], folded[0:1], kept[...], D)
    vec_ref[...] = vector_rows(gain_grad, bias_grad)


def feed_norm_back(pieces, grad, labels, x2, gain, branch, folded, kept):
    rows = x2.shape[0]
    return call(
        "feed_norm_back",
        feed_norm_back_body,
        [((rows, D), F32), ((rows + TAIL, D), BF16), ((8, D), F32)],
        [*pieces, grad, labels, x2, gain, branch, folded, kept],
    )


def first_norm_back_body(has_next, *refs):
    own, mate, far, dx2, x_ref, gain, *refs = refs
    upstream = own[...].astype(F32) + mate[...].astype(F32) + far[...].astype(F32)
    back, gain_grad, bias_grad = norm_back(x_ref[...].astype(F32), gain[...], upstream)
    total = (dx2[...] + back).astype(BF16)
    if has_next:
        labels, branch, folded, kept, g_ref, vec_ref, out_ref = refs
        masked = mask_column(labels, dx2.shape[0]) * total.astype(F32)
        out_ref[...] = payload_of(masked, branch[...], folded[0:1], kept[...], FF)
    else:
        g_ref, vec_ref = refs
    g_ref[...] = total
    vec_ref[...] = vector_rows(gain_grad, bias_grad)


def first_norm_back(pieces, dx2, x, gain, following=()):
    rows = x.shape[0]
    outs = [((rows, D), BF16), ((8, D), F32)]
    if following:
        outs.append(((rows + TAIL, D), BF16))
    return call(
        "first_norm_back",
        partial(first_norm_back_body, bool(following)),
        outs,
        [*pieces, dx2, x, gain, *following],
    )


def dp_scatter(parts):
    count = parts.shape[0]
    if count > 4:
        return lax.psum_scatter(parts, "dp", scatter_dimension=0, tiled=False)
    place = lax.axis_index("dp")
    total = lax.dynamic_index_in_dim(parts, place, 0, keepdims=False).astype(F32)
    for step in range(1, count):
        sent = lax.dynamic_index_in_dim(parts, (place + step) % count, 0, keepdims=False)
        got = lax.ppermute(sent, "dp", [(i, (i + step) % count) for i in range(count)])
        total += got.astype(F32)
    return total


def on_device(
    inputs,
    cotangent,
    doc_ids,
    norm_gain,
    norm_bias,
    w_query,
    w_key,
    w_value,
    inner_gain,
    inner_bias,
    w_output,
    feed_gain,
    feed_bias,
    w_up,
    middle_gain,
    middle_bias,
    w_down,
):
    core = lax.axis_index("section")
    lane = lax.axis_index("mp")
    lane_x = lane % 2
    lane_y = lane // 2
    count = lax.axis_size("dp")
    slice_len = inputs.shape[0] // MICRO
    rank = 2 * core + lane_x
    crossing = [(s * 4 + r, s * 4 + (r ^ 2)) for s in range(2) for r in range(4) if s == r // 2]
    returning = [(s * 4 + r, s * 4 + (r ^ 2)) for s in range(2) for r in range(4) if s != r // 2]

    def by_core(first, second):
        return jnp.where(core == 0, first, second)

    def rows_of(array, micro_index):
        return lax.dynamic_slice_in_dim(array, micro_index * slice_len, slice_len, 0)

    def own_slice(array):
        sent = lax.ppermute(rows_of(array, 1 - lane_y), BOTH, crossing)
        return jnp.where(core == lane_y, rows_of(array, lane_y), sent)

    def placed(pairs):
        stacked = jnp.stack([jnp.stack(pair) for pair in pairs], axis=1)
        sent = lax.ppermute(stacked, BOTH, returning)
        micros = jnp.stack(
            [jnp.where(lane_y == 0, stacked, sent), jnp.where(lane_y == 0, sent, stacked)], axis=2
        )
        other = core_swap(lax.dynamic_index_in_dim(micros, 1 - core, 0, keepdims=False))
        kept = lax.dynamic_index_in_dim(micros, core, 0, keepdims=False)
        held = jnp.where(core == lane_y, kept, other)
        return held.reshape(len(pairs), 1, MICRO * slice_len, D)

    label_grid = lax.dynamic_index_in_dim(
        doc_ids.reshape(LANES, MICRO, slice_len), lane_y, 1, keepdims=False
    )
    order = (rank, 2 * (1 - core) + lane_x, rank ^ 1, 2 * (1 - core) + (1 - lane_x))
    labels = jnp.concatenate(
        [lax.dynamic_index_in_dim(label_grid, item, 0, keepdims=False) for item in order]
    )
    labels = jnp.broadcast_to(labels.astype(F32)[None], (8, LANES * slice_len))

    first_block = jnp.concatenate([w_query[0], w_key[0], w_value[0], w_output[0].T], axis=1)
    up_block, down_block = w_up[0], w_down[0].T

    def fetch(block, layer):
        whole = lax.all_gather(block, "dp", axis=0, tiled=True)
        across = lax.ppermute(
            whole, BOTH, [(layer * 4 + r, (r // 2) * 4 + (r ^ 2)) for r in range(LANES)]
        )
        beside = lax.ppermute(
            whole, BOTH, [(layer * 4 + r, (r // 2) * 4 + r) for r in range(LANES)]
        )
        return jnp.where(core == lane_y, beside, across)

    lower_first = fetch(first_block, 0)
    lower_up, lower_down = fetch(up_block, 0), fetch(down_block, 0)
    upper_first = fetch(first_block, 1)
    upper_up, upper_down = fetch(up_block, 1), fetch(down_block, 1)

    outer_own = jnp.concatenate([norm_gain, norm_bias, feed_gain, feed_bias], axis=0)
    outer_other = core_swap(outer_own)
    split_own = jnp.concatenate([inner_gain, inner_bias, middle_gain, middle_bias], axis=1)
    split_far = y_swap(split_own)
    split_kept = jnp.where(lane_y == core, split_own, split_far)
    split_other = core_swap(jnp.where(lane_y == core, split_far, split_own))

    def small_of(outer, split):
        width = D // LANES
        return (
            [outer[i : i + 1] for i in range(4)],
            [
                split[:, :width],
                split[:, width : 2 * width],
                split[:, 2 * width : 2 * width + UNITS],
                split[:, 2 * width + UNITS :],
            ],
        )

    lower_outer, lower_split = small_of(
        by_core(outer_own, outer_other), by_core(split_kept, split_other)
    )
    upper_outer, upper_split = small_of(
        by_core(outer_other, outer_own), by_core(split_other, split_kept)
    )

    def attention(x, h, first, outer, split):
        pieces = gather_rows(h)
        near = project(pieces[0], pieces[1], first)
        far = project(pieces[2], pieces[3], first)
        half = 2 * slice_len
        o_far, p_far, p_far_mate, sum_far = attend(
            half, far, near, far, labels, first, split[0], split[1]
        )
        o_near, p_own, p_mate, sum_near = attend(
            0, near, near, far, labels, first, split[0], split[1], after=[p_far]
        )
        terms = settle(p_own, p_mate, p_far, p_far_mate)
        x2, branch, h2, folded, kept = after_attend(x, terms, outer[2], outer[3])
        state = (x, pieces, near, far, o_near, o_far, sum_near, sum_far, x2, branch, folded, kept)
        return x2, h2, state

    def attention_back(grad, sums, state, first, outer, split, following, after=()):
        x, pieces, near, far, o_near, o_far, sum_near, sum_far, x2, branch, folded, kept = state
        dx2, sent, feed_vec = feed_norm_back(
            sums, grad, labels, x2, outer[2], branch, folded, kept
        )
        backs = gather_rows(sent)
        do_near, u_near, vec_near = inner_back(backs[:2], o_near, split[0], split[1], first)
        do_far, u_far, vec_far = inner_back(backs[2:], o_far, split[0], split[1], first)
        dq_near, dq_far = attend_back(
            near, far, do_near, do_far, sum_near, sum_far, labels, after=after
        )
        p_far, p_far_mate = unproject(dq_far, first)
        p_own, p_mate = unproject(dq_near, first, after=[p_far])
        terms = settle(p_own, p_mate, p_far, p_far_mate)
        mat_grad = grads_of((pieces, (dq_near, dq_far)), (backs, (u_near, u_far)), after=[p_far])
        result = first_norm_back(terms, dx2, x, outer[0], following)
        return result, mat_grad, vec_near + vec_far, feed_vec

    lower_in = own_slice(inputs)
    upstream = own_slice(cotangent)
    masked = jnp.where(
        jnp.broadcast_to(labels[0, :slice_len, None], upstream.shape) >= 0,
        upstream,
        jnp.zeros_like(upstream),
    )
    top = gather_rows(masked)

    h = enter(lower_in, lower_outer[0], lower_outer[1])
    x2, h2, lower_state = attention(lower_in, h, lower_first, lower_outer, lower_split)
    lower_pieces = gather_rows(h2)
    f_near, p_own, p_mate = feed(lower_pieces[:2], (), lower_up, lower_down, *lower_split[2:])
    f_far, p_far, p_far_mate = feed(lower_pieces[2:], (), lower_up, lower_down, *lower_split[2:])
    lower_pre = (f_near, f_far)
    terms = settle(p_own, p_mate, p_far, p_far_mate)
    lower_out, lower_branch, h, lower_folded, lower_kept = after_feed(
        x2, terms, labels, upper_outer[0], upper_outer[1]
    )
    x2, h2, upper_state = attention(lower_out, h, upper_first, upper_outer, upper_split)
    upper_pieces = gather_rows(h2)
    f_near, p_own, p_mate, s_own, s_mate = feed(
        upper_pieces[:2], top[:2], upper_up, upper_down, *upper_split[2:]
    )
    f_far, p_far, p_far_mate, s_far, s_far_mate = feed(
        upper_pieces[2:], top[2:], upper_up, upper_down, *upper_split[2:]
    )
    upper_pre = (f_near, f_far)

    near_stats, far_stats = jnp.stack([s_own, s_mate]), jnp.stack([s_far, s_far_mate])
    stats = jnp.stack([near_stats, far_stats])
    got = core_swap(stats)
    stats = stats + jnp.stack([got[:, 1], got[:, 0]], axis=1)
    got = x_swap(stats)
    stats = (stats + jnp.stack([got[1], got[0]])) / FF
    mean = stats[:, :, 0:1]
    scaled = lax.rsqrt(stats[:, :, 1:2] - mean * mean + EPS)
    second = scaled * (stats[:, :, 3:4] - mean * stats[:, :, 2:3])
    stats = jnp.concatenate(
        [mean, scaled, stats[:, :, 2:3], second, jnp.zeros_like(stats[:, :, 4:])], axis=2
    )

    def feed_backward(pieces, rows, stat_pieces, pre, up, down, split):
        near_stats = [stat_pieces[0, 0], stat_pieces[0, 1]] if stat_pieces is not None else []
        far_stats = [stat_pieces[1, 0], stat_pieces[1, 1]] if stat_pieces is not None else []
        df_far, n_far, p_far, p_far_mate, vec_far = feed_back(
            pieces[2:], far_stats, pre[1], split[2], split[3], up, down
        )
        df_near, n_near, p_own, p_mate, vec_near = feed_back(
            pieces[:2], near_stats, pre[0], split[2], split[3], up, down, after=[p_far]
        )
        terms = settle(p_own, p_mate, p_far, p_far_mate)
        mat_grad = grads_of((rows, (df_near, df_far)), (pieces, (n_near, n_far)), after=[p_far])
        return terms, mat_grad, vec_near + vec_far

    sums, upper_feed_grad, upper_middle = feed_backward(
        top, upper_pieces, stats, upper_pre, upper_up, upper_down, upper_split
    )
    following = (labels, lower_branch, lower_folded, lower_kept)
    (upper_grad, upper_norm, sent), upper_first_grad, upper_inner, upper_feed = attention_back(
        upstream, sums, upper_state, upper_first, upper_outer, upper_split, following
    )
    upper_out = finish_feed(x2, settle(p_own, p_mate, p_far, p_far_mate), labels)

    backs = gather_rows(sent)
    sums, lower_feed_grad, lower_middle = feed_backward(
        backs, lower_pieces, None, lower_pre, lower_up, lower_down, lower_split
    )
    (lower_grad, lower_norm), lower_first_grad, lower_inner, lower_feed = attention_back(
        upper_grad, sums, lower_state, lower_first, lower_outer, lower_split, ()
    )

    layer_outputs, upper_grad_held = placed([(lower_out, upper_out), (upper_grad, upper_grad)])
    lower_grad_held = placed([(lower_grad, lower_grad)])[0]
    input_grads = by_core(lower_grad_held, upper_grad_held)

    def collect(grad):
        parts = grad.reshape(count, 2, D // count // 2, -1)
        kept = lax.dynamic_index_in_dim(parts, core, 1, keepdims=False)
        got = core_swap(lax.dynamic_index_in_dim(parts, 1 - core, 1, keepdims=False))
        both = jnp.stack([by_core(kept, got), by_core(got, kept)])
        line = lax.psum_scatter(
            both, "mp", scatter_dimension=0, axis_index_groups=Y_PAIRS, tiled=False
        )
        return lax.psum_scatter(line, "dp", scatter_dimension=0, tiled=False)

    upper_sum = jnp.concatenate([collect(upper_first_grad), collect(upper_feed_grad)], axis=1)
    lower_sum = jnp.concatenate([collect(lower_first_grad), collect(lower_feed_grad)], axis=1)
    sum_kept = by_core(lower_sum, upper_sum)
    sum_got = core_swap(by_core(upper_sum, lower_sum))
    summed = jnp.concatenate(
        [by_core(sum_kept, sum_got), by_core(sum_got, sum_kept)], axis=0
    ).astype(F32)
    width = D // LANES
    grad_query, grad_key, grad_value, grad_output, grad_up, grad_down = jnp.split(
        summed, [width, 2 * width, 3 * width, D, D + UNITS], axis=1
    )

    outer = jnp.concatenate([lower_norm[:2], lower_feed[:2], upper_norm[:2], upper_feed[:2]])
    split = jnp.stack(
        [
            jnp.concatenate([lower_inner[:2], lower_middle[:2]], axis=1),
            jnp.concatenate([upper_inner[:2], upper_middle[:2]], axis=1),
        ]
    )
    packed = jnp.concatenate([outer.reshape(-1), split.reshape(-1)])
    packed += y_swap(packed)
    outer = packed[: 8 * D].reshape(8, D)
    split = packed[8 * D :].reshape(2, 2, -1)
    outer += core_swap(outer)
    outer += x_swap(outer)

    def by_dest(items):
        return [item.reshape(-1, count, item.shape[-1] // count) for item in items]

    outer, inner, middle = by_dest([outer, split[:, :, :width], split[:, :, width:]])
    sizes = [item.shape[0] * item.shape[2] for item in (outer, inner, middle)]
    packed = jnp.concatenate(
        [item.transpose(1, 0, 2).reshape(count, -1) for item in (outer, inner, middle)], axis=1
    )
    packed = dp_scatter(packed)
    outer = packed[: sizes[0]].reshape(2, 4, LANES, -1)
    outer = lax.dynamic_index_in_dim(outer, core, 0, keepdims=False)
    outer = lax.dynamic_index_in_dim(outer, lane, 1, keepdims=False)
    split = packed[sizes[0] :]
    split = jnp.where(core == lane_y, split, core_swap(split))
    inner = lax.dynamic_index_in_dim(
        split[: sizes[1]].reshape(2, 2, -1), core, 0, keepdims=False
    )
    middle = lax.dynamic_index_in_dim(
        split[sizes[1] :].reshape(2, 2, -1), core, 0, keepdims=False
    )
    return (
        layer_outputs,
        input_grads,
        outer[0][None],
        outer[1][None],
        grad_query[None],
        grad_key[None],
        grad_value[None],
        inner[0][None],
        inner[1][None],
        grad_output.T[None],
        outer[2][None],
        outer[3][None],
        grad_up[None],
        middle[0][None],
        middle[1][None],
        grad_down.T[None],
    )


def solution(mesh):
    placed = (
        P(("dp", "mp"), None),
        P(("dp", "mp"), None),
        P("dp"),
        P("section", None),
        P("section", None),
        P("section", "dp", "mp"),
        P("section", "dp", "mp"),
        P("section", "dp", "mp"),
        P("section", "mp"),
        P("section", "mp"),
        P("section", "mp", "dp"),
        P("section", None),
        P("section", None),
        P("section", "dp", "mp"),
        P("section", "mp"),
        P("section", "mp"),
        P("section", "mp", "dp"),
    )
    return jax.shard_map(
        on_device,
        mesh=mesh,
        in_specs=placed,
        out_specs=(
            P("section", ("dp", "mp"), None),
            P("section", ("dp", "mp"), None),
            P("section", ("dp", "mp")),
            P("section", ("dp", "mp")),
            P("section", "dp", "mp"),
            P("section", "dp", "mp"),
            P("section", "dp", "mp"),
            P("section", ("mp", "dp")),
            P("section", ("mp", "dp")),
            P("section", "mp", "dp"),
            P("section", ("dp", "mp")),
            P("section", ("dp", "mp")),
            P("section", "dp", "mp"),
            P("section", ("mp", "dp")),
            P("section", ("mp", "dp")),
            P("section", "mp", "dp"),
        ),
        check_vma=False,
    )
```

```python
from functools import partial

import jax
import jax.numpy as jnp
from jax import lax
from jax.experimental import pallas as pl
from jax.experimental.pallas import tpu as pltpu
from jax.sharding import PartitionSpec as P

D = 768
HEAD_DIM = 64
FF = 3072
MICRO = 2
LANES = 4
EPS = 1e-05
SCALE = HEAD_DIM ** (-0.5)
LOG2E = 1.4426950408889634
SQRT_HALF = 0.7071067811865476
INV_SQRT_2PI = 0.3989422804014327
BOTH = ("section", "mp")
Y_PAIRS = [[0, 2], [1, 3]]
QKV = 3 * D // LANES
UNITS = FF // LANES
TAIL = 16
F32 = jnp.float32
BF16 = jnp.bfloat16

VMEM = pl.BlockSpec(memory_space=pltpu.VMEM)
SMEM = pl.BlockSpec(memory_space=pltpu.SMEM)
ANY = pl.BlockSpec(memory_space=pl.ANY)
PARAMS = pltpu.CompilerParams(vmem_limit_bytes=16 * 1024 * 1024)


def call(name, body, outs, ins, scratch=(), after=(), cost=None):
    count = len(ins)

    def kernel(*refs):
        body(*refs[:count], *refs[count + len(after) :])

    return pl.pallas_call(
        kernel,
        out_shape=tuple(jax.ShapeDtypeStruct(shape, kind) for shape, kind in outs),
        in_specs=[SMEM if item.ndim == 1 else VMEM for item in ins] + [ANY] * len(after),
        out_specs=(VMEM,) * len(outs),
        scratch_shapes=list(scratch),
        compiler_params=PARAMS,
        name=name,
        cost_estimate=cost,
    )(*ins, *after)


def work(flops, size):
    return pl.CostEstimate(flops=int(flops), bytes_accessed=int(size), transcendentals=0)


def nn(a, b):
    return jnp.dot(a, b, preferred_element_type=F32)


def nt(a, b):
    return lax.dot_general(a, b, (((1,), (1,)), ((), ())), preferred_element_type=F32)


def tn(a, b):
    return lax.dot_general(a, b, (((0,), (0,)), ((), ())), preferred_element_type=F32)


def to_rows(*columns):
    count = columns[0].shape[0]
    lane = lax.broadcasted_iota(jnp.int32, (count, 128), 1)
    tile = jnp.zeros((count, 128), F32)
    for place, column in enumerate(columns):
        tile = jnp.where(lane == place, column, tile)
    return tile.T[:8]


def to_columns(rows):
    return jnp.concatenate([rows, jnp.zeros((120, rows.shape[1]), F32)], axis=0).T


def split_three(values):
    high = values.astype(BF16)
    rest = values - high.astype(F32)
    middle = rest.astype(BF16)
    return high, middle, (rest - middle.astype(F32)).astype(BF16)


def encode(rows):
    return jnp.concatenate(split_three(rows), axis=1)


def decode(tail):
    tail = tail.astype(F32)
    count = tail.shape[1] // 3
    return tail[:, :count] + tail[:, count : 2 * count] + tail[:, 2 * count :]


def decode_vectors(tail):
    tail = tail.astype(F32)
    return jnp.concatenate(
        [jnp.sum(tail[0:3], axis=0, keepdims=True), jnp.sum(tail[3:6], axis=0, keepdims=True)],
        axis=0,
    )


def encode_vectors(first, second):
    return jnp.concatenate(
        [*split_three(first), *split_three(second), jnp.zeros((2, first.shape[1]), BF16)], axis=0
    )


def split_norm(values):
    mean = jnp.mean(values, axis=-1, keepdims=True)
    spread = jnp.mean(values * values, axis=-1, keepdims=True) - mean * mean
    scaled = lax.rsqrt(spread + EPS)
    return (values - mean) * scaled, scaled


def norm_back(values, gain, upstream):
    normal, scaled = split_norm(values)
    inner = upstream * gain
    one = jnp.mean(inner, axis=-1, keepdims=True)
    two = jnp.mean(inner * normal, axis=-1, keepdims=True)
    back = scaled * (inner - one - normal * two)
    return (
        back,
        jnp.sum(upstream * normal, axis=0, keepdims=True),
        jnp.sum(upstream, axis=0, keepdims=True),
    )


def vector_rows(first, second):
    return jnp.concatenate([first, second, jnp.zeros((6, first.shape[1]), F32)], axis=0)


def folded_vectors(mat, gain, bias):
    rows = jnp.concatenate(
        [*split_three(gain), *split_three(bias), jnp.zeros((10, gain.shape[1]), BF16)], axis=0
    )
    folded = nt(rows, mat)
    return encode_vectors(
        jnp.sum(folded[0:3], axis=0, keepdims=True), jnp.sum(folded[3:6], axis=0, keepdims=True)
    )


def core_swap(x):
    return lax.ppermute(x, "section", [(0, 1), (1, 0)])


def x_swap(x):
    return lax.ppermute(x, "mp", [(i, i ^ 1) for i in range(LANES)])


def y_swap(x):
    return lax.ppermute(x, "mp", [(i, i ^ 2) for i in range(LANES)])


def gather_rows(own):
    far = x_swap(own)
    return own, core_swap(own), far, core_swap(far)


def pair_sum_body(first, second, out):
    rows = out.shape[0] - TAIL
    out[:rows] = (first[:rows].astype(F32) + second[:rows].astype(F32)).astype(BF16)
    half = rows + TAIL // 2
    out[rows:half] = encode(decode(first[rows:half]) + decode(second[rows:half]))
    folded = decode_vectors(first[half:]) + decode_vectors(second[half:])
    out[half:] = encode_vectors(folded[0:1], folded[1:2])


def pair_add_body(first, second, out):
    out[...] = (first[...].astype(F32) + second[...].astype(F32)).astype(BF16)


def settle(own, mate, far, far_mate, after=()):
    body = pair_sum_body if own.shape[0] % 256 else pair_add_body
    got = core_swap(far_mate)
    sent = call("pair_sum", body, [(far.shape, BF16)], [far, got], after=after)[0]
    return own, core_swap(mate), x_swap(sent)


def project_body(first, second, mat, out):
    size = first.shape[0]
    for place, piece in enumerate((first, second)):
        out[place * size : (place + 1) * size, :] = nn(piece[...], mat[:, :QKV]).astype(BF16)


def project(first, second, mat):
    count = 2 * first.shape[0]
    return call(
        "project",
        project_body,
        [((count, QKV), BF16)],
        [first, second, mat],
        cost=work(2 * count * D * QKV, 2 * count * (D + QKV) + 2 * D * D),
    )[0]


def split_heads(source, target, first, start, head_count):
    size = source.shape[0]
    for head in range(head_count):
        lanes = slice(first + head * HEAD_DIM, first + (head + 1) * HEAD_DIM)
        target[head, start : start + size, :] = source[:, lanes]


def attend_body(
    q_start, q_ref, near, far, labels, mat, gain, bias, o_ref, p_one, p_two, sum_ref, ks, vs
):
    head_count = QKV // (3 * HEAD_DIM)
    width = head_count * HEAD_DIM
    half = near.shape[0]
    for start, ref in ((0, near), (half, far)):
        split_heads(ref, ks, width, start, head_count)
        split_heads(ref, vs, 2 * width, start, head_count)
    out_mat = mat[:, QKV:]
    folded = folded_vectors(out_mat, gain[...], bias[...])
    size = half // 2
    key_labels = labels[0:1, :]
    for place, p_ref in enumerate((p_one, p_two)):
        rows = slice(place * size, (place + 1) * size)
        first = q_start + place * size
        allowed = to_columns(labels[:, first : first + size])[:, 0:1] == key_labels
        outs = []
        sums = []
        for head in range(head_count):
            query = q_ref[rows, head * HEAD_DIM : (head + 1) * HEAD_DIM]
            scores = jnp.where(allowed, nt(query, ks[head]), -1e30)
            peak = jnp.max(scores, axis=-1, keepdims=True)
            terms = jnp.exp2((scores - peak) * (SCALE * LOG2E))
            total = jnp.sum(terms, axis=-1, keepdims=True)
            outs.append(nn(terms.astype(BF16), vs[head]) / total)
            sums.append(peak * (SCALE * LOG2E) + jnp.log(total) * LOG2E)
        out = jnp.concatenate(outs, axis=1)
        o_ref[rows, :] = out
        lane = lax.broadcasted_iota(jnp.int32, (size, 128), 1)
        tile = jnp.zeros((size, 128), F32)
        for spot, column in enumerate(sums):
            tile = jnp.where(lane == spot, column, tile)
        sum_ref[rows, :] = tile
        p_ref[:size] = nt((out * gain[...]).astype(BF16), out_mat).astype(BF16)
        stats = to_rows(
            jnp.sum(out, axis=-1, keepdims=True), jnp.sum(out * out, axis=-1, keepdims=True)
        )
        p_ref[size : size + TAIL // 2] = encode(stats)
        p_ref[size + TAIL // 2 :] = folded


def attend(q_start, queries, near, far, labels, mat, gain, bias, after=()):
    count, keys = queries.shape[0], 2 * near.shape[0]
    heads = QKV // (3 * HEAD_DIM)
    width = heads * HEAD_DIM
    by_head = pltpu.VMEM((heads, keys, HEAD_DIM), BF16)
    payload = ((count // 2 + TAIL, D), BF16)
    return call(
        "attend",
        partial(attend_body, q_start),
        [((count, width), F32), payload, payload, ((count, 128), F32)],
        [queries, near, far, labels, mat, gain, bias],
        [by_head, by_head],
        after,
        work(2 * count * (2 * keys * width * 4 + width * D), 4 * count * D),
    )


def attend_back_body(
    near, far, do_near, do_far, sum_near, sum_far, labels, near_out, far_out,
    qs, ks, vs, grads, dqs, dks, dvs, sums,
):
    head_count = QKV // (3 * HEAD_DIM)
    width = head_count * HEAD_DIM
    half = near.shape[0]
    for start, ref, grad in ((0, near, do_near), (half, far, do_far)):
        split_heads(ref, qs, 0, start, head_count)
        split_heads(ref, ks, width, start, head_count)
        split_heads(ref, vs, 2 * width, start, head_count)
        split_heads(grad, grads, 0, start, head_count)
    sums[:half] = sum_near[...]
    sums[half:] = sum_far[...]
    dks[...] = jnp.zeros_like(dks)
    dvs[...] = jnp.zeros_like(dvs)
    key_labels = labels[0:1, :]
    size = half // 2

    def block(index, carry):
        rows = pl.ds(pl.multiple_of(index * size, size), size)
        allowed = to_columns(labels[:, rows])[:, 0:1] == key_labels
        for head in range(head_count):
            query, grad = qs[head, rows, :], grads[head, rows, :]
            scores = jnp.where(allowed, nt(query, ks[head]), -1e30)
            prob = jnp.exp2(scores * (SCALE * LOG2E) - sums[rows, head : head + 1])
            prob_grad = nt(grad, vs[head])
            delta = jnp.sum(prob * prob_grad, axis=-1, keepdims=True)
            score_grad = (prob * (prob_grad - delta)).astype(BF16)
            dqs[head, rows, :] = nn(score_grad, ks[head]) * SCALE
            dks[head] += tn(query, score_grad)
            dvs[head] += tn(grad, prob.astype(BF16))
        return carry

    lax.fori_loop(0, 4, block, 0)
    for start, out in ((0, near_out), (half, far_out)):
        rows = slice(start, start + half)
        heads = range(head_count)
        out[...] = jnp.concatenate(
            [dqs[head, rows, :].astype(BF16) for head in heads]
            + [(dks[head, :, rows].T * SCALE).astype(BF16) for head in heads]
            + [dvs[head, :, rows].T.astype(BF16) for head in heads],
            axis=1,
        )


def attend_back(near, far, do_near, do_far, sum_near, sum_far, labels, after=()):
    half, width = do_near.shape
    keys = 2 * half
    heads = width // HEAD_DIM
    by_head = pltpu.VMEM((heads, keys, HEAD_DIM), BF16)
    turned = pltpu.VMEM((heads, HEAD_DIM, keys), F32)
    return call(
        "attend_back",
        attend_back_body,
        [(near.shape, BF16)] * 2,
        [near, far, do_near, do_far, sum_near, sum_far, labels],
        [by_head] * 4
        + [pltpu.VMEM((heads, keys, HEAD_DIM), F32), turned, turned, pltpu.VMEM((keys, 128), F32)],
        after,
        work(2 * keys * keys * width * 5 * 3, 8 * keys * D),
    )


def gelu_parts(x):
    spread = 0.5 + 0.5 * lax.erf(x * SQRT_HALF)
    return x * spread, spread


def feed_body(with_back, *refs):
    if with_back:
        one, two, back_one, back_two, mat, gain, bias, f_ref, p_one, p_two, s_ref = refs
    else:
        one, two, mat, gain, bias, f_ref, p_one, p_two = refs
        back_one = back_two = s_ref = None
    size = one.shape[0]
    up, down = mat.at[:, :UNITS], mat.at[:, UNITS:]
    folded = folded_vectors(down[...], gain[...], bias[...])
    for place, (piece, p_ref, back) in enumerate(((one, p_one, back_one), (two, p_two, back_two))):
        rows = slice(place * size, (place + 1) * size)
        pre = nn(piece[...], up[...])
        f_ref[rows, :] = pre
        act, _ = gelu_parts(pre)
        p_ref[:size] = nt((act * gain[...]).astype(BF16), down[...]).astype(BF16)
        columns = [
            jnp.sum(act, axis=-1, keepdims=True),
            jnp.sum(act * act, axis=-1, keepdims=True),
        ]
        p_ref[size : size + TAIL // 2] = encode(to_rows(*columns))
        p_ref[size + TAIL // 2 :] = folded
        if with_back:
            inner = nn(back[...], down[...]) * gain[...]
            columns.append(jnp.sum(inner, axis=-1, keepdims=True))
            columns.append(jnp.sum(inner * act, axis=-1, keepdims=True))
            s_ref[8 * place : 8 * place + 8, :] = to_rows(*columns)


def feed(pieces, backs, mat, gain, bias, after=()):
    size = pieces[0].shape[0]
    outs = [((2 * size, UNITS), F32)] + [((size + TAIL, D), BF16)] * 2
    if backs:
        outs += [((16, size), F32)]
    return call(
        "feed",
        partial(feed_body, bool(backs)),
        outs,
        [*pieces, *backs, mat, gain, bias],
        after=after,
        cost=work(2 * 2 * size * D * UNITS * 4, 8 * size * D * 4),
    )


def feed_back_body(first_piece, *refs):
    if first_piece is not None:
        one, two, s_ref, *refs = refs
    else:
        one, two, *refs = refs
        s_ref = None
    f_ref, gain, bias, mat, df_ref, n_ref, p_one, p_two, vec_ref = refs
    up, down = mat.at[:, :UNITS], mat.at[:, UNITS:]
    size = p_one.shape[0]
    gain_grad = jnp.zeros((1, UNITS), F32)
    bias_grad = jnp.zeros((1, UNITS), F32)
    for place, (piece, p_ref) in enumerate(((one, p_one), (two, p_two))):
        rows = slice(place * size, (place + 1) * size)
        upstream = nn(piece[:size], down[...])
        pre = f_ref[rows, :]
        if first_piece is not None:
            start = 8 * (first_piece + place)
            stats = s_ref[start : start + 8, :]
        else:
            stats = decode(piece[size : size + TAIL // 2])
        columns = to_columns(stats)
        mean, scaled, first, second = (columns[:, i : i + 1] for i in range(4))
        act, spread = gelu_parts(pre)
        normal = (act - mean) * scaled
        act_grad = scaled * (upstream * gain[...] - first - normal * second)
        slope = spread + pre * (jnp.exp(-0.5 * pre * pre) * INV_SQRT_2PI)
        pre_grad = (act_grad * slope).astype(BF16)
        df_ref[rows, :] = pre_grad
        n_ref[rows, :] = (normal * gain[...] + bias[...]).astype(BF16)
        p_ref[...] = nt(pre_grad, up[...]).astype(BF16)
        gain_grad += jnp.sum(upstream * normal, axis=0, keepdims=True)
        bias_grad += jnp.sum(upstream, axis=0, keepdims=True)
    vec_ref[...] = vector_rows(gain_grad, bias_grad)


def feed_back(pieces, stats, first_piece, pre, gain, bias, mat, after=()):
    count = pre.shape[0]
    size = count // 2
    return call(
        "feed_back",
        partial(feed_back_body, first_piece if stats else None),
        [((count, UNITS), BF16)] * 2 + [((size, D), BF16)] * 2 + [((8, UNITS), F32)],
        [*pieces, *stats, pre, gain, bias, mat],
        after=after,
        cost=work(2 * count * D * UNITS * 4, 8 * count * D),
    )


def stats_pack_body(near, far, out):
    out[:16] = near[...]
    out[16:] = far[...]


def stats_near_body(stats, got, out):
    for place in range(4):
        other = 8 * (place ^ 1)
        out[8 * place : 8 * place + 8] = stats[8 * place : 8 * place + 8] + got[other : other + 8]


def stats_far_body(stats, got, out):
    for place in range(4):
        other = 8 * (place ^ 2)
        rows = slice(8 * place, 8 * place + 8)
        total = (stats[rows] + got[other : other + 8]) * (1.0 / FF)
        mean, one = total[0:1], total[2:3]
        scaled = lax.rsqrt(total[1:2] - mean * mean + EPS)
        two = scaled * (total[3:4] - mean * one)
        out[rows] = jnp.concatenate([mean, scaled, one, two, total[4:8]], axis=0)


def group_stats(near, far):
    shape = [((32, near.shape[1]), F32)]
    stats = call("stats_pack", stats_pack_body, shape, [near, far])[0]
    stats = call("stats_near", stats_near_body, shape, [stats, core_swap(stats)])[0]
    return call("stats_far", stats_far_body, shape, [stats, x_swap(stats)])[0]


def grads_body(pieces, halves, size, *refs):
    *refs, out = refs
    place = 0
    column = 0
    for left_count, right_count in zip(pieces, halves):
        left = refs[place : place + left_count]
        right = refs[place + left_count : place + left_count + right_count]
        place += left_count + right_count
        width = right[0].shape[1]
        per = left_count // right_count
        total = None
        for index, piece in enumerate(left):
            start = (index % per) * size
            term = tn(piece[:size], right[index // per][start : start + size, :])
            total = term if total is None else total + term
        out[:, column : column + width] = total.astype(BF16)
        column += width


def grads_of(*pairs, after=()):
    pieces = tuple(len(left) for left, _ in pairs)
    halves = tuple(len(right) for _, right in pairs)
    size = pairs[0][1][0].shape[0] // 2
    args = [item for left, right in pairs for item in (*left, *right)]
    width = sum(right[0].shape[1] for _, right in pairs)
    return call(
        "grads",
        partial(grads_body, pieces, halves, size),
        [((D, width), BF16)],
        args,
        after=after,
        cost=work(2 * 4 * size * D * width, 8 * size * (D + width)),
    )[0]


def inner_back_body(one, two, o_ref, gain, bias, mat, do_ref, u_ref, vec_ref):
    size = o_ref.shape[0] // 2
    gain_grad = jnp.zeros((1, o_ref.shape[1]), F32)
    bias_grad = jnp.zeros((1, o_ref.shape[1]), F32)
    out_mat = mat[:, QKV:]
    for place, piece in enumerate((one, two)):
        rows = slice(place * size, (place + 1) * size)
        upstream = nn(piece[:size], out_mat)
        columns = to_columns(decode(piece[size : size + TAIL // 2]))
        mean, scaled, first, second = (columns[:, i : i + 1] for i in range(4))
        normal = (o_ref[rows, :] - mean) * scaled
        back = scaled * (upstream * gain[...] - first - normal * second)
        do_ref[rows, :] = back.astype(BF16)
        u_ref[rows, :] = (normal * gain[...] + bias[...]).astype(BF16)
        gain_grad += jnp.sum(upstream * normal, axis=0, keepdims=True)
        bias_grad += jnp.sum(upstream, axis=0, keepdims=True)
    vec_ref[...] = vector_rows(gain_grad, bias_grad)


def inner_back(pieces, out, gain, bias, mat, after=()):
    count, width = out.shape
    return call(
        "inner_back",
        inner_back_body,
        [((count, width), BF16)] * 2 + [((8, width), F32)],
        [*pieces, out, gain, bias, mat],
        after=after,
        cost=work(2 * count * D * width, 4 * count * D),
    )


def unproject_body(rows, mat, p_one, p_two):
    size = p_one.shape[0]
    for place, p_ref in enumerate((p_one, p_two)):
        p_ref[...] = nt(rows[place * size : (place + 1) * size], mat[:, :QKV]).astype(BF16)


def unproject(rows, mat, after=()):
    count = rows.shape[0]
    return call(
        "unproject",
        unproject_body,
        [((count // 2, D), BF16)] * 2,
        [rows, mat],
        after=after,
        cost=work(2 * count * D * QKV, 4 * count * D),
    )


def branch_of(own, mate, far, feature_count):
    rows = own.shape[0] - TAIL
    half = rows + TAIL // 2
    pieces = (own, mate, far)
    product = sum(piece[:rows].astype(F32) for piece in pieces)
    stats = sum(decode(piece[rows:half]) for piece in pieces) / feature_count
    folded = sum(decode_vectors(piece[half:]) for piece in pieces)
    mean = stats[0:1]
    scaled = lax.rsqrt(stats[1:2] - mean * mean + EPS)
    kept = jnp.concatenate([mean, scaled, jnp.zeros((6, rows), F32)], axis=0)
    columns = to_columns(kept)
    branch = columns[:, 1:2] * (product - columns[:, 0:1] * folded[0:1])
    return branch, folded[1:2], folded[0:1], kept


def enter_body(x_ref, gain, bias, h_ref):
    normal, _ = split_norm(x_ref[...].astype(F32))
    h_ref[...] = (normal * gain[...] + bias[...]).astype(BF16)


def enter(rows, gain, bias):
    return call("enter", enter_body, [(rows.shape, BF16)], [rows, gain, bias])[0]


def after_attend_body(x_ref, own, mate, far, gain, bias, x2_ref, z_ref, h_ref, fold_ref, kept_ref):
    branch, shift, folded, kept = branch_of(own, mate, far, D)
    mid = x_ref[...].astype(F32) + branch + shift
    x2_ref[...] = mid
    z_ref[...] = branch
    normal, _ = split_norm(mid)
    h_ref[...] = (normal * gain[...] + bias[...]).astype(BF16)
    fold_ref[...] = jnp.broadcast_to(folded, fold_ref.shape)
    kept_ref[...] = kept


def after_attend(x, pieces, gain, bias, after=()):
    rows = x.shape[0]
    return call(
        "after_attend",
        after_attend_body,
        [((rows, D), F32), ((rows, D), F32), ((rows, D), BF16), ((8, D), F32), ((8, rows), F32)],
        [x, *pieces, gain, bias],
        after=after,
    )


def mask_column(labels, rows):
    return (to_columns(labels[:, :rows])[:, 0:1] >= 0).astype(F32)


def after_feed_body(x2, own, mate, far, labels, gain, bias, y_ref, z_ref, h_ref, fold_ref, kept_ref):
    branch, shift, folded, kept = branch_of(own, mate, far, FF)
    out = (mask_column(labels, x2.shape[0]) * (x2[...] + branch + shift)).astype(BF16)
    y_ref[...] = out
    z_ref[...] = branch
    normal, _ = split_norm(out.astype(F32))
    h_ref[...] = (normal * gain[...] + bias[...]).astype(BF16)
    fold_ref[...] = jnp.broadcast_to(folded, fold_ref.shape)
    kept_ref[...] = kept


def after_feed(x2, pieces, labels, gain, bias, after=()):
    rows = x2.shape[0]
    return call(
        "after_feed",
        after_feed_body,
        [((rows, D), BF16), ((rows, D), F32), ((rows, D), BF16), ((8, D), F32), ((8, rows), F32)],
        [x2, *pieces, labels, gain, bias],
        after=after,
    )


def finish_feed_body(x2, own, mate, far, labels, y_ref):
    branch, shift, _, _ = branch_of(own, mate, far, FF)
    y_ref[...] = (mask_column(labels, x2.shape[0]) * (x2[...] + branch + shift)).astype(BF16)


def finish_feed(x2, pieces, labels):
    return call("finish_feed", finish_feed_body, [(x2.shape, BF16)], [x2, *pieces, labels])[0]


def payload_of(grad, branch, folded, kept, feature_count):
    sent = grad.astype(BF16)
    wide = sent.astype(F32)
    means = to_rows(
        jnp.sum(wide * folded, axis=-1, keepdims=True),
        jnp.sum(wide * branch, axis=-1, keepdims=True),
    )
    stats = jnp.concatenate([kept[0:2], means[0:2] / feature_count, kept[4:8]], axis=0)
    tail = jnp.concatenate([encode(stats), jnp.zeros((TAIL // 2, D), BF16)], axis=0)
    return jnp.concatenate([sent, tail], axis=0)


def feed_norm_back_body(
    own, mate, far, g_ref, labels, x2, gain, branch, folded, kept, dx_ref, out_ref, vec_ref
):
    upstream = own[...].astype(F32) + mate[...].astype(F32) + far[...].astype(F32)
    back, gain_grad, bias_grad = norm_back(x2[...], gain[...], upstream)
    total = mask_column(labels, x2.shape[0]) * g_ref[...].astype(F32) + back
    dx_ref[...] = total
    out_ref[...] = payload_of(total, branch[...], folded[0:1], kept[...], D)
    vec_ref[...] = vector_rows(gain_grad, bias_grad)


def feed_norm_back(pieces, grad, labels, x2, gain, branch, folded, kept, after=()):
    rows = x2.shape[0]
    return call(
        "feed_norm_back",
        feed_norm_back_body,
        [((rows, D), F32), ((rows + TAIL, D), BF16), ((8, D), F32)],
        [*pieces, grad, labels, x2, gain, branch, folded, kept],
        after=after,
    )


def first_norm_back_body(has_next, *refs):
    own, mate, far, dx2, x_ref, gain, *refs = refs
    upstream = own[...].astype(F32) + mate[...].astype(F32) + far[...].astype(F32)
    back, gain_grad, bias_grad = norm_back(x_ref[...].astype(F32), gain[...], upstream)
    total = (dx2[...] + back).astype(BF16)
    if has_next:
        labels, branch, folded, kept, g_ref, vec_ref, out_ref = refs
        masked = mask_column(labels, dx2.shape[0]) * total.astype(F32)
        out_ref[...] = payload_of(masked, branch[...], folded[0:1], kept[...], FF)
    else:
        g_ref, vec_ref = refs
    g_ref[...] = total
    vec_ref[...] = vector_rows(gain_grad, bias_grad)


def first_norm_back(pieces, dx2, x, gain, following=(), after=()):
    rows = x.shape[0]
    outs = [((rows, D), BF16), ((8, D), F32)]
    if following:
        outs.append(((rows + TAIL, D), BF16))
    return call(
        "first_norm_back",
        partial(first_norm_back_body, bool(following)),
        outs,
        [*pieces, dx2, x, gain, *following],
        after=after,
    )


def first_block_body(query, key, value, output, out):
    width = query.shape[1]
    for place, ref in enumerate((query, key, value)):
        out[:, place * width : (place + 1) * width] = ref[...]
    out[:, 3 * width :] = output[...].T


def first_block(query, key, value, output):
    rows = query.shape[0]
    return call("first_block", first_block_body, [((rows, D), BF16)], [query, key, value, output])[0]


def second_block_body(up, down, out):
    out[:, :UNITS] = up[...]
    out[:, UNITS:] = down[...].T


def second_block(up, down, after=()):
    rows = up.shape[0]
    return call(
        "second_block", second_block_body, [((rows, 2 * UNITS), BF16)], [up, down], after=after
    )[0]


def mask_body(rows, labels, out):
    out[...] = (mask_column(labels, rows.shape[0]) * rows[...].astype(F32)).astype(BF16)


def mask_rows(rows, labels):
    return call("mask_rows", mask_body, [(rows.shape, BF16)], [rows, labels])[0]


def pack_body(*refs):
    *items, out = refs
    size = items[0].shape[0]
    for place, item in enumerate(items):
        out[place * size : (place + 1) * size, :] = item[...]


def pack(items):
    rows, width = items[0].shape
    return call("pack", pack_body, [((len(items) * rows, width), BF16)], list(items))[0]


def unpack_body(flags, own, sent, got_own, got_sent, y_ref, g_ref):
    size = y_ref.shape[0] // 2
    width = y_ref.shape[1]
    here = jnp.full((1, width), flags[0], jnp.int32) == 1
    rows = pl.ds(pl.multiple_of(flags[2] * size, size), size)
    first = pl.ds(pl.multiple_of(flags[3] * size, size), size)
    second = pl.ds(pl.multiple_of((1 - flags[3]) * size, size), size)
    last = slice(2 * size, 3 * size)
    y_ref[first, :] = jnp.where(here, own[rows, :], got_own[rows, :])
    y_ref[second, :] = jnp.where(here, sent[rows, :], got_sent[rows, :])
    g_ref[first, :] = jnp.where(here, own[last, :], got_own[last, :])
    g_ref[second, :] = jnp.where(here, sent[last, :], got_sent[last, :])


def unpack(flags, own, sent, got_own, got_sent):
    rows = 2 * own.shape[0] // 3
    return call(
        "unpack",
        unpack_body,
        [((rows, own.shape[1]), BF16)] * 2,
        [flags, own, sent, got_own, got_sent],
    )


def share_body(count, flags, block, across, own, *sent):
    size = own.shape[0]
    for step, out in enumerate((own, *sent)):
        rows = pl.ds(pl.multiple_of((flags[1] ^ step) * size, size), size)
        out[...] = (block[rows, :].astype(F32) + across[rows, :].astype(F32)).astype(BF16)


def share(flags, block, across, count, after=()):
    rows, width = block.shape
    return call(
        "share",
        partial(share_body, count),
        [((rows // count, width), BF16)] * count,
        [flags, block, across],
        after=after,
    )


def total_body(*refs):
    *parts, out = refs
    out[...] = sum(part[...].astype(F32) for part in parts).astype(out.dtype)


def total_of(parts, kind=BF16):
    return call("total", total_body, [(parts[0].shape, kind)], list(parts))[0]


def final_first_body(flags, lower, upper, q_ref, k_ref, v_ref, o_ref):
    width = q_ref.shape[1]
    first = jnp.full((1, D), flags[2], jnp.int32) == 0
    total = jnp.where(first, lower[...].astype(F32), upper[...].astype(F32))
    for place, ref in enumerate((q_ref, k_ref, v_ref)):
        ref[...] = total[:, place * width : (place + 1) * width]
    o_ref[...] = total[:, 3 * width :].T


def final_first(flags, lower, upper):
    rows, width = lower.shape[0], D // LANES
    return call(
        "final_first",
        final_first_body,
        [((rows, width), F32)] * 3 + [((width, rows), F32)],
        [flags, lower, upper],
    )


def final_second_body(flags, lower, upper, up_ref, down_ref):
    first = jnp.full((1, 2 * UNITS), flags[2], jnp.int32) == 0
    total = jnp.where(first, lower[...].astype(F32), upper[...].astype(F32))
    up_ref[...] = total[:, :UNITS]
    down_ref[...] = total[:, UNITS:].T


def final_second(flags, lower, upper):
    rows = lower.shape[0]
    return call(
        "final_second",
        final_second_body,
        [((rows, UNITS), F32), ((UNITS, rows), F32)],
        [flags, lower, upper],
    )


def merge_body(flags, one, two, upper, out):
    size, width = one.shape
    first = jnp.full((1, width), flags[2], jnp.int32) == 0
    for place, ref in enumerate((one, two)):
        rows = slice(place * size, (place + 1) * size)
        out[rows] = jnp.where(first, ref[...], upper[rows])


def merge(flags, one, two, upper):
    return call("merge", merge_body, [(upper.shape, BF16)], [flags, one, two, upper])[0]


def vectors_body(*refs):
    *items, out = refs
    out[...] = jnp.zeros_like(out)
    for place, item in enumerate(items):
        out[2 * place : 2 * place + 2, : item.shape[1]] = item[0:2, :]


def vectors_of(items):
    return call("vectors", vectors_body, [((2 * len(items), D), F32)], list(items))[0]


def ranks_body(flags, own, got, out):
    here = jnp.full((1, D), flags[0], jnp.int32) == 1
    out[0:8] = own[0:8] + got[0:8]
    out[8:] = jnp.where(here, own[8:], got[8:])


def outer_body(own, got, out):
    out[0:8] = own[0:8] + got[...]
    out[8:] = own[8:]


def first_rows_body(own, out):
    out[...] = own[0:8]


def line_up_body(count, flags, *refs):
    *pieces, out = refs
    size = pieces[0].shape[0]
    for step, piece in enumerate(pieces):
        rows = pl.ds(pl.multiple_of((flags[1] ^ step) * size, size), size)
        out[rows, :] = piece[...]


def line_up(flags, pieces, after=()):
    count, (size, width) = len(pieces), pieces[0].shape
    return call(
        "line_up",
        partial(line_up_body, count),
        [((count * size, width), BF16)],
        [flags, *pieces],
        after=after,
    )[0]


def pick_body(flags, beside, across, out):
    near = jnp.full((1, out.shape[1]), flags[0], jnp.int32) == 1
    out[...] = jnp.where(near, beside[...], across[...])


def pick(flags, beside, across, after=()):
    return call(
        "pick", pick_body, [(beside.shape, BF16)], [flags, beside, across], after=after
    )[0]


def assemble_body(count, flags, *refs):
    beside, across, out = refs[:count], refs[count:-1], refs[-1]
    size = beside[0].shape[0]
    width = out.shape[1]
    near = jnp.full((1, width), flags[0], jnp.int32) == 1
    for step in range(count):
        rows = pl.ds(pl.multiple_of((flags[1] ^ step) * size, size), size)
        out[rows, :] = jnp.where(near, beside[step][...], across[step][...])


def assemble(flags, beside, across):
    count, (size, width) = len(beside), beside[0].shape
    return call(
        "assemble",
        partial(assemble_body, count),
        [((count * size, width), BF16)],
        [flags, *beside, *across],
    )[0]


def on_device(
    inputs,
    cotangent,
    doc_ids,
    norm_gain,
    norm_bias,
    w_query,
    w_key,
    w_value,
    inner_gain,
    inner_bias,
    w_output,
    feed_gain,
    feed_bias,
    w_up,
    middle_gain,
    middle_bias,
    w_down,
):
    core = lax.axis_index("section")
    lane = lax.axis_index("mp")
    lane_x = lane % 2
    lane_y = lane // 2
    count = lax.axis_size("dp")
    slice_len = inputs.shape[0] // MICRO
    rank = 2 * core + lane_x
    crossing = [(s * 4 + r, s * 4 + (r ^ 2)) for s in range(2) for r in range(4) if s == r // 2]
    returning = [(s * 4 + r, s * 4 + (r ^ 2)) for s in range(2) for r in range(4) if s != r // 2]

    def by_core(first, second):
        return jnp.where(core == 0, first, second)

    def rows_of(array, micro_index):
        return lax.dynamic_slice_in_dim(array, micro_index * slice_len, slice_len, 0)

    def own_slice(array):
        sent = lax.ppermute(rows_of(array, 1 - lane_y), BOTH, crossing)
        return jnp.where(core == lane_y, rows_of(array, lane_y), sent)

    def placed(array, layer):
        return [
            lax.ppermute(
                array,
                BOTH,
                [(s * 4 + 2 * m + x, layer * 4 + 2 * s + x) for s in range(2) for x in range(2)],
            )
            for m in range(MICRO)
        ]

    label_grid = lax.dynamic_index_in_dim(
        doc_ids.reshape(LANES, MICRO, slice_len), lane_y, 1, keepdims=False
    )
    order = (rank, 2 * (1 - core) + lane_x, rank ^ 1, 2 * (1 - core) + (1 - lane_x))
    labels = jnp.concatenate(
        [lax.dynamic_index_in_dim(label_grid, item, 0, keepdims=False) for item in order]
    )
    labels = jnp.broadcast_to(labels.astype(F32)[None], (8, LANES * slice_len))

    place = lax.axis_index("dp")
    flags = jnp.stack([core == lane_y, place, core, lane_y]).astype(jnp.int32)

    def line_pairs(step):
        return [
            ((r // 2 * count + i) * LANES + r, (r // 2 * count + (i ^ step)) * LANES + r)
            for i in range(count)
            for r in range(LANES)
        ]

    def along_line(block, step):
        return lax.ppermute(block, ("section", "dp", "mp"), line_pairs(step))

    def line_pieces(block, layer):
        if count != 4:
            block = lax.all_gather(block, "dp", axis=0, tiled=True)
        block = lax.ppermute(
            block, BOTH, [(layer * LANES + r, (r // 2) * LANES + r) for r in range(LANES)]
        )
        if count != 4:
            return [block]
        return [block] + [along_line(block, step) for step in range(1, count)]

    def fetched(pieces, hook=()):
        whole = line_up(flags, pieces, after=hook) if len(pieces) > 1 else pieces[0]
        across = lax.ppermute(whole, BOTH, crossing)
        return whole, across

    first = first_block(w_query[0], w_key[0], w_value[0], w_output[0])
    pieces = line_pieces(first, 0)
    across = [lax.ppermute(piece, BOTH, crossing) for piece in pieces]
    if count == 4:
        lower_first = assemble(flags, pieces, across)
    else:
        lower_first = pick(flags, pieces[0], across[0])
    second = second_block(w_up[0], w_down[0], after=[lower_first])
    lower_second_whole, lower_second_across = fetched(line_pieces(second, 0))
    lower_second = pick(flags, lower_second_whole, lower_second_across)
    upper_first_whole, upper_first_across = fetched(
        line_pieces(first, 1), [lower_second_whole]
    )
    upper_first = pick(flags, upper_first_whole, upper_first_across)
    upper_second_whole, upper_second_across = fetched(
        line_pieces(second, 1), [upper_first_whole]
    )
    upper_second = pick(flags, upper_second_whole, upper_second_across)

    outer_own = jnp.concatenate([norm_gain, norm_bias, feed_gain, feed_bias], axis=0)
    outer_other = core_swap(outer_own)
    split_own = jnp.concatenate([inner_gain, inner_bias, middle_gain, middle_bias], axis=1)
    split_far = y_swap(split_own)
    split_kept = jnp.where(lane_y == core, split_own, split_far)
    split_other = core_swap(jnp.where(lane_y == core, split_far, split_own))

    def small_of(outer, split):
        width = D // LANES
        return (
            [outer[i : i + 1] for i in range(4)],
            [
                split[:, :width],
                split[:, width : 2 * width],
                split[:, 2 * width : 2 * width + UNITS],
                split[:, 2 * width + UNITS :],
            ],
        )

    lower_outer, lower_split = small_of(
        by_core(outer_own, outer_other), by_core(split_kept, split_other)
    )
    upper_outer, upper_split = small_of(
        by_core(outer_other, outer_own), by_core(split_other, split_kept)
    )

    def attention(x, h, first, outer, split, hooks):
        pieces = gather_rows(h)
        near = project(pieces[0], pieces[1], first)
        far = project(pieces[2], pieces[3], first)
        half = 2 * slice_len
        o_far, p_far, p_far_mate, sum_far = attend(
            half, far, near, far, labels, first, split[0], split[1]
        )
        o_near, p_own, p_mate, sum_near = attend(
            0, near, near, far, labels, first, split[0], split[1], after=[p_far]
        )
        terms = settle(p_own, p_mate, p_far, p_far_mate, after=hooks[0])
        x2, branch, h2, folded, kept = after_attend(x, terms, outer[2], outer[3], after=hooks[1])
        state = (x, pieces, near, far, o_near, o_far, sum_near, sum_far, x2, branch, folded, kept)
        return x2, h2, state

    def attention_back(grad, sums, state, first, outer, split, following, hooks):
        x, pieces, near, far, o_near, o_far, sum_near, sum_far, x2, branch, folded, kept = state
        dx2, sent, feed_vec = feed_norm_back(
            sums, grad, labels, x2, outer[2], branch, folded, kept, after=hooks[0]
        )
        backs = gather_rows(sent)
        do_near, u_near, vec_near = inner_back(
            backs[:2], o_near, split[0], split[1], first, after=hooks[1]
        )
        do_far, u_far, vec_far = inner_back(
            backs[2:], o_far, split[0], split[1], first, after=hooks[2]
        )
        dq_near, dq_far = attend_back(
            near, far, do_near, do_far, sum_near, sum_far, labels, after=hooks[3]
        )
        p_far, p_far_mate = unproject(dq_far, first)
        p_own, p_mate = unproject(dq_near, first, after=[p_far])
        terms = settle(p_own, p_mate, p_far, p_far_mate)
        mat_grad = grads_of(
            (pieces, (dq_near, dq_far)), (backs, (u_near, u_far)), after=[p_far]
        )
        result = first_norm_back(terms, dx2, x, outer[0], following, after=hooks[4](mat_grad))
        return result, mat_grad, vec_near + vec_far, feed_vec

    def reduce_blocks(block, after=()):
        across = lax.ppermute(block, BOTH, returning)
        if count != 4:
            total = total_of([block, across])
            return [lax.psum_scatter(total, "dp", scatter_dimension=0, tiled=True)]
        return share(flags, block, across, count, after)

    def reduce_line(parts, layer):
        if count == 4:
            parts = [parts[0]] + [
                along_line(part, step) for step, part in enumerate(parts) if step > 0
            ]
            parts = [total_of(parts)]
        return lax.ppermute(
            parts[0], BOTH, [((r // 2) * LANES + r, layer * LANES + r) for r in range(LANES)]
        )

    lower_in = own_slice(inputs)

    upstream = own_slice(cotangent)
    top = gather_rows(mask_rows(upstream, labels))

    h = enter(lower_in, lower_outer[0], lower_outer[1])
    x2, h2, lower_state = attention(
        lower_in,
        h,
        lower_first,
        lower_outer,
        lower_split,
        ([lower_second_whole, top[3]], [upper_first_whole]),
    )
    lower_pieces = gather_rows(h2)
    f_near, p_own, p_mate = feed(lower_pieces[:2], (), lower_second, *lower_split[2:])
    f_far, p_far, p_far_mate = feed(lower_pieces[2:], (), lower_second, *lower_split[2:])
    lower_pre = (f_near, f_far)
    terms = settle(p_own, p_mate, p_far, p_far_mate)
    lower_out, lower_branch, h, lower_folded, lower_kept = after_feed(
        x2,
        terms,
        labels,
        upper_outer[0],
        upper_outer[1],
        after=[upper_first_across, upper_second_whole],
    )
    x2, h2, upper_state = attention(
        lower_out, h, upper_first, upper_outer, upper_split, ((), [upper_second_across])
    )
    upper_pieces = gather_rows(h2)
    f_near, p_own, p_mate, near_stats = feed(
        upper_pieces[:2], top[:2], upper_second, *upper_split[2:]
    )
    f_far, p_far, p_far_mate, far_stats = feed(
        upper_pieces[2:], top[2:], upper_second, *upper_split[2:]
    )
    upper_pre = (f_near, f_far)

    stats = group_stats(near_stats, far_stats)

    def feed_backward(pieces, rows, stats, pre, second, split, hooks):
        df_far, n_far, p_far, p_far_mate, vec_far = feed_back(
            pieces[2:], stats, 2, pre[1], split[2], split[3], second, after=hooks[0]
        )
        df_near, n_near, p_own, p_mate, vec_near = feed_back(
            pieces[:2], stats, 0, pre[0], split[2], split[3], second, after=[p_far, *hooks[1]]
        )
        terms = settle(p_own, p_mate, p_far, p_far_mate)
        mat_grad = grads_of(
            (rows, (df_near, df_far)), (pieces, (n_near, n_far)), after=[p_far, p_own]
        )
        return terms, mat_grad, vec_near + vec_far

    sums, block, upper_middle = feed_backward(
        top, upper_pieces, [stats], upper_pre, upper_second, upper_split, ((), ())
    )
    upper_second_parts = reduce_blocks(block)
    sent = call(
        "pair_sum", pair_sum_body, [(p_far.shape, BF16)], [p_far, core_swap(p_far_mate)]
    )[0]
    upper_out = finish_feed(x2, (p_own, core_swap(p_mate), x_swap(sent)), labels)
    following = (labels, lower_branch, lower_folded, lower_kept)
    (upper_grad, upper_norm, sent), block, upper_inner, upper_feed = attention_back(
        upstream,
        sums,
        upper_state,
        upper_first,
        upper_outer,
        upper_split,
        following,
        ([block], (), (), [upper_second_parts[0], sent], lambda item: [item, upper_out]),
    )
    upper_second_sum = reduce_line(upper_second_parts, 1)
    upper_first_parts = reduce_blocks(block)

    backs = gather_rows(sent)
    own = pack([lower_out, upper_out, upper_grad])
    swapped = lax.ppermute(own, BOTH, returning)
    inward = [((r // 2) * LANES + r, (1 - r // 2) * LANES + r) for r in range(LANES)]
    layer_outputs, upper_held = unpack(
        flags, own, swapped, lax.ppermute(own, BOTH, inward), lax.ppermute(swapped, BOTH, inward)
    )
    sums, block, lower_middle = feed_backward(
        backs,
        lower_pieces,
        (),
        lower_pre,
        lower_second,
        lower_split,
        ([own], [upper_first_parts[0], upper_second_sum]),
    )
    upper_first_sum = reduce_line(upper_first_parts, 1)
    lower_second_parts = reduce_blocks(block)
    lower_second_sum = reduce_line(lower_second_parts, 0)
    last_parts = []

    def reduced(item):
        last_parts.extend(reduce_blocks(item))
        return last_parts

    (lower_grad, lower_norm), _, lower_inner, lower_feed = attention_back(
        upper_grad,
        sums,
        lower_state,
        lower_first,
        lower_outer,
        lower_split,
        (),
        (
            [block, swapped],
            (),
            (),
            [lower_second_parts[0], upper_first_sum, layer_outputs],
            lambda item: [reduced(item)[0], lower_second_sum],
        ),
    )
    input_grads = merge(flags, *placed(lower_grad, 0), upper_held)
    grad_query, grad_key, grad_value, grad_output = final_first(
        flags, reduce_line(last_parts, 0), upper_first_sum
    )
    grad_up, grad_down = final_second(flags, lower_second_sum, upper_second_sum)

    vectors = vectors_of(
        [lower_norm, lower_feed, upper_norm, upper_feed, lower_middle, upper_middle]
        + [lower_inner, upper_inner]
    )
    shape = [(vectors.shape, F32)]
    vectors = total_of([vectors, y_swap(vectors)], F32)
    vectors = call("ranks", ranks_body, shape, [flags, vectors, core_swap(vectors)])[0]
    outer = call("first_rows", first_rows_body, [((8, D), F32)], [vectors])[0]
    vectors = call("outer", outer_body, shape, [vectors, x_swap(outer)])[0]
    if count == 4:
        vectors = total_of(
            [vectors]
            + [
                lax.ppermute(vectors, "dp", [(i, i ^ step) for i in range(count)])
                for step in range(1, count)
            ],
            F32,
        )
    else:
        vectors = lax.psum(vectors, "dp")

    def part(rows, start, size):
        rows = lax.dynamic_slice(rows, (core * rows.shape[0] // 2, start), (rows.shape[0] // 2, size))
        return [rows[i : i + 1] for i in range(rows.shape[0])]

    width = D // LANES
    size = D // count // LANES
    outer = part(vectors[:8], (place * LANES + lane) * size, size)
    middle = part(vectors[8:12], place * (UNITS // count), UNITS // count)
    inner = part(vectors[12:], place * (width // count), width // count)
    return (
        layer_outputs[None],
        input_grads[None],
        outer[0],
        outer[1],
        grad_query[None],
        grad_key[None],
        grad_value[None],
        inner[0],
        inner[1],
        grad_output[None],
        outer[2],
        outer[3],
        grad_up[None],
        middle[0],
        middle[1],
        grad_down[None],
    )


def solution(mesh):
    placed = (
        P(("dp", "mp"), None),
        P(("dp", "mp"), None),
        P("dp"),
        P("section", None),
        P("section", None),
        P("section", "dp", "mp"),
        P("section", "dp", "mp"),
        P("section", "dp", "mp"),
        P("section", "mp"),
        P("section", "mp"),
        P("section", "mp", "dp"),
        P("section", None),
        P("section", None),
        P("section", "dp", "mp"),
        P("section", "mp"),
        P("section", "mp"),
        P("section", "mp", "dp"),
    )
    return jax.shard_map(
        on_device,
        mesh=mesh,
        in_specs=placed,
        out_specs=(
            P("section", ("dp", "mp"), None),
            P("section", ("dp", "mp"), None),
            P("section", ("dp", "mp")),
            P("section", ("dp", "mp")),
            P("section", "dp", "mp"),
            P("section", "dp", "mp"),
            P("section", "dp", "mp"),
            P("section", ("mp", "dp")),
            P("section", ("mp", "dp")),
            P("section", "mp", "dp"),
            P("section", ("dp", "mp")),
            P("section", ("dp", "mp")),
            P("section", "dp", "mp"),
            P("section", ("mp", "dp")),
            P("section", ("mp", "dp")),
            P("section", "mp", "dp"),
        ),
        check_vma=False,
    )
```

```python
from functools import partial

import jax
import jax.numpy as jnp
from jax import lax
from jax.experimental import pallas as pl
from jax.experimental.pallas import tpu as pltpu
from jax.sharding import PartitionSpec as P

D = 768
HEAD_DIM = 64
FF = 3072
MICRO = 2
LANES = 4
EPS = 1e-05
SCALE = HEAD_DIM ** (-0.5)
LOG2E = 1.4426950408889634
SQRT_HALF = 0.7071067811865476
INV_SQRT_2PI = 0.3989422804014327
BOTH = ("section", "mp")
Y_PAIRS = [[0, 2], [1, 3]]
QKV = 3 * D // LANES
UNITS = FF // LANES
TAIL = 16
F32 = jnp.float32
BF16 = jnp.bfloat16

VMEM = pl.BlockSpec(memory_space=pltpu.VMEM)
SMEM = pl.BlockSpec(memory_space=pltpu.SMEM)
ANY = pl.BlockSpec(memory_space=pl.ANY)
HBM = pl.BlockSpec(memory_space=pltpu.HBM)
PARAMS = pltpu.CompilerParams(vmem_limit_bytes=16 * 1024 * 1024)


def call(name, body, outs, ins, scratch=(), after=(), cost=None):
    count = len(ins)

    def kernel(*refs):
        body(*refs[:count], *refs[count + len(after) :])

    return pl.pallas_call(
        kernel,
        out_shape=tuple(jax.ShapeDtypeStruct(shape, kind) for shape, kind in outs),
        in_specs=[SMEM if item.ndim == 1 else VMEM for item in ins] + [ANY] * len(after),
        out_specs=(VMEM,) * len(outs),
        scratch_shapes=list(scratch),
        compiler_params=PARAMS,
        name=name,
        cost_estimate=cost or work(1, 1),
    )(*ins, *after)


def work(flops, size):
    return pl.CostEstimate(flops=int(flops), bytes_accessed=int(size), transcendentals=0)


def nn(a, b):
    return jnp.dot(a, b, preferred_element_type=F32)


def nt(a, b):
    return lax.dot_general(a, b, (((1,), (1,)), ((), ())), preferred_element_type=F32)


def tn(a, b):
    return lax.dot_general(a, b, (((0,), (0,)), ((), ())), preferred_element_type=F32)


def to_rows(*columns):
    count = columns[0].shape[0]
    lane = lax.broadcasted_iota(jnp.int32, (count, 128), 1)
    tile = jnp.zeros((count, 128), F32)
    for place, column in enumerate(columns):
        tile = jnp.where(lane == place, column, tile)
    return tile.T[:8]


def to_columns(rows):
    return jnp.concatenate([rows, jnp.zeros((120, rows.shape[1]), F32)], axis=0).T


def split_three(values):
    high = values.astype(BF16)
    rest = values - high.astype(F32)
    middle = rest.astype(BF16)
    return high, middle, (rest - middle.astype(F32)).astype(BF16)


def encode(rows):
    return jnp.concatenate(split_three(rows), axis=1)


def decode(tail):
    tail = tail.astype(F32)
    count = tail.shape[1] // 3
    return tail[:, :count] + tail[:, count : 2 * count] + tail[:, 2 * count :]


def decode_vectors(tail):
    tail = tail.astype(F32)
    return jnp.concatenate(
        [jnp.sum(tail[0:3], axis=0, keepdims=True), jnp.sum(tail[3:6], axis=0, keepdims=True)],
        axis=0,
    )


def encode_vectors(first, second):
    return jnp.concatenate(
        [*split_three(first), *split_three(second), jnp.zeros((2, first.shape[1]), BF16)], axis=0
    )


def split_norm(values):
    mean = jnp.mean(values, axis=-1, keepdims=True)
    spread = jnp.mean(values * values, axis=-1, keepdims=True) - mean * mean
    scaled = lax.rsqrt(spread + EPS)
    return (values - mean) * scaled, scaled


def norm_back(values, gain, upstream):
    normal, scaled = split_norm(values)
    inner = upstream * gain
    one = jnp.mean(inner, axis=-1, keepdims=True)
    two = jnp.mean(inner * normal, axis=-1, keepdims=True)
    back = scaled * (inner - one - normal * two)
    return (
        back,
        jnp.sum(upstream * normal, axis=0, keepdims=True),
        jnp.sum(upstream, axis=0, keepdims=True),
    )


def vector_rows(first, second):
    return jnp.concatenate([first, second, jnp.zeros((6, first.shape[1]), F32)], axis=0)


def folded_vectors(mat, gain, bias):
    rows = jnp.concatenate(
        [*split_three(gain), *split_three(bias), jnp.zeros((10, gain.shape[1]), BF16)], axis=0
    )
    folded = nt(rows, mat)
    return encode_vectors(
        jnp.sum(folded[0:3], axis=0, keepdims=True), jnp.sum(folded[3:6], axis=0, keepdims=True)
    )


def core_swap(x):
    return lax.ppermute(x, "section", [(0, 1), (1, 0)])


def x_swap(x):
    return lax.ppermute(x, "mp", [(i, i ^ 1) for i in range(LANES)])


def y_swap(x):
    return lax.ppermute(x, "mp", [(i, i ^ 2) for i in range(LANES)])


def gather_rows(own):
    far = x_swap(own)
    return own, core_swap(own), far, core_swap(far)


def pair_sum_body(first, second, out):
    rows = out.shape[0] - TAIL
    out[:rows] = (first[:rows].astype(F32) + second[:rows].astype(F32)).astype(BF16)
    half = rows + TAIL // 2
    out[rows:half] = encode(decode(first[rows:half]) + decode(second[rows:half]))
    folded = decode_vectors(first[half:]) + decode_vectors(second[half:])
    out[half:] = encode_vectors(folded[0:1], folded[1:2])


def pair_add_body(first, second, out):
    out[...] = (first[...].astype(F32) + second[...].astype(F32)).astype(BF16)


def pair_sum(far, far_mate):
    body = pair_sum_body if far.shape[0] % 256 else pair_add_body
    return call("pair_sum", body, [(far.shape, BF16)], [far, core_swap(far_mate)])[0]


def settle(own, mate, far, far_mate):
    sent = pair_sum(far, far_mate)
    return own, core_swap(mate), x_swap(sent)


def project_body(first, second, mat, out):
    size = first.shape[0]
    for place, piece in enumerate((first, second)):
        out[place * size : (place + 1) * size, :] = nn(piece[...], mat[:, :QKV]).astype(BF16)


def project(first, second, mat):
    count = 2 * first.shape[0]
    return call(
        "project",
        project_body,
        [((count, QKV), BF16)],
        [first, second, mat],
    )[0]


def split_heads(source, target, first, start, head_count):
    size = source.shape[0]
    for head in range(head_count):
        lanes = slice(first + head * HEAD_DIM, first + (head + 1) * HEAD_DIM)
        target[head, start : start + size, :] = source[:, lanes]


def attend_body(
    q_start, q_ref, near, far, labels, mat, gain, bias, o_ref, p_one, p_two, sum_ref, ks, vs
):
    head_count = QKV // (3 * HEAD_DIM)
    width = head_count * HEAD_DIM
    half = near.shape[0]
    for start, ref in ((0, near), (half, far)):
        split_heads(ref, ks, width, start, head_count)
        split_heads(ref, vs, 2 * width, start, head_count)
    out_mat = mat[:, QKV:]
    folded = folded_vectors(out_mat, gain[...], bias[...])
    size = half // 2
    key_labels = labels[0:1, :]
    for place, p_ref in enumerate((p_one, p_two)):
        rows = slice(place * size, (place + 1) * size)
        first = q_start + place * size
        allowed = to_columns(labels[:, first : first + size])[:, 0:1] == key_labels
        outs = []
        sums = []
        for head in range(head_count):
            query = q_ref[rows, head * HEAD_DIM : (head + 1) * HEAD_DIM]
            scores = jnp.where(allowed, nt(query, ks[head]), -1e30)
            peak = jnp.max(scores, axis=-1, keepdims=True)
            terms = jnp.exp2((scores - peak) * (SCALE * LOG2E))
            total = jnp.sum(terms, axis=-1, keepdims=True)
            outs.append(nn(terms.astype(BF16), vs[head]) / total)
            sums.append(peak * (SCALE * LOG2E) + jnp.log(total) * LOG2E)
        out = jnp.concatenate(outs, axis=1)
        o_ref[rows, :] = out
        lane = lax.broadcasted_iota(jnp.int32, (size, 128), 1)
        tile = jnp.zeros((size, 128), F32)
        for spot, column in enumerate(sums):
            tile = jnp.where(lane == spot, column, tile)
        sum_ref[rows, :] = tile
        p_ref[:size] = nt((out * gain[...]).astype(BF16), out_mat).astype(BF16)
        stats = to_rows(
            jnp.sum(out, axis=-1, keepdims=True), jnp.sum(out * out, axis=-1, keepdims=True)
        )
        p_ref[size : size + TAIL // 2] = encode(stats)
        p_ref[size + TAIL // 2 :] = folded


def attend(q_start, queries, near, far, labels, mat, gain, bias, after=()):
    count, keys = queries.shape[0], 2 * near.shape[0]
    heads = QKV // (3 * HEAD_DIM)
    width = heads * HEAD_DIM
    by_head = pltpu.VMEM((heads, keys, HEAD_DIM), BF16)
    payload = ((count // 2 + TAIL, D), BF16)
    return call(
        "attend",
        partial(attend_body, q_start),
        [((count, width), F32), payload, payload, ((count, 128), F32)],
        [queries, near, far, labels, mat, gain, bias],
        [by_head, by_head],
        after,
        work(4e9, 1),
    )


def attend_back_body(
    near, far, do_near, do_far, sum_near, sum_far, labels, near_out, far_out,
    qs, ks, vs, grads, dqs, dks, dvs, sums,
):
    head_count = QKV // (3 * HEAD_DIM)
    width = head_count * HEAD_DIM
    half = near.shape[0]
    for start, ref, grad in ((0, near, do_near), (half, far, do_far)):
        split_heads(ref, qs, 0, start, head_count)
        split_heads(ref, ks, width, start, head_count)
        split_heads(ref, vs, 2 * width, start, head_count)
        split_heads(grad, grads, 0, start, head_count)
    sums[:half] = sum_near[...]
    sums[half:] = sum_far[...]
    dks[...] = jnp.zeros_like(dks)
    dvs[...] = jnp.zeros_like(dvs)
    key_labels = labels[0:1, :]
    size = half // 2

    def block(index, carry):
        rows = pl.ds(pl.multiple_of(index * size, size), size)
        allowed = to_columns(labels[:, rows])[:, 0:1] == key_labels
        for head in range(head_count):
            query, grad = qs[head, rows, :], grads[head, rows, :]
            scores = jnp.where(allowed, nt(query, ks[head]), -1e30)
            prob = jnp.exp2(scores * (SCALE * LOG2E) - sums[rows, head : head + 1])
            prob_grad = nt(grad, vs[head])
            delta = jnp.sum(prob * prob_grad, axis=-1, keepdims=True)
            score_grad = (prob * (prob_grad - delta)).astype(BF16)
            dqs[head, rows, :] = nn(score_grad, ks[head]) * SCALE
            dks[head] += tn(query, score_grad)
            dvs[head] += tn(grad, prob.astype(BF16))
        return carry

    lax.fori_loop(0, 4, block, 0)
    for start, out in ((0, near_out), (half, far_out)):
        rows = slice(start, start + half)
        heads = range(head_count)
        out[...] = jnp.concatenate(
            [dqs[head, rows, :].astype(BF16) for head in heads]
            + [(dks[head, :, rows].T * SCALE).astype(BF16) for head in heads]
            + [dvs[head, :, rows].T.astype(BF16) for head in heads],
            axis=1,
        )


def attend_back(near, far, do_near, do_far, sum_near, sum_far, labels, after=()):
    half, width = do_near.shape
    keys = 2 * half
    heads = width // HEAD_DIM
    by_head = pltpu.VMEM((heads, keys, HEAD_DIM), BF16)
    turned = pltpu.VMEM((heads, HEAD_DIM, keys), F32)
    return call(
        "attend_back",
        attend_back_body,
        [(near.shape, BF16)] * 2,
        [near, far, do_near, do_far, sum_near, sum_far, labels],
        [by_head] * 4
        + [pltpu.VMEM((heads, keys, HEAD_DIM), F32), turned, turned, pltpu.VMEM((keys, 128), F32)],
        after,
        work(1.4e10, 1),
    )


def gelu_parts(x):
    spread = 0.5 + 0.5 * lax.erf(x * SQRT_HALF)
    return x * spread, spread


def feed_body(with_back, *refs):
    if with_back:
        one, two, back_one, back_two, mat, gain, bias, f_ref, p_one, p_two, s_ref = refs
    else:
        one, two, mat, gain, bias, f_ref, p_one, p_two = refs
        back_one = back_two = s_ref = None
    size = one.shape[0]
    up, down = mat.at[:, :UNITS], mat.at[:, UNITS:]
    folded = folded_vectors(down[...], gain[...], bias[...])
    for place, (piece, p_ref, back) in enumerate(((one, p_one, back_one), (two, p_two, back_two))):
        rows = slice(place * size, (place + 1) * size)
        pre = nn(piece[...], up[...])
        f_ref[rows, :] = pre
        act, _ = gelu_parts(pre)
        p_ref[:size] = nt((act * gain[...]).astype(BF16), down[...]).astype(BF16)
        columns = [
            jnp.sum(act, axis=-1, keepdims=True),
            jnp.sum(act * act, axis=-1, keepdims=True),
        ]
        p_ref[size : size + TAIL // 2] = encode(to_rows(*columns))
        p_ref[size + TAIL // 2 :] = folded
        if with_back:
            inner = nn(back[...], down[...]) * gain[...]
            columns.append(jnp.sum(inner, axis=-1, keepdims=True))
            columns.append(jnp.sum(inner * act, axis=-1, keepdims=True))
            s_ref[8 * place : 8 * place + 8, :] = to_rows(*columns)


def feed(pieces, backs, mat, gain, bias, after=()):
    size = pieces[0].shape[0]
    outs = [((2 * size, UNITS), F32)] + [((size + TAIL, D), BF16)] * 2
    if backs:
        outs += [((16, size), F32)]
    return call(
        "feed",
        partial(feed_body, bool(backs)),
        outs,
        [*pieces, *backs, mat, gain, bias],
        after=after,
    )


def feed_back_body(first_piece, *refs):
    if first_piece is not None:
        one, two, s_ref, *refs = refs
    else:
        one, two, *refs = refs
        s_ref = None
    f_ref, gain, bias, mat, df_ref, n_ref, p_one, p_two, vec_ref = refs
    up, down = mat.at[:, :UNITS], mat.at[:, UNITS:]
    size = p_one.shape[0]
    gain_grad = jnp.zeros((1, UNITS), F32)
    bias_grad = jnp.zeros((1, UNITS), F32)
    for place, (piece, p_ref) in enumerate(((one, p_one), (two, p_two))):
        rows = slice(place * size, (place + 1) * size)
        upstream = nn(piece[:size], down[...])
        pre = f_ref[rows, :]
        if first_piece is not None:
            start = 8 * (first_piece + place)
            stats = s_ref[start : start + 8, :]
        else:
            stats = decode(piece[size : size + TAIL // 2])
        columns = to_columns(stats)
        mean, scaled, first, second = (columns[:, i : i + 1] for i in range(4))
        act, spread = gelu_parts(pre)
        normal = (act - mean) * scaled
        act_grad = scaled * (upstream * gain[...] - first - normal * second)
        slope = spread + pre * (jnp.exp(-0.5 * pre * pre) * INV_SQRT_2PI)
        pre_grad = (act_grad * slope).astype(BF16)
        df_ref[rows, :] = pre_grad
        n_ref[rows, :] = (normal * gain[...] + bias[...]).astype(BF16)
        p_ref[...] = nt(pre_grad, up[...]).astype(BF16)
        gain_grad += jnp.sum(upstream * normal, axis=0, keepdims=True)
        bias_grad += jnp.sum(upstream, axis=0, keepdims=True)
    vec_ref[...] = vector_rows(gain_grad, bias_grad)


def feed_back(pieces, stats, first_piece, pre, gain, bias, mat, after=()):
    count = pre.shape[0]
    size = count // 2
    return call(
        "feed_back",
        partial(feed_back_body, first_piece if stats else None),
        [((count, UNITS), BF16)] * 2 + [((size, D), BF16)] * 2 + [((8, UNITS), F32)],
        [*pieces, *stats, pre, gain, bias, mat],
        after=after,
    )


def stats_pack_body(near, far, out):
    out[:16] = near[...]
    out[16:] = far[...]


def stats_near_body(stats, got, out):
    for place in range(4):
        other = 8 * (place ^ 1)
        out[8 * place : 8 * place + 8] = stats[8 * place : 8 * place + 8] + got[other : other + 8]


def stats_far_body(stats, got, out):
    for place in range(4):
        other = 8 * (place ^ 2)
        rows = slice(8 * place, 8 * place + 8)
        total = (stats[rows] + got[other : other + 8]) * (1.0 / FF)
        mean, one = total[0:1], total[2:3]
        scaled = lax.rsqrt(total[1:2] - mean * mean + EPS)
        two = scaled * (total[3:4] - mean * one)
        out[rows] = jnp.concatenate([mean, scaled, one, two, total[4:8]], axis=0)


def group_stats(near, far):
    shape = [((32, near.shape[1]), F32)]
    stats = call("stats_pack", stats_pack_body, shape, [near, far])[0]
    stats = call("stats_near", stats_near_body, shape, [stats, core_swap(stats)])[0]
    return call("stats_far", stats_far_body, shape, [stats, x_swap(stats)])[0]


def grads_body(pieces, halves, size, *refs):
    *refs, out = refs
    place = 0
    column = 0
    for left_count, right_count in zip(pieces, halves):
        left = refs[place : place + left_count]
        right = refs[place + left_count : place + left_count + right_count]
        place += left_count + right_count
        width = right[0].shape[1]
        per = left_count // right_count
        total = None
        for index, piece in enumerate(left):
            start = (index % per) * size
            term = tn(piece[:size], right[index // per][start : start + size, :])
            total = term if total is None else total + term
        out[:, column : column + width] = total.astype(BF16)
        column += width


def grads_of(*pairs, after=()):
    pieces = tuple(len(left) for left, _ in pairs)
    halves = tuple(len(right) for _, right in pairs)
    size = pairs[0][1][0].shape[0] // 2
    args = [item for left, right in pairs for item in (*left, *right)]
    width = sum(right[0].shape[1] for _, right in pairs)
    return call(
        "grads",
        partial(grads_body, pieces, halves, size),
        [((D, width), BF16)],
        args,
        after=after,
    )[0]


def inner_back_body(one, two, o_ref, gain, bias, mat, do_ref, u_ref, vec_ref):
    size = o_ref.shape[0] // 2
    gain_grad = jnp.zeros((1, o_ref.shape[1]), F32)
    bias_grad = jnp.zeros((1, o_ref.shape[1]), F32)
    out_mat = mat[:, QKV:]
    for place, piece in enumerate((one, two)):
        rows = slice(place * size, (place + 1) * size)
        upstream = nn(piece[:size], out_mat)
        columns = to_columns(decode(piece[size : size + TAIL // 2]))
        mean, scaled, first, second = (columns[:, i : i + 1] for i in range(4))
        normal = (o_ref[rows, :] - mean) * scaled
        back = scaled * (upstream * gain[...] - first - normal * second)
        do_ref[rows, :] = back.astype(BF16)
        u_ref[rows, :] = (normal * gain[...] + bias[...]).astype(BF16)
        gain_grad += jnp.sum(upstream * normal, axis=0, keepdims=True)
        bias_grad += jnp.sum(upstream, axis=0, keepdims=True)
    vec_ref[...] = vector_rows(gain_grad, bias_grad)


def inner_back(pieces, out, gain, bias, mat, after=()):
    count, width = out.shape
    return call(
        "inner_back",
        inner_back_body,
        [((count, width), BF16)] * 2 + [((8, width), F32)],
        [*pieces, out, gain, bias, mat],
        after=after,
    )


def unproject_body(rows, mat, one, two, gain, bias, p_one, p_two, vec_ref):
    size = p_one.shape[0]
    gain_grad = jnp.zeros((1, D), F32)
    bias_grad = jnp.zeros((1, D), F32)
    for place, (piece, p_ref) in enumerate(((one, p_one), (two, p_two))):
        term = nt(rows[place * size : (place + 1) * size], mat[:, :QKV])
        p_ref[...] = term.astype(BF16)
        gain_grad += jnp.sum(term * (piece[...].astype(F32) - bias[...]), axis=0, keepdims=True)
        bias_grad += jnp.sum(term, axis=0, keepdims=True)
    vec_ref[...] = vector_rows(gain_grad / gain[...], bias_grad)


def unproject(rows, mat, pieces, gain, bias, after=()):
    count = rows.shape[0]
    return call(
        "unproject",
        unproject_body,
        [((count // 2, D), BF16)] * 2 + [((8, D), F32)],
        [rows, mat, *pieces, gain, bias],
        after=after,
    )


def branch_of(own, mate, far, feature_count):
    rows = own.shape[0] - TAIL
    half = rows + TAIL // 2
    pieces = (own, mate, far)
    product = sum(piece[:rows].astype(F32) for piece in pieces)
    stats = sum(decode(piece[rows:half]) for piece in pieces) / feature_count
    folded = sum(decode_vectors(piece[half:]) for piece in pieces)
    mean = stats[0:1]
    scaled = lax.rsqrt(stats[1:2] - mean * mean + EPS)
    kept = jnp.concatenate([mean, scaled, jnp.zeros((6, rows), F32)], axis=0)
    columns = to_columns(kept)
    branch = columns[:, 1:2] * (product - columns[:, 0:1] * folded[0:1])
    return branch, folded[1:2], folded[0:1], kept


def after_attend_body(x_ref, own, mate, far, gain, bias, x2_ref, z_ref, h_ref, fold_ref, kept_ref):
    branch, shift, folded, kept = branch_of(own, mate, far, D)
    mid = x_ref[...].astype(F32) + branch + shift
    x2_ref[...] = mid
    z_ref[...] = branch
    normal, _ = split_norm(mid)
    h_ref[...] = (normal * gain[...] + bias[...]).astype(BF16)
    fold_ref[...] = jnp.broadcast_to(folded, fold_ref.shape)
    kept_ref[...] = kept


def after_attend(x, pieces, gain, bias, after=()):
    rows = x.shape[0]
    return call(
        "after_attend",
        after_attend_body,
        [((rows, D), F32), ((rows, D), F32), ((rows, D), BF16), ((8, D), F32), ((8, rows), F32)],
        [x, *pieces, gain, bias],
        after=after,
    )


def mask_column(labels, rows):
    return (to_columns(labels[:, :rows])[:, 0:1] >= 0).astype(F32)


def after_feed_body(x2, own, mate, far, labels, gain, bias, y_ref, z_ref, h_ref, fold_ref, kept_ref):
    branch, shift, folded, kept = branch_of(own, mate, far, FF)
    out = (mask_column(labels, x2.shape[0]) * (x2[...] + branch + shift)).astype(BF16)
    y_ref[...] = out
    z_ref[...] = branch
    normal, _ = split_norm(out.astype(F32))
    h_ref[...] = (normal * gain[...] + bias[...]).astype(BF16)
    fold_ref[...] = jnp.broadcast_to(folded, fold_ref.shape)
    kept_ref[...] = kept


def after_feed(x2, pieces, labels, gain, bias, after=()):
    rows = x2.shape[0]
    return call(
        "after_feed",
        after_feed_body,
        [((rows, D), BF16), ((rows, D), F32), ((rows, D), BF16), ((8, D), F32), ((8, rows), F32)],
        [x2, *pieces, labels, gain, bias],
        after=after,
    )


def finish_feed_body(x2, own, mate, far, labels, y_ref):
    branch, shift, _, _ = branch_of(own, mate, far, FF)
    y_ref[...] = (mask_column(labels, x2.shape[0]) * (x2[...] + branch + shift)).astype(BF16)


def finish_feed(x2, pieces, labels):
    return call("finish_feed", finish_feed_body, [(x2.shape, BF16)], [x2, *pieces, labels])[0]


def payload_of(grad, branch, folded, kept, feature_count):
    sent = grad.astype(BF16)
    wide = sent.astype(F32)
    means = to_rows(
        jnp.sum(wide * folded, axis=-1, keepdims=True),
        jnp.sum(wide * branch, axis=-1, keepdims=True),
    )
    stats = jnp.concatenate([kept[0:2], means[0:2] / feature_count, kept[4:8]], axis=0)
    tail = jnp.concatenate([encode(stats), jnp.zeros((TAIL // 2, D), BF16)], axis=0)
    return jnp.concatenate([sent, tail], axis=0)


def feed_norm_back_body(
    own, mate, far, g_ref, labels, x2, gain, branch, folded, kept, dx_ref, out_ref, vec_ref
):
    upstream = own[...].astype(F32) + mate[...].astype(F32) + far[...].astype(F32)
    back, gain_grad, bias_grad = norm_back(x2[...], gain[...], upstream)
    total = mask_column(labels, x2.shape[0]) * g_ref[...].astype(F32) + back
    dx_ref[...] = total
    out_ref[...] = payload_of(total, branch[...], folded[0:1], kept[...], D)
    vec_ref[...] = vector_rows(gain_grad, bias_grad)


def feed_norm_back(pieces, grad, labels, x2, gain, branch, folded, kept, after=()):
    rows = x2.shape[0]
    return call(
        "feed_norm_back",
        feed_norm_back_body,
        [((rows, D), F32), ((rows + TAIL, D), BF16), ((8, D), F32)],
        [*pieces, grad, labels, x2, gain, branch, folded, kept],
        after=after,
    )


def first_norm_back_body(has_next, *refs):
    own, mate, far, dx2, x_ref, gain, *refs = refs
    upstream = own[...].astype(F32) + mate[...].astype(F32) + far[...].astype(F32)
    back, _, _ = norm_back(x_ref[...].astype(F32), gain[...], upstream)
    total = (dx2[...] + back).astype(BF16)
    if has_next:
        labels, branch, folded, kept, g_ref, out_ref = refs
        masked = mask_column(labels, dx2.shape[0]) * total.astype(F32)
        out_ref[...] = payload_of(masked, branch[...], folded[0:1], kept[...], FF)
    else:
        (g_ref,) = refs
    g_ref[...] = total


def first_norm_back(pieces, dx2, x, gain, following=(), after=()):
    rows = x.shape[0]
    outs = [((rows, D), BF16)]
    if following:
        outs.append(((rows + TAIL, D), BF16))
    return call(
        "first_norm_back",
        partial(first_norm_back_body, bool(following)),
        outs,
        [*pieces, dx2, x, gain, *following],
        after=after,
    )


def fetch_all(refs, held, sems):
    copies = [
        pltpu.make_async_copy(ref, spot, sems.at[place])
        for place, (ref, spot) in enumerate(zip(refs, held))
    ]
    for copy in copies:
        copy.start()
    for copy in copies:
        copy.wait()


def first_block_body(query, key, value, output, down, out, down_out, *scratch):
    *held, sems = scratch
    fetch_all((query, key, value, output, down), held, sems)
    width = query.shape[1]
    for place, ref in enumerate(held[:3]):
        out[:, place * width : (place + 1) * width] = ref[...]
    out[:, 3 * width :] = held[3][...].T
    down_out[...] = held[4][...].T


def first_block(*blocks):
    rows = blocks[0].shape[0]
    return pl.pallas_call(
        first_block_body,
        out_shape=(
            jax.ShapeDtypeStruct((rows, D), BF16),
            jax.ShapeDtypeStruct(blocks[4].shape[::-1], BF16),
        ),
        in_specs=[HBM] * 5,
        out_specs=(VMEM, VMEM),
        scratch_shapes=[pltpu.VMEM(block.shape, BF16) for block in blocks]
        + [pltpu.SemaphoreType.DMA((5,))],
        compiler_params=PARAMS,
        name="first_block",
    )(*blocks)


def beside_body(one, two, out):
    width = one.shape[1]
    out[:, :width] = one[...]
    out[:, width:] = two[...]


def beside(one, two, after=()):
    rows, width = one.shape
    return call("beside", beside_body, [((rows, 2 * width), BF16)], [one, two], after=after)[0]


def entry_body(flags, inputs, cotangent, out):
    size = inputs.shape[0] // 2
    rows = pl.ds(pl.multiple_of((1 - flags[3]) * size, size), size)
    out[:size] = inputs[rows, :]
    out[size:] = cotangent[rows, :]


def entry(flags, inputs, cotangent):
    return call("entry", entry_body, [(inputs.shape, BF16)], [flags, inputs, cotangent])[0]


def enter_body(flags, inputs, cotangent, got, labels, gain, bias, x_ref, g_ref, top_ref, h_ref):
    size, width = x_ref.shape
    here = jnp.full((1, width), flags[0], jnp.int32) == 1
    rows = pl.ds(pl.multiple_of(flags[3] * size, size), size)
    own = jnp.where(here, inputs[rows, :], got[:size])
    grad = jnp.where(here, cotangent[rows, :], got[size:])
    x_ref[...] = own
    g_ref[...] = grad
    top_ref[...] = (mask_column(labels, size) * grad.astype(F32)).astype(BF16)
    normal, _ = split_norm(own.astype(F32))
    h_ref[...] = (normal * gain[...] + bias[...]).astype(BF16)


def enter(flags, inputs, cotangent, got, labels, gain, bias):
    rows = inputs.shape[0] // 2
    return call(
        "enter",
        enter_body,
        [((rows, D), BF16)] * 4,
        [flags, inputs, cotangent, got, labels, gain, bias],
    )


def pack_body(*refs):
    *items, out = refs
    size = items[0].shape[0]
    for place, item in enumerate(items):
        out[place * size : (place + 1) * size, :] = item[...]


def pack(items):
    rows, width = items[0].shape
    return call("pack", pack_body, [((len(items) * rows, width), BF16)], list(items))[0]


def unpack_body(flags, own, sent, got_own, got_sent, y_ref, g_ref):
    size = y_ref.shape[0] // 2
    width = y_ref.shape[1]
    here = jnp.full((1, width), flags[0], jnp.int32) == 1
    rows = pl.ds(pl.multiple_of(flags[2] * size, size), size)
    first = pl.ds(pl.multiple_of(flags[3] * size, size), size)
    second = pl.ds(pl.multiple_of((1 - flags[3]) * size, size), size)
    last = slice(2 * size, 3 * size)
    y_ref[first, :] = jnp.where(here, own[rows, :], got_own[rows, :])
    y_ref[second, :] = jnp.where(here, sent[rows, :], got_sent[rows, :])
    g_ref[first, :] = jnp.where(here, own[last, :], got_own[last, :])
    g_ref[second, :] = jnp.where(here, sent[last, :], got_sent[last, :])


def unpack(flags, own, sent, got_own, got_sent):
    rows = 2 * own.shape[0] // 3
    return call(
        "unpack",
        unpack_body,
        [((rows, own.shape[1]), BF16)] * 2,
        [flags, own, sent, got_own, got_sent],
    )


def halve_body(flags, block, across, kept, sent):
    size = kept.shape[0] // 2
    for place, (out, step) in enumerate(((kept, 0), (kept, 2), (sent, 1), (sent, 3))):
        rows = pl.ds(pl.multiple_of((flags[1] ^ step) * size, size), size)
        spot = slice((place % 2) * size, (place % 2 + 1) * size)
        out[spot] = (block[rows, :].astype(F32) + across[rows, :].astype(F32)).astype(BF16)


def halve(flags, block, across, after=()):
    rows, width = block.shape
    return call(
        "halve",
        halve_body,
        [((rows // 2, width), BF16)] * 2,
        [flags, block, across],
        after=after,
    )


def quarter_body(kept, got, own, sent):
    size = own.shape[0]
    for place, out in enumerate((own, sent)):
        rows = slice(place * size, (place + 1) * size)
        out[...] = (kept[rows].astype(F32) + got[rows].astype(F32)).astype(BF16)


def quarter(kept, got, after=()):
    rows, width = kept.shape
    return call(
        "quarter", quarter_body, [((rows // 2, width), BF16)] * 2, [kept, got], after=after
    )


def total_body(*refs):
    *parts, out = refs
    out[...] = sum(part[...].astype(F32) for part in parts).astype(out.dtype)


def total_of(parts, kind=BF16, after=()):
    return call("total", total_body, [(parts[0].shape, kind)], list(parts), after=after)[0]


def final_first_body(flags, lower, upper, q_ref, k_ref, v_ref, o_ref):
    width = q_ref.shape[1]
    first = jnp.full((1, D), flags[2], jnp.int32) == 0
    total = jnp.where(first, lower[...].astype(F32), upper[...].astype(F32))
    for place, ref in enumerate((q_ref, k_ref, v_ref)):
        ref[...] = total[:, place * width : (place + 1) * width]
    o_ref[...] = total[:, 3 * width :].T


def final_first(flags, lower, upper):
    rows, width = lower.shape[0], D // LANES
    return call(
        "final_first",
        final_first_body,
        [((rows, width), F32)] * 3 + [((width, rows), F32)],
        [flags, lower, upper],
    )


def final_second_body(flags, lower, upper, up_ref, down_ref):
    first = jnp.full((1, 2 * UNITS), flags[2], jnp.int32) == 0
    total = jnp.where(first, lower[...].astype(F32), upper[...].astype(F32))
    up_ref[...] = total[:, :UNITS]
    down_ref[...] = total[:, UNITS:].T


def final_second(flags, lower, upper):
    rows = lower.shape[0]
    return call(
        "final_second",
        final_second_body,
        [((rows, UNITS), F32), ((UNITS, rows), F32)],
        [flags, lower, upper],
    )


def merge_body(flags, one, two, upper, out):
    size, width = one.shape
    first = jnp.full((1, width), flags[2], jnp.int32) == 0
    for place, ref in enumerate((one, two)):
        rows = slice(place * size, (place + 1) * size)
        out[rows] = jnp.where(first, ref[...], upper[rows])


def merge(flags, one, two, upper):
    return call("merge", merge_body, [(upper.shape, BF16)], [flags, one, two, upper])[0]


def vectors_body(*refs):
    *items, out = refs
    out[...] = jnp.zeros_like(out)
    for place, item in enumerate(items):
        out[2 * place : 2 * place + 2, : item.shape[1]] = item[0:2, :]


def vectors_of(items):
    return call("vectors", vectors_body, [((2 * len(items), D), F32)], list(items))[0]


def ranks_body(flags, own, got, out):
    here = jnp.full((1, D), flags[0], jnp.int32) == 1
    out[0:8] = own[0:8] + got[0:8]
    out[8:] = jnp.where(here, own[8:], got[8:])


def outer_body(own, got, out):
    out[0:8] = own[0:8] + got[...]
    out[8:] = own[8:]


def first_rows_body(own, out):
    out[...] = own[0:8]


def choose_body(flags, one, two, out):
    first = jnp.full((1, out.shape[1]), flags[2], jnp.int32) == 0
    out[...] = jnp.where(first, one[...], two[...])


def choose(flags, one, two, after=()):
    return call("choose", choose_body, [(one.shape, one.dtype)], [flags, one, two], after=after)[0]


def join_body(flags, own, got, out):
    half = own.shape[1]
    first = jnp.full((1, half), flags[2], jnp.int32) == 0
    out[:, :half] = jnp.where(first, own[...], got[...])
    out[:, half:] = jnp.where(first, got[...], own[...])


def join(flags, own, got, after=()):
    rows, half = own.shape
    return call(
        "join", join_body, [((rows, 2 * half), BF16)], [flags, own, got], after=after
    )[0]


def hold_body(ref, out):
    out[...] = ref[...]


def hold(x, after):
    return call("hold", hold_body, [(x.shape, x.dtype)], [x], after=after)[0]


def assemble_body(count, flags, *refs):
    beside, across, out = refs[:count], refs[count:-1], refs[-1]
    size = beside[0].shape[0]
    width = out.shape[1]
    near = jnp.full((1, width), flags[0], jnp.int32) == 1
    for step in range(count):
        rows = pl.ds(pl.multiple_of((flags[1] ^ step) * size, size), size)
        out[rows, :] = jnp.where(near, beside[step][...], across[step][...])


def assemble(flags, beside, across, after=()):
    count, (size, width) = len(beside), beside[0].shape
    return call(
        "assemble",
        partial(assemble_body, count),
        [((count * size, width), BF16)],
        [flags, *beside, *across],
        after=after,
    )[0]


def upper_block_body(flags, up, first, down, out):
    width = up.shape[1]
    lower = jnp.full((1, width), flags[2], jnp.int32) == 0
    out[:, :width] = jnp.where(lower, up[...], first[...])
    out[:, width:] = down[...]


def upper_block(flags, up, first, down, after):
    rows, width = up.shape
    return call(
        "upper_block",
        upper_block_body,
        [((rows, 2 * width), BF16)],
        [flags, up, first, down],
        after=after,
    )[0]


def halves_body(ref, one, two):
    width = one.shape[1]
    one[...] = ref[:, :width]
    two[...] = ref[:, width:]


def halves_of(x, after):
    rows, width = x.shape
    return call("halves", halves_body, [((rows, width // 2), x.dtype)] * 2, [x], after=after)


def pick_body(flags, beside, across, out):
    near = jnp.full((1, out.shape[1]), flags[0], jnp.int32) == 1
    out[...] = jnp.where(near, beside[...], across[...])


def pick(flags, beside, across, after=()):
    return call(
        "pick", pick_body, [(beside.shape, BF16)], [flags, beside, across], after=after
    )[0]


def on_device(
    inputs,
    cotangent,
    doc_ids,
    norm_gain,
    norm_bias,
    w_query,
    w_key,
    w_value,
    inner_gain,
    inner_bias,
    w_output,
    feed_gain,
    feed_bias,
    w_up,
    middle_gain,
    middle_bias,
    w_down,
):
    core = lax.axis_index("section")
    lane = lax.axis_index("mp")
    lane_x = lane % 2
    lane_y = lane // 2
    count = lax.axis_size("dp")
    slice_len = inputs.shape[0] // MICRO
    rank = 2 * core + lane_x
    crossing = [(s * 4 + r, s * 4 + (r ^ 2)) for s in range(2) for r in range(4) if s == r // 2]
    returning = [(s * 4 + r, s * 4 + (r ^ 2)) for s in range(2) for r in range(4) if s != r // 2]

    def by_core(first, second):
        return jnp.where(core == 0, first, second)

    def placed(array, layer):
        return [
            lax.ppermute(
                array,
                BOTH,
                [(s * 4 + 2 * m + x, layer * 4 + 2 * s + x) for s in range(2) for x in range(2)],
            )
            for m in range(MICRO)
        ]

    label_grid = lax.dynamic_index_in_dim(
        doc_ids.reshape(LANES, MICRO, slice_len), lane_y, 1, keepdims=False
    )
    order = (rank, 2 * (1 - core) + lane_x, rank ^ 1, 2 * (1 - core) + (1 - lane_x))
    labels = jnp.concatenate(
        [lax.dynamic_index_in_dim(label_grid, item, 0, keepdims=False) for item in order]
    )
    labels = jnp.broadcast_to(labels.astype(F32)[None], (8, LANES * slice_len))

    place = lax.axis_index("dp")
    flags = jnp.stack([core == lane_y, place, core, lane_y]).astype(jnp.int32)

    def line_pairs(step):
        return [
            ((r // 2 * count + i) * LANES + r, (r // 2 * count + (i ^ step)) * LANES + r)
            for i in range(count)
            for r in range(LANES)
        ]

    def along_line(block, step):
        return lax.ppermute(block, ("section", "dp", "mp"), line_pairs(step))

    first, down_block = first_block(w_query[0], w_key[0], w_value[0], w_output[0], w_down[0])
    up_block = w_up[0]
    to_second, to_first = [(r, LANES + r) for r in range(LANES)], [(LANES + r, r) for r in range(LANES)]
    inner_ranks = [((1 - r // 2) * LANES + r, (r // 2) * LANES + r) for r in range(LANES)]

    def along_dp(block):
        return lax.all_gather(block, "dp", axis=0, tiled=True)

    def fetched(line, hook=()):
        whole = join(flags, line, lax.ppermute(line, BOTH, inner_ranks), after=hook)
        return whole, lax.ppermute(whole, BOTH, crossing)

    def rank_of(line, source):
        return lax.ppermute(
            line, BOTH, [(source * LANES + r, (r // 2) * LANES + r) for r in range(LANES)]
        )

    outer_own = jnp.concatenate([norm_gain, norm_bias, feed_gain, feed_bias], axis=0)
    outer_other = core_swap(outer_own)
    split_own = jnp.concatenate([inner_gain, inner_bias, middle_gain, middle_bias], axis=1)
    split_far = y_swap(split_own)
    split_kept = jnp.where(lane_y == core, split_own, split_far)
    split_other = core_swap(jnp.where(lane_y == core, split_far, split_own))

    def small_of(outer, split):
        width = D // LANES
        return (
            [outer[i : i + 1] for i in range(4)],
            [
                split[:, :width],
                split[:, width : 2 * width],
                split[:, 2 * width : 2 * width + UNITS],
                split[:, 2 * width + UNITS :],
            ],
        )

    lower_outer, lower_split = small_of(
        by_core(outer_own, outer_other), by_core(split_kept, split_other)
    )
    upper_outer, upper_split = small_of(
        by_core(outer_other, outer_own), by_core(split_other, split_kept)
    )

    def gather_around(own, near_of, far=None, after=()):
        if far is None:
            far = x_swap(own)
        mate = core_swap(own)
        near = near_of([own, mate])
        far = hold(far, after=[near[0], *after])
        return (own, mate, far, core_swap(far)), near

    def attention(x, h, first, outer, split, hooks, far=None):
        pieces, (near,) = gather_around(h, lambda rows: [project(*rows, first)], far)
        far = project(pieces[2], pieces[3], first)
        half = 2 * slice_len
        o_far, p_far, p_far_mate, sum_far = attend(
            half, far, near, far, labels, first, split[0], split[1]
        )
        sent = pair_sum(p_far, p_far_mate)
        o_near, p_own, p_mate, sum_near = attend(
            0, near, near, far, labels, first, split[0], split[1], after=[sent, *hooks[0]]
        )
        arrived = hold(x_swap(sent), after=[p_own])
        terms = (p_own, core_swap(p_mate), arrived)
        x2, branch, h2, folded, kept = after_attend(x, terms, outer[2], outer[3], after=hooks[1])
        state = (pieces, near, far, o_near, o_far, sum_near, sum_far, x, x2, branch, folded, kept)
        return x2, h2, state, arrived

    def attention_back(grad, sums, state, first, outer, split, following, hooks):
        pieces, near, far, o_near, o_far, sum_near, sum_far, x, x2, branch, folded, kept = state
        dx2, sent, feed_vec = feed_norm_back(
            sums, grad, labels, x2, outer[2], branch, folded, kept, after=hooks[0]
        )
        block = hooks[3](sent)
        backs, (do_near, u_near, vec_near) = gather_around(
            sent, lambda rows: inner_back(rows, o_near, split[0], split[1], first), after=block
        )
        do_far, u_far, vec_far = inner_back(backs[2:], o_far, split[0], split[1], first)
        dq_near, dq_far = attend_back(
            near, far, do_near, do_far, sum_near, sum_far, labels, after=hooks[1]
        )
        p_far, p_far_mate, norm_far = unproject(
            dq_far, first, pieces[2:], outer[0], outer[1], after=hooks[4]
        )
        sent = pair_sum(p_far, p_far_mate)
        p_own, p_mate, norm_near = unproject(
            dq_near, first, pieces[:2], outer[0], outer[1], after=[sent]
        )
        mat_grad = grads_of(
            (pieces, (dq_near, dq_far)), (backs, (u_near, u_far)), after=[sent]
        )
        terms = (p_own, core_swap(p_mate), hold(x_swap(sent), after=[p_own, mat_grad]))
        result = first_norm_back(
            terms, dx2, x, outer[0], following, after=hooks[2](mat_grad, dq_far)
        )
        return result, vec_near + vec_far, feed_vec, norm_near + norm_far

    def reduce_across(block):
        across = lax.ppermute(block, BOTH, returning)
        if count != 4:
            total = total_of([block, across])
            return [lax.psum_scatter(total, "dp", scatter_dimension=0, tiled=True)]
        return block, across

    def reduce_near(pair, after=()):
        if count != 4:
            return pair
        kept, sent = halve(flags, *pair, after)
        return kept, along_line(sent, 1)

    def reduce_far(pair, after=()):
        if count != 4:
            return pair
        kept, sent = quarter(*pair, after)
        return kept, along_line(sent, 2)

    def reduce_end(pair, layer, after=()):
        total = total_of(pair, after=after) if count == 4 else pair[0]
        return lax.ppermute(
            total, BOTH, [((r // 2) * LANES + r, layer * LANES + r) for r in range(LANES)]
        )

    got = lax.ppermute(entry(flags, inputs, cotangent), BOTH, crossing)
    lower_in, upstream, masked, h = enter(
        flags, inputs, cotangent, got, labels, lower_outer[0], lower_outer[1]
    )
    far = x_swap(h)
    moved = rank_of(first, 0)
    if count == 4:
        pieces = [moved] + [along_line(moved, step) for step in range(1, count)]
        lower_first = assemble(
            flags, pieces, [lax.ppermute(piece, BOTH, crossing) for piece in pieces], after=[far]
        )
    else:
        pieces = [along_dp(moved)]
        lower_first = pick(flags, pieces[0], lax.ppermute(pieces[0], BOTH, crossing))
    lower_second_line = along_dp(
        choose(
            flags, up_block, lax.ppermute(down_block, BOTH, to_second), after=[pieces[-1]]
        )
    )
    upper_line = along_dp(
        upper_block(
            flags, lax.ppermute(up_block, BOTH, to_first), first, down_block, [pieces[-1]]
        )
    )
    top = gather_rows(masked)
    x2, h2, lower_state, arrived = attention(
        lower_in, h, lower_first, lower_outer, lower_split, ([top[3]], ()), far
    )
    lower_second = pick(flags, *fetched(hold(lower_second_line, after=[arrived])))
    lower_pieces, (f_near, p_own, p_mate) = gather_around(
        h2, lambda rows: feed(rows, (), lower_second, *lower_split[2:])
    )
    f_far, p_far, p_far_mate = feed(lower_pieces[2:], (), lower_second, *lower_split[2:])
    lower_pre = (f_near, f_far)
    upper_left, upper_right = halves_of(upper_line, [f_far])
    upper_first_whole = rank_of(upper_left, 1)
    upper_first_across = lax.ppermute(upper_first_whole, BOTH, crossing)
    upper_first = pick(flags, upper_first_whole, upper_first_across)
    terms = settle(p_own, p_mate, p_far, p_far_mate)
    lower_out, lower_branch, h, lower_folded, lower_kept = after_feed(
        x2, terms, labels, upper_outer[0], upper_outer[1]
    )
    upper_second_whole = beside(
        rank_of(upper_left, 0), rank_of(upper_right, 1), after=[lower_out]
    )
    upper_second_across = lax.ppermute(upper_second_whole, BOTH, crossing)
    upper_second = pick(flags, upper_second_whole, upper_second_across)
    x2, h2, upper_state, _ = attention(
        lower_out, h, upper_first, upper_outer, upper_split, ((), [upper_second])
    )
    upper_pieces, (f_near, p_own, p_mate, near_stats) = gather_around(
        h2, lambda rows: feed(rows, top[:2], upper_second, *upper_split[2:])
    )
    f_far, p_far, p_far_mate, far_stats = feed(
        upper_pieces[2:], top[2:], upper_second, *upper_split[2:]
    )
    upper_pre = (f_near, f_far)

    stats = group_stats(near_stats, far_stats)
    df_far, n_far, q_far, q_far_mate, vec_far = feed_back(
        top[2:], [stats], 2, upper_pre[1], *upper_split[2:], upper_second
    )
    sent = pair_sum(q_far, q_far_mate)
    df_near, n_near, q_own, q_mate, vec_near = feed_back(
        top[:2], [stats], 0, upper_pre[0], *upper_split[2:], upper_second, after=[sent]
    )
    upper_middle = vec_near + vec_far
    sums = (q_own, core_swap(q_mate), hold(x_swap(sent), after=[q_own]))
    ended = pair_sum(p_far, p_far_mate)
    ended_far = hold(x_swap(ended), after=[ended])
    following = (labels, lower_branch, lower_folded, lower_kept)
    pairs = {}

    def upper_second_grads(after):
        block = grads_of(
            (upper_pieces, (df_near, df_far)), (top, (n_near, n_far)), after=[after]
        )
        pairs["second"] = reduce_near(reduce_across(block))
        return [block]

    def upper_hook(item, last):
        pairs["upper"] = reduce_across(item)
        return [item]

    (upper_grad, sent), upper_inner, upper_feed, upper_norm = attention_back(
        upstream,
        sums,
        upper_state,
        upper_first,
        upper_outer,
        upper_split,
        following,
        ((), [ended], upper_hook, upper_second_grads, [ended_far]),
    )

    upper_out = finish_feed(x2, (p_own, core_swap(p_mate), ended_far), labels)
    own = pack([lower_out, upper_out, upper_grad])
    swapped = lax.ppermute(own, BOTH, returning)
    upper_second_pair = reduce_far(pairs["second"], [own])
    backs, (df_near, n_near, q_own, q_mate, vec_near) = gather_around(
        sent,
        lambda rows: feed_back(
            rows, (), 0, lower_pre[0], *lower_split[2:], lower_second, after=[own]
        ),
    )
    upper_first_pair = reduce_near(pairs["upper"])
    df_far, n_far, q_far, q_far_mate, vec_far = feed_back(
        backs[2:],
        (),
        2,
        lower_pre[1],
        *lower_split[2:],
        lower_second,
        after=[own, upper_first_pair[0], upper_second_pair[0]],
    )
    lower_middle = vec_near + vec_far
    sent = pair_sum(q_far, q_far_mate)
    sums = (q_own, core_swap(q_mate), x_swap(sent))

    def lower_second_grads(after):
        block = grads_of(
            (lower_pieces, (df_near, df_far)), (backs, (n_near, n_far)), after=[after]
        )
        pairs["second"] = reduce_near(reduce_across(block))
        pairs["sum"] = reduce_end(upper_second_pair, 1, after=[block])
        pairs["first"] = reduce_far(upper_first_pair, after=[block])
        return [block]

    inward = [((r // 2) * LANES + r, (1 - r // 2) * LANES + r) for r in range(LANES)]
    layer_outputs, upper_held = unpack(
        flags, own, swapped, lax.ppermute(own, BOTH, inward), lax.ppermute(swapped, BOTH, inward)
    )

    def lower_hook(item, last):
        pairs["lower"] = reduce_across(item)
        pairs["second"] = reduce_far(pairs["second"], after=[item])
        return [item]

    (lower_grad,), lower_inner, lower_feed, lower_norm = attention_back(
        upper_grad,
        sums,
        lower_state,
        lower_first,
        lower_outer,
        lower_split,
        (),
        ((), [layer_outputs], lower_hook, lower_second_grads, ()),
    )
    upper_second_sum = pairs["sum"]
    upper_first_sum = reduce_end(pairs["first"], 1)
    lower_second_pair = pairs["second"]
    vectors = vectors_of(
        [lower_norm, lower_feed, upper_norm, upper_feed, lower_middle, upper_middle]
        + [lower_inner, upper_inner]
    )
    shape = [(vectors.shape, F32)]
    vectors = total_of([vectors, y_swap(vectors)], F32)
    vectors = call("ranks", ranks_body, shape, [flags, vectors, core_swap(vectors)])[0]
    outer = call("first_rows", first_rows_body, [((8, D), F32)], [vectors])[0]
    vectors = call("outer", outer_body, shape, [vectors, x_swap(outer)])[0]
    lower_held = placed(lower_grad, 0)
    lower_first_pair = reduce_near(pairs["lower"], after=[vectors])
    if count == 4:
        for step in (1, 2):
            got = lax.ppermute(vectors, "dp", [(i, i ^ step) for i in range(count)])
            vectors = total_of([vectors, got], F32)
            if step == 1:
                lower_first_pair = reduce_far(lower_first_pair, after=[vectors, *lower_held])
    else:
        vectors = lax.psum(vectors, "dp")
    lower_second_sum = reduce_end(lower_second_pair, 0)
    input_grads = merge(flags, *lower_held, upper_held)
    grad_query, grad_key, grad_value, grad_output = final_first(
        flags, reduce_end(lower_first_pair, 0), upper_first_sum
    )
    grad_up, grad_down = final_second(flags, lower_second_sum, upper_second_sum)

    def part(rows, start, size):
        rows = lax.dynamic_slice(rows, (core * rows.shape[0] // 2, start), (rows.shape[0] // 2, size))
        return [rows[i : i + 1] for i in range(rows.shape[0])]

    width = D // LANES
    size = D // count // LANES
    outer = part(vectors[:8], (place * LANES + lane) * size, size)
    middle = part(vectors[8:12], place * (UNITS // count), UNITS // count)
    inner = part(vectors[12:], place * (width // count), width // count)
    return (
        layer_outputs[None],
        input_grads[None],
        outer[0],
        outer[1],
        grad_query[None],
        grad_key[None],
        grad_value[None],
        inner[0],
        inner[1],
        grad_output[None],
        outer[2],
        outer[3],
        grad_up[None],
        middle[0],
        middle[1],
        grad_down[None],
    )


def solution(mesh):
    placed = (
        P(("dp", "mp"), None),
        P(("dp", "mp"), None),
        P("dp"),
        P("section", None),
        P("section", None),
        P("section", "dp", "mp"),
        P("section", "dp", "mp"),
        P("section", "dp", "mp"),
        P("section", "mp"),
        P("section", "mp"),
        P("section", "mp", "dp"),
        P("section", None),
        P("section", None),
        P("section", "dp", "mp"),
        P("section", "mp"),
        P("section", "mp"),
        P("section", "mp", "dp"),
    )
    return jax.shard_map(
        on_device,
        mesh=mesh,
        in_specs=placed,
        out_specs=(
            P("section", ("dp", "mp"), None),
            P("section", ("dp", "mp"), None),
            P("section", ("dp", "mp")),
            P("section", ("dp", "mp")),
            P("section", "dp", "mp"),
            P("section", "dp", "mp"),
            P("section", "dp", "mp"),
            P("section", ("mp", "dp")),
            P("section", ("mp", "dp")),
            P("section", "mp", "dp"),
            P("section", ("dp", "mp")),
            P("section", ("dp", "mp")),
            P("section", "dp", "mp"),
            P("section", ("mp", "dp")),
            P("section", ("mp", "dp")),
            P("section", "mp", "dp"),
        ),
        check_vma=False,
    )
```

```python
from functools import partial

import jax
import jax.numpy as jnp
from jax import lax
from jax.experimental import pallas as pl
from jax.experimental.pallas import tpu as pltpu
from jax.sharding import PartitionSpec as P

D = 768
HEAD_DIM = 64
FF = 3072
MICRO = 2
LANES = 4
EPS = 1e-05
SCALE = HEAD_DIM ** (-0.5)
LOG2E = 1.4426950408889634
SQRT_HALF = 0.7071067811865476
INV_SQRT_2PI = 0.3989422804014327
BOTH = ("section", "mp")
Y_PAIRS = [[0, 2], [1, 3]]
QKV = 3 * D // LANES
UNITS = FF // LANES
TAIL = 16
F32 = jnp.float32
BF16 = jnp.bfloat16

VMEM = pl.BlockSpec(memory_space=pltpu.VMEM)
SMEM = pl.BlockSpec(memory_space=pltpu.SMEM)
ANY = pl.BlockSpec(memory_space=pl.ANY)
HBM = pl.BlockSpec(memory_space=pltpu.HBM)
PARAMS = pltpu.CompilerParams(vmem_limit_bytes=16 * 1024 * 1024)


def call(name, body, outs, ins, scratch=(), after=(), cost=None):
    count = len(ins)

    def kernel(*refs):
        body(*refs[:count], *refs[count + len(after) :])

    return pl.pallas_call(
        kernel,
        out_shape=tuple(jax.ShapeDtypeStruct(shape, kind) for shape, kind in outs),
        in_specs=[SMEM if item.ndim == 1 else VMEM for item in ins] + [ANY] * len(after),
        out_specs=(VMEM,) * len(outs),
        scratch_shapes=list(scratch),
        compiler_params=PARAMS,
        name=name,
        cost_estimate=cost or work(1, 1),
    )(*ins, *after)


def work(flops, size):
    return pl.CostEstimate(flops=int(flops), bytes_accessed=int(size), transcendentals=0)


def nn(a, b):
    return jnp.dot(a, b, preferred_element_type=F32)


def nt(a, b):
    return lax.dot_general(a, b, (((1,), (1,)), ((), ())), preferred_element_type=F32)


def tn(a, b):
    return lax.dot_general(a, b, (((0,), (0,)), ((), ())), preferred_element_type=F32)


def to_rows(*columns):
    count = columns[0].shape[0]
    lane = lax.broadcasted_iota(jnp.int32, (count, 128), 1)
    tile = jnp.zeros((count, 128), F32)
    for place, column in enumerate(columns):
        tile = jnp.where(lane == place, column, tile)
    return tile.T[:8]


def to_columns(rows):
    return jnp.concatenate([rows, jnp.zeros((120, rows.shape[1]), F32)], axis=0).T


def split_three(values):
    high = values.astype(BF16)
    rest = values - high.astype(F32)
    middle = rest.astype(BF16)
    return high, middle, (rest - middle.astype(F32)).astype(BF16)


def encode(rows):
    return jnp.concatenate(split_three(rows), axis=1)


def decode(tail):
    tail = tail.astype(F32)
    count = tail.shape[1] // 3
    return tail[:, :count] + tail[:, count : 2 * count] + tail[:, 2 * count :]


def decode_vectors(tail):
    tail = tail.astype(F32)
    return jnp.concatenate(
        [jnp.sum(tail[0:3], axis=0, keepdims=True), jnp.sum(tail[3:6], axis=0, keepdims=True)],
        axis=0,
    )


def encode_vectors(first, second):
    return jnp.concatenate(
        [*split_three(first), *split_three(second), jnp.zeros((2, first.shape[1]), BF16)], axis=0
    )


def split_norm(values):
    mean = jnp.mean(values, axis=-1, keepdims=True)
    spread = jnp.mean(values * values, axis=-1, keepdims=True) - mean * mean
    scaled = lax.rsqrt(spread + EPS)
    return (values - mean) * scaled, scaled


def norm_back(values, gain, upstream):
    normal, scaled = split_norm(values)
    inner = upstream * gain
    one = jnp.mean(inner, axis=-1, keepdims=True)
    two = jnp.mean(inner * normal, axis=-1, keepdims=True)
    back = scaled * (inner - one - normal * two)
    return (
        back,
        jnp.sum(upstream * normal, axis=0, keepdims=True),
        jnp.sum(upstream, axis=0, keepdims=True),
    )


def vector_rows(first, second):
    return jnp.concatenate([first, second, jnp.zeros((6, first.shape[1]), F32)], axis=0)


def folded_vectors(mat, gain, bias):
    rows = jnp.concatenate(
        [*split_three(gain), *split_three(bias), jnp.zeros((10, gain.shape[1]), BF16)], axis=0
    )
    folded = nt(rows, mat)
    return encode_vectors(
        jnp.sum(folded[0:3], axis=0, keepdims=True), jnp.sum(folded[3:6], axis=0, keepdims=True)
    )


def core_swap(x):
    return lax.ppermute(x, "section", [(0, 1), (1, 0)])


def x_swap(x):
    return lax.ppermute(x, "mp", [(i, i ^ 1) for i in range(LANES)])


def y_swap(x):
    return lax.ppermute(x, "mp", [(i, i ^ 2) for i in range(LANES)])


def gather_rows(own):
    far = x_swap(own)
    return own, core_swap(own), far, core_swap(far)


def pair_sum_body(first, second, out):
    rows = out.shape[0] - TAIL
    out[:rows] = (first[:rows].astype(F32) + second[:rows].astype(F32)).astype(BF16)
    half = rows + TAIL // 2
    out[rows:half] = encode(decode(first[rows:half]) + decode(second[rows:half]))
    folded = decode_vectors(first[half:]) + decode_vectors(second[half:])
    out[half:] = encode_vectors(folded[0:1], folded[1:2])


def pair_add_body(first, second, out):
    out[...] = (first[...].astype(F32) + second[...].astype(F32)).astype(BF16)


def pair_ride_body(first, second, out):
    rows = out.shape[0] - 32
    out[:rows] = (first[:rows].astype(F32) + second[:rows].astype(F32)).astype(BF16)
    total = decode_rows(first[rows : rows + 24]) + decode_rows(second[rows : rows + 24])
    out[rows:] = jnp.concatenate([encode_rows(total), jnp.zeros((8, D), BF16)], axis=0)


def pair_sum(far, far_mate):
    body = {0: pair_add_body, TAIL: pair_sum_body, 32: pair_ride_body}[far.shape[0] % 256]
    return call("pair_sum", body, [(far.shape, BF16)], [far, core_swap(far_mate)])[0]


def settle(own, mate, far, far_mate):
    sent = pair_sum(far, far_mate)
    return own, core_swap(mate), x_swap(sent)


def project_body(first, second, mat, out):
    size = first.shape[0]
    for place, piece in enumerate((first, second)):
        out[place * size : (place + 1) * size, :] = nn(piece[...], mat[:, :QKV]).astype(BF16)


def project(first, second, mat):
    count = 2 * first.shape[0]
    return call(
        "project",
        project_body,
        [((count, QKV), BF16)],
        [first, second, mat],
    )[0]


def split_heads(source, target, first, start, head_count):
    size = source.shape[0]
    for head in range(head_count):
        lanes = slice(first + head * HEAD_DIM, first + (head + 1) * HEAD_DIM)
        target[head, start : start + size, :] = source[:, lanes]


def attend_body(
    q_start, q_ref, near, far, labels, mat, gain, bias, o_ref, p_one, p_two, sum_ref, ks, vs
):
    head_count = QKV // (3 * HEAD_DIM)
    width = head_count * HEAD_DIM
    half = near.shape[0]
    for start, ref in ((0, near), (half, far)):
        split_heads(ref, ks, width, start, head_count)
        split_heads(ref, vs, 2 * width, start, head_count)
    out_mat = mat[:, QKV:]
    folded = folded_vectors(out_mat, gain[...], bias[...])
    size = half // 2
    key_labels = labels[0:1, :]
    for place, p_ref in enumerate((p_one, p_two)):
        rows = slice(place * size, (place + 1) * size)
        first = q_start + place * size
        allowed = to_columns(labels[:, first : first + size])[:, 0:1] == key_labels
        outs = []
        sums = []
        for head in range(head_count):
            query = q_ref[rows, head * HEAD_DIM : (head + 1) * HEAD_DIM]
            scores = jnp.where(allowed, nt(query, ks[head]), -1e30)
            peak = jnp.max(scores, axis=-1, keepdims=True)
            terms = jnp.exp2((scores - peak) * (SCALE * LOG2E))
            total = jnp.sum(terms, axis=-1, keepdims=True)
            outs.append(nn(terms.astype(BF16), vs[head]) / total)
            sums.append(peak * (SCALE * LOG2E) + jnp.log(total) * LOG2E)
        out = jnp.concatenate(outs, axis=1)
        o_ref[rows, :] = out
        lane = lax.broadcasted_iota(jnp.int32, (size, 128), 1)
        tile = jnp.zeros((size, 128), F32)
        for spot, column in enumerate(sums):
            tile = jnp.where(lane == spot, column, tile)
        sum_ref[rows, :] = tile
        p_ref[:size] = nt((out * gain[...]).astype(BF16), out_mat).astype(BF16)
        stats = to_rows(
            jnp.sum(out, axis=-1, keepdims=True), jnp.sum(out * out, axis=-1, keepdims=True)
        )
        p_ref[size : size + TAIL // 2] = encode(stats)
        p_ref[size + TAIL // 2 :] = folded


def attend(q_start, queries, near, far, labels, mat, gain, bias, after=()):
    count, keys = queries.shape[0], 2 * near.shape[0]
    heads = QKV // (3 * HEAD_DIM)
    width = heads * HEAD_DIM
    by_head = pltpu.VMEM((heads, keys, HEAD_DIM), BF16)
    payload = ((count // 2 + TAIL, D), BF16)
    return call(
        "attend",
        partial(attend_body, q_start),
        [((count, width), F32), payload, payload, ((count, 128), F32)],
        [queries, near, far, labels, mat, gain, bias],
        [by_head, by_head],
        after,
        work(4e9, 1),
    )


def attend_back_body(
    near, far, do_near, do_far, sum_near, sum_far, labels, near_out, far_out,
    qs, ks, vs, grads, dqs, dks, dvs, sums,
):
    head_count = QKV // (3 * HEAD_DIM)
    width = head_count * HEAD_DIM
    half = near.shape[0]
    for start, ref, grad in ((0, near, do_near), (half, far, do_far)):
        split_heads(ref, qs, 0, start, head_count)
        split_heads(ref, ks, width, start, head_count)
        split_heads(ref, vs, 2 * width, start, head_count)
        split_heads(grad, grads, 0, start, head_count)
    sums[:half] = sum_near[...]
    sums[half:] = sum_far[...]
    dks[...] = jnp.zeros_like(dks)
    dvs[...] = jnp.zeros_like(dvs)
    key_labels = labels[0:1, :]
    size = half // 2

    def block(index, carry):
        rows = pl.ds(pl.multiple_of(index * size, size), size)
        allowed = to_columns(labels[:, rows])[:, 0:1] == key_labels
        for head in range(head_count):
            query, grad = qs[head, rows, :], grads[head, rows, :]
            scores = jnp.where(allowed, nt(query, ks[head]), -1e30)
            prob = jnp.exp2(scores * (SCALE * LOG2E) - sums[rows, head : head + 1])
            prob_grad = nt(grad, vs[head])
            delta = jnp.sum(prob * prob_grad, axis=-1, keepdims=True)
            score_grad = (prob * (prob_grad - delta)).astype(BF16)
            dqs[head, rows, :] = nn(score_grad, ks[head]) * SCALE
            dks[head] += tn(query, score_grad)
            dvs[head] += tn(grad, prob.astype(BF16))
        return carry

    lax.fori_loop(0, 4, block, 0)
    for start, out in ((0, near_out), (half, far_out)):
        rows = slice(start, start + half)
        heads = range(head_count)
        out[...] = jnp.concatenate(
            [dqs[head, rows, :].astype(BF16) for head in heads]
            + [(dks[head, :, rows].T * SCALE).astype(BF16) for head in heads]
            + [dvs[head, :, rows].T.astype(BF16) for head in heads],
            axis=1,
        )


def attend_back(near, far, do_near, do_far, sum_near, sum_far, labels, after=()):
    half, width = do_near.shape
    keys = 2 * half
    heads = width // HEAD_DIM
    by_head = pltpu.VMEM((heads, keys, HEAD_DIM), BF16)
    turned = pltpu.VMEM((heads, HEAD_DIM, keys), F32)
    return call(
        "attend_back",
        attend_back_body,
        [(near.shape, BF16)] * 2,
        [near, far, do_near, do_far, sum_near, sum_far, labels],
        [by_head] * 4
        + [pltpu.VMEM((heads, keys, HEAD_DIM), F32), turned, turned, pltpu.VMEM((keys, 128), F32)],
        after,
        work(1.4e10, 1),
    )


def gelu_parts(x):
    spread = 0.5 + 0.5 * lax.erf(x * SQRT_HALF)
    return x * spread, spread


def feed_body(with_back, *refs):
    if with_back:
        one, two, back_one, back_two, mat, gain, bias, f_ref, p_one, p_two, s_ref = refs
    else:
        one, two, mat, gain, bias, f_ref, p_one, p_two = refs
        back_one = back_two = s_ref = None
    size = one.shape[0]
    up, down = mat.at[:, :UNITS], mat.at[:, UNITS:]
    folded = folded_vectors(down[...], gain[...], bias[...])
    for place, (piece, p_ref, back) in enumerate(((one, p_one, back_one), (two, p_two, back_two))):
        rows = slice(place * size, (place + 1) * size)
        pre = nn(piece[...], up[...])
        f_ref[rows, :] = pre
        act, _ = gelu_parts(pre)
        p_ref[:size] = nt((act * gain[...]).astype(BF16), down[...]).astype(BF16)
        columns = [
            jnp.sum(act, axis=-1, keepdims=True),
            jnp.sum(act * act, axis=-1, keepdims=True),
        ]
        p_ref[size : size + TAIL // 2] = encode(to_rows(*columns))
        p_ref[size + TAIL // 2 :] = folded
        if with_back:
            inner = nn(back[...], down[...]) * gain[...]
            columns.append(jnp.sum(inner, axis=-1, keepdims=True))
            columns.append(jnp.sum(inner * act, axis=-1, keepdims=True))
            s_ref[8 * place : 8 * place + 8, :] = to_rows(*columns)


def feed(pieces, backs, mat, gain, bias, after=()):
    size = pieces[0].shape[0]
    outs = [((2 * size, UNITS), F32)] + [((size + TAIL, D), BF16)] * 2
    if backs:
        outs += [((16, size), F32)]
    return call(
        "feed",
        partial(feed_body, bool(backs)),
        outs,
        [*pieces, *backs, mat, gain, bias],
        after=after,
    )


def feed_back_body(first_piece, *refs):
    if first_piece is not None:
        one, two, s_ref, *refs = refs
    else:
        one, two, *refs = refs
        s_ref = None
    f_ref, gain, bias, mat, df_ref, n_ref, p_one, p_two, vec_ref = refs
    up, down = mat.at[:, :UNITS], mat.at[:, UNITS:]
    size = p_one.shape[0]
    gain_grad = jnp.zeros((1, UNITS), F32)
    bias_grad = jnp.zeros((1, UNITS), F32)
    for place, (piece, p_ref) in enumerate(((one, p_one), (two, p_two))):
        rows = slice(place * size, (place + 1) * size)
        upstream = nn(piece[:size], down[...])
        pre = f_ref[rows, :]
        if first_piece is not None:
            start = 8 * (first_piece + place)
            stats = s_ref[start : start + 8, :]
        else:
            stats = decode(piece[size : size + TAIL // 2])
        columns = to_columns(stats)
        mean, scaled, first, second = (columns[:, i : i + 1] for i in range(4))
        act, spread = gelu_parts(pre)
        normal = (act - mean) * scaled
        act_grad = scaled * (upstream * gain[...] - first - normal * second)
        slope = spread + pre * (jnp.exp(-0.5 * pre * pre) * INV_SQRT_2PI)
        pre_grad = (act_grad * slope).astype(BF16)
        df_ref[rows, :] = pre_grad
        n_ref[rows, :] = (normal * gain[...] + bias[...]).astype(BF16)
        p_ref[...] = nt(pre_grad, up[...]).astype(BF16)
        gain_grad += jnp.sum(upstream * normal, axis=0, keepdims=True)
        bias_grad += jnp.sum(upstream, axis=0, keepdims=True)
    vec_ref[...] = vector_rows(gain_grad, bias_grad)


def feed_back(pieces, stats, first_piece, pre, gain, bias, mat, after=()):
    count = pre.shape[0]
    size = count // 2
    return call(
        "feed_back",
        partial(feed_back_body, first_piece if stats else None),
        [((count, UNITS), BF16)] * 2 + [((size, D), BF16)] * 2 + [((8, UNITS), F32)],
        [*pieces, *stats, pre, gain, bias, mat],
        after=after,
    )


def stats_pack_body(near, far, out):
    out[:16] = near[...]
    out[16:] = far[...]


def stats_near_body(stats, got, out):
    for place in range(4):
        other = 8 * (place ^ 1)
        out[8 * place : 8 * place + 8] = stats[8 * place : 8 * place + 8] + got[other : other + 8]


def stats_far_body(stats, got, out):
    for place in range(4):
        other = 8 * (place ^ 2)
        rows = slice(8 * place, 8 * place + 8)
        total = (stats[rows] + got[other : other + 8]) * (1.0 / FF)
        mean, one = total[0:1], total[2:3]
        scaled = lax.rsqrt(total[1:2] - mean * mean + EPS)
        two = scaled * (total[3:4] - mean * one)
        out[rows] = jnp.concatenate([mean, scaled, one, two, total[4:8]], axis=0)


def group_stats(near, far):
    shape = [((32, near.shape[1]), F32)]
    stats = call("stats_pack", stats_pack_body, shape, [near, far])[0]
    stats = call("stats_near", stats_near_body, shape, [stats, core_swap(stats)])[0]
    return call("stats_far", stats_far_body, shape, [stats, x_swap(stats)])[0]


def grads_body(pieces, halves, size, *refs):
    *refs, out = refs
    place = 0
    column = 0
    for left_count, right_count in zip(pieces, halves):
        left = refs[place : place + left_count]
        right = refs[place + left_count : place + left_count + right_count]
        place += left_count + right_count
        width = right[0].shape[1]
        per = left_count // right_count
        total = None
        for index, piece in enumerate(left):
            start = (index % per) * size
            term = tn(piece[:size], right[index // per][start : start + size, :])
            total = term if total is None else total + term
        out[:, column : column + width] = total.astype(BF16)
        column += width


def grads_of(*pairs, after=()):
    pieces = tuple(len(left) for left, _ in pairs)
    halves = tuple(len(right) for _, right in pairs)
    size = pairs[0][1][0].shape[0] // 2
    args = [item for left, right in pairs for item in (*left, *right)]
    width = sum(right[0].shape[1] for _, right in pairs)
    return call(
        "grads",
        partial(grads_body, pieces, halves, size),
        [((D, width), BF16)],
        args,
        after=after,
    )[0]


def inner_back_body(one, two, o_ref, gain, bias, mat, do_ref, u_ref, vec_ref):
    size = o_ref.shape[0] // 2
    gain_grad = jnp.zeros((1, o_ref.shape[1]), F32)
    bias_grad = jnp.zeros((1, o_ref.shape[1]), F32)
    out_mat = mat[:, QKV:]
    for place, piece in enumerate((one, two)):
        rows = slice(place * size, (place + 1) * size)
        upstream = nn(piece[:size], out_mat)
        columns = to_columns(decode(piece[size : size + TAIL // 2]))
        mean, scaled, first, second = (columns[:, i : i + 1] for i in range(4))
        normal = (o_ref[rows, :] - mean) * scaled
        back = scaled * (upstream * gain[...] - first - normal * second)
        do_ref[rows, :] = back.astype(BF16)
        u_ref[rows, :] = (normal * gain[...] + bias[...]).astype(BF16)
        gain_grad += jnp.sum(upstream * normal, axis=0, keepdims=True)
        bias_grad += jnp.sum(upstream, axis=0, keepdims=True)
    vec_ref[...] = vector_rows(gain_grad, bias_grad)


def inner_back(pieces, out, gain, bias, mat, after=()):
    count, width = out.shape
    return call(
        "inner_back",
        inner_back_body,
        [((count, width), BF16)] * 2 + [((8, width), F32)],
        [*pieces, out, gain, bias, mat],
        after=after,
    )


def encode_rows(values):
    return jnp.concatenate(split_three(values), axis=0)


def decode_rows(rows):
    rows = rows.astype(F32)
    count = rows.shape[0] // 3
    return rows[:count] + rows[count : 2 * count] + rows[2 * count :]


def unproject_body(riding, rows, mat, one, two, gain, bias, *refs):
    if riding:
        near, *others, p_one, p_two = refs
        vec_ref = None
    else:
        others = []
        near = None
        p_one, p_two, vec_ref = refs
    size = one.shape[0]
    gain_grad = jnp.zeros((1, D), F32)
    bias_grad = jnp.zeros((1, D), F32)
    for place, (piece, p_ref) in enumerate(((one, p_one), (two, p_two))):
        term = nt(rows[place * size : (place + 1) * size], mat[:, :QKV])
        p_ref[:size] = term.astype(BF16)
        gain_grad += jnp.sum(term * (piece[...].astype(F32) - bias[...]), axis=0, keepdims=True)
        bias_grad += jnp.sum(term, axis=0, keepdims=True)
    gain_grad = gain_grad / gain[...]
    if riding:
        vectors = jnp.concatenate(
            [gain_grad + near[0:1], bias_grad + near[1:2]] + [item[0:2, :] for item in others],
            axis=0,
        )
        ride = jnp.concatenate([encode_rows(vectors), jnp.zeros((8, D), BF16)], axis=0)
        p_one[size:] = ride
        p_two[size:] = ride
    else:
        vec_ref[...] = vector_rows(gain_grad, bias_grad)


def unproject(rows, mat, pieces, gain, bias, riding=(), after=()):
    size = rows.shape[0] // 2
    outs = [((size + 32 if riding else size, D), BF16)] * 2
    if not riding:
        outs.append(((8, D), F32))
    return call(
        "unproject",
        partial(unproject_body, bool(riding)),
        outs,
        [rows, mat, *pieces, gain, bias, *riding],
        after=after,
    )


def branch_of(own, mate, far, feature_count):
    rows = own.shape[0] - TAIL
    half = rows + TAIL // 2
    pieces = (own, mate, far)
    product = sum(piece[:rows].astype(F32) for piece in pieces)
    stats = sum(decode(piece[rows:half]) for piece in pieces) / feature_count
    folded = sum(decode_vectors(piece[half:]) for piece in pieces)
    mean = stats[0:1]
    scaled = lax.rsqrt(stats[1:2] - mean * mean + EPS)
    kept = jnp.concatenate([mean, scaled, jnp.zeros((6, rows), F32)], axis=0)
    columns = to_columns(kept)
    branch = columns[:, 1:2] * (product - columns[:, 0:1] * folded[0:1])
    return branch, folded[1:2], folded[0:1], kept


def after_attend_body(x_ref, own, mate, far, gain, bias, x2_ref, z_ref, h_ref, fold_ref, kept_ref):
    branch, shift, folded, kept = branch_of(own, mate, far, D)
    mid = x_ref[...].astype(F32) + branch + shift
    x2_ref[...] = mid
    z_ref[...] = branch
    normal, _ = split_norm(mid)
    h_ref[...] = (normal * gain[...] + bias[...]).astype(BF16)
    fold_ref[...] = jnp.broadcast_to(folded, fold_ref.shape)
    kept_ref[...] = kept


def after_attend(x, pieces, gain, bias, after=()):
    rows = x.shape[0]
    return call(
        "after_attend",
        after_attend_body,
        [((rows, D), F32), ((rows, D), F32), ((rows, D), BF16), ((8, D), F32), ((8, rows), F32)],
        [x, *pieces, gain, bias],
        after=after,
    )


def mask_column(labels, rows):
    return (to_columns(labels[:, :rows])[:, 0:1] >= 0).astype(F32)


def after_feed_body(x2, own, mate, far, labels, gain, bias, y_ref, z_ref, h_ref, fold_ref, kept_ref):
    branch, shift, folded, kept = branch_of(own, mate, far, FF)
    out = (mask_column(labels, x2.shape[0]) * (x2[...] + branch + shift)).astype(BF16)
    y_ref[...] = out
    z_ref[...] = branch
    normal, _ = split_norm(out.astype(F32))
    h_ref[...] = (normal * gain[...] + bias[...]).astype(BF16)
    fold_ref[...] = jnp.broadcast_to(folded, fold_ref.shape)
    kept_ref[...] = kept


def after_feed(x2, pieces, labels, gain, bias, after=()):
    rows = x2.shape[0]
    return call(
        "after_feed",
        after_feed_body,
        [((rows, D), BF16), ((rows, D), F32), ((rows, D), BF16), ((8, D), F32), ((8, rows), F32)],
        [x2, *pieces, labels, gain, bias],
        after=after,
    )


def finish_feed_body(x2, own, mate, far, labels, y_ref):
    branch, shift, _, _ = branch_of(own, mate, far, FF)
    y_ref[...] = (mask_column(labels, x2.shape[0]) * (x2[...] + branch + shift)).astype(BF16)


def finish_feed(x2, pieces, labels):
    return call("finish_feed", finish_feed_body, [(x2.shape, BF16)], [x2, *pieces, labels])[0]


def payload_of(grad, branch, folded, kept, feature_count):
    sent = grad.astype(BF16)
    wide = sent.astype(F32)
    means = to_rows(
        jnp.sum(wide * folded, axis=-1, keepdims=True),
        jnp.sum(wide * branch, axis=-1, keepdims=True),
    )
    stats = jnp.concatenate([kept[0:2], means[0:2] / feature_count, kept[4:8]], axis=0)
    tail = jnp.concatenate([encode(stats), jnp.zeros((TAIL // 2, D), BF16)], axis=0)
    return jnp.concatenate([sent, tail], axis=0)


def feed_norm_back_body(
    own, mate, far, g_ref, labels, x2, gain, branch, folded, kept, dx_ref, out_ref, vec_ref
):
    upstream = own[...].astype(F32) + mate[...].astype(F32) + far[...].astype(F32)
    back, gain_grad, bias_grad = norm_back(x2[...], gain[...], upstream)
    total = mask_column(labels, x2.shape[0]) * g_ref[...].astype(F32) + back
    dx_ref[...] = total
    out_ref[...] = payload_of(total, branch[...], folded[0:1], kept[...], D)
    vec_ref[...] = vector_rows(gain_grad, bias_grad)


def feed_norm_back(pieces, grad, labels, x2, gain, branch, folded, kept, after=()):
    rows = x2.shape[0]
    return call(
        "feed_norm_back",
        feed_norm_back_body,
        [((rows, D), F32), ((rows + TAIL, D), BF16), ((8, D), F32)],
        [*pieces, grad, labels, x2, gain, branch, folded, kept],
        after=after,
    )


def first_norm_back_body(has_next, *refs):
    own, mate, far, dx2, x_ref, gain, *refs = refs
    rows = dx2.shape[0]
    upstream = own[:rows].astype(F32) + mate[:rows].astype(F32) + far[:rows].astype(F32)
    back, _, _ = norm_back(x_ref[...].astype(F32), gain[...], upstream)
    total = (dx2[...] + back).astype(BF16)
    if has_next:
        labels, branch, folded, kept, g_ref, out_ref = refs
        masked = mask_column(labels, rows) * total.astype(F32)
        out_ref[...] = payload_of(masked, branch[...], folded[0:1], kept[...], FF)
    else:
        here, *items, g_ref, vec_ref = refs
        spot = slice(rows, rows + 24)
        vec_ref[...] = jnp.zeros_like(vec_ref)
        vec_ref[0:8, :] = decode_rows(here[spot]) + decode_rows(far[spot])
        for place, item in enumerate(items):
            first = 8 + 2 * place
            vec_ref[first : first + 2, : item.shape[1]] = item[0:2, :]
    g_ref[...] = total


def first_norm_back(pieces, dx2, x, gain, following=(), ending=(), after=()):
    rows = x.shape[0]
    outs = [((rows, D), BF16)]
    outs.append(((rows + TAIL, D), BF16) if following else ((16, D), F32))
    return call(
        "first_norm_back",
        partial(first_norm_back_body, bool(following)),
        outs,
        [*pieces, dx2, x, gain, *following, *ending],
        after=after,
    )


def in_hbm(x):
    return pltpu.with_memory_space_constraint(x, pltpu.HBM)


def fetch_all(refs, held, sems):
    copies = [
        pltpu.make_async_copy(ref, spot, sems.at[place])
        for place, (ref, spot) in enumerate(zip(refs, held))
    ]
    for copy in copies:
        copy.start()
    for copy in copies:
        copy.wait()


def first_block_body(
    flags, query, key, value, output, down, up, out, down_out, swap_out, *scratch
):
    *held, sems = scratch
    fetch_all((query, key, value, output, down, up), held, sems)
    width = query.shape[1]
    for place, ref in enumerate(held[:3]):
        out[:, place * width : (place + 1) * width] = ref[...]
    out[:, 3 * width :] = held[3][...].T
    down_out[...] = held[4][...].T
    lower = jnp.full((1, D), flags[2], jnp.int32) == 0
    swap_out[:, :D] = jnp.where(lower, down_out[...], held[5][...])
    swap_out[:, D:] = out[:, : D // 2]


def first_block(flags, *blocks):
    return pl.pallas_call(
        first_block_body,
        out_shape=tuple(
            jax.ShapeDtypeStruct((blocks[0].shape[0], width), BF16)
            for width in (D, D, 3 * D // 2)
        ),
        in_specs=[SMEM] + [HBM] * 6,
        out_specs=(VMEM,) * 3,
        scratch_shapes=[pltpu.VMEM(block.shape, BF16) for block in blocks]
        + [pltpu.SemaphoreType.DMA((6,))],
        compiler_params=PARAMS,
        name="first_block",
    )(flags, *map(in_hbm, blocks))


def beside_body(one, two, out):
    width = one.shape[1]
    out[:, :width] = one[...]
    out[:, width:] = two[...]


def beside(one, two, after=()):
    rows, width = one.shape
    return call("beside", beside_body, [((rows, 2 * width), BF16)], [one, two], after=after)[0]


def entry_body(flags, inputs, cotangent, out, far_out, own_in, own_grad, sems):
    size = own_in.shape[0]

    def rows_of(micro):
        return pl.ds(pl.multiple_of(micro * size, size), size)

    across, far, own = rows_of(1 - flags[3]), rows_of(flags[2]), rows_of(flags[3])
    copies = [
        pltpu.make_async_copy(source, target, sems.at[place])
        for place, (source, target) in enumerate(
            (
                (inputs.at[across], out.at[:size]),
                (cotangent.at[across], out.at[size:]),
                (inputs.at[far], far_out.at[:size]),
                (cotangent.at[far], far_out.at[size:]),
                (inputs.at[own], own_in),
                (cotangent.at[own], own_grad),
            )
        )
    ]
    for copy in copies:
        copy.start()
    for copy in copies:
        copy.wait()


def entry(flags, inputs, cotangent):
    rows = inputs.shape[0]
    shapes = [rows, rows, rows // 2, rows // 2]
    return pl.pallas_call(
        entry_body,
        out_shape=tuple(jax.ShapeDtypeStruct((count, D), BF16) for count in shapes),
        in_specs=[SMEM, HBM, HBM],
        out_specs=(VMEM,) * 4,
        scratch_shapes=[pltpu.SemaphoreType.DMA((6,))],
        compiler_params=PARAMS,
        name="entry",
    )(flags, in_hbm(inputs), in_hbm(cotangent))


def enter_body(
    flags, own_in, own_grad, got, labels, gain, bias, x_ref, g_ref, top_ref, h_ref
):
    size, width = x_ref.shape
    here = jnp.full((1, width), flags[0], jnp.int32) == 1
    own = jnp.where(here, own_in[...], got[:size])
    grad = jnp.where(here, own_grad[...], got[size:])
    x_ref[...] = own
    g_ref[...] = grad
    top_ref[...] = (mask_column(labels, size) * grad.astype(F32)).astype(BF16)
    normal, _ = split_norm(own.astype(F32))
    h_ref[...] = (normal * gain[...] + bias[...]).astype(BF16)


def enter(flags, own_in, own_grad, got, labels, gain, bias):
    return call(
        "enter",
        enter_body,
        [(own_in.shape, BF16)] * 4,
        [flags, own_in, own_grad, got, labels, gain, bias],
    )


def enter_far_body(got, labels, gain, bias, top_ref, h_ref):
    size = top_ref.shape[0]
    mask = (to_columns(labels[:, 2 * size : 3 * size])[:, 0:1] >= 0).astype(F32)
    top_ref[...] = (mask * got[size:].astype(F32)).astype(BF16)
    normal, _ = split_norm(got[:size].astype(F32))
    h_ref[...] = (normal * gain[...] + bias[...]).astype(BF16)


def enter_far(got, labels, gain, bias):
    rows = got.shape[0] // 2
    return call(
        "enter_far", enter_far_body, [((rows, D), BF16)] * 2, [got, labels, gain, bias]
    )


def pack_body(*refs):
    *items, out = refs
    size = items[0].shape[0]
    for place, item in enumerate(items):
        out[place * size : (place + 1) * size, :] = item[...]


def pack(items):
    rows, width = items[0].shape
    return call("pack", pack_body, [((len(items) * rows, width), BF16)], list(items))[0]


def unpack_body(flags, own, sent, got_own, got_sent, y_ref, g_ref):
    size = y_ref.shape[0] // 2
    width = y_ref.shape[1]
    here = jnp.full((1, width), flags[0], jnp.int32) == 1
    rows = pl.ds(pl.multiple_of(flags[2] * size, size), size)
    first = pl.ds(pl.multiple_of(flags[3] * size, size), size)
    second = pl.ds(pl.multiple_of((1 - flags[3]) * size, size), size)
    last = slice(2 * size, 3 * size)
    y_ref[first, :] = jnp.where(here, own[rows, :], got_own[rows, :])
    y_ref[second, :] = jnp.where(here, sent[rows, :], got_sent[rows, :])
    g_ref[first, :] = jnp.where(here, own[last, :], got_own[last, :])
    g_ref[second, :] = jnp.where(here, sent[last, :], got_sent[last, :])


def unpack(flags, own, sent, got_own, got_sent):
    rows = 2 * own.shape[0] // 3
    return call(
        "unpack",
        unpack_body,
        [((rows, own.shape[1]), BF16)] * 2,
        [flags, own, sent, got_own, got_sent],
    )


def halve_body(with_vectors, flags, block, across, *refs):
    if with_vectors:
        vectors, got, kept, sent, vec_ref = refs
        total = vectors[...] + got[...]
        vec_ref[...] = total
    else:
        kept, sent = refs
    size = kept.shape[0] // 2
    for place, (out, step) in enumerate(((kept, 0), (kept, 2), (sent, 1), (sent, 3))):
        rows = pl.ds(pl.multiple_of((flags[1] ^ step) * size, size), size)
        spot = slice((place % 2) * size, (place % 2 + 1) * size)
        out[spot] = (block[rows, :].astype(F32) + across[rows, :].astype(F32)).astype(BF16)
    if with_vectors:
        sent[2 * size :] = encode_rows(total)


def halve(flags, block, across, vectors=(), after=()):
    rows, width = block.shape
    outs = [((rows // 2, width), BF16)] * 2
    if vectors:
        outs = [outs[0], ((rows // 2 + 48, width), BF16), (vectors[0].shape, F32)]
    return call(
        "halve",
        partial(halve_body, bool(vectors)),
        outs,
        [flags, block, across, *vectors],
        after=after,
    )


def quarter_body(with_vectors, kept, got, *refs):
    if with_vectors:
        vectors, own, sent, vec_ref = refs
    else:
        own, sent = refs
    size = own.shape[0]
    for place, out in enumerate((own, sent)):
        rows = slice(place * size, (place + 1) * size)
        out[:size] = (kept[rows].astype(F32) + got[rows].astype(F32)).astype(BF16)
    if with_vectors:
        vec_ref[...] = vectors[...]
        sent[size:] = encode_rows(vectors[...])


def quarter(kept, got, vectors=(), after=()):
    rows, width = kept.shape
    outs = [((rows // 2, width), BF16)] * 2
    if vectors:
        outs = [outs[0], ((rows // 2 + 48, width), BF16), (vectors[0].shape, F32)]
    return call(
        "quarter",
        partial(quarter_body, bool(vectors)),
        outs,
        [kept, got, *vectors],
        after=after,
    )


def last_body(kept, got, vectors, out, vec_ref):
    size = kept.shape[0]
    out[...] = (kept[...].astype(F32) + got[:size].astype(F32)).astype(BF16)
    vec_ref[...] = vectors[...] + decode_rows(got[size:])


def last_of(kept, got, vectors):
    outs = [(kept.shape, BF16), (vectors.shape, F32)]
    return call("last", last_body, outs, [kept, got, vectors])


def total_body(*refs):
    *parts, out = refs
    out[...] = sum(part[...].astype(F32) for part in parts).astype(out.dtype)


def total_of(parts, kind=BF16, after=()):
    return call("total", total_body, [(parts[0].shape, kind)], list(parts), after=after)[0]


def final_first_body(flags, lower, upper, vec, vec_got, q_ref, k_ref, v_ref, o_ref, vec_ref):
    width = q_ref.shape[1]
    first = jnp.full((1, D), flags[2], jnp.int32) == 0
    total = jnp.where(first, lower[...].astype(F32), upper[...].astype(F32))
    for place, ref in enumerate((q_ref, k_ref, v_ref)):
        ref[...] = total[:, place * width : (place + 1) * width]
    o_ref[...] = total[:, 3 * width :].T
    here = jnp.full((1, D), flags[0], jnp.int32) == 1
    vec_ref[...] = jnp.where(here, vec[...], vec_got[...])


def final_first(flags, lower, upper, vec, vec_got):
    rows, width = upper.shape[0], D // LANES
    return call(
        "final_first",
        final_first_body,
        [((rows, width), F32)] * 3 + [((width, rows), F32), ((16, D), F32)],
        [flags, lower, upper, vec, vec_got],
    )


def final_second_body(flags, lower, upper, up_ref, down_ref):
    first = jnp.full((1, 2 * UNITS), flags[2], jnp.int32) == 0
    total = jnp.where(first, lower[...].astype(F32), upper[...].astype(F32))
    up_ref[...] = total[:, :UNITS]
    down_ref[...] = total[:, UNITS:].T


def final_second(flags, lower, upper):
    rows = lower.shape[0]
    return call(
        "final_second",
        final_second_body,
        [((rows, UNITS), F32), ((UNITS, rows), F32)],
        [flags, lower, upper],
    )


def merge_body(flags, one, two, upper, out):
    size, width = one.shape
    first = jnp.full((1, width), flags[2], jnp.int32) == 0
    for place, ref in enumerate((one, two)):
        rows = slice(place * size, (place + 1) * size)
        out[rows] = jnp.where(first, ref[...], upper[rows])


def merge(flags, one, two, upper):
    return call("merge", merge_body, [(upper.shape, BF16)], [flags, one, two, upper])[0]


def choose_body(flags, one, two, out):
    first = jnp.full((1, out.shape[1]), flags[2], jnp.int32) == 0
    out[...] = jnp.where(first, one[...], two[...])


def choose(flags, one, two, after=()):
    return call("choose", choose_body, [(one.shape, one.dtype)], [flags, one, two], after=after)[0]


def join_body(flags, own, got, out):
    half = own.shape[1]
    first = jnp.full((1, half), flags[2], jnp.int32) == 0
    out[:, :half] = jnp.where(first, own[...], got[...])
    out[:, half:] = jnp.where(first, got[...], own[...])


def join(flags, own, got, after=()):
    rows, half = own.shape
    return call(
        "join", join_body, [((rows, 2 * half), BF16)], [flags, own, got], after=after
    )[0]


def hold_body(ref, out):
    out[...] = ref[...]


def hold(x, after):
    return call("hold", hold_body, [(x.shape, x.dtype)], [x], after=after)[0]


def assemble_body(count, flags, *refs):
    beside, across, out = refs[:count], refs[count:-1], refs[-1]
    size = beside[0].shape[0]
    width = out.shape[1]
    near = jnp.full((1, width), flags[0], jnp.int32) == 1
    for step in range(count):
        rows = pl.ds(pl.multiple_of((flags[1] ^ step) * size, size), size)
        out[rows, :] = jnp.where(near, beside[step][...], across[step][...])


def assemble(flags, beside, across, after=()):
    count, (size, width) = len(beside), beside[0].shape
    return call(
        "assemble",
        partial(assemble_body, count),
        [((count * size, width), BF16)],
        [flags, *beside, *across],
        after=after,
    )[0]


def early_block_body(flags, up, got, first, out):
    width = up.shape[1]
    lower = jnp.full((1, width), flags[2], jnp.int32) == 0
    out[:, :width] = jnp.where(lower, up[...], got[:, :width])
    half = first.shape[1] // 2
    lower = jnp.full((1, half), flags[2], jnp.int32) == 0
    out[:, width:] = jnp.where(lower, got[:, width:], first[:, half:])


def early_block(flags, up, got, first, after=()):
    rows, width = up.shape
    return call(
        "early_block",
        early_block_body,
        [((rows, width + first.shape[1] // 2), BF16)],
        [flags, up, got, first],
        after=after,
    )[0]


def late_block_body(flags, got, down, out):
    width = down.shape[1]
    lower = jnp.full((1, width), flags[2], jnp.int32) == 0
    out[...] = jnp.where(lower, got[:, :width], down[...])


def late_block(flags, got, down, after=()):
    return call(
        "late_block", late_block_body, [(down.shape, BF16)], [flags, got, down], after=after
    )[0]


def parts_body(ref, one, two):
    width = one.shape[1]
    one[...] = ref[:, :width]
    two[...] = ref[:, width:]


def parts_of(x, width, after):
    rows, whole = x.shape
    shapes = [((rows, width), x.dtype), ((rows, whole - width), x.dtype)]
    return call("parts", parts_body, shapes, [x], after=after)


def pick_body(flags, beside, across, out):
    near = jnp.full((1, out.shape[1]), flags[0], jnp.int32) == 1
    out[...] = jnp.where(near, beside[...], across[...])


def pick(flags, beside, across, after=()):
    return call(
        "pick", pick_body, [(beside.shape, BF16)], [flags, beside, across], after=after
    )[0]


def on_device(
    inputs,
    cotangent,
    doc_ids,
    norm_gain,
    norm_bias,
    w_query,
    w_key,
    w_value,
    inner_gain,
    inner_bias,
    w_output,
    feed_gain,
    feed_bias,
    w_up,
    middle_gain,
    middle_bias,
    w_down,
):
    core = lax.axis_index("section")
    lane = lax.axis_index("mp")
    lane_x = lane % 2
    lane_y = lane // 2
    count = lax.axis_size("dp")
    slice_len = inputs.shape[0] // MICRO
    rank = 2 * core + lane_x
    crossing = [(s * 4 + r, s * 4 + (r ^ 2)) for s in range(2) for r in range(4) if s == r // 2]
    returning = [(s * 4 + r, s * 4 + (r ^ 2)) for s in range(2) for r in range(4) if s != r // 2]

    def by_core(first, second):
        return jnp.where(core == 0, first, second)

    def placed(array, layer):
        return [
            lax.ppermute(
                array,
                BOTH,
                [(s * 4 + 2 * m + x, layer * 4 + 2 * s + x) for s in range(2) for x in range(2)],
            )
            for m in range(MICRO)
        ]

    label_grid = lax.dynamic_index_in_dim(
        doc_ids.reshape(LANES, MICRO, slice_len), lane_y, 1, keepdims=False
    )
    order = (rank, 2 * (1 - core) + lane_x, rank ^ 1, 2 * (1 - core) + (1 - lane_x))
    labels = jnp.concatenate(
        [lax.dynamic_index_in_dim(label_grid, item, 0, keepdims=False) for item in order]
    )
    labels = jnp.broadcast_to(labels.astype(F32)[None], (8, LANES * slice_len))

    place = lax.axis_index("dp")
    flags = jnp.stack([core == lane_y, place, core, lane_y]).astype(jnp.int32)

    def line_pairs(step):
        return [
            ((r // 2 * count + i) * LANES + r, (r // 2 * count + (i ^ step)) * LANES + r)
            for i in range(count)
            for r in range(LANES)
        ]

    def along_line(block, step):
        return lax.ppermute(block, ("section", "dp", "mp"), line_pairs(step))

    first, down_block, swapped = first_block(
        flags, w_query[0], w_key[0], w_value[0], w_output[0], w_down[0], w_up[0]
    )
    up_block = w_up[0]
    to_first = [(LANES + r, r) for r in range(LANES)]
    inner_ranks = [((1 - r // 2) * LANES + r, (r // 2) * LANES + r) for r in range(LANES)]

    def along_dp(block):
        return lax.all_gather(block, "dp", axis=0, tiled=True)

    def fetched(line, hook=()):
        whole = join(flags, line, lax.ppermute(line, BOTH, inner_ranks), after=hook)
        return whole, lax.ppermute(whole, BOTH, crossing)

    def rank_of(line, source):
        return lax.ppermute(
            line, BOTH, [(source * LANES + r, (r // 2) * LANES + r) for r in range(LANES)]
        )

    outer_own = jnp.concatenate([norm_gain, norm_bias, feed_gain, feed_bias], axis=0)
    outer_other = core_swap(outer_own)
    split_own = jnp.concatenate([inner_gain, inner_bias, middle_gain, middle_bias], axis=1)
    split_far = y_swap(split_own)
    split_kept = jnp.where(lane_y == core, split_own, split_far)
    split_other = core_swap(jnp.where(lane_y == core, split_far, split_own))

    def small_of(outer, split):
        width = D // LANES
        return (
            [outer[i : i + 1] for i in range(4)],
            [
                split[:, :width],
                split[:, width : 2 * width],
                split[:, 2 * width : 2 * width + UNITS],
                split[:, 2 * width + UNITS :],
            ],
        )

    lower_outer, lower_split = small_of(
        by_core(outer_own, outer_other), by_core(split_kept, split_other)
    )
    upper_outer, upper_split = small_of(
        by_core(outer_other, outer_own), by_core(split_other, split_kept)
    )

    def gather_around(own, near_of, far=None, after=()):
        if far is None:
            far = x_swap(own)
        mate = core_swap(own)
        near = near_of([own, mate])
        far = hold(far, after=[near[0], *after])
        return (own, mate, far, core_swap(far)), near

    def attention(x, h, first, outer, split, hooks, far=None):
        pieces, (near,) = gather_around(
            h, lambda rows: [project(*rows, first)], far, after=hooks[2]
        )
        far = project(pieces[2], pieces[3], first)
        half = 2 * slice_len
        o_far, p_far, p_far_mate, sum_far = attend(
            half, far, near, far, labels, first, split[0], split[1]
        )
        sent = pair_sum(p_far, p_far_mate)
        o_near, p_own, p_mate, sum_near = attend(
            0, near, near, far, labels, first, split[0], split[1], after=[sent]
        )
        hooks[0](p_own)
        arrived = hold(x_swap(sent), after=[p_own])
        terms = (p_own, core_swap(p_mate), arrived)
        x2, branch, h2, folded, kept = after_attend(x, terms, outer[2], outer[3], after=hooks[1])
        state = (pieces, near, far, o_near, o_far, sum_near, sum_far, x, x2, branch, folded, kept)
        return x2, h2, state, arrived

    def attention_back(grad, sums, state, first, outer, split, following, hooks):
        pieces, near, far, o_near, o_far, sum_near, sum_far, x, x2, branch, folded, kept = state
        dx2, sent, feed_vec = feed_norm_back(
            sums, grad, labels, x2, outer[2], branch, folded, kept, after=hooks[0]
        )
        block = hooks[3](sent)
        backs, (do_near, u_near, vec_near) = gather_around(
            sent, lambda rows: inner_back(rows, o_near, split[0], split[1], first), after=block
        )
        do_far, u_far, vec_far = inner_back(backs[2:], o_far, split[0], split[1], first)
        dq_near, dq_far = attend_back(
            near, far, do_near, do_far, sum_near, sum_far, labels, after=hooks[1]
        )
        norm = (outer[0], outer[1])
        if following:
            p_far, p_far_mate, norm_far = unproject(
                dq_far, first, pieces[2:], *norm, after=hooks[4](dq_far)
            )
            sent = pair_sum(p_far, p_far_mate)
            p_own, p_mate, norm_near = unproject(
                dq_near, first, pieces[:2], *norm, after=[sent, *hooks[5]()]
            )
            norm_vec = norm_near + norm_far
            ending = ()
        else:
            p_own, p_mate, norm_near = unproject(
                dq_near, first, pieces[:2], *norm, after=hooks[7]
            )
            riding = (norm_near, feed_vec, *hooks[4])
            p_far, p_far_mate = unproject(dq_far, first, pieces[2:], *norm, riding=riding)
            sent = pair_sum(p_far, p_far_mate)
            norm_vec = None
            ending = (sent, *hooks[5], vec_near + vec_far, hooks[6])
        mat_grad = grads_of(
            (pieces, (dq_near, dq_far)), (backs, (u_near, u_far)), after=[sent]
        )
        terms = (p_own, core_swap(p_mate), hold(x_swap(sent), after=[p_own, mat_grad]))
        result = first_norm_back(
            terms, dx2, x, outer[0], following, ending, after=hooks[2](mat_grad)
        )
        return result, vec_near + vec_far, feed_vec, norm_vec

    def reduce_across(block):
        across = lax.ppermute(block, BOTH, returning)
        if count != 4:
            total = total_of([block, across])
            return [lax.psum_scatter(total, "dp", scatter_dimension=0, tiled=True)]
        return block, across

    def reduce_near(pair, after=()):
        if count != 4:
            return pair
        kept, sent = halve(flags, *pair, after=after)
        return kept, along_line(sent, 1)

    def reduce_far(pair, after=()):
        if count != 4:
            return pair
        kept, sent = quarter(*pair, after=after)
        return kept, along_line(sent, 2)

    def reduce_end(pair, layer, after=()):
        total = total_of(pair, after=after) if count == 4 else pair[0]
        return lax.ppermute(
            total, BOTH, [((r // 2) * LANES + r, layer * LANES + r) for r in range(LANES)]
        )

    sent, far_sent, own_in, own_grad = entry(flags, inputs, cotangent)
    got = lax.ppermute(sent, BOTH, crossing)
    far_got = lax.ppermute(
        far_sent,
        BOTH,
        [
            (s * LANES + r, s * LANES + (r ^ 1) if s == r // 2 else (r // 2) * LANES + (r ^ 3))
            for s in range(2)
            for r in range(LANES)
        ],
    )
    lower_in, upstream, masked, h = enter(
        flags, own_in, own_grad, got, labels, lower_outer[0], lower_outer[1]
    )
    masked_far, far = enter_far(far_got, labels, lower_outer[0], lower_outer[1])
    top = (masked, core_swap(masked), masked_far, core_swap(masked_far))
    moved = rank_of(first, 0)
    if count == 4:
        pieces = [moved] + [along_line(moved, step) for step in range(1, count)]
        lower_first = assemble(
            flags, pieces, [lax.ppermute(piece, BOTH, crossing) for piece in pieces], after=[far]
        )
    else:
        pieces = [along_dp(moved)]
        lower_first = pick(flags, pieces[0], lax.ppermute(pieces[0], BOTH, crossing))
    got = core_swap(swapped)
    early_line = along_dp(early_block(flags, up_block, got, first, after=pieces[-1:]))
    late_line = along_dp(late_block(flags, got, down_block))
    coming = {}

    def early_matrices(last):
        coming["second"], coming["first"] = parts_of(early_line, UNITS, [last])

    x2, h2, lower_state, arrived = attention(
        lower_in, h, lower_first, lower_outer, lower_split, (early_matrices, (), ()), far
    )
    lower_second_whole, lower_second_across = fetched(coming["second"])
    lower_second = pick(flags, lower_second_whole, lower_second_across)
    upper_first_whole, upper_first_across = fetched(coming["first"], [h2])
    upper_first = pick(flags, upper_first_whole, upper_first_across)
    lower_pieces, (f_near, p_own, p_mate) = gather_around(
        h2, lambda rows: feed(rows, (), lower_second, *lower_split[2:])
    )
    f_far, p_far, p_far_mate = feed(lower_pieces[2:], (), lower_second, *lower_split[2:])
    lower_pre = (f_near, f_far)
    sent = pair_sum(p_far, p_far_mate)
    upper_second_whole, upper_second_across = fetched(hold(late_line, after=[sent]))
    upper_second = pick(flags, upper_second_whole, upper_second_across)
    arrived = hold(x_swap(sent), after=[upper_second_whole])
    terms = (p_own, core_swap(p_mate), arrived)
    lower_out, lower_branch, h, lower_folded, lower_kept = after_feed(
        x2, terms, labels, upper_outer[0], upper_outer[1]
    )
    x2, h2, upper_state, _ = attention(
        lower_out,
        h,
        upper_first,
        upper_outer,
        upper_split,
        (lambda last: None, (), [upper_second_whole]),
    )
    upper_pieces, (f_near, p_own, p_mate, near_stats) = gather_around(
        h2, lambda rows: feed(rows, top[:2], upper_second, *upper_split[2:])
    )
    f_far, p_far, p_far_mate, far_stats = feed(
        upper_pieces[2:], top[2:], upper_second, *upper_split[2:]
    )
    upper_pre = (f_near, f_far)

    stats = group_stats(near_stats, far_stats)
    df_far, n_far, q_far, q_far_mate, vec_far = feed_back(
        top[2:], [stats], 2, upper_pre[1], *upper_split[2:], upper_second
    )
    sent = pair_sum(q_far, q_far_mate)
    df_near, n_near, q_own, q_mate, vec_near = feed_back(
        top[:2], [stats], 0, upper_pre[0], *upper_split[2:], upper_second, after=[sent]
    )
    upper_middle = vec_near + vec_far
    sums = (q_own, core_swap(q_mate), hold(x_swap(sent), after=[q_own]))
    ended = pair_sum(p_far, p_far_mate)
    ended_far = []

    def ended_hook(last):
        ended_far.append(hold(x_swap(ended), after=[last]))
        return ended_far

    following = (labels, lower_branch, lower_folded, lower_kept)
    pairs = {}

    def upper_second_grads(after):
        block = grads_of(
            (upper_pieces, (df_near, df_far)), (top, (n_near, n_far)), after=[after]
        )
        pairs["second"] = reduce_near(reduce_across(block))
        return [block]

    def upper_hook(item):
        pairs["upper"] = reduce_across(item)
        return [item]

    (upper_grad, sent), upper_inner, upper_feed, upper_norm = attention_back(
        upstream,
        sums,
        upper_state,
        upper_first,
        upper_outer,
        upper_split,
        following,
        ((), [ended], upper_hook, upper_second_grads, ended_hook, lambda: ()),
    )

    upper_out = finish_feed(x2, (p_own, core_swap(p_mate), ended_far[0]), labels)
    own = pack([lower_out, upper_out, upper_grad])
    swapped = lax.ppermute(own, BOTH, returning)
    upper_second_pair = reduce_far(pairs["second"], [own])
    upper_first_pair = reduce_near(pairs["upper"])
    backs, (df_near, n_near, q_own, q_mate, vec_near) = gather_around(
        sent,
        lambda rows: feed_back(
            rows, (), 0, lower_pre[0], *lower_split[2:], lower_second, after=[own]
        ),
        after=upper_first_pair[:1],
    )
    df_far, n_far, q_far, q_far_mate, vec_far = feed_back(
        backs[2:],
        (),
        2,
        lower_pre[1],
        *lower_split[2:],
        lower_second,
        after=[swapped, upper_second_pair[0]],
    )
    lower_middle = vec_near + vec_far
    sent = pair_sum(q_far, q_far_mate)
    sums = (q_own, core_swap(q_mate), x_swap(sent))

    def lower_second_grads(after):
        block = grads_of(
            (lower_pieces, (df_near, df_far)), (backs, (n_near, n_far)), after=[after]
        )
        pairs["second"] = reduce_across(block)
        return [block]

    upper_second_sum = reduce_end(upper_second_pair, 1, after=[q_far])
    upper_first_pair = reduce_far(upper_first_pair, after=[q_far])
    upper_first_sum = reduce_end(upper_first_pair, 1)

    inward = [((r // 2) * LANES + r, (1 - r // 2) * LANES + r) for r in range(LANES)]
    layer_outputs, upper_held = unpack(
        flags, own, swapped, lax.ppermute(own, BOTH, inward), lax.ppermute(swapped, BOTH, inward)
    )

    def lower_hook(item):
        pairs["lower"] = reduce_across(item)
        pairs["second"] = reduce_far(reduce_near(pairs["second"], after=[item]))
        return [item, upper_first_sum, pairs["second"][0]]

    (lower_grad, vectors), _, _, _ = attention_back(
        upper_grad,
        sums,
        lower_state,
        lower_first,
        lower_outer,
        lower_split,
        (),
        (
            [layer_outputs],
            [upper_second_sum],
            lower_hook,
            lower_second_grads,
            (upper_norm, upper_feed),
            (lower_middle, upper_middle),
            upper_inner,
            [upper_first_pair[0]],
        ),
    )
    lower_second_pair = pairs["second"]
    lower_held = placed(lower_grad, 0)
    if count == 4:
        kept, got = reduce_near(pairs["lower"], after=[vectors])
        vectors = total_of([vectors, y_swap(vectors)], F32)
        vectors = total_of([vectors, along_line(vectors, 1)], F32)
        kept, sent, vectors = quarter(kept, got, [vectors])
        ended, vectors = last_of(kept, along_line(sent, 2), vectors)
    else:
        vectors = lax.psum(vectors + y_swap(vectors), "dp")
        ended = pairs["lower"][0]
    ended = lax.ppermute(ended, BOTH, [((r // 2) * LANES + r, r) for r in range(LANES)])
    vectors_got = lax.ppermute(vectors, BOTH, inward)
    lower_second_sum = reduce_end(lower_second_pair, 0)
    input_grads = merge(flags, *lower_held, upper_held)
    grad_query, grad_key, grad_value, grad_output, vectors = final_first(
        flags, ended, upper_first_sum, vectors, vectors_got
    )
    grad_up, grad_down = final_second(flags, lower_second_sum, upper_second_sum)

    def part(rows, start, size):
        rows = lax.dynamic_slice(rows, (core * rows.shape[0] // 2, start), (rows.shape[0] // 2, size))
        return [rows[i : i + 1] for i in range(rows.shape[0])]

    width = D // LANES
    size = D // count // LANES
    outer = part(vectors[:8], (place * LANES + lane) * size, size)
    middle = part(vectors[8:12], place * (UNITS // count), UNITS // count)
    inner = part(vectors[12:], place * (width // count), width // count)
    return (
        layer_outputs[None],
        input_grads[None],
        outer[0],
        outer[1],
        grad_query[None],
        grad_key[None],
        grad_value[None],
        inner[0],
        inner[1],
        grad_output[None],
        outer[2],
        outer[3],
        grad_up[None],
        middle[0],
        middle[1],
        grad_down[None],
    )


def solution(mesh):
    placed = (
        P(("dp", "mp"), None),
        P(("dp", "mp"), None),
        P("dp"),
        P("section", None),
        P("section", None),
        P("section", "dp", "mp"),
        P("section", "dp", "mp"),
        P("section", "dp", "mp"),
        P("section", "mp"),
        P("section", "mp"),
        P("section", "mp", "dp"),
        P("section", None),
        P("section", None),
        P("section", "dp", "mp"),
        P("section", "mp"),
        P("section", "mp"),
        P("section", "mp", "dp"),
    )
    return jax.shard_map(
        on_device,
        mesh=mesh,
        in_specs=placed,
        out_specs=(
            P("section", ("dp", "mp"), None),
            P("section", ("dp", "mp"), None),
            P("section", ("dp", "mp")),
            P("section", ("dp", "mp")),
            P("section", "dp", "mp"),
            P("section", "dp", "mp"),
            P("section", "dp", "mp"),
            P("section", ("mp", "dp")),
            P("section", ("mp", "dp")),
            P("section", "mp", "dp"),
            P("section", ("dp", "mp")),
            P("section", ("dp", "mp")),
            P("section", "dp", "mp"),
            P("section", ("mp", "dp")),
            P("section", ("mp", "dp")),
            P("section", "mp", "dp"),
        ),
        check_vma=False,
    )
```

```python
from functools import partial

import jax
import jax.numpy as jnp
from jax import lax
from jax.experimental import pallas as pl
from jax.experimental.pallas import tpu as pltpu
from jax.sharding import PartitionSpec as P

D = 768
HEAD_DIM = 64
FF = 3072
MICRO = 2
LANES = 4
EPS = 1e-05
SCALE = HEAD_DIM ** (-0.5)
LOG2E = 1.4426950408889634
SQRT_HALF = 0.7071067811865476
INV_SQRT_2PI = 0.3989422804014327
BOTH = ("section", "mp")
Y_PAIRS = [[0, 2], [1, 3]]
QKV = 3 * D // LANES
UNITS = FF // LANES
TAIL = 16
F32 = jnp.float32
BF16 = jnp.bfloat16

VMEM = pl.BlockSpec(memory_space=pltpu.VMEM)
SMEM = pl.BlockSpec(memory_space=pltpu.SMEM)
ANY = pl.BlockSpec(memory_space=pl.ANY)
HBM = pl.BlockSpec(memory_space=pltpu.HBM)
PARAMS = pltpu.CompilerParams(vmem_limit_bytes=16 * 1024 * 1024)


def call(name, body, outs, ins, scratch=(), after=(), cost=None):
    count = len(ins)

    def kernel(*refs):
        body(*refs[:count], *refs[count + len(after) :])

    return pl.pallas_call(
        kernel,
        out_shape=tuple(jax.ShapeDtypeStruct(shape, kind) for shape, kind in outs),
        in_specs=[SMEM if item.ndim == 1 else VMEM for item in ins] + [ANY] * len(after),
        out_specs=(VMEM,) * len(outs),
        scratch_shapes=list(scratch),
        compiler_params=PARAMS,
        name=name,
        cost_estimate=cost or work(1, 1),
    )(*ins, *after)


def work(flops, size):
    return pl.CostEstimate(flops=int(flops), bytes_accessed=int(size), transcendentals=0)


def nn(a, b):
    return jnp.dot(a, b, preferred_element_type=F32)


def nt(a, b):
    return lax.dot_general(a, b, (((1,), (1,)), ((), ())), preferred_element_type=F32)


def tn(a, b):
    return lax.dot_general(a, b, (((0,), (0,)), ((), ())), preferred_element_type=F32)


def to_rows(*columns):
    count = columns[0].shape[0]
    lane = lax.broadcasted_iota(jnp.int32, (count, 128), 1)
    tile = jnp.zeros((count, 128), F32)
    for place, column in enumerate(columns):
        tile = jnp.where(lane == place, column, tile)
    return tile.T[:8]


def to_columns(rows):
    return jnp.concatenate([rows, jnp.zeros((120, rows.shape[1]), F32)], axis=0).T


def split_three(values):
    high = values.astype(BF16)
    rest = values - high.astype(F32)
    middle = rest.astype(BF16)
    return high, middle, (rest - middle.astype(F32)).astype(BF16)


def encode(rows):
    return jnp.concatenate(split_three(rows), axis=1)


def decode(tail):
    tail = tail.astype(F32)
    count = tail.shape[1] // 3
    return tail[:, :count] + tail[:, count : 2 * count] + tail[:, 2 * count :]


def decode_vectors(tail):
    tail = tail.astype(F32)
    return jnp.concatenate(
        [jnp.sum(tail[0:3], axis=0, keepdims=True), jnp.sum(tail[3:6], axis=0, keepdims=True)],
        axis=0,
    )


def encode_vectors(first, second):
    return jnp.concatenate(
        [*split_three(first), *split_three(second), jnp.zeros((2, first.shape[1]), BF16)], axis=0
    )


def split_norm(values):
    mean = jnp.mean(values, axis=-1, keepdims=True)
    spread = jnp.mean(values * values, axis=-1, keepdims=True) - mean * mean
    scaled = lax.rsqrt(spread + EPS)
    return (values - mean) * scaled, scaled


def norm_back(values, gain, upstream):
    normal, scaled = split_norm(values)
    inner = upstream * gain
    one = jnp.mean(inner, axis=-1, keepdims=True)
    two = jnp.mean(inner * normal, axis=-1, keepdims=True)
    back = scaled * (inner - one - normal * two)
    return (
        back,
        jnp.sum(upstream * normal, axis=0, keepdims=True),
        jnp.sum(upstream, axis=0, keepdims=True),
    )


def vector_rows(first, second):
    return jnp.concatenate([first, second, jnp.zeros((6, first.shape[1]), F32)], axis=0)


def folded_vectors(mat, gain, bias):
    rows = jnp.concatenate(
        [*split_three(gain), *split_three(bias), jnp.zeros((10, gain.shape[1]), BF16)], axis=0
    )
    folded = nt(rows, mat)
    return encode_vectors(
        jnp.sum(folded[0:3], axis=0, keepdims=True), jnp.sum(folded[3:6], axis=0, keepdims=True)
    )


def core_swap(x):
    return lax.ppermute(x, "section", [(0, 1), (1, 0)])


def x_swap(x):
    return lax.ppermute(x, "mp", [(i, i ^ 1) for i in range(LANES)])


def y_swap(x):
    return lax.ppermute(x, "mp", [(i, i ^ 2) for i in range(LANES)])


def gather_rows(own):
    far = x_swap(own)
    return own, core_swap(own), far, core_swap(far)


def pair_sum_body(first, second, out):
    rows = out.shape[0] - TAIL
    out[:rows] = (first[:rows].astype(F32) + second[:rows].astype(F32)).astype(BF16)
    half = rows + TAIL // 2
    out[rows:half] = encode(decode(first[rows:half]) + decode(second[rows:half]))
    folded = decode_vectors(first[half:]) + decode_vectors(second[half:])
    out[half:] = encode_vectors(folded[0:1], folded[1:2])


def pair_add_body(first, second, out):
    out[...] = (first[...].astype(F32) + second[...].astype(F32)).astype(BF16)


def pair_sum(far, far_mate):
    body = pair_sum_body if far.shape[0] % 256 else pair_add_body
    return call("pair_sum", body, [(far.shape, BF16)], [far, core_swap(far_mate)])[0]


def settle(own, mate, far, far_mate):
    sent = pair_sum(far, far_mate)
    return own, core_swap(mate), x_swap(sent)


def project_body(first, second, mat, out):
    size = first.shape[0]
    for place, piece in enumerate((first, second)):
        out[place * size : (place + 1) * size, :] = nn(piece[...], mat[:, :QKV]).astype(BF16)


def project(first, second, mat):
    count = 2 * first.shape[0]
    return call(
        "project",
        project_body,
        [((count, QKV), BF16)],
        [first, second, mat],
    )[0]


def split_heads(source, target, first, start, head_count):
    size = source.shape[0]
    for head in range(head_count):
        lanes = slice(first + head * HEAD_DIM, first + (head + 1) * HEAD_DIM)
        target[head, start : start + size, :] = source[:, lanes]


def attend_body(
    q_start, q_ref, near, far, labels, mat, gain, bias, o_ref, p_one, p_two, sum_ref, ks, vs
):
    head_count = QKV // (3 * HEAD_DIM)
    width = head_count * HEAD_DIM
    half = near.shape[0]
    for start, ref in ((0, near), (half, far)):
        split_heads(ref, ks, width, start, head_count)
        split_heads(ref, vs, 2 * width, start, head_count)
    out_mat = mat[:, QKV:]
    folded = folded_vectors(out_mat, gain[...], bias[...])
    size = half // 2
    key_labels = labels[0:1, :]
    for place, p_ref in enumerate((p_one, p_two)):
        rows = slice(place * size, (place + 1) * size)
        first = q_start + place * size
        allowed = to_columns(labels[:, first : first + size])[:, 0:1] == key_labels
        outs = []
        sums = []
        for head in range(head_count):
            query = q_ref[rows, head * HEAD_DIM : (head + 1) * HEAD_DIM]
            scores = jnp.where(allowed, nt(query, ks[head]), -1e30)
            peak = jnp.max(scores, axis=-1, keepdims=True)
            terms = jnp.exp2((scores - peak) * (SCALE * LOG2E))
            total = jnp.sum(terms, axis=-1, keepdims=True)
            outs.append(nn(terms.astype(BF16), vs[head]) / total)
            sums.append(peak * (SCALE * LOG2E) + jnp.log(total) * LOG2E)
        out = jnp.concatenate(outs, axis=1)
        o_ref[rows, :] = out
        lane = lax.broadcasted_iota(jnp.int32, (size, 128), 1)
        tile = jnp.zeros((size, 128), F32)
        for spot, column in enumerate(sums):
            tile = jnp.where(lane == spot, column, tile)
        sum_ref[rows, :] = tile
        p_ref[:size] = nt((out * gain[...]).astype(BF16), out_mat).astype(BF16)
        stats = to_rows(
            jnp.sum(out, axis=-1, keepdims=True), jnp.sum(out * out, axis=-1, keepdims=True)
        )
        p_ref[size : size + TAIL // 2] = encode(stats)
        p_ref[size + TAIL // 2 :] = folded


def attend(q_start, queries, near, far, labels, mat, gain, bias, after=()):
    count, keys = queries.shape[0], 2 * near.shape[0]
    heads = QKV // (3 * HEAD_DIM)
    width = heads * HEAD_DIM
    by_head = pltpu.VMEM((heads, keys, HEAD_DIM), BF16)
    payload = ((count // 2 + TAIL, D), BF16)
    return call(
        "attend",
        partial(attend_body, q_start),
        [((count, width), F32), payload, payload, ((count, 128), F32)],
        [queries, near, far, labels, mat, gain, bias],
        [by_head, by_head],
        after,
        work(4e9, 1),
    )


def attend_back_body(
    near, far, do_near, do_far, sum_near, sum_far, labels, near_out, far_out,
    qs, ks, vs, grads, dqs, dks, dvs, sums,
):
    head_count = QKV // (3 * HEAD_DIM)
    width = head_count * HEAD_DIM
    half = near.shape[0]
    for start, ref, grad in ((0, near, do_near), (half, far, do_far)):
        split_heads(ref, qs, 0, start, head_count)
        split_heads(ref, ks, width, start, head_count)
        split_heads(ref, vs, 2 * width, start, head_count)
        split_heads(grad, grads, 0, start, head_count)
    sums[:half] = sum_near[...]
    sums[half:] = sum_far[...]
    dks[...] = jnp.zeros_like(dks)
    dvs[...] = jnp.zeros_like(dvs)
    key_labels = labels[0:1, :]
    size = half // 2

    def block(index, carry):
        rows = pl.ds(pl.multiple_of(index * size, size), size)
        allowed = to_columns(labels[:, rows])[:, 0:1] == key_labels
        for head in range(head_count):
            query, grad = qs[head, rows, :], grads[head, rows, :]
            scores = jnp.where(allowed, nt(query, ks[head]), -1e30)
            prob = jnp.exp2(scores * (SCALE * LOG2E) - sums[rows, head : head + 1])
            prob_grad = nt(grad, vs[head])
            delta = jnp.sum(prob * prob_grad, axis=-1, keepdims=True)
            score_grad = (prob * (prob_grad - delta)).astype(BF16)
            dqs[head, rows, :] = nn(score_grad, ks[head]) * SCALE
            dks[head] += tn(query, score_grad)
            dvs[head] += tn(grad, prob.astype(BF16))
        return carry

    lax.fori_loop(0, 4, block, 0)
    for start, out in ((0, near_out), (half, far_out)):
        rows = slice(start, start + half)
        heads = range(head_count)
        out[...] = jnp.concatenate(
            [dqs[head, rows, :].astype(BF16) for head in heads]
            + [(dks[head, :, rows].T * SCALE).astype(BF16) for head in heads]
            + [dvs[head, :, rows].T.astype(BF16) for head in heads],
            axis=1,
        )


def attend_back(near, far, do_near, do_far, sum_near, sum_far, labels, after=()):
    half, width = do_near.shape
    keys = 2 * half
    heads = width // HEAD_DIM
    by_head = pltpu.VMEM((heads, keys, HEAD_DIM), BF16)
    turned = pltpu.VMEM((heads, HEAD_DIM, keys), F32)
    return call(
        "attend_back",
        attend_back_body,
        [(near.shape, BF16)] * 2,
        [near, far, do_near, do_far, sum_near, sum_far, labels],
        [by_head] * 4
        + [pltpu.VMEM((heads, keys, HEAD_DIM), F32), turned, turned, pltpu.VMEM((keys, 128), F32)],
        after,
        work(1.4e10, 1),
    )


def gelu_parts(x):
    spread = 0.5 + 0.5 * lax.erf(x * SQRT_HALF)
    return x * spread, spread


def feed_body(with_back, *refs):
    if with_back:
        one, two, back_one, back_two, mat, gain, bias, f_ref, p_one, p_two, s_ref = refs
    else:
        one, two, mat, gain, bias, f_ref, p_one, p_two = refs
        back_one = back_two = s_ref = None
    size = one.shape[0]
    up, down = mat.at[:, :UNITS], mat.at[:, UNITS:]
    folded = folded_vectors(down[...], gain[...], bias[...])
    for place, (piece, p_ref, back) in enumerate(((one, p_one, back_one), (two, p_two, back_two))):
        rows = slice(place * size, (place + 1) * size)
        pre = nn(piece[...], up[...])
        f_ref[rows, :] = pre
        act, _ = gelu_parts(pre)
        p_ref[:size] = nt((act * gain[...]).astype(BF16), down[...]).astype(BF16)
        columns = [
            jnp.sum(act, axis=-1, keepdims=True),
            jnp.sum(act * act, axis=-1, keepdims=True),
        ]
        p_ref[size : size + TAIL // 2] = encode(to_rows(*columns))
        p_ref[size + TAIL // 2 :] = folded
        if with_back:
            inner = nn(back[...], down[...]) * gain[...]
            columns.append(jnp.sum(inner, axis=-1, keepdims=True))
            columns.append(jnp.sum(inner * act, axis=-1, keepdims=True))
            s_ref[8 * place : 8 * place + 8, :] = to_rows(*columns)


def feed(pieces, backs, mat, gain, bias, after=()):
    size = pieces[0].shape[0]
    outs = [((2 * size, UNITS), F32)] + [((size + TAIL, D), BF16)] * 2
    if backs:
        outs += [((16, size), F32)]
    return call(
        "feed",
        partial(feed_body, bool(backs)),
        outs,
        [*pieces, *backs, mat, gain, bias],
        after=after,
    )


def feed_back_body(first_piece, *refs):
    if first_piece is not None:
        one, two, s_ref, *refs = refs
    else:
        one, two, *refs = refs
        s_ref = None
    f_ref, gain, bias, mat, df_ref, n_ref, p_one, p_two, vec_ref = refs
    up, down = mat.at[:, :UNITS], mat.at[:, UNITS:]
    size = p_one.shape[0]
    gain_grad = jnp.zeros((1, UNITS), F32)
    bias_grad = jnp.zeros((1, UNITS), F32)
    for place, (piece, p_ref) in enumerate(((one, p_one), (two, p_two))):
        rows = slice(place * size, (place + 1) * size)
        upstream = nn(piece[:size], down[...])
        pre = f_ref[rows, :]
        if first_piece is not None:
            start = 8 * (first_piece + place)
            stats = s_ref[start : start + 8, :]
        else:
            stats = decode(piece[size : size + TAIL // 2])
        columns = to_columns(stats)
        mean, scaled, first, second = (columns[:, i : i + 1] for i in range(4))
        act, spread = gelu_parts(pre)
        normal = (act - mean) * scaled
        act_grad = scaled * (upstream * gain[...] - first - normal * second)
        slope = spread + pre * (jnp.exp(-0.5 * pre * pre) * INV_SQRT_2PI)
        pre_grad = (act_grad * slope).astype(BF16)
        df_ref[rows, :] = pre_grad
        n_ref[rows, :] = (normal * gain[...] + bias[...]).astype(BF16)
        p_ref[...] = nt(pre_grad, up[...]).astype(BF16)
        gain_grad += jnp.sum(upstream * normal, axis=0, keepdims=True)
        bias_grad += jnp.sum(upstream, axis=0, keepdims=True)
    vec_ref[...] = vector_rows(gain_grad, bias_grad)


def feed_back(pieces, stats, first_piece, pre, gain, bias, mat, after=()):
    count = pre.shape[0]
    size = count // 2
    return call(
        "feed_back",
        partial(feed_back_body, first_piece if stats else None),
        [((count, UNITS), BF16)] * 2 + [((size, D), BF16)] * 2 + [((8, UNITS), F32)],
        [*pieces, *stats, pre, gain, bias, mat],
        after=after,
    )


def stats_pack_body(near, far, out):
    out[:16] = near[...]
    out[16:] = far[...]


def stats_near_body(stats, got, out):
    for place in range(4):
        other = 8 * (place ^ 1)
        out[8 * place : 8 * place + 8] = stats[8 * place : 8 * place + 8] + got[other : other + 8]


def stats_far_body(stats, got, out):
    for place in range(4):
        other = 8 * (place ^ 2)
        rows = slice(8 * place, 8 * place + 8)
        total = (stats[rows] + got[other : other + 8]) * (1.0 / FF)
        mean, one = total[0:1], total[2:3]
        scaled = lax.rsqrt(total[1:2] - mean * mean + EPS)
        two = scaled * (total[3:4] - mean * one)
        out[rows] = jnp.concatenate([mean, scaled, one, two, total[4:8]], axis=0)


def group_stats(near, far):
    shape = [((32, near.shape[1]), F32)]
    stats = call("stats_pack", stats_pack_body, shape, [near, far])[0]
    stats = call("stats_near", stats_near_body, shape, [stats, core_swap(stats)])[0]
    return call("stats_far", stats_far_body, shape, [stats, x_swap(stats)])[0]


def grads_body(pieces, halves, size, *refs):
    *refs, out = refs
    place = 0
    column = 0
    for left_count, right_count in zip(pieces, halves):
        left = refs[place : place + left_count]
        right = refs[place + left_count : place + left_count + right_count]
        place += left_count + right_count
        width = right[0].shape[1]
        per = left_count // right_count
        total = None
        for index, piece in enumerate(left):
            start = (index % per) * size
            term = tn(piece[:size], right[index // per][start : start + size, :])
            total = term if total is None else total + term
        out[:, column : column + width] = total.astype(BF16)
        column += width


def grads_of(*pairs, after=()):
    pieces = tuple(len(left) for left, _ in pairs)
    halves = tuple(len(right) for _, right in pairs)
    size = pairs[0][1][0].shape[0] // 2
    args = [item for left, right in pairs for item in (*left, *right)]
    width = sum(right[0].shape[1] for _, right in pairs)
    return call(
        "grads",
        partial(grads_body, pieces, halves, size),
        [((D, width), BF16)],
        args,
        after=after,
    )[0]


def inner_back_body(one, two, o_ref, gain, bias, mat, do_ref, u_ref, vec_ref):
    size = o_ref.shape[0] // 2
    gain_grad = jnp.zeros((1, o_ref.shape[1]), F32)
    bias_grad = jnp.zeros((1, o_ref.shape[1]), F32)
    out_mat = mat[:, QKV:]
    for place, piece in enumerate((one, two)):
        rows = slice(place * size, (place + 1) * size)
        upstream = nn(piece[:size], out_mat)
        columns = to_columns(decode(piece[size : size + TAIL // 2]))
        mean, scaled, first, second = (columns[:, i : i + 1] for i in range(4))
        normal = (o_ref[rows, :] - mean) * scaled
        back = scaled * (upstream * gain[...] - first - normal * second)
        do_ref[rows, :] = back.astype(BF16)
        u_ref[rows, :] = (normal * gain[...] + bias[...]).astype(BF16)
        gain_grad += jnp.sum(upstream * normal, axis=0, keepdims=True)
        bias_grad += jnp.sum(upstream, axis=0, keepdims=True)
    vec_ref[...] = vector_rows(gain_grad, bias_grad)


def inner_back(pieces, out, gain, bias, mat, after=()):
    count, width = out.shape
    return call(
        "inner_back",
        inner_back_body,
        [((count, width), BF16)] * 2 + [((8, width), F32)],
        [*pieces, out, gain, bias, mat],
        after=after,
    )


def encode_rows(values):
    return jnp.concatenate(split_three(values), axis=0)


def decode_rows(rows):
    rows = rows.astype(F32)
    count = rows.shape[0] // 3
    return rows[:count] + rows[count : 2 * count] + rows[2 * count :]


def unproject_body(rows, mat, one, two, gain, bias, p_one, p_two, vec_ref):
    size = p_one.shape[0]
    gain_grad = jnp.zeros((1, D), F32)
    bias_grad = jnp.zeros((1, D), F32)
    for place, (piece, p_ref) in enumerate(((one, p_one), (two, p_two))):
        term = nt(rows[place * size : (place + 1) * size], mat[:, :QKV])
        p_ref[...] = term.astype(BF16)
        gain_grad += jnp.sum(term * (piece[...].astype(F32) - bias[...]), axis=0, keepdims=True)
        bias_grad += jnp.sum(term, axis=0, keepdims=True)
    vec_ref[...] = vector_rows(gain_grad / gain[...], bias_grad)


def unproject(rows, mat, pieces, gain, bias, after=()):
    count = rows.shape[0]
    return call(
        "unproject",
        unproject_body,
        [((count // 2, D), BF16)] * 2 + [((8, D), F32)],
        [rows, mat, *pieces, gain, bias],
        after=after,
    )


def vectors_body(*refs):
    *items, out = refs
    out[...] = jnp.zeros_like(out)
    out[0:2, :] = items[0][0:2, :] + items[1][0:2, :]
    for place, item in enumerate(items[2:]):
        first = 2 * place + 2
        out[first : first + 2, : item.shape[1]] = item[0:2, :]


def vectors_of(items):
    return call("vectors", vectors_body, [((16, D), F32)], list(items))[0]


def outer_body(own, got, out):
    out[...] = own[0:8] + got[0:8]


def all_body(own, outer, got, out):
    out[0:8] = outer[...] + got[...]
    out[8:] = own[8:]


def encode_rows(values):
    return jnp.concatenate(split_three(values), axis=0)


def decode_rows(rows):
    rows = rows.astype(F32)
    count = rows.shape[0] // 3
    return rows[:count] + rows[count : 2 * count] + rows[2 * count :]


def branch_of(own, mate, far, feature_count):
    rows = own.shape[0] - TAIL
    half = rows + TAIL // 2
    pieces = (own, mate, far)
    product = sum(piece[:rows].astype(F32) for piece in pieces)
    stats = sum(decode(piece[rows:half]) for piece in pieces) / feature_count
    folded = sum(decode_vectors(piece[half:]) for piece in pieces)
    mean = stats[0:1]
    scaled = lax.rsqrt(stats[1:2] - mean * mean + EPS)
    kept = jnp.concatenate([mean, scaled, jnp.zeros((6, rows), F32)], axis=0)
    columns = to_columns(kept)
    branch = columns[:, 1:2] * (product - columns[:, 0:1] * folded[0:1])
    return branch, folded[1:2], folded[0:1], kept


def after_attend_body(x_ref, own, mate, far, gain, bias, x2_ref, z_ref, h_ref, fold_ref, kept_ref):
    branch, shift, folded, kept = branch_of(own, mate, far, D)
    mid = x_ref[...].astype(F32) + branch + shift
    x2_ref[...] = mid
    z_ref[...] = branch
    normal, _ = split_norm(mid)
    h_ref[...] = (normal * gain[...] + bias[...]).astype(BF16)
    fold_ref[...] = jnp.broadcast_to(folded, fold_ref.shape)
    kept_ref[...] = kept


def after_attend(x, pieces, gain, bias, after=()):
    rows = x.shape[0]
    return call(
        "after_attend",
        after_attend_body,
        [((rows, D), F32), ((rows, D), F32), ((rows, D), BF16), ((8, D), F32), ((8, rows), F32)],
        [x, *pieces, gain, bias],
        after=after,
    )


def mask_column(labels, rows):
    return (to_columns(labels[:, :rows])[:, 0:1] >= 0).astype(F32)


def after_feed_body(x2, own, mate, far, labels, gain, bias, y_ref, z_ref, h_ref, fold_ref, kept_ref):
    branch, shift, folded, kept = branch_of(own, mate, far, FF)
    out = (mask_column(labels, x2.shape[0]) * (x2[...] + branch + shift)).astype(BF16)
    y_ref[...] = out
    z_ref[...] = branch
    normal, _ = split_norm(out.astype(F32))
    h_ref[...] = (normal * gain[...] + bias[...]).astype(BF16)
    fold_ref[...] = jnp.broadcast_to(folded, fold_ref.shape)
    kept_ref[...] = kept


def after_feed(x2, pieces, labels, gain, bias, after=()):
    rows = x2.shape[0]
    return call(
        "after_feed",
        after_feed_body,
        [((rows, D), BF16), ((rows, D), F32), ((rows, D), BF16), ((8, D), F32), ((8, rows), F32)],
        [x2, *pieces, labels, gain, bias],
        after=after,
    )


def finish_feed_body(x2, own, mate, far, labels, y_ref):
    branch, shift, _, _ = branch_of(own, mate, far, FF)
    y_ref[...] = (mask_column(labels, x2.shape[0]) * (x2[...] + branch + shift)).astype(BF16)


def finish_feed(x2, pieces, labels):
    return call("finish_feed", finish_feed_body, [(x2.shape, BF16)], [x2, *pieces, labels])[0]


def payload_of(grad, branch, folded, kept, feature_count):
    sent = grad.astype(BF16)
    wide = sent.astype(F32)
    means = to_rows(
        jnp.sum(wide * folded, axis=-1, keepdims=True),
        jnp.sum(wide * branch, axis=-1, keepdims=True),
    )
    stats = jnp.concatenate([kept[0:2], means[0:2] / feature_count, kept[4:8]], axis=0)
    tail = jnp.concatenate([encode(stats), jnp.zeros((TAIL // 2, D), BF16)], axis=0)
    return jnp.concatenate([sent, tail], axis=0)


def feed_norm_back_body(
    own, mate, far, g_ref, labels, x2, gain, branch, folded, kept, dx_ref, out_ref, vec_ref
):
    upstream = own[...].astype(F32) + mate[...].astype(F32) + far[...].astype(F32)
    back, gain_grad, bias_grad = norm_back(x2[...], gain[...], upstream)
    total = mask_column(labels, x2.shape[0]) * g_ref[...].astype(F32) + back
    dx_ref[...] = total
    out_ref[...] = payload_of(total, branch[...], folded[0:1], kept[...], D)
    vec_ref[...] = vector_rows(gain_grad, bias_grad)


def feed_norm_back(pieces, grad, labels, x2, gain, branch, folded, kept, after=()):
    rows = x2.shape[0]
    return call(
        "feed_norm_back",
        feed_norm_back_body,
        [((rows, D), F32), ((rows + TAIL, D), BF16), ((8, D), F32)],
        [*pieces, grad, labels, x2, gain, branch, folded, kept],
        after=after,
    )


def first_norm_back_body(has_next, *refs):
    own, mate, far, dx2, x_ref, gain, *refs = refs
    upstream = own[...].astype(F32) + mate[...].astype(F32) + far[...].astype(F32)
    back, _, _ = norm_back(x_ref[...].astype(F32), gain[...], upstream)
    total = (dx2[...] + back).astype(BF16)
    if has_next:
        labels, branch, folded, kept, g_ref, out_ref = refs
        masked = mask_column(labels, dx2.shape[0]) * total.astype(F32)
        out_ref[...] = payload_of(masked, branch[...], folded[0:1], kept[...], FF)
    else:
        (g_ref,) = refs
    g_ref[...] = total


def first_norm_back(pieces, dx2, x, gain, following=(), after=()):
    rows = x.shape[0]
    outs = [((rows, D), BF16)]
    if following:
        outs.append(((rows + TAIL, D), BF16))
    return call(
        "first_norm_back",
        partial(first_norm_back_body, bool(following)),
        outs,
        [*pieces, dx2, x, gain, *following],
        after=after,
    )


def in_hbm(x):
    return pltpu.with_memory_space_constraint(x, pltpu.HBM)


def fetch_all(refs, held, sems):
    copies = [
        pltpu.make_async_copy(ref, spot, sems.at[place])
        for place, (ref, spot) in enumerate(zip(refs, held))
    ]
    for copy in copies:
        copy.start()
    for copy in copies:
        copy.wait()


def first_block_body(
    flags, query, key, value, output, down, up, out, down_out, swap_out, *scratch
):
    *held, sems = scratch
    fetch_all((query, key, value, output, down, up), held, sems)
    width = query.shape[1]
    for place, ref in enumerate(held[:3]):
        out[:, place * width : (place + 1) * width] = ref[...]
    out[:, 3 * width :] = held[3][...].T
    down_out[...] = held[4][...].T
    lower = jnp.full((1, D), flags[2], jnp.int32) == 0
    swap_out[:, :D] = jnp.where(lower, down_out[...], held[5][...])
    swap_out[:, D:] = out[:, : D // 2]


def first_block(flags, *blocks):
    return pl.pallas_call(
        first_block_body,
        out_shape=tuple(
            jax.ShapeDtypeStruct((blocks[0].shape[0], width), BF16)
            for width in (D, D, 3 * D // 2)
        ),
        in_specs=[SMEM] + [HBM] * 6,
        out_specs=(VMEM,) * 3,
        scratch_shapes=[pltpu.VMEM(block.shape, BF16) for block in blocks]
        + [pltpu.SemaphoreType.DMA((6,))],
        compiler_params=PARAMS,
        name="first_block",
    )(flags, *map(in_hbm, blocks))


def beside_body(one, two, out):
    width = one.shape[1]
    out[:, :width] = one[...]
    out[:, width:] = two[...]


def beside(one, two, after=()):
    rows, width = one.shape
    return call("beside", beside_body, [((rows, 2 * width), BF16)], [one, two], after=after)[0]


def entry_body(flags, inputs, cotangent, out, far_out, own_in, own_grad, sems):
    size = own_in.shape[0]

    def rows_of(micro):
        return pl.ds(pl.multiple_of(micro * size, size), size)

    across, far, own = rows_of(1 - flags[3]), rows_of(flags[2]), rows_of(flags[3])
    copies = [
        pltpu.make_async_copy(source, target, sems.at[place])
        for place, (source, target) in enumerate(
            (
                (inputs.at[across], out.at[:size]),
                (cotangent.at[across], out.at[size:]),
                (inputs.at[far], far_out.at[:size]),
                (cotangent.at[far], far_out.at[size:]),
                (inputs.at[own], own_in),
                (cotangent.at[own], own_grad),
            )
        )
    ]
    for copy in copies:
        copy.start()
    for copy in copies:
        copy.wait()


def entry(flags, inputs, cotangent):
    rows = inputs.shape[0]
    shapes = [rows, rows, rows // 2, rows // 2]
    return pl.pallas_call(
        entry_body,
        out_shape=tuple(jax.ShapeDtypeStruct((count, D), BF16) for count in shapes),
        in_specs=[SMEM, HBM, HBM],
        out_specs=(VMEM,) * 4,
        scratch_shapes=[pltpu.SemaphoreType.DMA((6,))],
        compiler_params=PARAMS,
        name="entry",
    )(flags, in_hbm(inputs), in_hbm(cotangent))


def enter_body(
    flags, own_in, own_grad, got, labels, gain, bias, x_ref, g_ref, top_ref, h_ref
):
    size, width = x_ref.shape
    here = jnp.full((1, width), flags[0], jnp.int32) == 1
    own = jnp.where(here, own_in[...], got[:size])
    grad = jnp.where(here, own_grad[...], got[size:])
    x_ref[...] = own
    g_ref[...] = grad
    top_ref[...] = (mask_column(labels, size) * grad.astype(F32)).astype(BF16)
    normal, _ = split_norm(own.astype(F32))
    h_ref[...] = (normal * gain[...] + bias[...]).astype(BF16)


def enter(flags, own_in, own_grad, got, labels, gain, bias):
    return call(
        "enter",
        enter_body,
        [(own_in.shape, BF16)] * 4,
        [flags, own_in, own_grad, got, labels, gain, bias],
    )


def enter_far_body(got, labels, gain, bias, top_ref, h_ref):
    size = top_ref.shape[0]
    mask = (to_columns(labels[:, 2 * size : 3 * size])[:, 0:1] >= 0).astype(F32)
    top_ref[...] = (mask * got[size:].astype(F32)).astype(BF16)
    normal, _ = split_norm(got[:size].astype(F32))
    h_ref[...] = (normal * gain[...] + bias[...]).astype(BF16)


def enter_far(got, labels, gain, bias):
    rows = got.shape[0] // 2
    return call(
        "enter_far", enter_far_body, [((rows, D), BF16)] * 2, [got, labels, gain, bias]
    )


def pack_body(*refs):
    *items, out = refs
    size = items[0].shape[0]
    for place, item in enumerate(items):
        out[place * size : (place + 1) * size, :] = item[...]


def pack(items):
    rows, width = items[0].shape
    return call("pack", pack_body, [((len(items) * rows, width), BF16)], list(items))[0]


def unpack_body(flags, own, sent, got_own, got_sent, y_ref, g_ref):
    size = y_ref.shape[0] // 2
    width = y_ref.shape[1]
    here = jnp.full((1, width), flags[0], jnp.int32) == 1
    rows = pl.ds(pl.multiple_of(flags[2] * size, size), size)
    first = pl.ds(pl.multiple_of(flags[3] * size, size), size)
    second = pl.ds(pl.multiple_of((1 - flags[3]) * size, size), size)
    last = slice(2 * size, 3 * size)
    y_ref[first, :] = jnp.where(here, own[rows, :], got_own[rows, :])
    y_ref[second, :] = jnp.where(here, sent[rows, :], got_sent[rows, :])
    g_ref[first, :] = jnp.where(here, own[last, :], got_own[last, :])
    g_ref[second, :] = jnp.where(here, sent[last, :], got_sent[last, :])


def unpack(flags, own, sent, got_own, got_sent):
    rows = 2 * own.shape[0] // 3
    return call(
        "unpack",
        unpack_body,
        [((rows, own.shape[1]), BF16)] * 2,
        [flags, own, sent, got_own, got_sent],
    )


def halve_body(with_vectors, flags, block, across, *refs):
    if with_vectors:
        vectors, got, kept, sent, vec_ref = refs
        total = vectors[...] + got[...]
        vec_ref[...] = total
    else:
        kept, sent = refs
    size = kept.shape[0] // 2
    for place, (out, step) in enumerate(((kept, 0), (kept, 2), (sent, 1), (sent, 3))):
        rows = pl.ds(pl.multiple_of((flags[1] ^ step) * size, size), size)
        spot = slice((place % 2) * size, (place % 2 + 1) * size)
        out[spot] = (block[rows, :].astype(F32) + across[rows, :].astype(F32)).astype(BF16)
    if with_vectors:
        sent[2 * size :] = encode_rows(total)


def halve(flags, block, across, vectors=(), after=(), cost=None):
    rows, width = block.shape
    outs = [((rows // 2, width), BF16)] * 2
    if vectors:
        outs = [outs[0], ((rows // 2 + 48, width), BF16), (vectors[0].shape, F32)]
    return call(
        "halve",
        partial(halve_body, bool(vectors)),
        outs,
        [flags, block, across, *vectors],
        after=after,
        cost=cost,
    )


def quarter_body(with_vectors, kept, got, *refs):
    if with_vectors:
        vectors, own, sent, vec_ref = refs
    else:
        own, sent = refs
    size = own.shape[0]
    for place, out in enumerate((own, sent)):
        rows = slice(place * size, (place + 1) * size)
        out[:size] = (kept[rows].astype(F32) + got[rows].astype(F32)).astype(BF16)
    if with_vectors:
        total = vectors[...] + decode_rows(got[2 * size :])
        vec_ref[...] = total
        sent[size:] = encode_rows(total)


def quarter(kept, got, vectors=(), after=()):
    rows, width = kept.shape
    outs = [((rows // 2, width), BF16)] * 2
    if vectors:
        outs = [outs[0], ((rows // 2 + 48, width), BF16), (vectors[0].shape, F32)]
    return call(
        "quarter",
        partial(quarter_body, bool(vectors)),
        outs,
        [kept, got, *vectors],
        after=after,
    )


def last_body(kept, got, vectors, out, vec_ref):
    size = kept.shape[0]
    out[...] = (kept[...].astype(F32) + got[:size].astype(F32)).astype(BF16)
    vec_ref[...] = vectors[...] + decode_rows(got[size:])


def last_of(kept, got, vectors, after=()):
    outs = [(kept.shape, BF16), (vectors.shape, F32)]
    return call("last", last_body, outs, [kept, got, vectors], after=after)


def total_body(*refs):
    *parts, out = refs
    out[...] = sum(part[...].astype(F32) for part in parts).astype(out.dtype)


def total_of(parts, kind=BF16, after=(), cost=None):
    shape = [(parts[0].shape, kind)]
    return call("total", total_body, shape, list(parts), after=after, cost=cost)[0]


def layers_of(flags, lower, lower_got, upper, upper_got):
    width = lower.shape[1]
    here = jnp.full((1, width), flags[0], jnp.int32) == 1
    first = jnp.full((1, width), flags[2], jnp.int32) == 0
    one = jnp.where(here, lower[...], lower_got[...])
    two = jnp.where(here, upper[...], upper_got[...])
    return jnp.where(first, one, two).astype(F32)


def final_first_body(
    flags, lower, lower_got, upper, upper_got, vec, vec_got, q_ref, k_ref, v_ref, o_ref, vec_ref
):
    width = q_ref.shape[1]
    total = layers_of(flags, lower, lower_got, upper, upper_got)
    for place, ref in enumerate((q_ref, k_ref, v_ref)):
        ref[...] = total[:, place * width : (place + 1) * width]
    o_ref[...] = total[:, 3 * width :].T
    here = jnp.full((1, D), flags[0], jnp.int32) == 1
    vec_ref[...] = jnp.where(here, vec[...], vec_got[...])


def final_first(flags, lower, upper, vectors):
    rows, width = lower[0].shape[0], D // LANES
    return call(
        "final_first",
        final_first_body,
        [((rows, width), F32)] * 3 + [((width, rows), F32), ((16, D), F32)],
        [flags, *lower, *upper, *vectors],
    )


def final_second_body(flags, lower, lower_got, upper, upper_got, up_ref, down_ref):
    total = layers_of(flags, lower, lower_got, upper, upper_got)
    up_ref[...] = total[:, :UNITS]
    down_ref[...] = total[:, UNITS:].T


def final_second(flags, lower, upper):
    rows = lower[0].shape[0]
    return call(
        "final_second",
        final_second_body,
        [((rows, UNITS), F32), ((UNITS, rows), F32)],
        [flags, *lower, *upper],
    )


def merge_body(flags, one, two, upper, out):
    size, width = one.shape
    first = jnp.full((1, width), flags[2], jnp.int32) == 0
    for place, ref in enumerate((one, two)):
        rows = slice(place * size, (place + 1) * size)
        out[rows] = jnp.where(first, ref[...], upper[rows])


def merge(flags, one, two, upper):
    return call("merge", merge_body, [(upper.shape, BF16)], [flags, one, two, upper])[0]


def choose_body(flags, one, two, out):
    first = jnp.full((1, out.shape[1]), flags[2], jnp.int32) == 0
    out[...] = jnp.where(first, one[...], two[...])


def choose(flags, one, two, after=()):
    return call("choose", choose_body, [(one.shape, one.dtype)], [flags, one, two], after=after)[0]


def join_body(flags, own, got, out):
    half = own.shape[1]
    first = jnp.full((1, half), flags[2], jnp.int32) == 0
    out[:, :half] = jnp.where(first, own[...], got[...])
    out[:, half:] = jnp.where(first, got[...], own[...])


def join(flags, own, got, after=()):
    rows, half = own.shape
    return call(
        "join", join_body, [((rows, 2 * half), BF16)], [flags, own, got], after=after
    )[0]


def hold_body(ref, out):
    out[...] = ref[...]


def hold(x, after):
    return call("hold", hold_body, [(x.shape, x.dtype)], [x], after=after)[0]


def assemble_body(count, flags, *refs):
    beside, across, out = refs[:count], refs[count:-1], refs[-1]
    size = beside[0].shape[0]
    width = out.shape[1]
    near = jnp.full((1, width), flags[0], jnp.int32) == 1
    for step in range(count):
        rows = pl.ds(pl.multiple_of((flags[1] ^ step) * size, size), size)
        out[rows, :] = jnp.where(near, beside[step][...], across[step][...])


def assemble(flags, beside, across, after=()):
    count, (size, width) = len(beside), beside[0].shape
    return call(
        "assemble",
        partial(assemble_body, count),
        [((count * size, width), BF16)],
        [flags, *beside, *across],
        after=after,
    )[0]


def early_block_body(flags, up, got, first, out):
    width = up.shape[1]
    lower = jnp.full((1, width), flags[2], jnp.int32) == 0
    out[:, :width] = jnp.where(lower, up[...], got[:, :width])
    half = first.shape[1] // 2
    lower = jnp.full((1, half), flags[2], jnp.int32) == 0
    out[:, width:] = jnp.where(lower, got[:, width:], first[:, half:])


def early_block(flags, up, got, first, after=()):
    rows, width = up.shape
    return call(
        "early_block",
        early_block_body,
        [((rows, width + first.shape[1] // 2), BF16)],
        [flags, up, got, first],
        after=after,
    )[0]


def late_block_body(flags, got, down, out):
    width = down.shape[1]
    lower = jnp.full((1, width), flags[2], jnp.int32) == 0
    out[...] = jnp.where(lower, got[:, :width], down[...])


def late_block(flags, got, down, after=()):
    return call(
        "late_block", late_block_body, [(down.shape, BF16)], [flags, got, down], after=after
    )[0]


def parts_body(ref, one, two):
    width = one.shape[1]
    one[...] = ref[:, :width]
    two[...] = ref[:, width:]


def parts_of(x, width, after):
    rows, whole = x.shape
    shapes = [((rows, width), x.dtype), ((rows, whole - width), x.dtype)]
    return call("parts", parts_body, shapes, [x], after=after)


def pick_body(flags, beside, across, out):
    near = jnp.full((1, out.shape[1]), flags[0], jnp.int32) == 1
    out[...] = jnp.where(near, beside[...], across[...])


def pick(flags, beside, across, cost=None):
    return call(
        "pick", pick_body, [(beside.shape, BF16)], [flags, beside, across], cost=cost
    )[0]


def on_device(
    inputs,
    cotangent,
    doc_ids,
    norm_gain,
    norm_bias,
    w_query,
    w_key,
    w_value,
    inner_gain,
    inner_bias,
    w_output,
    feed_gain,
    feed_bias,
    w_up,
    middle_gain,
    middle_bias,
    w_down,
):
    core = lax.axis_index("section")
    lane = lax.axis_index("mp")
    lane_x = lane % 2
    lane_y = lane // 2
    count = lax.axis_size("dp")
    slice_len = inputs.shape[0] // MICRO
    rank = 2 * core + lane_x
    crossing = [(s * 4 + r, s * 4 + (r ^ 2)) for s in range(2) for r in range(4) if s == r // 2]
    returning = [(s * 4 + r, s * 4 + (r ^ 2)) for s in range(2) for r in range(4) if s != r // 2]

    def by_core(first, second):
        return jnp.where(core == 0, first, second)

    def placed(array, layer):
        return [
            lax.ppermute(
                array,
                BOTH,
                [(s * 4 + 2 * m + x, layer * 4 + 2 * s + x) for s in range(2) for x in range(2)],
            )
            for m in range(MICRO)
        ]

    label_grid = lax.dynamic_index_in_dim(
        doc_ids.reshape(LANES, MICRO, slice_len), lane_y, 1, keepdims=False
    )
    order = (rank, 2 * (1 - core) + lane_x, rank ^ 1, 2 * (1 - core) + (1 - lane_x))
    labels = jnp.concatenate(
        [lax.dynamic_index_in_dim(label_grid, item, 0, keepdims=False) for item in order]
    )
    labels = jnp.broadcast_to(labels.astype(F32)[None], (8, LANES * slice_len))

    place = lax.axis_index("dp")
    flags = jnp.stack([core == lane_y, place, core, lane_y]).astype(jnp.int32)

    def line_pairs(step):
        return [
            ((r // 2 * count + i) * LANES + r, (r // 2 * count + (i ^ step)) * LANES + r)
            for i in range(count)
            for r in range(LANES)
        ]

    def along_line(block, step):
        return lax.ppermute(block, ("section", "dp", "mp"), line_pairs(step))

    first, down_block, swapped = first_block(
        flags, w_query[0], w_key[0], w_value[0], w_output[0], w_down[0], w_up[0]
    )
    up_block = w_up[0]

    def along_dp(block):
        return lax.all_gather(block, "dp", axis=0, tiled=True)

    def fetched(line, hook=()):
        whole = join(flags, line, core_swap(line), after=hook)
        return whole, lax.ppermute(whole, BOTH, crossing)

    outer_own = jnp.concatenate([norm_gain, norm_bias, feed_gain, feed_bias], axis=0)
    outer_other = core_swap(outer_own)
    split_own = jnp.concatenate([inner_gain, inner_bias, middle_gain, middle_bias], axis=1)
    split_far = y_swap(split_own)
    split_kept = jnp.where(lane_y == core, split_own, split_far)
    split_other = core_swap(jnp.where(lane_y == core, split_far, split_own))

    def small_of(outer, split):
        width = D // LANES
        return (
            [outer[i : i + 1] for i in range(4)],
            [
                split[:, :width],
                split[:, width : 2 * width],
                split[:, 2 * width : 2 * width + UNITS],
                split[:, 2 * width + UNITS :],
            ],
        )

    lower_outer, lower_split = small_of(
        by_core(outer_own, outer_other), by_core(split_kept, split_other)
    )
    upper_outer, upper_split = small_of(
        by_core(outer_other, outer_own), by_core(split_other, split_kept)
    )

    def gather_around(own, near_of, far=None, after=()):
        if far is None:
            far = x_swap(own)
        mate = core_swap(own)
        near = near_of([own, mate])
        far = hold(far, after=[near[0], *after])
        return (own, mate, far, core_swap(far)), near

    def attention(x, h, first, outer, split, hooks, far=None):
        pieces, (near,) = gather_around(
            h, lambda rows: [project(*rows, first)], far, after=hooks[2]
        )
        far = project(pieces[2], pieces[3], first)
        half = 2 * slice_len
        o_far, p_far, p_far_mate, sum_far = attend(
            half, far, near, far, labels, first, split[0], split[1]
        )
        sent = pair_sum(p_far, p_far_mate)
        hooks[0](p_far)
        o_near, p_own, p_mate, sum_near = attend(
            0, near, near, far, labels, first, split[0], split[1], after=[sent]
        )
        arrived = hold(x_swap(sent), after=[p_own])
        terms = (p_own, core_swap(p_mate), arrived)
        x2, branch, h2, folded, kept = after_attend(x, terms, outer[2], outer[3], after=hooks[1])
        state = (pieces, near, far, o_near, o_far, sum_near, sum_far, x, x2, branch, folded, kept)
        return x2, h2, state, arrived

    def attention_back(grad, sums, state, first, outer, split, following, hooks):
        pieces, near, far, o_near, o_far, sum_near, sum_far, x, x2, branch, folded, kept = state
        dx2, sent, feed_vec = feed_norm_back(
            sums, grad, labels, x2, outer[2], branch, folded, kept, after=hooks[0]
        )
        block = hooks[3](sent)
        backs, (do_near, u_near, vec_near) = gather_around(
            sent, lambda rows: inner_back(rows, o_near, split[0], split[1], first), after=block
        )
        do_far, u_far, vec_far = inner_back(backs[2:], o_far, split[0], split[1], first)
        dq_near, dq_far = attend_back(
            near, far, do_near, do_far, sum_near, sum_far, labels, after=hooks[1]
        )
        norm = (outer[0], outer[1])
        p_far, p_far_mate, norm_far = unproject(
            dq_far, first, pieces[2:], *norm, after=hooks[4](dq_far)
        )
        sent = pair_sum(p_far, p_far_mate)
        p_own, p_mate, norm_near = unproject(
            dq_near, first, pieces[:2], *norm, after=[sent, *hooks[5]()]
        )
        mat_grad = grads_of(
            (pieces, (dq_near, dq_far)), (backs, (u_near, u_far)), after=[sent]
        )
        terms = (p_own, core_swap(p_mate), hold(x_swap(sent), after=[p_own, mat_grad]))
        result = first_norm_back(
            terms, dx2, x, outer[0], following, after=hooks[2](mat_grad)
        )
        return result, vec_near + vec_far, feed_vec, (norm_near, norm_far)

    def reduce_across(block):
        across = lax.ppermute(block, BOTH, returning)
        if count != 4:
            total = total_of([block, across])
            return [lax.psum_scatter(total, "dp", scatter_dimension=0, tiled=True)]
        return block, across

    def reduce_near(pair, after=(), cost=None):
        if count != 4:
            return pair
        kept, sent = halve(flags, *pair, after=after, cost=cost)
        return kept, along_line(sent, 1)

    def reduce_far(pair, after=()):
        if count != 4:
            return pair
        kept, sent = quarter(*pair, after=after)
        return kept, along_line(sent, 2)

    def reduce_end(pair, after=(), cost=None):
        total = total_of(pair, after=after, cost=cost) if count == 4 else pair[0]
        return total, core_swap(total)

    sent, far_sent, own_in, own_grad = entry(flags, inputs, cotangent)
    got = lax.ppermute(sent, BOTH, crossing)
    far_got = lax.ppermute(
        far_sent,
        BOTH,
        [
            (s * LANES + r, s * LANES + (r ^ 1) if s == r // 2 else (r // 2) * LANES + (r ^ 3))
            for s in range(2)
            for r in range(LANES)
        ],
    )
    lower_in, upstream, masked, h = enter(
        flags, own_in, own_grad, got, labels, lower_outer[0], lower_outer[1]
    )
    masked_far, far = enter_far(far_got, labels, lower_outer[0], lower_outer[1])
    top = (masked, core_swap(masked), masked_far, core_swap(masked_far))
    moved = choose(flags, first, core_swap(first))
    if count == 4:
        pieces = [moved] + [along_line(moved, step) for step in range(1, count)]
        lower_first = assemble(
            flags, pieces, [lax.ppermute(piece, BOTH, crossing) for piece in pieces], after=[far]
        )
    else:
        pieces = [along_dp(moved)]
        lower_first = pick(flags, pieces[0], lax.ppermute(pieces[0], BOTH, crossing))
    got = core_swap(swapped)
    early_line = along_dp(early_block(flags, up_block, got, first, after=pieces[-1:]))
    late_line = along_dp(late_block(flags, got, down_block))
    coming = {}

    def early_matrices(last):
        coming["second"], coming["first"] = parts_of(early_line, UNITS, [last])

    x2, h2, lower_state, arrived = attention(
        lower_in, h, lower_first, lower_outer, lower_split, (early_matrices, (), ()), far
    )
    lower_second_whole, lower_second_across = fetched(coming["second"])
    lower_second = pick(flags, lower_second_whole, lower_second_across)
    upper_first_whole, upper_first_across = fetched(coming["first"], [h2])
    upper_first = pick(flags, upper_first_whole, upper_first_across)
    lower_pieces, (f_near, p_own, p_mate) = gather_around(
        h2, lambda rows: feed(rows, (), lower_second, *lower_split[2:])
    )
    f_far, p_far, p_far_mate = feed(lower_pieces[2:], (), lower_second, *lower_split[2:])
    lower_pre = (f_near, f_far)
    sent = pair_sum(p_far, p_far_mate)
    upper_second_whole, upper_second_across = fetched(hold(late_line, after=[sent]))
    upper_second = pick(flags, upper_second_whole, upper_second_across, work(1e10, 1))
    arrived = hold(x_swap(sent), after=[upper_second_whole])
    terms = (p_own, core_swap(p_mate), arrived)
    lower_out, lower_branch, h, lower_folded, lower_kept = after_feed(
        x2, terms, labels, upper_outer[0], upper_outer[1]
    )
    x2, h2, upper_state, _ = attention(
        lower_out,
        h,
        upper_first,
        upper_outer,
        upper_split,
        (lambda last: None, (), [upper_second_whole]),
    )
    upper_pieces, (f_near, p_own, p_mate, near_stats) = gather_around(
        h2, lambda rows: feed(rows, top[:2], upper_second, *upper_split[2:])
    )
    f_far, p_far, p_far_mate, far_stats = feed(
        upper_pieces[2:], top[2:], upper_second, *upper_split[2:]
    )
    upper_pre = (f_near, f_far)

    stats = group_stats(near_stats, far_stats)
    df_far, n_far, q_far, q_far_mate, vec_far = feed_back(
        top[2:], [stats], 2, upper_pre[1], *upper_split[2:], upper_second
    )
    sent = pair_sum(q_far, q_far_mate)
    df_near, n_near, q_own, q_mate, vec_near = feed_back(
        top[:2], [stats], 0, upper_pre[0], *upper_split[2:], upper_second, after=[sent]
    )
    upper_middle = vec_near + vec_far
    sums = (q_own, core_swap(q_mate), hold(x_swap(sent), after=[q_own]))
    ended = pair_sum(p_far, p_far_mate)
    ended_far = []

    def ended_hook(last):
        ended_far.append(hold(x_swap(ended), after=[last]))
        return ended_far

    following = (labels, lower_branch, lower_folded, lower_kept)
    pairs = {}

    def upper_second_grads(after):
        block = grads_of(
            (upper_pieces, (df_near, df_far)), (top, (n_near, n_far)), after=[after]
        )
        pairs["second"] = reduce_near(reduce_across(block), cost=work(9e9, 1))
        return [block]

    def upper_hook(item):
        pairs["upper"] = reduce_across(item)
        return [item]

    (upper_grad, sent), upper_inner, upper_feed, upper_norm = attention_back(
        upstream,
        sums,
        upper_state,
        upper_first,
        upper_outer,
        upper_split,
        following,
        ((), [ended], upper_hook, upper_second_grads, ended_hook, lambda: ()),
    )

    upper_out = finish_feed(x2, (p_own, core_swap(p_mate), ended_far[0]), labels)
    own = pack([lower_out, upper_out, upper_grad])
    swapped = lax.ppermute(own, BOTH, returning)
    upper_second_pair = reduce_far(pairs["second"], [own])
    upper_first_pair = reduce_near(pairs["upper"])
    backs, (df_near, n_near, q_own, q_mate, vec_near) = gather_around(
        sent,
        lambda rows: feed_back(
            rows, (), 0, lower_pre[0], *lower_split[2:], lower_second, after=[own]
        ),
        after=upper_first_pair[:1],
    )
    df_far, n_far, q_far, q_far_mate, vec_far = feed_back(
        backs[2:],
        (),
        2,
        lower_pre[1],
        *lower_split[2:],
        lower_second,
        after=[upper_second_pair[0]],
    )
    lower_middle = vec_near + vec_far
    sent = pair_sum(q_far, q_far_mate)
    sums = (q_own, core_swap(q_mate), x_swap(sent))

    def lower_second_grads(after):
        block = grads_of(
            (lower_pieces, (df_near, df_far)), (backs, (n_near, n_far)), after=[after]
        )
        pairs["second"] = reduce_across(block)
        return [block]

    upper_first_pair = reduce_far(upper_first_pair, after=[q_far])

    layer_outputs, upper_held = unpack(
        flags, own, swapped, core_swap(own), core_swap(swapped)
    )

    def lower_hook(item):
        pairs["lower"] = reduce_across(item)
        pairs["second"] = reduce_far(reduce_near(pairs["second"], after=[item]))
        return [item]

    def upper_ended(last):
        pairs["ended"] = reduce_end(upper_second_pair, after=[last])
        pairs["first"] = reduce_end(upper_first_pair, after=[last])
        return pairs["ended"][:1]

    (lower_grad,), lower_inner, lower_feed, lower_norm = attention_back(
        upper_grad,
        sums,
        lower_state,
        lower_first,
        lower_outer,
        lower_split,
        (),
        (
            [upper_first_pair[0]],
            [layer_outputs],
            lower_hook,
            lower_second_grads,
            upper_ended,
            lambda: (),
        ),
    )
    vectors = vectors_of(
        [*lower_norm, lower_feed, upper_norm[0] + upper_norm[1], upper_feed]
        + [lower_middle, upper_middle, lower_inner, upper_inner]
    )
    outer = call("outer", outer_body, [((8, D), F32)], [vectors, core_swap(vectors)])[0]
    vectors = call("all", all_body, [((16, D), F32)], [vectors, outer, x_swap(outer)])[0]
    lower_second_pair = pairs["second"]
    lower_held = placed(lower_grad, 0)
    input_grads = merge(flags, *lower_held, upper_held)
    lower_second_sum = reduce_end(lower_second_pair)
    grad_up, grad_down = final_second(flags, lower_second_sum, pairs["ended"])
    if count == 4:
        kept, sent, vectors = halve(
            flags,
            *pairs["lower"],
            (vectors, y_swap(vectors)),
            after=[lower_second_pair[0], lower_grad, pairs["first"][0]],
        )
        kept, sent, vectors = quarter(kept, along_line(sent, 1), [vectors])
        ended, vectors = last_of(
            kept, along_line(sent, 2), vectors, after=[input_grads, grad_up]
        )
    else:
        vectors = lax.psum(vectors + y_swap(vectors), "dp")
        ended = pairs["lower"][0]
    grad_query, grad_key, grad_value, grad_output, vectors = final_first(
        flags, (ended, core_swap(ended)), pairs["first"], (vectors, core_swap(vectors))
    )

    def part(rows, start, size):
        rows = lax.dynamic_slice(rows, (core * rows.shape[0] // 2, start), (rows.shape[0] // 2, size))
        return [rows[i : i + 1] for i in range(rows.shape[0])]

    width = D // LANES
    size = D // count // LANES
    outer = part(vectors[:8], (place * LANES + lane) * size, size)
    middle = part(vectors[8:12], place * (UNITS // count), UNITS // count)
    inner = part(vectors[12:], place * (width // count), width // count)
    return (
        layer_outputs[None],
        input_grads[None],
        outer[0],
        outer[1],
        grad_query[None],
        grad_key[None],
        grad_value[None],
        inner[0],
        inner[1],
        grad_output[None],
        outer[2],
        outer[3],
        grad_up[None],
        middle[0],
        middle[1],
        grad_down[None],
    )


def solution(mesh):
    placed = (
        P(("dp", "mp"), None),
        P(("dp", "mp"), None),
        P("dp"),
        P("section", None),
        P("section", None),
        P("section", "dp", "mp"),
        P("section", "dp", "mp"),
        P("section", "dp", "mp"),
        P("section", "mp"),
        P("section", "mp"),
        P("section", "mp", "dp"),
        P("section", None),
        P("section", None),
        P("section", "dp", "mp"),
        P("section", "mp"),
        P("section", "mp"),
        P("section", "mp", "dp"),
    )
    return jax.shard_map(
        on_device,
        mesh=mesh,
        in_specs=placed,
        out_specs=(
            P("section", ("dp", "mp"), None),
            P("section", ("dp", "mp"), None),
            P("section", ("dp", "mp")),
            P("section", ("dp", "mp")),
            P("section", "dp", "mp"),
            P("section", "dp", "mp"),
            P("section", "dp", "mp"),
            P("section", ("mp", "dp")),
            P("section", ("mp", "dp")),
            P("section", "mp", "dp"),
            P("section", ("dp", "mp")),
            P("section", ("dp", "mp")),
            P("section", "dp", "mp"),
            P("section", ("mp", "dp")),
            P("section", ("mp", "dp")),
            P("section", "mp", "dp"),
        ),
        check_vma=False,
    )
```

```python
from functools import partial

import jax
import jax.numpy as jnp
from jax import lax
from jax.experimental import pallas as pl
from jax.experimental.pallas import tpu as pltpu
from jax.sharding import PartitionSpec as P

D = 768
HEAD_DIM = 64
FF = 3072
MICRO = 2
LANES = 4
EPS = 1e-05
SCALE = HEAD_DIM ** (-0.5)
LOG2E = 1.4426950408889634
SQRT_HALF = 0.7071067811865476
INV_SQRT_2PI = 0.3989422804014327
BOTH = ("section", "mp")
Y_PAIRS = [[0, 2], [1, 3]]
QKV = 3 * D // LANES
UNITS = FF // LANES
TAIL = 16
F32 = jnp.float32
BF16 = jnp.bfloat16

VMEM = pl.BlockSpec(memory_space=pltpu.VMEM)
SMEM = pl.BlockSpec(memory_space=pltpu.SMEM)
ANY = pl.BlockSpec(memory_space=pl.ANY)
HBM = pl.BlockSpec(memory_space=pltpu.HBM)
PARAMS = pltpu.CompilerParams(vmem_limit_bytes=16 * 1024 * 1024)


def call(name, body, outs, ins, scratch=(), after=(), cost=None):
    count = len(ins)

    def kernel(*refs):
        body(*refs[:count], *refs[count + len(after) :])

    return pl.pallas_call(
        kernel,
        out_shape=tuple(jax.ShapeDtypeStruct(shape, kind) for shape, kind in outs),
        in_specs=[SMEM if item.ndim == 1 else VMEM for item in ins] + [ANY] * len(after),
        out_specs=(VMEM,) * len(outs),
        scratch_shapes=list(scratch),
        compiler_params=PARAMS,
        name=name,
        cost_estimate=cost or work(1, 1),
    )(*ins, *after)


def work(flops, size):
    return pl.CostEstimate(flops=int(flops), bytes_accessed=int(size), transcendentals=0)


def nn(a, b):
    return jnp.dot(a, b, preferred_element_type=F32)


def nt(a, b):
    return lax.dot_general(a, b, (((1,), (1,)), ((), ())), preferred_element_type=F32)


def tn(a, b):
    return lax.dot_general(a, b, (((0,), (0,)), ((), ())), preferred_element_type=F32)


def to_rows(*columns):
    count = columns[0].shape[0]
    lane = lax.broadcasted_iota(jnp.int32, (count, 128), 1)
    tile = jnp.zeros((count, 128), F32)
    for place, column in enumerate(columns):
        tile = jnp.where(lane == place, column, tile)
    return tile.T[:8]


def to_columns(rows):
    return jnp.concatenate([rows, jnp.zeros((120, rows.shape[1]), F32)], axis=0).T


def split_three(values):
    high = values.astype(BF16)
    rest = values - high.astype(F32)
    middle = rest.astype(BF16)
    return high, middle, (rest - middle.astype(F32)).astype(BF16)


def encode(rows):
    return jnp.concatenate(split_three(rows), axis=1)


def decode(tail):
    tail = tail.astype(F32)
    count = tail.shape[1] // 3
    return tail[:, :count] + tail[:, count : 2 * count] + tail[:, 2 * count :]


def decode_vectors(tail):
    tail = tail.astype(F32)
    return jnp.concatenate(
        [jnp.sum(tail[0:3], axis=0, keepdims=True), jnp.sum(tail[3:6], axis=0, keepdims=True)],
        axis=0,
    )


def encode_vectors(first, second):
    return jnp.concatenate(
        [*split_three(first), *split_three(second), jnp.zeros((2, first.shape[1]), BF16)], axis=0
    )


def split_norm(values):
    mean = jnp.mean(values, axis=-1, keepdims=True)
    spread = jnp.mean(values * values, axis=-1, keepdims=True) - mean * mean
    scaled = lax.rsqrt(spread + EPS)
    return (values - mean) * scaled, scaled


def norm_back(values, gain, upstream):
    normal, scaled = split_norm(values)
    inner = upstream * gain
    one = jnp.mean(inner, axis=-1, keepdims=True)
    two = jnp.mean(inner * normal, axis=-1, keepdims=True)
    back = scaled * (inner - one - normal * two)
    return (
        back,
        jnp.sum(upstream * normal, axis=0, keepdims=True),
        jnp.sum(upstream, axis=0, keepdims=True),
    )


def vector_rows(first, second):
    return jnp.concatenate([first, second, jnp.zeros((6, first.shape[1]), F32)], axis=0)


def folded_vectors(mat, gain, bias):
    rows = jnp.concatenate(
        [*split_three(gain), *split_three(bias), jnp.zeros((10, gain.shape[1]), BF16)], axis=0
    )
    folded = nt(rows, mat)
    return encode_vectors(
        jnp.sum(folded[0:3], axis=0, keepdims=True), jnp.sum(folded[3:6], axis=0, keepdims=True)
    )


def core_swap(x):
    return lax.ppermute(x, "section", [(0, 1), (1, 0)])


def x_swap(x):
    return lax.ppermute(x, "mp", [(i, i ^ 1) for i in range(LANES)])


def y_swap(x):
    return lax.ppermute(x, "mp", [(i, i ^ 2) for i in range(LANES)])


def gather_rows(own):
    far = x_swap(own)
    return own, core_swap(own), far, core_swap(far)


def pair_sum_body(first, second, out):
    rows = out.shape[0] - TAIL
    out[:rows] = (first[:rows].astype(F32) + second[:rows].astype(F32)).astype(BF16)
    half = rows + TAIL // 2
    out[rows:half] = encode(decode(first[rows:half]) + decode(second[rows:half]))
    folded = decode_vectors(first[half:]) + decode_vectors(second[half:])
    out[half:] = encode_vectors(folded[0:1], folded[1:2])


def pair_add_body(first, second, out):
    out[...] = (first[...].astype(F32) + second[...].astype(F32)).astype(BF16)


def pair_sum(far, far_mate):
    body = pair_sum_body if far.shape[0] % 256 else pair_add_body
    return call("pair_sum", body, [(far.shape, BF16)], [far, core_swap(far_mate)])[0]


def settle(own, mate, far, far_mate):
    sent = pair_sum(far, far_mate)
    return own, core_swap(mate), x_swap(sent)


def project_body(first, second, mat, out):
    size = first.shape[0]
    for place, piece in enumerate((first, second)):
        out[place * size : (place + 1) * size, :] = nn(piece[...], mat[:, :QKV]).astype(BF16)


def project(first, second, mat):
    count = 2 * first.shape[0]
    return call(
        "project",
        project_body,
        [((count, QKV), BF16)],
        [first, second, mat],
    )[0]


def split_heads(source, target, first, start, head_count):
    size = source.shape[0]
    for head in range(head_count):
        lanes = slice(first + head * HEAD_DIM, first + (head + 1) * HEAD_DIM)
        target[head, start : start + size, :] = source[:, lanes]


def attend_body(
    q_start, q_ref, near, far, labels, mat, gain, bias, o_ref, p_one, p_two, sum_ref, ks, vs
):
    head_count = QKV // (3 * HEAD_DIM)
    width = head_count * HEAD_DIM
    half = near.shape[0]
    for start, ref in ((0, near), (half, far)):
        split_heads(ref, ks, width, start, head_count)
        split_heads(ref, vs, 2 * width, start, head_count)
    out_mat = mat[:, QKV:]
    folded = folded_vectors(out_mat, gain[...], bias[...])
    size = half // 2
    key_labels = labels[0:1, :]
    for place, p_ref in enumerate((p_one, p_two)):
        rows = slice(place * size, (place + 1) * size)
        first = q_start + place * size
        allowed = to_columns(labels[:, first : first + size])[:, 0:1] == key_labels
        outs = []
        sums = []
        for head in range(head_count):
            query = q_ref[rows, head * HEAD_DIM : (head + 1) * HEAD_DIM]
            scores = jnp.where(allowed, nt(query, ks[head]), -1e30)
            peak = jnp.max(scores, axis=-1, keepdims=True)
            terms = jnp.exp2((scores - peak) * (SCALE * LOG2E))
            total = jnp.sum(terms, axis=-1, keepdims=True)
            outs.append(nn(terms.astype(BF16), vs[head]) / total)
            sums.append(peak * (SCALE * LOG2E) + jnp.log(total) * LOG2E)
        out = jnp.concatenate(outs, axis=1)
        o_ref[rows, :] = out
        lane = lax.broadcasted_iota(jnp.int32, (size, 128), 1)
        tile = jnp.zeros((size, 128), F32)
        for spot, column in enumerate(sums):
            tile = jnp.where(lane == spot, column, tile)
        sum_ref[rows, :] = tile
        p_ref[:size] = nt((out * gain[...]).astype(BF16), out_mat).astype(BF16)
        stats = to_rows(
            jnp.sum(out, axis=-1, keepdims=True), jnp.sum(out * out, axis=-1, keepdims=True)
        )
        p_ref[size : size + TAIL // 2] = encode(stats)
        p_ref[size + TAIL // 2 :] = folded


def attend(q_start, queries, near, far, labels, mat, gain, bias, after=()):
    count, keys = queries.shape[0], 2 * near.shape[0]
    heads = QKV // (3 * HEAD_DIM)
    width = heads * HEAD_DIM
    by_head = pltpu.VMEM((heads, keys, HEAD_DIM), BF16)
    payload = ((count // 2 + TAIL, D), BF16)
    return call(
        "attend",
        partial(attend_body, q_start),
        [((count, width), F32), payload, payload, ((count, 128), F32)],
        [queries, near, far, labels, mat, gain, bias],
        [by_head, by_head],
        after,
        work(4e9, 1),
    )


def attend_back_body(
    near, far, do_near, do_far, sum_near, sum_far, labels, near_out, far_out,
    qs, ks, vs, grads, dqs, dks, dvs, sums,
):
    head_count = QKV // (3 * HEAD_DIM)
    width = head_count * HEAD_DIM
    half = near.shape[0]
    for start, ref, grad in ((0, near, do_near), (half, far, do_far)):
        split_heads(ref, qs, 0, start, head_count)
        split_heads(ref, ks, width, start, head_count)
        split_heads(ref, vs, 2 * width, start, head_count)
        split_heads(grad, grads, 0, start, head_count)
    sums[:half] = sum_near[...]
    sums[half:] = sum_far[...]
    dks[...] = jnp.zeros_like(dks)
    dvs[...] = jnp.zeros_like(dvs)
    key_labels = labels[0:1, :]
    size = half // 2

    def block(index, carry):
        rows = pl.ds(pl.multiple_of(index * size, size), size)
        allowed = to_columns(labels[:, rows])[:, 0:1] == key_labels
        for head in range(head_count):
            query, grad = qs[head, rows, :], grads[head, rows, :]
            scores = jnp.where(allowed, nt(query, ks[head]), -1e30)
            prob = jnp.exp2(scores * (SCALE * LOG2E) - sums[rows, head : head + 1])
            prob_grad = nt(grad, vs[head])
            delta = jnp.sum(prob * prob_grad, axis=-1, keepdims=True)
            score_grad = (prob * (prob_grad - delta)).astype(BF16)
            dqs[head, rows, :] = nn(score_grad, ks[head]) * SCALE
            dks[head] += tn(query, score_grad)
            dvs[head] += tn(grad, prob.astype(BF16))
        return carry

    lax.fori_loop(0, 4, block, 0)
    for start, out in ((0, near_out), (half, far_out)):
        rows = slice(start, start + half)
        heads = range(head_count)
        out[...] = jnp.concatenate(
            [dqs[head, rows, :].astype(BF16) for head in heads]
            + [(dks[head, :, rows].T * SCALE).astype(BF16) for head in heads]
            + [dvs[head, :, rows].T.astype(BF16) for head in heads],
            axis=1,
        )


def attend_back(near, far, do_near, do_far, sum_near, sum_far, labels, after=()):
    half, width = do_near.shape
    keys = 2 * half
    heads = width // HEAD_DIM
    by_head = pltpu.VMEM((heads, keys, HEAD_DIM), BF16)
    turned = pltpu.VMEM((heads, HEAD_DIM, keys), F32)
    return call(
        "attend_back",
        attend_back_body,
        [(near.shape, BF16)] * 2,
        [near, far, do_near, do_far, sum_near, sum_far, labels],
        [by_head] * 4
        + [pltpu.VMEM((heads, keys, HEAD_DIM), F32), turned, turned, pltpu.VMEM((keys, 128), F32)],
        after,
        work(1.4e10, 1),
    )


def gelu_parts(x):
    spread = 0.5 + 0.5 * lax.erf(x * SQRT_HALF)
    return x * spread, spread


def feed_body(with_back, *refs):
    if with_back:
        one, two, back_one, back_two, mat, gain, bias, f_ref, p_one, p_two, s_ref = refs
    else:
        one, two, mat, gain, bias, f_ref, p_one, p_two = refs
        back_one = back_two = s_ref = None
    size = one.shape[0]
    up, down = mat.at[:, :UNITS], mat.at[:, UNITS:]
    folded = folded_vectors(down[...], gain[...], bias[...])
    for place, (piece, p_ref, back) in enumerate(((one, p_one, back_one), (two, p_two, back_two))):
        rows = slice(place * size, (place + 1) * size)
        pre = nn(piece[...], up[...])
        f_ref[rows, :] = pre
        act, _ = gelu_parts(pre)
        p_ref[:size] = nt((act * gain[...]).astype(BF16), down[...]).astype(BF16)
        columns = [
            jnp.sum(act, axis=-1, keepdims=True),
            jnp.sum(act * act, axis=-1, keepdims=True),
        ]
        p_ref[size : size + TAIL // 2] = encode(to_rows(*columns))
        p_ref[size + TAIL // 2 :] = folded
        if with_back:
            inner = nn(back[...], down[...]) * gain[...]
            columns.append(jnp.sum(inner, axis=-1, keepdims=True))
            columns.append(jnp.sum(inner * act, axis=-1, keepdims=True))
            s_ref[8 * place : 8 * place + 8, :] = to_rows(*columns)


def feed(pieces, backs, mat, gain, bias, after=()):
    size = pieces[0].shape[0]
    outs = [((2 * size, UNITS), F32)] + [((size + TAIL, D), BF16)] * 2
    if backs:
        outs += [((16, size), F32)]
    return call(
        "feed",
        partial(feed_body, bool(backs)),
        outs,
        [*pieces, *backs, mat, gain, bias],
        after=after,
    )


def feed_back_body(first_piece, *refs):
    if first_piece is not None:
        one, two, s_ref, *refs = refs
    else:
        one, two, *refs = refs
        s_ref = None
    f_ref, gain, bias, mat, df_ref, n_ref, p_one, p_two, vec_ref = refs
    up, down = mat.at[:, :UNITS], mat.at[:, UNITS:]
    size = p_one.shape[0]
    gain_grad = jnp.zeros((1, UNITS), F32)
    bias_grad = jnp.zeros((1, UNITS), F32)
    for place, (piece, p_ref) in enumerate(((one, p_one), (two, p_two))):
        rows = slice(place * size, (place + 1) * size)
        upstream = nn(piece[:size], down[...])
        pre = f_ref[rows, :]
        if first_piece is not None:
            start = 8 * (first_piece + place)
            stats = s_ref[start : start + 8, :]
        else:
            stats = decode(piece[size : size + TAIL // 2])
        columns = to_columns(stats)
        mean, scaled, first, second = (columns[:, i : i + 1] for i in range(4))
        act, spread = gelu_parts(pre)
        normal = (act - mean) * scaled
        act_grad = scaled * (upstream * gain[...] - first - normal * second)
        slope = spread + pre * (jnp.exp(-0.5 * pre * pre) * INV_SQRT_2PI)
        pre_grad = (act_grad * slope).astype(BF16)
        df_ref[rows, :] = pre_grad
        n_ref[rows, :] = (normal * gain[...] + bias[...]).astype(BF16)
        p_ref[...] = nt(pre_grad, up[...]).astype(BF16)
        gain_grad += jnp.sum(upstream * normal, axis=0, keepdims=True)
        bias_grad += jnp.sum(upstream, axis=0, keepdims=True)
    vec_ref[...] = vector_rows(gain_grad, bias_grad)


def feed_back(pieces, stats, first_piece, pre, gain, bias, mat, after=()):
    count = pre.shape[0]
    size = count // 2
    return call(
        "feed_back",
        partial(feed_back_body, first_piece if stats else None),
        [((count, UNITS), BF16)] * 2 + [((size, D), BF16)] * 2 + [((8, UNITS), F32)],
        [*pieces, *stats, pre, gain, bias, mat],
        after=after,
    )


def stats_pack_body(near, far, out):
    out[:16] = near[...]
    out[16:] = far[...]


def stats_near_body(stats, got, out):
    for place in range(4):
        other = 8 * (place ^ 1)
        out[8 * place : 8 * place + 8] = stats[8 * place : 8 * place + 8] + got[other : other + 8]


def stats_far_body(stats, got, out):
    for place in range(4):
        other = 8 * (place ^ 2)
        rows = slice(8 * place, 8 * place + 8)
        total = (stats[rows] + got[other : other + 8]) * (1.0 / FF)
        mean, one = total[0:1], total[2:3]
        scaled = lax.rsqrt(total[1:2] - mean * mean + EPS)
        two = scaled * (total[3:4] - mean * one)
        out[rows] = jnp.concatenate([mean, scaled, one, two, total[4:8]], axis=0)


def group_stats(near, far):
    shape = [((32, near.shape[1]), F32)]
    stats = call("stats_pack", stats_pack_body, shape, [near, far])[0]
    stats = call("stats_near", stats_near_body, shape, [stats, core_swap(stats)])[0]
    return call("stats_far", stats_far_body, shape, [stats, x_swap(stats)])[0]


def grads_body(pieces, halves, size, *refs):
    *refs, out = refs
    place = 0
    column = 0
    for left_count, right_count in zip(pieces, halves):
        left = refs[place : place + left_count]
        right = refs[place + left_count : place + left_count + right_count]
        place += left_count + right_count
        width = right[0].shape[1]
        per = left_count // right_count
        total = None
        for index, piece in enumerate(left):
            start = (index % per) * size
            term = tn(piece[:size], right[index // per][start : start + size, :])
            total = term if total is None else total + term
        out[:, column : column + width] = total.astype(BF16)
        column += width


def grads_of(*pairs, after=()):
    pieces = tuple(len(left) for left, _ in pairs)
    halves = tuple(len(right) for _, right in pairs)
    size = pairs[0][1][0].shape[0] // 2
    args = [item for left, right in pairs for item in (*left, *right)]
    width = sum(right[0].shape[1] for _, right in pairs)
    return call(
        "grads",
        partial(grads_body, pieces, halves, size),
        [((D, width), BF16)],
        args,
        after=after,
    )[0]


def inner_back_body(one, two, o_ref, gain, bias, mat, do_ref, u_ref, vec_ref):
    size = o_ref.shape[0] // 2
    gain_grad = jnp.zeros((1, o_ref.shape[1]), F32)
    bias_grad = jnp.zeros((1, o_ref.shape[1]), F32)
    out_mat = mat[:, QKV:]
    for place, piece in enumerate((one, two)):
        rows = slice(place * size, (place + 1) * size)
        upstream = nn(piece[:size], out_mat)
        columns = to_columns(decode(piece[size : size + TAIL // 2]))
        mean, scaled, first, second = (columns[:, i : i + 1] for i in range(4))
        normal = (o_ref[rows, :] - mean) * scaled
        back = scaled * (upstream * gain[...] - first - normal * second)
        do_ref[rows, :] = back.astype(BF16)
        u_ref[rows, :] = (normal * gain[...] + bias[...]).astype(BF16)
        gain_grad += jnp.sum(upstream * normal, axis=0, keepdims=True)
        bias_grad += jnp.sum(upstream, axis=0, keepdims=True)
    vec_ref[...] = vector_rows(gain_grad, bias_grad)


def inner_back(pieces, out, gain, bias, mat, after=()):
    count, width = out.shape
    return call(
        "inner_back",
        inner_back_body,
        [((count, width), BF16)] * 2 + [((8, width), F32)],
        [*pieces, out, gain, bias, mat],
        after=after,
    )


def encode_rows(values):
    return jnp.concatenate(split_three(values), axis=0)


def decode_rows(rows):
    rows = rows.astype(F32)
    count = rows.shape[0] // 3
    return rows[:count] + rows[count : 2 * count] + rows[2 * count :]


def unproject_body(rows, mat, one, two, gain, bias, p_one, p_two, vec_ref):
    size = p_one.shape[0]
    gain_grad = jnp.zeros((1, D), F32)
    bias_grad = jnp.zeros((1, D), F32)
    for place, (piece, p_ref) in enumerate(((one, p_one), (two, p_two))):
        term = nt(rows[place * size : (place + 1) * size], mat[:, :QKV])
        p_ref[...] = term.astype(BF16)
        gain_grad += jnp.sum(term * (piece[...].astype(F32) - bias[...]), axis=0, keepdims=True)
        bias_grad += jnp.sum(term, axis=0, keepdims=True)
    vec_ref[...] = vector_rows(gain_grad / gain[...], bias_grad)


def unproject(rows, mat, pieces, gain, bias, after=()):
    count = rows.shape[0]
    return call(
        "unproject",
        unproject_body,
        [((count // 2, D), BF16)] * 2 + [((8, D), F32)],
        [rows, mat, *pieces, gain, bias],
        after=after,
    )


def vectors_body(*refs):
    *items, out = refs
    out[...] = jnp.zeros_like(out)
    out[0:2, :] = items[0][0:2, :] + items[1][0:2, :]
    for place, item in enumerate(items[2:]):
        first = 2 * place + 2
        out[first : first + 2, : item.shape[1]] = item[0:2, :]


def vectors_of(items):
    return call("vectors", vectors_body, [((16, D), F32)], list(items))[0]


def outer_body(own, got, out):
    out[...] = own[0:8] + got[0:8]


def all_body(own, outer, got, out):
    out[0:8] = outer[...] + got[...]
    out[8:] = own[8:]


def encode_rows(values):
    return jnp.concatenate(split_three(values), axis=0)


def decode_rows(rows):
    rows = rows.astype(F32)
    count = rows.shape[0] // 3
    return rows[:count] + rows[count : 2 * count] + rows[2 * count :]


def branch_of(own, mate, far, feature_count):
    rows = own.shape[0] - TAIL
    half = rows + TAIL // 2
    pieces = (own, mate, far)
    product = sum(piece[:rows].astype(F32) for piece in pieces)
    stats = sum(decode(piece[rows:half]) for piece in pieces) / feature_count
    folded = sum(decode_vectors(piece[half:]) for piece in pieces)
    mean = stats[0:1]
    scaled = lax.rsqrt(stats[1:2] - mean * mean + EPS)
    kept = jnp.concatenate([mean, scaled, jnp.zeros((6, rows), F32)], axis=0)
    columns = to_columns(kept)
    branch = columns[:, 1:2] * (product - columns[:, 0:1] * folded[0:1])
    return branch, folded[1:2], folded[0:1], kept


def after_attend_body(x_ref, own, mate, far, gain, bias, x2_ref, z_ref, h_ref, fold_ref, kept_ref):
    branch, shift, folded, kept = branch_of(own, mate, far, D)
    mid = x_ref[...].astype(F32) + branch + shift
    x2_ref[...] = mid
    z_ref[...] = branch
    normal, _ = split_norm(mid)
    h_ref[...] = (normal * gain[...] + bias[...]).astype(BF16)
    fold_ref[...] = jnp.broadcast_to(folded, fold_ref.shape)
    kept_ref[...] = kept


def after_attend(x, pieces, gain, bias, after=()):
    rows = x.shape[0]
    return call(
        "after_attend",
        after_attend_body,
        [((rows, D), F32), ((rows, D), F32), ((rows, D), BF16), ((8, D), F32), ((8, rows), F32)],
        [x, *pieces, gain, bias],
        after=after,
    )


def mask_column(labels, rows):
    return (to_columns(labels[:, :rows])[:, 0:1] >= 0).astype(F32)


def after_feed_body(x2, own, mate, far, labels, gain, bias, y_ref, z_ref, h_ref, fold_ref, kept_ref):
    branch, shift, folded, kept = branch_of(own, mate, far, FF)
    out = (mask_column(labels, x2.shape[0]) * (x2[...] + branch + shift)).astype(BF16)
    y_ref[...] = out
    z_ref[...] = branch
    normal, _ = split_norm(out.astype(F32))
    h_ref[...] = (normal * gain[...] + bias[...]).astype(BF16)
    fold_ref[...] = jnp.broadcast_to(folded, fold_ref.shape)
    kept_ref[...] = kept


def after_feed(x2, pieces, labels, gain, bias, after=()):
    rows = x2.shape[0]
    return call(
        "after_feed",
        after_feed_body,
        [((rows, D), BF16), ((rows, D), F32), ((rows, D), BF16), ((8, D), F32), ((8, rows), F32)],
        [x2, *pieces, labels, gain, bias],
        after=after,
    )


def finish_feed_body(x2, own, mate, far, labels, y_ref):
    branch, shift, _, _ = branch_of(own, mate, far, FF)
    y_ref[...] = (mask_column(labels, x2.shape[0]) * (x2[...] + branch + shift)).astype(BF16)


def finish_feed(x2, pieces, labels):
    return call("finish_feed", finish_feed_body, [(x2.shape, BF16)], [x2, *pieces, labels])[0]


def payload_of(grad, branch, folded, kept, feature_count):
    sent = grad.astype(BF16)
    wide = sent.astype(F32)
    means = to_rows(
        jnp.sum(wide * folded, axis=-1, keepdims=True),
        jnp.sum(wide * branch, axis=-1, keepdims=True),
    )
    stats = jnp.concatenate([kept[0:2], means[0:2] / feature_count, kept[4:8]], axis=0)
    tail = jnp.concatenate([encode(stats), jnp.zeros((TAIL // 2, D), BF16)], axis=0)
    return jnp.concatenate([sent, tail], axis=0)


def feed_norm_back_body(
    own, mate, far, g_ref, labels, x2, gain, branch, folded, kept, dx_ref, out_ref, vec_ref
):
    upstream = own[...].astype(F32) + mate[...].astype(F32) + far[...].astype(F32)
    back, gain_grad, bias_grad = norm_back(x2[...], gain[...], upstream)
    total = mask_column(labels, x2.shape[0]) * g_ref[...].astype(F32) + back
    dx_ref[...] = total
    out_ref[...] = payload_of(total, branch[...], folded[0:1], kept[...], D)
    vec_ref[...] = vector_rows(gain_grad, bias_grad)


def feed_norm_back(pieces, grad, labels, x2, gain, branch, folded, kept, after=()):
    rows = x2.shape[0]
    return call(
        "feed_norm_back",
        feed_norm_back_body,
        [((rows, D), F32), ((rows + TAIL, D), BF16), ((8, D), F32)],
        [*pieces, grad, labels, x2, gain, branch, folded, kept],
        after=after,
    )


def first_norm_back_body(has_next, *refs):
    own, mate, far, dx2, x_ref, gain, *refs = refs
    upstream = own[...].astype(F32) + mate[...].astype(F32) + far[...].astype(F32)
    back, _, _ = norm_back(x_ref[...].astype(F32), gain[...], upstream)
    total = (dx2[...] + back).astype(BF16)
    if has_next:
        labels, branch, folded, kept, g_ref, out_ref = refs
        masked = mask_column(labels, dx2.shape[0]) * total.astype(F32)
        out_ref[...] = payload_of(masked, branch[...], folded[0:1], kept[...], FF)
    else:
        (g_ref,) = refs
    g_ref[...] = total


def first_norm_back(pieces, dx2, x, gain, following=(), after=()):
    rows = x.shape[0]
    outs = [((rows, D), BF16)]
    if following:
        outs.append(((rows + TAIL, D), BF16))
    return call(
        "first_norm_back",
        partial(first_norm_back_body, bool(following)),
        outs,
        [*pieces, dx2, x, gain, *following],
        after=after,
    )


def in_hbm(x):
    return pltpu.with_memory_space_constraint(x, pltpu.HBM)


def fetch_all(refs, held, sems):
    copies = [
        pltpu.make_async_copy(ref, spot, sems.at[place])
        for place, (ref, spot) in enumerate(zip(refs, held))
    ]
    for copy in copies:
        copy.start()
    for copy in copies:
        copy.wait()


def first_block_body(
    flags, query, key, value, output, down, up, out, down_out, swap_out, *scratch
):
    *held, sems = scratch
    fetch_all((query, key, value, output, down, up), held, sems)
    width = query.shape[1]
    for place, ref in enumerate(held[:3]):
        out[:, place * width : (place + 1) * width] = ref[...]
    out[:, 3 * width :] = held[3][...].T
    down_out[...] = held[4][...]
    lower = jnp.full((1, D), flags[2], jnp.int32) == 0
    swap_out[:, :D] = jnp.where(lower, down_out[...], held[5][...])
    swap_out[:, D:] = out[:, : D // 2]


def first_block(flags, *blocks):
    return pl.pallas_call(
        first_block_body,
        out_shape=tuple(
            jax.ShapeDtypeStruct((blocks[0].shape[0], width), BF16)
            for width in (D, D, 3 * D // 2)
        ),
        in_specs=[SMEM] + [HBM] * 6,
        out_specs=(VMEM,) * 3,
        scratch_shapes=[pltpu.VMEM(block.shape, BF16) for block in blocks]
        + [pltpu.SemaphoreType.DMA((6,))],
        compiler_params=PARAMS,
        name="first_block",
    )(flags, *map(in_hbm, blocks))


def beside_body(one, two, out):
    width = one.shape[1]
    out[:, :width] = one[...]
    out[:, width:] = two[...]


def beside(one, two, after=()):
    rows, width = one.shape
    return call("beside", beside_body, [((rows, 2 * width), BF16)], [one, two], after=after)[0]


def entry_body(flags, inputs, cotangent, out, far_out, own_in, own_grad, sems):
    size = own_in.shape[0]

    def rows_of(micro):
        return pl.ds(pl.multiple_of(micro * size, size), size)

    across, far, own = rows_of(1 - flags[3]), rows_of(flags[2]), rows_of(flags[3])
    copies = [
        pltpu.make_async_copy(source, target, sems.at[place])
        for place, (source, target) in enumerate(
            (
                (inputs.at[across], out.at[:size]),
                (cotangent.at[across], out.at[size:]),
                (inputs.at[far], far_out.at[:size]),
                (cotangent.at[far], far_out.at[size:]),
                (inputs.at[own], own_in),
                (cotangent.at[own], own_grad),
            )
        )
    ]
    for copy in copies:
        copy.start()
    for copy in copies:
        copy.wait()


def entry(flags, inputs, cotangent):
    rows = inputs.shape[0]
    shapes = [rows, rows, rows // 2, rows // 2]
    return pl.pallas_call(
        entry_body,
        out_shape=tuple(jax.ShapeDtypeStruct((count, D), BF16) for count in shapes),
        in_specs=[SMEM, HBM, HBM],
        out_specs=(VMEM,) * 4,
        scratch_shapes=[pltpu.SemaphoreType.DMA((6,))],
        compiler_params=PARAMS,
        name="entry",
    )(flags, in_hbm(inputs), in_hbm(cotangent))


def enter_body(
    flags, own_in, own_grad, got, labels, gain, bias, x_ref, g_ref, top_ref, h_ref
):
    size, width = x_ref.shape
    here = jnp.full((1, width), flags[0], jnp.int32) == 1
    own = jnp.where(here, own_in[...], got[:size])
    grad = jnp.where(here, own_grad[...], got[size:])
    x_ref[...] = own
    g_ref[...] = grad
    top_ref[...] = (mask_column(labels, size) * grad.astype(F32)).astype(BF16)
    normal, _ = split_norm(own.astype(F32))
    h_ref[...] = (normal * gain[...] + bias[...]).astype(BF16)


def enter(flags, own_in, own_grad, got, labels, gain, bias):
    return call(
        "enter",
        enter_body,
        [(own_in.shape, BF16)] * 4,
        [flags, own_in, own_grad, got, labels, gain, bias],
    )


def enter_far_body(got, labels, gain, bias, top_ref, h_ref):
    size = top_ref.shape[0]
    mask = (to_columns(labels[:, 2 * size : 3 * size])[:, 0:1] >= 0).astype(F32)
    top_ref[...] = (mask * got[size:].astype(F32)).astype(BF16)
    normal, _ = split_norm(got[:size].astype(F32))
    h_ref[...] = (normal * gain[...] + bias[...]).astype(BF16)


def enter_far(got, labels, gain, bias):
    rows = got.shape[0] // 2
    return call(
        "enter_far", enter_far_body, [((rows, D), BF16)] * 2, [got, labels, gain, bias]
    )


def pack_body(*refs):
    *items, out = refs
    size = items[0].shape[0]
    for place, item in enumerate(items):
        out[place * size : (place + 1) * size, :] = item[...]


def pack(items):
    rows, width = items[0].shape
    return call("pack", pack_body, [((len(items) * rows, width), BF16)], list(items))[0]


def unpack_body(flags, own, sent, got_own, got_sent, y_ref, g_ref):
    size = y_ref.shape[0] // 2
    width = y_ref.shape[1]
    here = jnp.full((1, width), flags[0], jnp.int32) == 1
    rows = pl.ds(pl.multiple_of(flags[2] * size, size), size)
    first = pl.ds(pl.multiple_of(flags[3] * size, size), size)
    second = pl.ds(pl.multiple_of((1 - flags[3]) * size, size), size)
    last = slice(2 * size, 3 * size)
    y_ref[first, :] = jnp.where(here, own[rows, :], got_own[rows, :])
    y_ref[second, :] = jnp.where(here, sent[rows, :], got_sent[rows, :])
    g_ref[first, :] = jnp.where(here, own[last, :], got_own[last, :])
    g_ref[second, :] = jnp.where(here, sent[last, :], got_sent[last, :])


def unpack(flags, own, sent, got_own, got_sent):
    rows = 2 * own.shape[0] // 3
    return call(
        "unpack",
        unpack_body,
        [((rows, own.shape[1]), BF16)] * 2,
        [flags, own, sent, got_own, got_sent],
    )


def halve_body(with_vectors, flags, block, across, *refs):
    if with_vectors:
        vectors, got, kept, sent, vec_ref = refs
        total = vectors[...] + got[...]
        vec_ref[...] = total
    else:
        kept, sent = refs
    size = kept.shape[0] // 2
    for place, (out, step) in enumerate(((kept, 0), (kept, 2), (sent, 1), (sent, 3))):
        rows = pl.ds(pl.multiple_of((flags[1] ^ step) * size, size), size)
        spot = slice((place % 2) * size, (place % 2 + 1) * size)
        out[spot] = (block[rows, :].astype(F32) + across[rows, :].astype(F32)).astype(BF16)
    if with_vectors:
        sent[2 * size :] = encode_rows(total)


def halve(flags, block, across, vectors=(), after=(), cost=None):
    rows, width = block.shape
    outs = [((rows // 2, width), BF16)] * 2
    if vectors:
        outs = [outs[0], ((rows // 2 + 48, width), BF16), (vectors[0].shape, F32)]
    return call(
        "halve",
        partial(halve_body, bool(vectors)),
        outs,
        [flags, block, across, *vectors],
        after=after,
        cost=cost,
    )


def quarter_body(with_vectors, kept, got, *refs):
    if with_vectors:
        vectors, own, sent, vec_ref = refs
    else:
        own, sent = refs
    size = own.shape[0]
    for place, out in enumerate((own, sent)):
        rows = slice(place * size, (place + 1) * size)
        out[:size] = (kept[rows].astype(F32) + got[rows].astype(F32)).astype(BF16)
    if with_vectors:
        total = vectors[...] + decode_rows(got[2 * size :])
        vec_ref[...] = total
        sent[size:] = encode_rows(total)


def quarter(kept, got, vectors=(), after=()):
    rows, width = kept.shape
    outs = [((rows // 2, width), BF16)] * 2
    if vectors:
        outs = [outs[0], ((rows // 2 + 48, width), BF16), (vectors[0].shape, F32)]
    return call(
        "quarter",
        partial(quarter_body, bool(vectors)),
        outs,
        [kept, got, *vectors],
        after=after,
    )


def last_body(kept, got, vectors, out, vec_ref):
    size = kept.shape[0]
    out[...] = (kept[...].astype(F32) + got[:size].astype(F32)).astype(BF16)
    vec_ref[...] = vectors[...] + decode_rows(got[size:])


def last_of(kept, got, vectors, after=()):
    outs = [(kept.shape, BF16), (vectors.shape, F32)]
    return call("last", last_body, outs, [kept, got, vectors], after=after)


def total_body(*refs):
    *parts, out = refs
    out[...] = sum(part[...].astype(F32) for part in parts).astype(out.dtype)


def total_of(parts, kind=BF16, after=(), cost=None):
    shape = [(parts[0].shape, kind)]
    return call("total", total_body, shape, list(parts), after=after, cost=cost)[0]


def layers_of(flags, lower, lower_got, upper, upper_got):
    width = lower.shape[1]
    here = jnp.full((1, width), flags[0], jnp.int32) == 1
    first = jnp.full((1, width), flags[2], jnp.int32) == 0
    one = jnp.where(here, lower[...], lower_got[...])
    two = jnp.where(here, upper[...], upper_got[...])
    return jnp.where(first, one, two).astype(F32)


def final_first_body(
    flags, lower, lower_got, upper, upper_got, vec, vec_got, q_ref, k_ref, v_ref, o_ref, vec_ref
):
    width = q_ref.shape[1]
    total = layers_of(flags, lower, lower_got, upper, upper_got)
    for place, ref in enumerate((q_ref, k_ref, v_ref)):
        ref[...] = total[:, place * width : (place + 1) * width]
    o_ref[...] = total[:, 3 * width :].T
    here = jnp.full((1, D), flags[0], jnp.int32) == 1
    vec_ref[...] = jnp.where(here, vec[...], vec_got[...])


def final_first(flags, lower, upper, vectors):
    rows, width = lower[0].shape[0], D // LANES
    return call(
        "final_first",
        final_first_body,
        [((rows, width), F32)] * 3 + [((width, rows), F32), ((16, D), F32)],
        [flags, *lower, *upper, *vectors],
    )


def final_second_body(flags, lower, lower_got, upper, upper_got, up_ref, down_ref):
    total = layers_of(flags, lower, lower_got, upper, upper_got)
    up_ref[...] = total[:, :UNITS]
    down_ref[...] = total[:, UNITS:]


def final_second(flags, lower, upper):
    rows = lower[0].shape[0]
    return call(
        "final_second",
        final_second_body,
        [((rows, UNITS), F32)] * 2,
        [flags, *lower, *upper],
    )


def merge_body(flags, one, two, upper, out):
    size, width = one.shape
    first = jnp.full((1, width), flags[2], jnp.int32) == 0
    for place, ref in enumerate((one, two)):
        rows = slice(place * size, (place + 1) * size)
        out[rows] = jnp.where(first, ref[...], upper[rows])


def merge(flags, one, two, upper):
    return call("merge", merge_body, [(upper.shape, BF16)], [flags, one, two, upper])[0]


def choose_body(flags, one, two, out):
    first = jnp.full((1, out.shape[1]), flags[2], jnp.int32) == 0
    out[...] = jnp.where(first, one[...], two[...])


def choose(flags, one, two, after=()):
    return call("choose", choose_body, [(one.shape, one.dtype)], [flags, one, two], after=after)[0]


def join_body(flags, own, got, out):
    half = own.shape[1]
    first = jnp.full((1, half), flags[2], jnp.int32) == 0
    out[:, :half] = jnp.where(first, own[...], got[...])
    out[:, half:] = jnp.where(first, got[...], own[...])


def join(flags, own, got, after=()):
    rows, half = own.shape
    return call(
        "join", join_body, [((rows, 2 * half), BF16)], [flags, own, got], after=after
    )[0]


def hold_body(ref, out):
    out[...] = ref[...]


def hold(x, after):
    return call("hold", hold_body, [(x.shape, x.dtype)], [x], after=after)[0]


def assemble_body(count, flags, *refs):
    beside, across, out = refs[:count], refs[count:-1], refs[-1]
    size = beside[0].shape[0]
    width = out.shape[1]
    near = jnp.full((1, width), flags[0], jnp.int32) == 1
    for step in range(count):
        rows = pl.ds(pl.multiple_of((flags[1] ^ step) * size, size), size)
        out[rows, :] = jnp.where(near, beside[step][...], across[step][...])


def assemble(flags, beside, across, after=()):
    count, (size, width) = len(beside), beside[0].shape
    return call(
        "assemble",
        partial(assemble_body, count),
        [((count * size, width), BF16)],
        [flags, *beside, *across],
        after=after,
    )[0]


def early_block_body(flags, up, got, first, out):
    width = up.shape[1]
    lower = jnp.full((1, width), flags[2], jnp.int32) == 0
    out[:, :width] = jnp.where(lower, up[...], got[:, :width])
    half = first.shape[1] // 2
    lower = jnp.full((1, half), flags[2], jnp.int32) == 0
    out[:, width:] = jnp.where(lower, got[:, width:], first[:, half:])


def early_block(flags, up, got, first, after=()):
    rows, width = up.shape
    return call(
        "early_block",
        early_block_body,
        [((rows, width + first.shape[1] // 2), BF16)],
        [flags, up, got, first],
        after=after,
    )[0]


def late_block_body(flags, got, down, out):
    width = down.shape[1]
    lower = jnp.full((1, width), flags[2], jnp.int32) == 0
    out[...] = jnp.where(lower, got[:, :width], down[...])


def late_block(flags, got, down, after=()):
    return call(
        "late_block", late_block_body, [(down.shape, BF16)], [flags, got, down], after=after
    )[0]


def parts_body(ref, one, two):
    width = one.shape[1]
    one[...] = ref[:, :width]
    two[...] = ref[:, width:]


def parts_of(x, width, after):
    rows, whole = x.shape
    shapes = [((rows, width), x.dtype), ((rows, whole - width), x.dtype)]
    return call("parts", parts_body, shapes, [x], after=after)


def pick_body(flags, beside, across, out):
    near = jnp.full((1, out.shape[1]), flags[0], jnp.int32) == 1
    out[...] = jnp.where(near, beside[...], across[...])


def pick(flags, beside, across, cost=None):
    return call(
        "pick", pick_body, [(beside.shape, BF16)], [flags, beside, across], cost=cost
    )[0]


def on_device(
    inputs,
    cotangent,
    doc_ids,
    norm_gain,
    norm_bias,
    w_query,
    w_key,
    w_value,
    inner_gain,
    inner_bias,
    w_output,
    feed_gain,
    feed_bias,
    w_up,
    middle_gain,
    middle_bias,
    w_down,
):
    core = lax.axis_index("section")
    lane = lax.axis_index("mp")
    lane_x = lane % 2
    lane_y = lane // 2
    count = lax.axis_size("dp")
    slice_len = inputs.shape[0] // MICRO
    rank = 2 * core + lane_x
    crossing = [(s * 4 + r, s * 4 + (r ^ 2)) for s in range(2) for r in range(4) if s == r // 2]
    returning = [(s * 4 + r, s * 4 + (r ^ 2)) for s in range(2) for r in range(4) if s != r // 2]

    def by_core(first, second):
        return jnp.where(core == 0, first, second)

    def placed(array, layer):
        return [
            lax.ppermute(
                array,
                BOTH,
                [(s * 4 + 2 * m + x, layer * 4 + 2 * s + x) for s in range(2) for x in range(2)],
            )
            for m in range(MICRO)
        ]

    label_grid = lax.dynamic_index_in_dim(
        doc_ids.reshape(LANES, MICRO, slice_len), lane_y, 1, keepdims=False
    )
    order = (rank, 2 * (1 - core) + lane_x, rank ^ 1, 2 * (1 - core) + (1 - lane_x))
    labels = jnp.concatenate(
        [lax.dynamic_index_in_dim(label_grid, item, 0, keepdims=False) for item in order]
    )
    labels = jnp.broadcast_to(labels.astype(F32)[None], (8, LANES * slice_len))

    place = lax.axis_index("dp")
    flags = jnp.stack([core == lane_y, place, core, lane_y]).astype(jnp.int32)

    def line_pairs(step):
        return [
            ((r // 2 * count + i) * LANES + r, (r // 2 * count + (i ^ step)) * LANES + r)
            for i in range(count)
            for r in range(LANES)
        ]

    def along_line(block, step):
        return lax.ppermute(block, ("section", "dp", "mp"), line_pairs(step))

    first, down_block, swapped = first_block(
        flags, w_query[0], w_key[0], w_value[0], w_output[0], w_down[0].T, w_up[0]
    )
    up_block = w_up[0]

    def along_dp(block):
        return lax.all_gather(block, "dp", axis=0, tiled=True)

    def fetched(line, hook=()):
        whole = join(flags, line, core_swap(line), after=hook)
        return whole, lax.ppermute(whole, BOTH, crossing)

    outer_own = jnp.concatenate([norm_gain, norm_bias, feed_gain, feed_bias], axis=0)
    outer_other = core_swap(outer_own)
    split_own = jnp.concatenate([inner_gain, inner_bias, middle_gain, middle_bias], axis=1)
    split_far = y_swap(split_own)
    split_kept = jnp.where(lane_y == core, split_own, split_far)
    split_other = core_swap(jnp.where(lane_y == core, split_far, split_own))

    def small_of(outer, split):
        width = D // LANES
        return (
            [outer[i : i + 1] for i in range(4)],
            [
                split[:, :width],
                split[:, width : 2 * width],
                split[:, 2 * width : 2 * width + UNITS],
                split[:, 2 * width + UNITS :],
            ],
        )

    lower_outer, lower_split = small_of(
        by_core(outer_own, outer_other), by_core(split_kept, split_other)
    )
    upper_outer, upper_split = small_of(
        by_core(outer_other, outer_own), by_core(split_other, split_kept)
    )

    def gather_around(own, near_of, far=None, after=()):
        if far is None:
            far = x_swap(own)
        mate = core_swap(own)
        near = near_of([own, mate])
        far = hold(far, after=[near[0], *after])
        return (own, mate, far, core_swap(far)), near

    def attention(x, h, first, outer, split, hooks, far=None):
        pieces, (near,) = gather_around(
            h, lambda rows: [project(*rows, first)], far, after=hooks[2]
        )
        far = project(pieces[2], pieces[3], first)
        half = 2 * slice_len
        o_far, p_far, p_far_mate, sum_far = attend(
            half, far, near, far, labels, first, split[0], split[1]
        )
        sent = pair_sum(p_far, p_far_mate)
        hooks[0](p_far)
        o_near, p_own, p_mate, sum_near = attend(
            0, near, near, far, labels, first, split[0], split[1], after=[sent]
        )
        arrived = hold(x_swap(sent), after=[p_own])
        terms = (p_own, core_swap(p_mate), arrived)
        x2, branch, h2, folded, kept = after_attend(x, terms, outer[2], outer[3], after=hooks[1])
        state = (pieces, near, far, o_near, o_far, sum_near, sum_far, x, x2, branch, folded, kept)
        return x2, h2, state, arrived

    def attention_back(grad, sums, state, first, outer, split, following, hooks):
        pieces, near, far, o_near, o_far, sum_near, sum_far, x, x2, branch, folded, kept = state
        dx2, sent, feed_vec = feed_norm_back(
            sums, grad, labels, x2, outer[2], branch, folded, kept, after=hooks[0]
        )
        block = hooks[3](sent)
        backs, (do_near, u_near, vec_near) = gather_around(
            sent, lambda rows: inner_back(rows, o_near, split[0], split[1], first), after=block
        )
        do_far, u_far, vec_far = inner_back(backs[2:], o_far, split[0], split[1], first)
        dq_near, dq_far = attend_back(
            near, far, do_near, do_far, sum_near, sum_far, labels, after=hooks[1]
        )
        norm = (outer[0], outer[1])
        p_far, p_far_mate, norm_far = unproject(
            dq_far, first, pieces[2:], *norm, after=hooks[4](dq_far)
        )
        sent = pair_sum(p_far, p_far_mate)
        p_own, p_mate, norm_near = unproject(
            dq_near, first, pieces[:2], *norm, after=[sent, *hooks[5]()]
        )
        mat_grad = grads_of(
            (pieces, (dq_near, dq_far)), (backs, (u_near, u_far)), after=[sent]
        )
        terms = (p_own, core_swap(p_mate), hold(x_swap(sent), after=[p_own, mat_grad]))
        result = first_norm_back(
            terms, dx2, x, outer[0], following, after=hooks[2](mat_grad)
        )
        return result, vec_near + vec_far, feed_vec, (norm_near, norm_far)

    def reduce_across(block):
        across = lax.ppermute(block, BOTH, returning)
        if count != 4:
            total = total_of([block, across])
            return [lax.psum_scatter(total, "dp", scatter_dimension=0, tiled=True)]
        return block, across

    def reduce_near(pair, after=(), cost=None):
        if count != 4:
            return pair
        kept, sent = halve(flags, *pair, after=after, cost=cost)
        return kept, along_line(sent, 1)

    def reduce_far(pair, after=()):
        if count != 4:
            return pair
        kept, sent = quarter(*pair, after=after)
        return kept, along_line(sent, 2)

    def reduce_end(pair, after=(), cost=None):
        total = total_of(pair, after=after, cost=cost) if count == 4 else pair[0]
        return total, core_swap(total)

    sent, far_sent, own_in, own_grad = entry(flags, inputs, cotangent)
    got = lax.ppermute(sent, BOTH, crossing)
    far_got = lax.ppermute(
        far_sent,
        BOTH,
        [
            (s * LANES + r, s * LANES + (r ^ 1) if s == r // 2 else (r // 2) * LANES + (r ^ 3))
            for s in range(2)
            for r in range(LANES)
        ],
    )
    lower_in, upstream, masked, h = enter(
        flags, own_in, own_grad, got, labels, lower_outer[0], lower_outer[1]
    )
    masked_far, far = enter_far(far_got, labels, lower_outer[0], lower_outer[1])
    top = (masked, core_swap(masked), masked_far, core_swap(masked_far))
    moved = choose(flags, first, core_swap(first))
    if count == 4:
        pieces = [moved] + [along_line(moved, step) for step in range(1, count)]
        lower_first = assemble(
            flags, pieces, [lax.ppermute(piece, BOTH, crossing) for piece in pieces], after=[far]
        )
    else:
        pieces = [along_dp(moved)]
        lower_first = pick(flags, pieces[0], lax.ppermute(pieces[0], BOTH, crossing))
    got = core_swap(swapped)
    early_line = along_dp(early_block(flags, up_block, got, first, after=pieces[-1:]))
    late_line = along_dp(late_block(flags, got, down_block))
    coming = {}

    def early_matrices(last):
        coming["second"], coming["first"] = parts_of(early_line, UNITS, [last])

    x2, h2, lower_state, arrived = attention(
        lower_in, h, lower_first, lower_outer, lower_split, (early_matrices, (), ()), far
    )
    lower_second_whole, lower_second_across = fetched(coming["second"])
    lower_second = pick(flags, lower_second_whole, lower_second_across)
    upper_first_whole, upper_first_across = fetched(coming["first"], [h2])
    upper_first = pick(flags, upper_first_whole, upper_first_across)
    lower_pieces, (f_near, p_own, p_mate) = gather_around(
        h2, lambda rows: feed(rows, (), lower_second, *lower_split[2:])
    )
    f_far, p_far, p_far_mate = feed(lower_pieces[2:], (), lower_second, *lower_split[2:])
    lower_pre = (f_near, f_far)
    sent = pair_sum(p_far, p_far_mate)
    upper_second_whole, upper_second_across = fetched(hold(late_line, after=[sent]))
    upper_second = pick(flags, upper_second_whole, upper_second_across, work(1e10, 1))
    arrived = hold(x_swap(sent), after=[upper_second_whole])
    terms = (p_own, core_swap(p_mate), arrived)
    lower_out, lower_branch, h, lower_folded, lower_kept = after_feed(
        x2, terms, labels, upper_outer[0], upper_outer[1]
    )
    x2, h2, upper_state, _ = attention(
        lower_out,
        h,
        upper_first,
        upper_outer,
        upper_split,
        (lambda last: None, (), [upper_second_whole]),
    )
    upper_pieces, (f_near, p_own, p_mate, near_stats) = gather_around(
        h2, lambda rows: feed(rows, top[:2], upper_second, *upper_split[2:])
    )
    f_far, p_far, p_far_mate, far_stats = feed(
        upper_pieces[2:], top[2:], upper_second, *upper_split[2:]
    )
    upper_pre = (f_near, f_far)

    stats = group_stats(near_stats, far_stats)
    df_far, n_far, q_far, q_far_mate, vec_far = feed_back(
        top[2:], [stats], 2, upper_pre[1], *upper_split[2:], upper_second
    )
    sent = pair_sum(q_far, q_far_mate)
    df_near, n_near, q_own, q_mate, vec_near = feed_back(
        top[:2], [stats], 0, upper_pre[0], *upper_split[2:], upper_second, after=[sent]
    )
    upper_middle = vec_near + vec_far
    sums = (q_own, core_swap(q_mate), hold(x_swap(sent), after=[q_own]))
    ended = pair_sum(p_far, p_far_mate)
    ended_far = []

    def ended_hook(last):
        ended_far.append(hold(x_swap(ended), after=[last]))
        return ended_far

    following = (labels, lower_branch, lower_folded, lower_kept)
    pairs = {}

    def upper_second_grads(after):
        block = grads_of(
            (upper_pieces, (df_near, df_far)), (top, (n_near, n_far)), after=[after]
        )
        pairs["second"] = reduce_near(reduce_across(block), cost=work(9e9, 1))
        return [block]

    def upper_hook(item):
        pairs["upper"] = reduce_across(item)
        return [item]

    (upper_grad, sent), upper_inner, upper_feed, upper_norm = attention_back(
        upstream,
        sums,
        upper_state,
        upper_first,
        upper_outer,
        upper_split,
        following,
        ((), [ended], upper_hook, upper_second_grads, ended_hook, lambda: ()),
    )

    upper_out = finish_feed(x2, (p_own, core_swap(p_mate), ended_far[0]), labels)
    own = pack([lower_out, upper_out, upper_grad])
    swapped = lax.ppermute(own, BOTH, returning)
    upper_second_pair = reduce_far(pairs["second"], [own])
    upper_first_pair = reduce_near(pairs["upper"])
    backs, (df_near, n_near, q_own, q_mate, vec_near) = gather_around(
        sent,
        lambda rows: feed_back(
            rows, (), 0, lower_pre[0], *lower_split[2:], lower_second, after=[own]
        ),
        after=upper_first_pair[:1],
    )
    df_far, n_far, q_far, q_far_mate, vec_far = feed_back(
        backs[2:],
        (),
        2,
        lower_pre[1],
        *lower_split[2:],
        lower_second,
        after=[upper_second_pair[0]],
    )
    lower_middle = vec_near + vec_far
    sent = pair_sum(q_far, q_far_mate)
    sums = (q_own, core_swap(q_mate), x_swap(sent))

    def lower_second_grads(after):
        block = grads_of(
            (lower_pieces, (df_near, df_far)), (backs, (n_near, n_far)), after=[after]
        )
        pairs["second"] = reduce_across(block)
        return [block]

    upper_first_pair = reduce_far(upper_first_pair, after=[q_far])

    layer_outputs, upper_held = unpack(
        flags, own, swapped, core_swap(own), core_swap(swapped)
    )

    def lower_hook(item):
        pairs["lower"] = reduce_across(item)
        pairs["second"] = reduce_near(pairs["second"], after=[item])
        return [item]

    def upper_ended(last):
        pairs["ended"] = reduce_end(upper_second_pair, after=[last])
        pairs["first"] = reduce_end(upper_first_pair, after=[last])
        return [pairs["ended"][0], pairs["first"][0]]

    (lower_grad,), lower_inner, lower_feed, lower_norm = attention_back(
        upper_grad,
        sums,
        lower_state,
        lower_first,
        lower_outer,
        lower_split,
        (),
        (
            [upper_first_pair[0]],
            [layer_outputs],
            lower_hook,
            lower_second_grads,
            upper_ended,
            lambda: (),
        ),
    )
    vectors = vectors_of(
        [*lower_norm, lower_feed, upper_norm[0] + upper_norm[1], upper_feed]
        + [lower_middle, upper_middle, lower_inner, upper_inner]
    )
    outer = call("outer", outer_body, [((8, D), F32)], [vectors, core_swap(vectors)])[0]
    vectors = call("all", all_body, [((16, D), F32)], [vectors, outer, x_swap(outer)])[0]
    lower_held = placed(lower_grad, 0)
    input_grads = merge(flags, *lower_held, upper_held)
    if count == 4:
        first_kept, sent, vectors = halve(
            flags,
            *pairs["lower"],
            (vectors, y_swap(vectors)),
            after=[pairs["first"][0], lower_grad],
        )
        got = along_line(sent, 1)
        lower_second_sum = reduce_end(reduce_far(pairs["second"], after=[first_kept]))
        grad_up, grad_down = final_second(flags, lower_second_sum, pairs["ended"])
        kept, sent, vectors = quarter(first_kept, got, [vectors])
        ended, vectors = last_of(
            kept, along_line(sent, 2), vectors, after=[input_grads, grad_up]
        )
    else:
        vectors = lax.psum(vectors + y_swap(vectors), "dp")
        ended = pairs["lower"][0]
        lower_second_sum = reduce_end(pairs["second"])
        grad_up, grad_down = final_second(flags, lower_second_sum, pairs["ended"])
    grad_query, grad_key, grad_value, grad_output, vectors = final_first(
        flags, (ended, core_swap(ended)), pairs["first"], (vectors, core_swap(vectors))
    )

    def part(rows, start, size):
        rows = lax.dynamic_slice(rows, (core * rows.shape[0] // 2, start), (rows.shape[0] // 2, size))
        return [rows[i : i + 1] for i in range(rows.shape[0])]

    width = D // LANES
    size = D // count // LANES
    outer = part(vectors[:8], (place * LANES + lane) * size, size)
    middle = part(vectors[8:12], place * (UNITS // count), UNITS // count)
    inner = part(vectors[12:], place * (width // count), width // count)
    return (
        layer_outputs[None],
        input_grads[None],
        outer[0],
        outer[1],
        grad_query[None],
        grad_key[None],
        grad_value[None],
        inner[0],
        inner[1],
        grad_output[None],
        outer[2],
        outer[3],
        grad_up[None],
        middle[0],
        middle[1],
        grad_down.T[None],
    )


def solution(mesh):
    placed = (
        P(("dp", "mp"), None),
        P(("dp", "mp"), None),
        P("dp"),
        P("section", None),
        P("section", None),
        P("section", "dp", "mp"),
        P("section", "dp", "mp"),
        P("section", "dp", "mp"),
        P("section", "mp"),
        P("section", "mp"),
        P("section", "mp", "dp"),
        P("section", None),
        P("section", None),
        P("section", "dp", "mp"),
        P("section", "mp"),
        P("section", "mp"),
        P("section", "mp", "dp"),
    )
    return jax.shard_map(
        on_device,
        mesh=mesh,
        in_specs=placed,
        out_specs=(
            P("section", ("dp", "mp"), None),
            P("section", ("dp", "mp"), None),
            P("section", ("dp", "mp")),
            P("section", ("dp", "mp")),
            P("section", "dp", "mp"),
            P("section", "dp", "mp"),
            P("section", "dp", "mp"),
            P("section", ("mp", "dp")),
            P("section", ("mp", "dp")),
            P("section", "mp", "dp"),
            P("section", ("dp", "mp")),
            P("section", ("dp", "mp")),
            P("section", "dp", "mp"),
            P("section", ("mp", "dp")),
            P("section", ("mp", "dp")),
            P("section", "mp", "dp"),
        ),
        check_vma=False,
    )
```

```python
from functools import partial

import jax
import jax.numpy as jnp
from jax import lax
from jax.experimental import pallas as pl
from jax.experimental.pallas import tpu as pltpu
from jax.sharding import PartitionSpec as P

D = 768
HEAD_DIM = 64
FF = 3072
MICRO = 2
LANES = 4
EPS = 1e-05
SCALE = HEAD_DIM ** (-0.5)
LOG2E = 1.4426950408889634
SQRT_HALF = 0.7071067811865476
INV_SQRT_2PI = 0.3989422804014327
BOTH = ("section", "mp")
Y_PAIRS = [[0, 2], [1, 3]]
QKV = 3 * D // LANES
UNITS = FF // LANES
TAIL = 16
F32 = jnp.float32
BF16 = jnp.bfloat16

VMEM = pl.BlockSpec(memory_space=pltpu.VMEM)
SMEM = pl.BlockSpec(memory_space=pltpu.SMEM)
ANY = pl.BlockSpec(memory_space=pl.ANY)
HBM = pl.BlockSpec(memory_space=pltpu.HBM)
PARAMS = pltpu.CompilerParams(vmem_limit_bytes=16 * 1024 * 1024)


def call(name, body, outs, ins, scratch=(), after=(), cost=None):
    count = len(ins)

    def kernel(*refs):
        body(*refs[:count], *refs[count + len(after) :])

    return pl.pallas_call(
        kernel,
        out_shape=tuple(jax.ShapeDtypeStruct(shape, kind) for shape, kind in outs),
        in_specs=[SMEM if item.ndim == 1 else VMEM for item in ins] + [ANY] * len(after),
        out_specs=(VMEM,) * len(outs),
        scratch_shapes=list(scratch),
        compiler_params=PARAMS,
        name=name,
        cost_estimate=cost or work(1, 1),
    )(*ins, *after)


def work(flops, size):
    return pl.CostEstimate(flops=int(flops), bytes_accessed=int(size), transcendentals=0)


def nn(a, b):
    return jnp.dot(a, b, preferred_element_type=F32)


def nt(a, b):
    return lax.dot_general(a, b, (((1,), (1,)), ((), ())), preferred_element_type=F32)


def tn(a, b):
    return lax.dot_general(a, b, (((0,), (0,)), ((), ())), preferred_element_type=F32)


def to_rows(*columns):
    count = columns[0].shape[0]
    lane = lax.broadcasted_iota(jnp.int32, (count, 128), 1)
    tile = jnp.zeros((count, 128), F32)
    for place, column in enumerate(columns):
        tile = jnp.where(lane == place, column, tile)
    return tile.T[:8]


def to_columns(rows):
    return jnp.concatenate([rows, jnp.zeros((120, rows.shape[1]), F32)], axis=0).T


def split_three(values):
    high = values.astype(BF16)
    rest = values - high.astype(F32)
    middle = rest.astype(BF16)
    return high, middle, (rest - middle.astype(F32)).astype(BF16)


def encode(rows):
    return jnp.concatenate(split_three(rows), axis=1)


def decode(tail):
    tail = tail.astype(F32)
    count = tail.shape[1] // 3
    return tail[:, :count] + tail[:, count : 2 * count] + tail[:, 2 * count :]


def decode_vectors(tail):
    tail = tail.astype(F32)
    return jnp.concatenate(
        [jnp.sum(tail[0:3], axis=0, keepdims=True), jnp.sum(tail[3:6], axis=0, keepdims=True)],
        axis=0,
    )


def encode_vectors(first, second):
    return jnp.concatenate(
        [*split_three(first), *split_three(second), jnp.zeros((2, first.shape[1]), BF16)], axis=0
    )


def split_norm(values):
    mean = jnp.mean(values, axis=-1, keepdims=True)
    spread = jnp.mean(values * values, axis=-1, keepdims=True) - mean * mean
    scaled = lax.rsqrt(spread + EPS)
    return (values - mean) * scaled, scaled


def norm_back(values, gain, upstream):
    normal, scaled = split_norm(values)
    inner = upstream * gain
    one = jnp.mean(inner, axis=-1, keepdims=True)
    two = jnp.mean(inner * normal, axis=-1, keepdims=True)
    back = scaled * (inner - one - normal * two)
    return (
        back,
        jnp.sum(upstream * normal, axis=0, keepdims=True),
        jnp.sum(upstream, axis=0, keepdims=True),
    )


def vector_rows(first, second):
    return jnp.concatenate([first, second, jnp.zeros((6, first.shape[1]), F32)], axis=0)


def folded_vectors(mat, gain, bias):
    rows = jnp.concatenate(
        [*split_three(gain), *split_three(bias), jnp.zeros((10, gain.shape[1]), BF16)], axis=0
    )
    folded = nt(rows, mat)
    return encode_vectors(
        jnp.sum(folded[0:3], axis=0, keepdims=True), jnp.sum(folded[3:6], axis=0, keepdims=True)
    )


def core_swap(x):
    return lax.ppermute(x, "section", [(0, 1), (1, 0)])


def x_swap(x):
    return lax.ppermute(x, "mp", [(i, i ^ 1) for i in range(LANES)])


def y_swap(x):
    return lax.ppermute(x, "mp", [(i, i ^ 2) for i in range(LANES)])


def gather_rows(own):
    far = x_swap(own)
    return own, core_swap(own), far, core_swap(far)


def pair_sum_body(first, second, out):
    rows = out.shape[0] - TAIL
    out[:rows] = (first[:rows].astype(F32) + second[:rows].astype(F32)).astype(BF16)
    half = rows + TAIL // 2
    out[rows:half] = encode(decode(first[rows:half]) + decode(second[rows:half]))
    folded = decode_vectors(first[half:]) + decode_vectors(second[half:])
    out[half:] = encode_vectors(folded[0:1], folded[1:2])


def pair_add_body(first, second, out):
    out[...] = (first[...].astype(F32) + second[...].astype(F32)).astype(BF16)


def pair_sum(far, far_mate):
    body = pair_sum_body if far.shape[0] % 256 else pair_add_body
    return call("pair_sum", body, [(far.shape, BF16)], [far, core_swap(far_mate)])[0]


def settle(own, mate, far, far_mate):
    sent = pair_sum(far, far_mate)
    return own, core_swap(mate), x_swap(sent)


def project_body(first, second, mat, out):
    size = first.shape[0]
    for place, piece in enumerate((first, second)):
        out[place * size : (place + 1) * size, :] = nn(piece[...], mat[:, :QKV]).astype(BF16)


def project(first, second, mat):
    count = 2 * first.shape[0]
    return call(
        "project",
        project_body,
        [((count, QKV), BF16)],
        [first, second, mat],
    )[0]


def split_heads(source, target, first, start, head_count):
    size = source.shape[0]
    for head in range(head_count):
        lanes = slice(first + head * HEAD_DIM, first + (head + 1) * HEAD_DIM)
        target[head, start : start + size, :] = source[:, lanes]


def attend_body(
    q_start, q_ref, near, far, labels, mat, gain, bias, o_ref, p_one, p_two, sum_ref, ks, vs
):
    head_count = QKV // (3 * HEAD_DIM)
    width = head_count * HEAD_DIM
    half = near.shape[0]
    for start, ref in ((0, near), (half, far)):
        split_heads(ref, ks, width, start, head_count)
        split_heads(ref, vs, 2 * width, start, head_count)
    out_mat = mat[:, QKV:]
    folded = folded_vectors(out_mat, gain[...], bias[...])
    size = half // 2
    key_labels = labels[0:1, :]
    for place, p_ref in enumerate((p_one, p_two)):
        rows = slice(place * size, (place + 1) * size)
        first = q_start + place * size
        allowed = to_columns(labels[:, first : first + size])[:, 0:1] == key_labels
        outs = []
        sums = []
        for head in range(head_count):
            query = q_ref[rows, head * HEAD_DIM : (head + 1) * HEAD_DIM]
            scores = jnp.where(allowed, nt(query, ks[head]), -1e30)
            peak = jnp.max(scores, axis=-1, keepdims=True)
            terms = jnp.exp2((scores - peak) * (SCALE * LOG2E))
            total = jnp.sum(terms, axis=-1, keepdims=True)
            outs.append(nn(terms.astype(BF16), vs[head]) / total)
            sums.append(peak * (SCALE * LOG2E) + jnp.log(total) * LOG2E)
        out = jnp.concatenate(outs, axis=1)
        o_ref[rows, :] = out
        lane = lax.broadcasted_iota(jnp.int32, (size, 128), 1)
        tile = jnp.zeros((size, 128), F32)
        for spot, column in enumerate(sums):
            tile = jnp.where(lane == spot, column, tile)
        sum_ref[rows, :] = tile
        p_ref[:size] = nt((out * gain[...]).astype(BF16), out_mat).astype(BF16)
        stats = to_rows(
            jnp.sum(out, axis=-1, keepdims=True), jnp.sum(out * out, axis=-1, keepdims=True)
        )
        p_ref[size : size + TAIL // 2] = encode(stats)
        p_ref[size + TAIL // 2 :] = folded


def attend(q_start, queries, near, far, labels, mat, gain, bias, after=()):
    count, keys = queries.shape[0], 2 * near.shape[0]
    heads = QKV // (3 * HEAD_DIM)
    width = heads * HEAD_DIM
    by_head = pltpu.VMEM((heads, keys, HEAD_DIM), BF16)
    payload = ((count // 2 + TAIL, D), BF16)
    return call(
        "attend",
        partial(attend_body, q_start),
        [((count, width), F32), payload, payload, ((count, 128), F32)],
        [queries, near, far, labels, mat, gain, bias],
        [by_head, by_head],
        after,
        work(4e9, 1),
    )


def attend_back_body(
    near, far, do_near, do_far, sum_near, sum_far, labels, near_out, far_out,
    qs, ks, vs, grads, dqs, dks, dvs, sums,
):
    head_count = QKV // (3 * HEAD_DIM)
    width = head_count * HEAD_DIM
    half = near.shape[0]
    for start, ref, grad in ((0, near, do_near), (half, far, do_far)):
        split_heads(ref, qs, 0, start, head_count)
        split_heads(ref, ks, width, start, head_count)
        split_heads(ref, vs, 2 * width, start, head_count)
        split_heads(grad, grads, 0, start, head_count)
    sums[:half] = sum_near[...]
    sums[half:] = sum_far[...]
    dks[...] = jnp.zeros_like(dks)
    dvs[...] = jnp.zeros_like(dvs)
    key_labels = labels[0:1, :]
    size = half // 2

    def block(index, carry):
        rows = pl.ds(pl.multiple_of(index * size, size), size)
        allowed = to_columns(labels[:, rows])[:, 0:1] == key_labels
        for head in range(head_count):
            query, grad = qs[head, rows, :], grads[head, rows, :]
            scores = jnp.where(allowed, nt(query, ks[head]), -1e30)
            prob = jnp.exp2(scores * (SCALE * LOG2E) - sums[rows, head : head + 1])
            prob_grad = nt(grad, vs[head])
            delta = jnp.sum(prob * prob_grad, axis=-1, keepdims=True)
            score_grad = (prob * (prob_grad - delta)).astype(BF16)
            dqs[head, rows, :] = nn(score_grad, ks[head]) * SCALE
            dks[head] += tn(query, score_grad)
            dvs[head] += tn(grad, prob.astype(BF16))
        return carry

    lax.fori_loop(0, 4, block, 0)
    for start, out in ((0, near_out), (half, far_out)):
        rows = slice(start, start + half)
        heads = range(head_count)
        out[...] = jnp.concatenate(
            [dqs[head, rows, :].astype(BF16) for head in heads]
            + [(dks[head, :, rows].T * SCALE).astype(BF16) for head in heads]
            + [dvs[head, :, rows].T.astype(BF16) for head in heads],
            axis=1,
        )


def attend_back(near, far, do_near, do_far, sum_near, sum_far, labels, after=()):
    half, width = do_near.shape
    keys = 2 * half
    heads = width // HEAD_DIM
    by_head = pltpu.VMEM((heads, keys, HEAD_DIM), BF16)
    turned = pltpu.VMEM((heads, HEAD_DIM, keys), F32)
    return call(
        "attend_back",
        attend_back_body,
        [(near.shape, BF16)] * 2,
        [near, far, do_near, do_far, sum_near, sum_far, labels],
        [by_head] * 4
        + [pltpu.VMEM((heads, keys, HEAD_DIM), F32), turned, turned, pltpu.VMEM((keys, 128), F32)],
        after,
        work(1.4e10, 1),
    )


def gelu_parts(x):
    spread = 0.5 + 0.5 * lax.erf(x * SQRT_HALF)
    return x * spread, spread


def feed_body(with_back, *refs):
    if with_back:
        one, two, back_one, back_two, mat, gain, bias, f_ref, p_one, p_two, s_ref = refs
    else:
        one, two, mat, gain, bias, f_ref, p_one, p_two = refs
        back_one = back_two = s_ref = None
    size = one.shape[0]
    up, down = mat.at[:, :UNITS], mat.at[:, UNITS:]
    folded = folded_vectors(down[...], gain[...], bias[...])
    for place, (piece, p_ref, back) in enumerate(((one, p_one, back_one), (two, p_two, back_two))):
        rows = slice(place * size, (place + 1) * size)
        pre = nn(piece[...], up[...])
        f_ref[rows, :] = pre
        act, _ = gelu_parts(pre)
        p_ref[:size] = nt((act * gain[...]).astype(BF16), down[...]).astype(BF16)
        columns = [
            jnp.sum(act, axis=-1, keepdims=True),
            jnp.sum(act * act, axis=-1, keepdims=True),
        ]
        p_ref[size : size + TAIL // 2] = encode(to_rows(*columns))
        p_ref[size + TAIL // 2 :] = folded
        if with_back:
            inner = nn(back[...], down[...]) * gain[...]
            columns.append(jnp.sum(inner, axis=-1, keepdims=True))
            columns.append(jnp.sum(inner * act, axis=-1, keepdims=True))
            s_ref[8 * place : 8 * place + 8, :] = to_rows(*columns)


def feed(pieces, backs, mat, gain, bias, after=()):
    size = pieces[0].shape[0]
    outs = [((2 * size, UNITS), F32)] + [((size + TAIL, D), BF16)] * 2
    if backs:
        outs += [((16, size), F32)]
    return call(
        "feed",
        partial(feed_body, bool(backs)),
        outs,
        [*pieces, *backs, mat, gain, bias],
        after=after,
    )


def feed_back_body(first_piece, *refs):
    if first_piece is not None:
        one, two, s_ref, *refs = refs
    else:
        one, two, *refs = refs
        s_ref = None
    f_ref, gain, bias, mat, df_ref, n_ref, p_one, p_two, vec_ref = refs
    up, down = mat.at[:, :UNITS], mat.at[:, UNITS:]
    size = p_one.shape[0]
    gain_grad = jnp.zeros((1, UNITS), F32)
    bias_grad = jnp.zeros((1, UNITS), F32)
    for place, (piece, p_ref) in enumerate(((one, p_one), (two, p_two))):
        rows = slice(place * size, (place + 1) * size)
        upstream = nn(piece[:size], down[...])
        pre = f_ref[rows, :]
        if first_piece is not None:
            start = 8 * (first_piece + place)
            stats = s_ref[start : start + 8, :]
        else:
            stats = decode(piece[size : size + TAIL // 2])
        columns = to_columns(stats)
        mean, scaled, first, second = (columns[:, i : i + 1] for i in range(4))
        act, spread = gelu_parts(pre)
        normal = (act - mean) * scaled
        act_grad = scaled * (upstream * gain[...] - first - normal * second)
        slope = spread + pre * (jnp.exp(-0.5 * pre * pre) * INV_SQRT_2PI)
        pre_grad = (act_grad * slope).astype(BF16)
        df_ref[rows, :] = pre_grad
        n_ref[rows, :] = (normal * gain[...] + bias[...]).astype(BF16)
        p_ref[...] = nt(pre_grad, up[...]).astype(BF16)
        gain_grad += jnp.sum(upstream * normal, axis=0, keepdims=True)
        bias_grad += jnp.sum(upstream, axis=0, keepdims=True)
    vec_ref[...] = vector_rows(gain_grad, bias_grad)


def feed_back(pieces, stats, first_piece, pre, gain, bias, mat, after=()):
    count = pre.shape[0]
    size = count // 2
    return call(
        "feed_back",
        partial(feed_back_body, first_piece if stats else None),
        [((count, UNITS), BF16)] * 2 + [((size, D), BF16)] * 2 + [((8, UNITS), F32)],
        [*pieces, *stats, pre, gain, bias, mat],
        after=after,
    )


def stats_pack_body(near, far, out):
    out[:16] = near[...]
    out[16:] = far[...]


def stats_near_body(stats, got, out):
    for place in range(4):
        other = 8 * (place ^ 1)
        out[8 * place : 8 * place + 8] = stats[8 * place : 8 * place + 8] + got[other : other + 8]


def stats_far_body(stats, got, out):
    for place in range(4):
        other = 8 * (place ^ 2)
        rows = slice(8 * place, 8 * place + 8)
        total = (stats[rows] + got[other : other + 8]) * (1.0 / FF)
        mean, one = total[0:1], total[2:3]
        scaled = lax.rsqrt(total[1:2] - mean * mean + EPS)
        two = scaled * (total[3:4] - mean * one)
        out[rows] = jnp.concatenate([mean, scaled, one, two, total[4:8]], axis=0)


def group_stats(near, far):
    shape = [((32, near.shape[1]), F32)]
    stats = call("stats_pack", stats_pack_body, shape, [near, far])[0]
    stats = call("stats_near", stats_near_body, shape, [stats, core_swap(stats)])[0]
    return call("stats_far", stats_far_body, shape, [stats, x_swap(stats)])[0]


def grads_body(pieces, halves, size, *refs):
    *refs, out = refs
    place = 0
    column = 0
    for left_count, right_count in zip(pieces, halves):
        left = refs[place : place + left_count]
        right = refs[place + left_count : place + left_count + right_count]
        place += left_count + right_count
        width = right[0].shape[1]
        per = left_count // right_count
        total = None
        for index, piece in enumerate(left):
            start = (index % per) * size
            term = tn(piece[:size], right[index // per][start : start + size, :])
            total = term if total is None else total + term
        out[:, column : column + width] = total.astype(BF16)
        column += width


def grads_of(*pairs, after=()):
    pieces = tuple(len(left) for left, _ in pairs)
    halves = tuple(len(right) for _, right in pairs)
    size = pairs[0][1][0].shape[0] // 2
    args = [item for left, right in pairs for item in (*left, *right)]
    width = sum(right[0].shape[1] for _, right in pairs)
    return call(
        "grads",
        partial(grads_body, pieces, halves, size),
        [((D, width), BF16)],
        args,
        after=after,
    )[0]


def inner_back_body(one, two, o_ref, gain, bias, mat, do_ref, u_ref, vec_ref):
    size = o_ref.shape[0] // 2
    gain_grad = jnp.zeros((1, o_ref.shape[1]), F32)
    bias_grad = jnp.zeros((1, o_ref.shape[1]), F32)
    out_mat = mat[:, QKV:]
    for place, piece in enumerate((one, two)):
        rows = slice(place * size, (place + 1) * size)
        upstream = nn(piece[:size], out_mat)
        columns = to_columns(decode(piece[size : size + TAIL // 2]))
        mean, scaled, first, second = (columns[:, i : i + 1] for i in range(4))
        normal = (o_ref[rows, :] - mean) * scaled
        back = scaled * (upstream * gain[...] - first - normal * second)
        do_ref[rows, :] = back.astype(BF16)
        u_ref[rows, :] = (normal * gain[...] + bias[...]).astype(BF16)
        gain_grad += jnp.sum(upstream * normal, axis=0, keepdims=True)
        bias_grad += jnp.sum(upstream, axis=0, keepdims=True)
    vec_ref[...] = vector_rows(gain_grad, bias_grad)


def inner_back(pieces, out, gain, bias, mat, after=()):
    count, width = out.shape
    return call(
        "inner_back",
        inner_back_body,
        [((count, width), BF16)] * 2 + [((8, width), F32)],
        [*pieces, out, gain, bias, mat],
        after=after,
    )


def encode_rows(values):
    return jnp.concatenate(split_three(values), axis=0)


def decode_rows(rows):
    rows = rows.astype(F32)
    count = rows.shape[0] // 3
    return rows[:count] + rows[count : 2 * count] + rows[2 * count :]


def unproject_body(rows, mat, one, two, gain, bias, p_one, p_two, vec_ref):
    size = p_one.shape[0]
    gain_grad = jnp.zeros((1, D), F32)
    bias_grad = jnp.zeros((1, D), F32)
    for place, (piece, p_ref) in enumerate(((one, p_one), (two, p_two))):
        term = nt(rows[place * size : (place + 1) * size], mat[:, :QKV])
        p_ref[...] = term.astype(BF16)
        gain_grad += jnp.sum(term * (piece[...].astype(F32) - bias[...]), axis=0, keepdims=True)
        bias_grad += jnp.sum(term, axis=0, keepdims=True)
    vec_ref[...] = vector_rows(gain_grad / gain[...], bias_grad)


def unproject(rows, mat, pieces, gain, bias, after=()):
    count = rows.shape[0]
    return call(
        "unproject",
        unproject_body,
        [((count // 2, D), BF16)] * 2 + [((8, D), F32)],
        [rows, mat, *pieces, gain, bias],
        after=after,
    )


def vectors_body(*refs):
    *items, out = refs
    out[...] = jnp.zeros_like(out)
    out[0:2, :] = items[0][0:2, :] + items[1][0:2, :]
    for place, item in enumerate(items[2:]):
        first = 2 * place + 2
        out[first : first + 2, : item.shape[1]] = item[0:2, :]


def vectors_of(items):
    return call("vectors", vectors_body, [((16, D), F32)], list(items))[0]


def outer_body(own, got, out):
    out[...] = own[0:8] + got[0:8]


def all_body(own, outer, got, out):
    out[0:8] = outer[...] + got[...]
    out[8:] = own[8:]


def encode_rows(values):
    return jnp.concatenate(split_three(values), axis=0)


def decode_rows(rows):
    rows = rows.astype(F32)
    count = rows.shape[0] // 3
    return rows[:count] + rows[count : 2 * count] + rows[2 * count :]


def branch_of(own, mate, far, feature_count):
    rows = own.shape[0] - TAIL
    half = rows + TAIL // 2
    pieces = (own, mate, far)
    product = sum(piece[:rows].astype(F32) for piece in pieces)
    stats = sum(decode(piece[rows:half]) for piece in pieces) / feature_count
    folded = sum(decode_vectors(piece[half:]) for piece in pieces)
    mean = stats[0:1]
    scaled = lax.rsqrt(stats[1:2] - mean * mean + EPS)
    kept = jnp.concatenate([mean, scaled, jnp.zeros((6, rows), F32)], axis=0)
    columns = to_columns(kept)
    branch = columns[:, 1:2] * (product - columns[:, 0:1] * folded[0:1])
    return branch, folded[1:2], folded[0:1], kept


def after_attend_body(x_ref, own, mate, far, gain, bias, x2_ref, z_ref, h_ref, fold_ref, kept_ref):
    branch, shift, folded, kept = branch_of(own, mate, far, D)
    mid = x_ref[...].astype(F32) + branch + shift
    x2_ref[...] = mid
    z_ref[...] = branch
    normal, _ = split_norm(mid)
    h_ref[...] = (normal * gain[...] + bias[...]).astype(BF16)
    fold_ref[...] = jnp.broadcast_to(folded, fold_ref.shape)
    kept_ref[...] = kept


def after_attend(x, pieces, gain, bias, after=()):
    rows = x.shape[0]
    return call(
        "after_attend",
        after_attend_body,
        [((rows, D), F32), ((rows, D), F32), ((rows, D), BF16), ((8, D), F32), ((8, rows), F32)],
        [x, *pieces, gain, bias],
        after=after,
    )


def mask_column(labels, rows):
    return (to_columns(labels[:, :rows])[:, 0:1] >= 0).astype(F32)


def after_feed_body(x2, own, mate, far, labels, gain, bias, y_ref, z_ref, h_ref, fold_ref, kept_ref):
    branch, shift, folded, kept = branch_of(own, mate, far, FF)
    out = (mask_column(labels, x2.shape[0]) * (x2[...] + branch + shift)).astype(BF16)
    y_ref[...] = out
    z_ref[...] = branch
    normal, _ = split_norm(out.astype(F32))
    h_ref[...] = (normal * gain[...] + bias[...]).astype(BF16)
    fold_ref[...] = jnp.broadcast_to(folded, fold_ref.shape)
    kept_ref[...] = kept


def after_feed(x2, pieces, labels, gain, bias, after=()):
    rows = x2.shape[0]
    return call(
        "after_feed",
        after_feed_body,
        [((rows, D), BF16), ((rows, D), F32), ((rows, D), BF16), ((8, D), F32), ((8, rows), F32)],
        [x2, *pieces, labels, gain, bias],
        after=after,
    )


def finish_feed_body(x2, own, mate, far, labels, y_ref):
    branch, shift, _, _ = branch_of(own, mate, far, FF)
    y_ref[...] = (mask_column(labels, x2.shape[0]) * (x2[...] + branch + shift)).astype(BF16)


def finish_feed(x2, pieces, labels):
    return call("finish_feed", finish_feed_body, [(x2.shape, BF16)], [x2, *pieces, labels])[0]


def payload_of(grad, branch, folded, kept, feature_count):
    sent = grad.astype(BF16)
    wide = sent.astype(F32)
    means = to_rows(
        jnp.sum(wide * folded, axis=-1, keepdims=True),
        jnp.sum(wide * branch, axis=-1, keepdims=True),
    )
    stats = jnp.concatenate([kept[0:2], means[0:2] / feature_count, kept[4:8]], axis=0)
    tail = jnp.concatenate([encode(stats), jnp.zeros((TAIL // 2, D), BF16)], axis=0)
    return jnp.concatenate([sent, tail], axis=0)


def feed_norm_back_body(
    own, mate, far, g_ref, labels, x2, gain, branch, folded, kept, dx_ref, out_ref, vec_ref
):
    upstream = own[...].astype(F32) + mate[...].astype(F32) + far[...].astype(F32)
    back, gain_grad, bias_grad = norm_back(x2[...], gain[...], upstream)
    total = mask_column(labels, x2.shape[0]) * g_ref[...].astype(F32) + back
    dx_ref[...] = total
    out_ref[...] = payload_of(total, branch[...], folded[0:1], kept[...], D)
    vec_ref[...] = vector_rows(gain_grad, bias_grad)


def feed_norm_back(pieces, grad, labels, x2, gain, branch, folded, kept, after=()):
    rows = x2.shape[0]
    return call(
        "feed_norm_back",
        feed_norm_back_body,
        [((rows, D), F32), ((rows + TAIL, D), BF16), ((8, D), F32)],
        [*pieces, grad, labels, x2, gain, branch, folded, kept],
        after=after,
    )


def first_norm_back_body(has_next, *refs):
    own, mate, far, dx2, x_ref, gain, *refs = refs
    upstream = own[...].astype(F32) + mate[...].astype(F32) + far[...].astype(F32)
    back, _, _ = norm_back(x_ref[...].astype(F32), gain[...], upstream)
    total = (dx2[...] + back).astype(BF16)
    if has_next:
        labels, branch, folded, kept, g_ref, out_ref = refs
        masked = mask_column(labels, dx2.shape[0]) * total.astype(F32)
        out_ref[...] = payload_of(masked, branch[...], folded[0:1], kept[...], FF)
    else:
        (g_ref,) = refs
    g_ref[...] = total


def first_norm_back(pieces, dx2, x, gain, following=(), after=()):
    rows = x.shape[0]
    outs = [((rows, D), BF16)]
    if following:
        outs.append(((rows + TAIL, D), BF16))
    return call(
        "first_norm_back",
        partial(first_norm_back_body, bool(following)),
        outs,
        [*pieces, dx2, x, gain, *following],
        after=after,
    )


def in_hbm(x):
    return pltpu.with_memory_space_constraint(x, pltpu.HBM)


def fetch_all(refs, held, sems):
    copies = [
        pltpu.make_async_copy(ref, spot, sems.at[place])
        for place, (ref, spot) in enumerate(zip(refs, held))
    ]
    for copy in copies:
        copy.start()
    for copy in copies:
        copy.wait()


def first_block_body(
    flags, query, key, value, output, down, up, out, down_out, swap_out, *scratch
):
    *held, sems = scratch
    fetch_all((query, key, value, output, down, up), held, sems)
    width = query.shape[1]
    for place, ref in enumerate(held[:3]):
        out[:, place * width : (place + 1) * width] = ref[...]
    out[:, 3 * width :] = held[3][...].T
    down_out[...] = held[4][...]
    lower = jnp.full((1, D), flags[2], jnp.int32) == 0
    swap_out[:, :D] = jnp.where(lower, down_out[...], held[5][...])
    swap_out[:, D:] = out[:, : D // 2]


def first_block(flags, *blocks):
    return pl.pallas_call(
        first_block_body,
        out_shape=tuple(
            jax.ShapeDtypeStruct((blocks[0].shape[0], width), BF16)
            for width in (D, D, 3 * D // 2)
        ),
        in_specs=[SMEM] + [HBM] * 6,
        out_specs=(VMEM,) * 3,
        scratch_shapes=[pltpu.VMEM(block.shape, BF16) for block in blocks]
        + [pltpu.SemaphoreType.DMA((6,))],
        compiler_params=PARAMS,
        name="first_block",
    )(flags, *map(in_hbm, blocks))


def beside_body(one, two, out):
    width = one.shape[1]
    out[:, :width] = one[...]
    out[:, width:] = two[...]


def beside(one, two, after=()):
    rows, width = one.shape
    return call("beside", beside_body, [((rows, 2 * width), BF16)], [one, two], after=after)[0]


def entry_body(flags, inputs, cotangent, out, far_out, own_in, own_grad, sems):
    size = own_in.shape[0]

    def rows_of(micro):
        return pl.ds(pl.multiple_of(micro * size, size), size)

    across, far, own = rows_of(1 - flags[3]), rows_of(flags[2]), rows_of(flags[3])
    copies = [
        pltpu.make_async_copy(source, target, sems.at[place])
        for place, (source, target) in enumerate(
            (
                (inputs.at[across], out.at[:size]),
                (cotangent.at[across], out.at[size:]),
                (inputs.at[far], far_out.at[:size]),
                (cotangent.at[far], far_out.at[size:]),
                (inputs.at[own], own_in),
                (cotangent.at[own], own_grad),
            )
        )
    ]
    for copy in copies:
        copy.start()
    for copy in copies:
        copy.wait()


def entry(flags, inputs, cotangent):
    rows = inputs.shape[0]
    shapes = [rows, rows, rows // 2, rows // 2]
    return pl.pallas_call(
        entry_body,
        out_shape=tuple(jax.ShapeDtypeStruct((count, D), BF16) for count in shapes),
        in_specs=[SMEM, HBM, HBM],
        out_specs=(VMEM,) * 4,
        scratch_shapes=[pltpu.SemaphoreType.DMA((6,))],
        compiler_params=PARAMS,
        name="entry",
    )(flags, in_hbm(inputs), in_hbm(cotangent))


def enter_body(
    flags, own_in, own_grad, got, labels, gain, bias, x_ref, g_ref, top_ref, h_ref
):
    size, width = x_ref.shape
    here = jnp.full((1, width), flags[0], jnp.int32) == 1
    own = jnp.where(here, own_in[...], got[:size])
    grad = jnp.where(here, own_grad[...], got[size:])
    x_ref[...] = own
    g_ref[...] = grad
    top_ref[...] = (mask_column(labels, size) * grad.astype(F32)).astype(BF16)
    normal, _ = split_norm(own.astype(F32))
    h_ref[...] = (normal * gain[...] + bias[...]).astype(BF16)


def enter(flags, own_in, own_grad, got, labels, gain, bias):
    return call(
        "enter",
        enter_body,
        [(own_in.shape, BF16)] * 4,
        [flags, own_in, own_grad, got, labels, gain, bias],
    )


def enter_far_body(got, labels, gain, bias, top_ref, h_ref):
    size = top_ref.shape[0]
    mask = (to_columns(labels[:, 2 * size : 3 * size])[:, 0:1] >= 0).astype(F32)
    top_ref[...] = (mask * got[size:].astype(F32)).astype(BF16)
    normal, _ = split_norm(got[:size].astype(F32))
    h_ref[...] = (normal * gain[...] + bias[...]).astype(BF16)


def enter_far(got, labels, gain, bias):
    rows = got.shape[0] // 2
    return call(
        "enter_far", enter_far_body, [((rows, D), BF16)] * 2, [got, labels, gain, bias]
    )


def pack_body(*refs):
    *items, out = refs
    size = items[0].shape[0]
    for place, item in enumerate(items):
        out[place * size : (place + 1) * size, :] = item[...]


def pack(items):
    rows, width = items[0].shape
    return call("pack", pack_body, [((len(items) * rows, width), BF16)], list(items))[0]


def unpack_body(flags, own, sent, got_own, got_sent, y_ref, g_ref):
    size = y_ref.shape[0] // 2
    width = y_ref.shape[1]
    here = jnp.full((1, width), flags[0], jnp.int32) == 1
    rows = pl.ds(pl.multiple_of(flags[2] * size, size), size)
    first = pl.ds(pl.multiple_of(flags[3] * size, size), size)
    second = pl.ds(pl.multiple_of((1 - flags[3]) * size, size), size)
    last = slice(2 * size, 3 * size)
    y_ref[first, :] = jnp.where(here, own[rows, :], got_own[rows, :])
    y_ref[second, :] = jnp.where(here, sent[rows, :], got_sent[rows, :])
    g_ref[first, :] = jnp.where(here, own[last, :], got_own[last, :])
    g_ref[second, :] = jnp.where(here, sent[last, :], got_sent[last, :])


def unpack(flags, own, sent, got_own, got_sent):
    rows = 2 * own.shape[0] // 3
    return call(
        "unpack",
        unpack_body,
        [((rows, own.shape[1]), BF16)] * 2,
        [flags, own, sent, got_own, got_sent],
    )


def halve_body(with_vectors, flags, block, across, *refs):
    if with_vectors:
        vectors, got, kept, sent, vec_ref = refs
        total = vectors[...] + got[...]
        vec_ref[...] = total
    else:
        kept, sent = refs
    size = kept.shape[0] // 2
    for place, (out, step) in enumerate(((kept, 0), (kept, 2), (sent, 1), (sent, 3))):
        rows = pl.ds(pl.multiple_of((flags[1] ^ step) * size, size), size)
        spot = slice((place % 2) * size, (place % 2 + 1) * size)
        out[spot] = (block[rows, :].astype(F32) + across[rows, :].astype(F32)).astype(BF16)
    if with_vectors:
        sent[2 * size :] = encode_rows(total)


def halve(flags, block, across, vectors=(), after=(), cost=None):
    rows, width = block.shape
    outs = [((rows // 2, width), BF16)] * 2
    if vectors:
        outs = [outs[0], ((rows // 2 + 48, width), BF16), (vectors[0].shape, F32)]
    return call(
        "halve",
        partial(halve_body, bool(vectors)),
        outs,
        [flags, block, across, *vectors],
        after=after,
        cost=cost,
    )


def quarter_body(with_vectors, kept, got, *refs):
    if with_vectors:
        vectors, own, sent, vec_ref = refs
    else:
        own, sent = refs
    size = own.shape[0]
    for place, out in enumerate((own, sent)):
        rows = slice(place * size, (place + 1) * size)
        out[:size] = (kept[rows].astype(F32) + got[rows].astype(F32)).astype(BF16)
    if with_vectors:
        total = vectors[...] + decode_rows(got[2 * size :])
        vec_ref[...] = total
        sent[size:] = encode_rows(total)


def quarter(kept, got, vectors=(), after=()):
    rows, width = kept.shape
    outs = [((rows // 2, width), BF16)] * 2
    if vectors:
        outs = [outs[0], ((rows // 2 + 48, width), BF16), (vectors[0].shape, F32)]
    return call(
        "quarter",
        partial(quarter_body, bool(vectors)),
        outs,
        [kept, got, *vectors],
        after=after,
    )


def last_body(kept, got, vectors, out, vec_ref):
    size = kept.shape[0]
    out[...] = (kept[...].astype(F32) + got[:size].astype(F32)).astype(BF16)
    vec_ref[...] = vectors[...] + decode_rows(got[size:])


def last_of(kept, got, vectors, after=()):
    outs = [(kept.shape, BF16), (vectors.shape, F32)]
    return call("last", last_body, outs, [kept, got, vectors], after=after)


def total_body(*refs):
    *parts, out = refs
    out[...] = sum(part[...].astype(F32) for part in parts).astype(out.dtype)


def total_of(parts, kind=BF16, after=(), cost=None):
    shape = [(parts[0].shape, kind)]
    return call("total", total_body, shape, list(parts), after=after, cost=cost)[0]


def layers_of(flags, lower, lower_got, upper, upper_got):
    width = lower.shape[1]
    here = jnp.full((1, width), flags[0], jnp.int32) == 1
    first = jnp.full((1, width), flags[2], jnp.int32) == 0
    one = jnp.where(here, lower[...], lower_got[...])
    two = jnp.where(here, upper[...], upper_got[...])
    return jnp.where(first, one, two).astype(F32)


def final_first_body(
    flags, lower, lower_got, upper, upper_got, vec, vec_got, q_ref, k_ref, v_ref, o_ref, vec_ref
):
    width = q_ref.shape[1]
    total = layers_of(flags, lower, lower_got, upper, upper_got)
    for place, ref in enumerate((q_ref, k_ref, v_ref)):
        ref[...] = total[:, place * width : (place + 1) * width]
    o_ref[...] = total[:, 3 * width :].T
    here = jnp.full((1, D), flags[0], jnp.int32) == 1
    vec_ref[...] = jnp.where(here, vec[...], vec_got[...])


def final_first(flags, lower, upper, vectors):
    rows, width = lower[0].shape[0], D // LANES
    return call(
        "final_first",
        final_first_body,
        [((rows, width), F32)] * 3 + [((width, rows), F32), ((16, D), F32)],
        [flags, *lower, *upper, *vectors],
    )


def final_second_body(flags, lower, lower_got, upper, upper_got, up_ref, down_ref):
    total = layers_of(flags, lower, lower_got, upper, upper_got)
    up_ref[...] = total[:, :UNITS]
    down_ref[...] = total[:, UNITS:]


def final_second(flags, lower, upper):
    rows = lower[0].shape[0]
    return call(
        "final_second",
        final_second_body,
        [((rows, UNITS), F32)] * 2,
        [flags, *lower, *upper],
    )


def merge_body(flags, one, two, upper, out):
    size, width = one.shape
    first = jnp.full((1, width), flags[2], jnp.int32) == 0
    for place, ref in enumerate((one, two)):
        rows = slice(place * size, (place + 1) * size)
        out[rows] = jnp.where(first, ref[...], upper[rows])


def merge(flags, one, two, upper):
    return call("merge", merge_body, [(upper.shape, BF16)], [flags, one, two, upper])[0]


def choose_body(flags, one, two, out):
    first = jnp.full((1, out.shape[1]), flags[2], jnp.int32) == 0
    out[...] = jnp.where(first, one[...], two[...])


def choose(flags, one, two, after=()):
    return call("choose", choose_body, [(one.shape, one.dtype)], [flags, one, two], after=after)[0]


def join_body(flags, own, got, out):
    half = own.shape[1]
    first = jnp.full((1, half), flags[2], jnp.int32) == 0
    out[:, :half] = jnp.where(first, own[...], got[...])
    out[:, half:] = jnp.where(first, got[...], own[...])


def join(flags, own, got, after=()):
    rows, half = own.shape
    return call(
        "join", join_body, [((rows, 2 * half), BF16)], [flags, own, got], after=after
    )[0]


def hold_body(ref, out):
    out[...] = ref[...]


def hold(x, after):
    return call("hold", hold_body, [(x.shape, x.dtype)], [x], after=after)[0]


def assemble_body(count, flags, *refs):
    beside, across, out = refs[:count], refs[count:-1], refs[-1]
    size = beside[0].shape[0]
    width = out.shape[1]
    near = jnp.full((1, width), flags[0], jnp.int32) == 1
    for step in range(count):
        rows = pl.ds(pl.multiple_of((flags[1] ^ step) * size, size), size)
        out[rows, :] = jnp.where(near, beside[step][...], across[step][...])


def assemble(flags, beside, across, after=()):
    count, (size, width) = len(beside), beside[0].shape
    return call(
        "assemble",
        partial(assemble_body, count),
        [((count * size, width), BF16)],
        [flags, *beside, *across],
        after=after,
    )[0]


def early_block_body(flags, up, got, first, out):
    width = up.shape[1]
    lower = jnp.full((1, width), flags[2], jnp.int32) == 0
    out[:, :width] = jnp.where(lower, up[...], got[:, :width])
    half = first.shape[1] // 2
    lower = jnp.full((1, half), flags[2], jnp.int32) == 0
    out[:, width:] = jnp.where(lower, got[:, width:], first[:, half:])


def early_block(flags, up, got, first, after=()):
    rows, width = up.shape
    return call(
        "early_block",
        early_block_body,
        [((rows, width + first.shape[1] // 2), BF16)],
        [flags, up, got, first],
        after=after,
    )[0]


def late_block_body(flags, got, down, out):
    width = down.shape[1]
    lower = jnp.full((1, width), flags[2], jnp.int32) == 0
    out[...] = jnp.where(lower, got[:, :width], down[...])


def late_block(flags, got, down, after=()):
    return call(
        "late_block", late_block_body, [(down.shape, BF16)], [flags, got, down], after=after
    )[0]


def parts_body(ref, one, two):
    width = one.shape[1]
    one[...] = ref[:, :width]
    two[...] = ref[:, width:]


def parts_of(x, width, after):
    rows, whole = x.shape
    shapes = [((rows, width), x.dtype), ((rows, whole - width), x.dtype)]
    return call("parts", parts_body, shapes, [x], after=after)


def pick_body(flags, beside, across, out):
    near = jnp.full((1, out.shape[1]), flags[0], jnp.int32) == 1
    out[...] = jnp.where(near, beside[...], across[...])


def pick(flags, beside, across, cost=None):
    return call(
        "pick", pick_body, [(beside.shape, BF16)], [flags, beside, across], cost=cost
    )[0]


def on_device(
    inputs,
    cotangent,
    doc_ids,
    norm_gain,
    norm_bias,
    w_query,
    w_key,
    w_value,
    inner_gain,
    inner_bias,
    w_output,
    feed_gain,
    feed_bias,
    w_up,
    middle_gain,
    middle_bias,
    w_down,
):
    core = lax.axis_index("section")
    lane = lax.axis_index("mp")
    lane_x = lane % 2
    lane_y = lane // 2
    count = lax.axis_size("dp")
    slice_len = inputs.shape[0] // MICRO
    rank = 2 * core + lane_x
    crossing = [(s * 4 + r, s * 4 + (r ^ 2)) for s in range(2) for r in range(4) if s == r // 2]
    returning = [(s * 4 + r, s * 4 + (r ^ 2)) for s in range(2) for r in range(4) if s != r // 2]

    def by_core(first, second):
        return jnp.where(core == 0, first, second)

    def placed(array, layer):
        return [
            lax.ppermute(
                array,
                BOTH,
                [(s * 4 + 2 * m + x, layer * 4 + 2 * s + x) for s in range(2) for x in range(2)],
            )
            for m in range(MICRO)
        ]

    label_grid = lax.dynamic_index_in_dim(
        doc_ids.reshape(LANES, MICRO, slice_len), lane_y, 1, keepdims=False
    )
    order = (rank, 2 * (1 - core) + lane_x, rank ^ 1, 2 * (1 - core) + (1 - lane_x))
    labels = jnp.concatenate(
        [lax.dynamic_index_in_dim(label_grid, item, 0, keepdims=False) for item in order]
    )
    labels = jnp.broadcast_to(labels.astype(F32)[None], (8, LANES * slice_len))

    place = lax.axis_index("dp")
    flags = jnp.stack([core == lane_y, place, core, lane_y]).astype(jnp.int32)

    def line_pairs(step):
        return [
            ((r // 2 * count + i) * LANES + r, (r // 2 * count + (i ^ step)) * LANES + r)
            for i in range(count)
            for r in range(LANES)
        ]

    def along_line(block, step):
        return lax.ppermute(block, ("section", "dp", "mp"), line_pairs(step))

    first, down_block, swapped = first_block(
        flags, w_query[0], w_key[0], w_value[0], w_output[0], w_down[0].T, w_up[0]
    )
    up_block = w_up[0]

    def along_dp(block):
        return lax.all_gather(block, "dp", axis=0, tiled=True)

    def fetched(line, hook=()):
        whole = join(flags, line, core_swap(line), after=hook)
        return whole, lax.ppermute(whole, BOTH, crossing)

    outer_own = jnp.concatenate([norm_gain, norm_bias, feed_gain, feed_bias], axis=0)
    outer_other = core_swap(outer_own)
    split_own = jnp.concatenate([inner_gain, inner_bias, middle_gain, middle_bias], axis=1)
    split_far = y_swap(split_own)
    split_kept = jnp.where(lane_y == core, split_own, split_far)
    split_other = core_swap(jnp.where(lane_y == core, split_far, split_own))

    def small_of(outer, split):
        width = D // LANES
        return (
            [outer[i : i + 1] for i in range(4)],
            [
                split[:, :width],
                split[:, width : 2 * width],
                split[:, 2 * width : 2 * width + UNITS],
                split[:, 2 * width + UNITS :],
            ],
        )

    lower_outer, lower_split = small_of(
        by_core(outer_own, outer_other), by_core(split_kept, split_other)
    )
    upper_outer, upper_split = small_of(
        by_core(outer_other, outer_own), by_core(split_other, split_kept)
    )

    def gather_around(own, near_of, far=None, after=()):
        if far is None:
            far = x_swap(own)
        mate = core_swap(own)
        near = near_of([own, mate])
        far = hold(far, after=[near[0], *after])
        return (own, mate, far, core_swap(far)), near

    def attention(x, h, first, outer, split, hooks, far=None):
        pieces, (near,) = gather_around(
            h, lambda rows: [project(*rows, first)], far, after=hooks[2]
        )
        far = project(pieces[2], pieces[3], first)
        half = 2 * slice_len
        o_far, p_far, p_far_mate, sum_far = attend(
            half, far, near, far, labels, first, split[0], split[1]
        )
        sent = pair_sum(p_far, p_far_mate)
        hooks[0](p_far)
        o_near, p_own, p_mate, sum_near = attend(
            0, near, near, far, labels, first, split[0], split[1], after=[sent]
        )
        arrived = hold(x_swap(sent), after=[p_own])
        terms = (p_own, core_swap(p_mate), arrived)
        x2, branch, h2, folded, kept = after_attend(x, terms, outer[2], outer[3], after=hooks[1])
        state = (pieces, near, far, o_near, o_far, sum_near, sum_far, x, x2, branch, folded, kept)
        return x2, h2, state, arrived

    def attention_back(grad, sums, state, first, outer, split, following, hooks):
        pieces, near, far, o_near, o_far, sum_near, sum_far, x, x2, branch, folded, kept = state
        dx2, sent, feed_vec = feed_norm_back(
            sums, grad, labels, x2, outer[2], branch, folded, kept, after=hooks[0]
        )
        block = hooks[3](sent)
        backs, (do_near, u_near, vec_near) = gather_around(
            sent, lambda rows: inner_back(rows, o_near, split[0], split[1], first), after=block
        )
        do_far, u_far, vec_far = inner_back(backs[2:], o_far, split[0], split[1], first)
        dq_near, dq_far = attend_back(
            near, far, do_near, do_far, sum_near, sum_far, labels, after=hooks[1]
        )
        norm = (outer[0], outer[1])
        p_far, p_far_mate, norm_far = unproject(
            dq_far, first, pieces[2:], *norm, after=hooks[4](dq_far)
        )
        sent = pair_sum(p_far, p_far_mate)
        p_own, p_mate, norm_near = unproject(
            dq_near, first, pieces[:2], *norm, after=[sent, *hooks[5]()]
        )
        mat_grad = grads_of(
            (pieces, (dq_near, dq_far)), (backs, (u_near, u_far)), after=[sent]
        )
        terms = (p_own, core_swap(p_mate), hold(x_swap(sent), after=[p_own, mat_grad]))
        result = first_norm_back(
            terms, dx2, x, outer[0], following, after=hooks[2](mat_grad)
        )
        return result, vec_near + vec_far, feed_vec, (norm_near, norm_far)

    def reduce_across(block):
        across = lax.ppermute(block, BOTH, returning)
        if count != 4:
            total = total_of([block, across])
            return [lax.psum_scatter(total, "dp", scatter_dimension=0, tiled=True)]
        return block, across

    def reduce_near(pair, after=(), cost=None):
        if count != 4:
            return pair
        kept, sent = halve(flags, *pair, after=after, cost=cost)
        return kept, along_line(sent, 1)

    def reduce_far(pair, after=()):
        if count != 4:
            return pair
        kept, sent = quarter(*pair, after=after)
        return kept, along_line(sent, 2)

    def reduce_end(pair, after=(), cost=None):
        total = total_of(pair, after=after, cost=cost) if count == 4 else pair[0]
        return total, core_swap(total)

    sent, far_sent, own_in, own_grad = entry(flags, inputs, cotangent)
    got = lax.ppermute(sent, BOTH, crossing)
    far_got = lax.ppermute(
        far_sent,
        BOTH,
        [
            (s * LANES + r, s * LANES + (r ^ 1) if s == r // 2 else (r // 2) * LANES + (r ^ 3))
            for s in range(2)
            for r in range(LANES)
        ],
    )
    lower_in, upstream, masked, h = enter(
        flags, own_in, own_grad, got, labels, lower_outer[0], lower_outer[1]
    )
    masked_far, far = enter_far(far_got, labels, lower_outer[0], lower_outer[1])
    top = (masked, core_swap(masked), masked_far, core_swap(masked_far))
    moved = choose(flags, first, core_swap(first))
    if count == 4:
        pieces = [moved] + [along_line(moved, step) for step in range(1, count)]
        lower_first = assemble(
            flags, pieces, [lax.ppermute(piece, BOTH, crossing) for piece in pieces], after=[far]
        )
    else:
        pieces = [along_dp(moved)]
        lower_first = pick(flags, pieces[0], lax.ppermute(pieces[0], BOTH, crossing))
    got = core_swap(swapped)
    early_line = along_dp(early_block(flags, up_block, got, first, after=[pieces[-1], own_in]))
    late_line = along_dp(late_block(flags, got, down_block))
    coming = {}

    def early_matrices(last):
        coming["second"], coming["first"] = parts_of(early_line, UNITS, [last])

    x2, h2, lower_state, arrived = attention(
        lower_in, h, lower_first, lower_outer, lower_split, (early_matrices, (), ()), far
    )
    lower_second_whole, lower_second_across = fetched(coming["second"])
    lower_second = pick(flags, lower_second_whole, lower_second_across)
    upper_first_whole, upper_first_across = fetched(coming["first"], [h2])
    upper_first = pick(flags, upper_first_whole, upper_first_across)
    lower_pieces, (f_near, p_own, p_mate) = gather_around(
        h2, lambda rows: feed(rows, (), lower_second, *lower_split[2:])
    )
    f_far, p_far, p_far_mate = feed(lower_pieces[2:], (), lower_second, *lower_split[2:])
    lower_pre = (f_near, f_far)
    sent = pair_sum(p_far, p_far_mate)
    upper_second_whole, upper_second_across = fetched(hold(late_line, after=[sent]))
    upper_second = pick(flags, upper_second_whole, upper_second_across, work(1e10, 1))
    arrived = hold(x_swap(sent), after=[upper_second_whole])
    terms = (p_own, core_swap(p_mate), arrived)
    lower_out, lower_branch, h, lower_folded, lower_kept = after_feed(
        x2, terms, labels, upper_outer[0], upper_outer[1]
    )
    x2, h2, upper_state, _ = attention(
        lower_out,
        h,
        upper_first,
        upper_outer,
        upper_split,
        (lambda last: None, (), [upper_second_whole]),
    )
    upper_pieces, (f_near, p_own, p_mate, near_stats) = gather_around(
        h2, lambda rows: feed(rows, top[:2], upper_second, *upper_split[2:])
    )
    f_far, p_far, p_far_mate, far_stats = feed(
        upper_pieces[2:], top[2:], upper_second, *upper_split[2:]
    )
    upper_pre = (f_near, f_far)

    stats = group_stats(near_stats, far_stats)
    df_far, n_far, q_far, q_far_mate, vec_far = feed_back(
        top[2:], [stats], 2, upper_pre[1], *upper_split[2:], upper_second
    )
    sent = pair_sum(q_far, q_far_mate)
    df_near, n_near, q_own, q_mate, vec_near = feed_back(
        top[:2], [stats], 0, upper_pre[0], *upper_split[2:], upper_second, after=[sent]
    )
    upper_middle = vec_near + vec_far
    sums = (q_own, core_swap(q_mate), hold(x_swap(sent), after=[q_own]))
    ended = pair_sum(p_far, p_far_mate)
    ended_far = []

    def ended_hook(last):
        ended_far.append(hold(x_swap(ended), after=[last]))
        return ended_far

    following = (labels, lower_branch, lower_folded, lower_kept)
    pairs = {}

    def upper_second_grads(after):
        block = grads_of(
            (upper_pieces, (df_near, df_far)), (top, (n_near, n_far)), after=[after]
        )
        pairs["second"] = reduce_near(reduce_across(block), cost=work(9e9, 1))
        return [block]

    def upper_hook(item):
        pairs["upper"] = reduce_across(item)
        return [item]

    (upper_grad, sent), upper_inner, upper_feed, upper_norm = attention_back(
        upstream,
        sums,
        upper_state,
        upper_first,
        upper_outer,
        upper_split,
        following,
        ((), [ended], upper_hook, upper_second_grads, ended_hook, lambda: ()),
    )

    upper_out = finish_feed(x2, (p_own, core_swap(p_mate), ended_far[0]), labels)
    own = pack([lower_out, upper_out, upper_grad])
    swapped = lax.ppermute(own, BOTH, returning)
    upper_second_pair = reduce_far(pairs["second"], [own])
    upper_first_pair = reduce_near(pairs["upper"])
    backs, (df_near, n_near, q_own, q_mate, vec_near) = gather_around(
        sent,
        lambda rows: feed_back(
            rows, (), 0, lower_pre[0], *lower_split[2:], lower_second, after=[own]
        ),
        after=upper_first_pair[:1],
    )
    df_far, n_far, q_far, q_far_mate, vec_far = feed_back(
        backs[2:],
        (),
        2,
        lower_pre[1],
        *lower_split[2:],
        lower_second,
        after=[upper_second_pair[0]],
    )
    lower_middle = vec_near + vec_far
    sent = pair_sum(q_far, q_far_mate)
    sums = (q_own, core_swap(q_mate), x_swap(sent))

    def lower_second_grads(after):
        block = grads_of(
            (lower_pieces, (df_near, df_far)), (backs, (n_near, n_far)), after=[after]
        )
        pairs["second"] = reduce_across(block)
        return [block]

    upper_first_pair = reduce_far(upper_first_pair, after=[q_far])

    layer_outputs, upper_held = unpack(
        flags, own, swapped, core_swap(own), core_swap(swapped)
    )

    def lower_hook(item):
        pairs["lower"] = reduce_across(item)
        pairs["second"] = reduce_near(pairs["second"], after=[item])
        return [item]

    def upper_ended(last):
        pairs["ended"] = reduce_end(upper_second_pair, after=[last])
        pairs["first"] = reduce_end(upper_first_pair, after=[last])
        return [pairs["ended"][0], pairs["first"][0]]

    (lower_grad,), lower_inner, lower_feed, lower_norm = attention_back(
        upper_grad,
        sums,
        lower_state,
        lower_first,
        lower_outer,
        lower_split,
        (),
        (
            [upper_first_pair[0]],
            [layer_outputs],
            lower_hook,
            lower_second_grads,
            upper_ended,
            lambda: (),
        ),
    )
    vectors = vectors_of(
        [*lower_norm, lower_feed, upper_norm[0] + upper_norm[1], upper_feed]
        + [lower_middle, upper_middle, lower_inner, upper_inner]
    )
    outer = call("outer", outer_body, [((8, D), F32)], [vectors, core_swap(vectors)])[0]
    vectors = call("all", all_body, [((16, D), F32)], [vectors, outer, x_swap(outer)])[0]
    lower_held = placed(lower_grad, 0)
    input_grads = merge(flags, *lower_held, upper_held)
    if count == 4:
        first_kept, sent, vectors = halve(
            flags,
            *pairs["lower"],
            (vectors, y_swap(vectors)),
            after=[pairs["first"][0], lower_grad],
        )
        got = along_line(sent, 1)
        lower_second_sum = reduce_end(reduce_far(pairs["second"], after=[first_kept]))
        grad_up, grad_down = final_second(flags, lower_second_sum, pairs["ended"])
        kept, sent, vectors = quarter(first_kept, got, [vectors])
        ended, vectors = last_of(
            kept, along_line(sent, 2), vectors, after=[input_grads, grad_up]
        )
    else:
        vectors = lax.psum(vectors + y_swap(vectors), "dp")
        ended = pairs["lower"][0]
        lower_second_sum = reduce_end(pairs["second"])
        grad_up, grad_down = final_second(flags, lower_second_sum, pairs["ended"])
    grad_query, grad_key, grad_value, grad_output, vectors = final_first(
        flags, (ended, core_swap(ended)), pairs["first"], (vectors, core_swap(vectors))
    )

    def part(rows, start, size):
        rows = lax.dynamic_slice(rows, (core * rows.shape[0] // 2, start), (rows.shape[0] // 2, size))
        return [rows[i : i + 1] for i in range(rows.shape[0])]

    width = D // LANES
    size = D // count // LANES
    outer = part(vectors[:8], (place * LANES + lane) * size, size)
    middle = part(vectors[8:12], place * (UNITS // count), UNITS // count)
    inner = part(vectors[12:], place * (width // count), width // count)
    return (
        layer_outputs[None],
        input_grads[None],
        outer[0],
        outer[1],
        grad_query[None],
        grad_key[None],
        grad_value[None],
        inner[0],
        inner[1],
        grad_output[None],
        outer[2],
        outer[3],
        grad_up[None],
        middle[0],
        middle[1],
        grad_down.T[None],
    )


def solution(mesh):
    placed = (
        P(("dp", "mp"), None),
        P(("dp", "mp"), None),
        P("dp"),
        P("section", None),
        P("section", None),
        P("section", "dp", "mp"),
        P("section", "dp", "mp"),
        P("section", "dp", "mp"),
        P("section", "mp"),
        P("section", "mp"),
        P("section", "mp", "dp"),
        P("section", None),
        P("section", None),
        P("section", "dp", "mp"),
        P("section", "mp"),
        P("section", "mp"),
        P("section", "mp", "dp"),
    )
    return jax.shard_map(
        on_device,
        mesh=mesh,
        in_specs=placed,
        out_specs=(
            P("section", ("dp", "mp"), None),
            P("section", ("dp", "mp"), None),
            P("section", ("dp", "mp")),
            P("section", ("dp", "mp")),
            P("section", "dp", "mp"),
            P("section", "dp", "mp"),
            P("section", "dp", "mp"),
            P("section", ("mp", "dp")),
            P("section", ("mp", "dp")),
            P("section", "mp", "dp"),
            P("section", ("dp", "mp")),
            P("section", ("dp", "mp")),
            P("section", "dp", "mp"),
            P("section", ("mp", "dp")),
            P("section", ("mp", "dp")),
            P("section", "mp", "dp"),
        ),
        check_vma=False,
    )
```
